32 devices in a mesh: dp: 4 (over x, core), row: 4 (over z), col: 2 (over y).
Axes of the slice: x: 2, y: 2, z: 4, core: 2. Of those that a mesh axis runs over, the one named last changes fastest.
Arguments:
- tokens: bfloat16 [32768, 1024], P(('dp', 'col'), 'row'), may hold values from -7.6 to 7.6
- segments: int32 [32768], P(('dp', 'row')), may hold values from 0 to 17, as said below
- w_query: bfloat16 [1024, 1024], P('row', 'col'), may hold values from -0.1875 to 0.1875
- b_query: bfloat16 [1024], P('col'), may hold values from -3 to 3
- w_key: bfloat16 [1024, 1024], P('row', 'col'), may hold values from -0.1875 to 0.1875
- w_value: bfloat16 [1024, 1024], P('row', 'col'), may hold values from -0.1875 to 0.1875
- b_value: bfloat16 [1024], P('col'), may hold values from -3 to 3
- w_out: bfloat16 [1024, 1024], P('col', 'row'), may hold values from -1 to 1
- b_out: bfloat16 [1024], P('row'), may hold values from -2 to 2
- norm1_gain: bfloat16 [1024], P('row'), may hold values from 0.099609375 to 1.8984375
- norm1_shift: bfloat16 [1024], P('row'), may hold values from -2 to 2
- w_up: bfloat16 [1024, 4096], P('row', 'col'), may hold values from -0.1875 to 0.1875
- b_up: bfloat16 [4096], P('col'), may hold values from -2 to 2
- w_down: bfloat16 [4096, 1024], P('col', 'row'), may hold values from -0.09375 to 0.09375
- b_down: bfloat16 [1024], P('row'), may hold values from -2 to 2
- norm2_gain: bfloat16 [1024], P('row'), may hold values from 0.099609375 to 1.8984375
- norm2_shift: bfloat16 [1024], P('row'), may hold values from -2 to 2
- cotangent: bfloat16 [32768, 1024], P(('dp', 'col'), 'row'), may hold values from -6 to 6
Outputs:
- output: bfloat16 [32768, 1024], P(('dp', 'col'), 'row')
- tokens_grad: bfloat16 [32768, 1024], P(('dp', 'col'), 'row')
- w_query_grad: float32 [1024, 1024], P('row', 'col')
- b_query_grad: float32 [1024], P('col')
- w_key_grad: float32 [1024, 1024], P('row', 'col')
- w_value_grad: float32 [1024, 1024], P('row', 'col')
- b_value_grad: float32 [1024], P('col')
- w_out_grad: float32 [1024, 1024], P('col', 'row')
- b_out_grad: float32 [1024], P('row')
- norm1_gain_grad: float32 [1024], P('row')
- norm1_shift_grad: float32 [1024], P('row')
- w_up_grad: float32 [1024, 4096], P('row', 'col')
- b_up_grad: float32 [4096], P('col')
- w_down_grad: float32 [4096, 1024], P('col', 'row')
- b_down_grad: float32 [1024], P('row')
- norm2_gain_grad: float32 [1024], P('row')
- norm2_shift_grad: float32 [1024], P('row')
The draws below stay inside these ranges and needn't reach their ends.
Inputs may be any that keep to these rules, and one draw needn't show every extreme that they name: `segments`: each sequence of 1024 tokens holds documents numbered 1, 2, 3 in order, each of 60 to 800 tokens, then padding numbered 0; the last token of every sequence is padding; some sequence holds (1024 - 1) // 60 documents.
All inputs are finite; a program needn't handle non-finite values.
Results may differ from the reference program's by a relative error of at most 0.015.
The reference program's roundings to bfloat16 on the way count: a program that leaves them out, or rounds other values in their place, can miss the bound.
Values may be sent and summed in bfloat16 or wider, within the bound.
A program may use at most 320 MiB of HBM per device.

```python
import math
import jax
import jax.numpy as jnp
from jax import lax

D = 1024
H = 16
HD = 64
FF = 4096
SEQ = 1024
DOC_MIN = 60
DOC_MAX = 800
TOKENS = 32768


def draw_tokens(key, part):
    key = jax.random.fold_in(key, 5)
    column = jnp.arange(D, dtype=jnp.float32) / D
    spread = 0.6 + 1.2 * column
    values = jnp.clip(jax.random.normal(key, (TOKENS, D), jnp.float32), -4.0, 4.0) * spread
    return values.astype(jnp.bfloat16)


def draw_segments(key, part):
    key = jax.random.fold_in(key, 17)
    key_len, key_pick = jax.random.split(key)
    seq_count = TOKENS // SEQ
    doc_slots = SEQ // DOC_MIN + 1
    lengths = jax.random.randint(key_len, (seq_count, doc_slots), DOC_MIN, DOC_MAX + 1)
    chosen = jax.random.randint(key_pick, (), 0, seq_count)
    seq_index = jnp.arange(seq_count, dtype=jnp.int32)[:, None]
    lengths = jnp.where(seq_index == chosen, DOC_MIN, lengths)
    doc_ends = jnp.cumsum(lengths, axis=1)
    position = jnp.arange(SEQ, dtype=jnp.int32)
    number = jnp.sum((doc_ends[:, None, :] <= position[None, :, None]).astype(jnp.int32), axis=2) + 1
    complete = jnp.sum((doc_ends <= SEQ - 1).astype(jnp.int32), axis=1)
    return jnp.where(number <= complete[:, None], number, 0).astype(jnp.int32).reshape(TOKENS)


def block_scale(stream_key, extent, pieces, least, top_value):
    level = 1.0
    for axis_at, parts in pieces:
        heights = jax.random.uniform(jax.random.fold_in(jax.random.fold_in(stream_key, 6), axis_at), (parts,), jnp.float32, least / len(pieces), top_value / len(pieces))
        level = level * jnp.repeat(jnp.exp(heights), extent[axis_at] // parts).reshape((-1,) + (1,) * (len(extent) - 1 - axis_at))
    return level


def bell_draw(key, extent, width, reach, cuts=(), kind=jnp.bfloat16):
    array = jax.random.normal(key, extent, jnp.float32) * width
    if len(cuts) > 0:
        array = block_scale(key, extent, cuts, -0.22, 0.18) * array
    return jnp.clip(array, min=-reach, max=reach).astype(kind)


def setup_inputs(seed: int = 0) -> dict:
    key_of = jax.random.split(jax.random.key(seed), 19)
    return {
        "tokens": draw_tokens(jax.random.fold_in(key_of[18], 71), 0),
        "segments": draw_segments(jax.random.fold_in(key_of[18], 71), 0),
        "w_query": bell_draw(key_of[2], (D, D), D ** -0.5, 0.1875, ((0, 4), (1, 2))),
        "b_query": bell_draw(key_of[3], (D,), 0.5, 3.0, ((0, 2),)),
        "w_key": bell_draw(key_of[4], (D, D), D ** -0.5, 0.1875, ((0, 4), (1, 2))),
        "w_value": bell_draw(key_of[5], (D, D), D ** -0.5, 0.1875, ((0, 4), (1, 2))),
        "b_value": bell_draw(key_of[6], (D,), 0.5, 3.0, ((0, 2),)),
        "w_out": bell_draw(key_of[7], (D, D), (D // 32) ** -0.5, 1.0, ((0, 2), (1, 4))),
        "b_out": bell_draw(key_of[8], (D,), 0.3, 2.0, ((0, 4),)),
        "norm1_gain": jnp.clip(1.0 + 0.18 * jax.random.normal(key_of[9], (D,), jnp.float32), 0.099609375, 1.8984375).astype(jnp.bfloat16),
        "norm1_shift": bell_draw(key_of[10], (D,), 0.3, 2.0, ((0, 4),)),
        "w_up": bell_draw(key_of[11], (D, FF), D ** -0.5, 0.1875, ((0, 4), (1, 2))),
        "b_up": bell_draw(key_of[12], (FF,), 0.3, 2.0, ((0, 2),)),
        "w_down": bell_draw(key_of[13], (FF, D), FF ** -0.5, 0.09375, ((0, 2), (1, 4))),
        "b_down": bell_draw(key_of[14], (D,), 0.3, 2.0, ((0, 4),)),
        "norm2_gain": jnp.clip(1.0 + 0.18 * jax.random.normal(key_of[15], (D,), jnp.float32), 0.099609375, 1.8984375).astype(jnp.bfloat16),
        "norm2_shift": bell_draw(key_of[16], (D,), 0.3, 2.0, ((0, 4),)),
        "cotangent": bell_draw(key_of[17], (TOKENS, D), 1.0, 6.0, ((0, 8), (1, 4))),
    }


@jax.custom_vjp
def low(v):
    return lax.optimization_barrier(v.astype(jnp.bfloat16)).astype(jnp.float32)

@jax.custom_vjp
def low_back(v):
    return v

def low_keep(v):
    return (low(v), None)

def low_pass(kept, grad):
    return (grad,)

def back_keep(v):
    return (v, None)

def back_low(kept, grad):
    return (low(grad),)
low.defvjp(low_keep, low_pass)
low_back.defvjp(back_keep, back_low)
NORM_EPS = 1e-05
PRECISE = lax.Precision.HIGHEST

def matmul(left, right):
    return jnp.dot(left, right, precision=PRECISE, preferred_element_type=jnp.float32)

def layer_norm(residual, norm_gain, norm_shift):
    row_mean = lax.optimization_barrier(jnp.mean(residual, axis=-1, keepdims=True))
    variance = lax.optimization_barrier(jnp.mean(residual * residual, axis=-1, keepdims=True)) - row_mean * row_mean
    return (residual - row_mean) * lax.rsqrt(variance + NORM_EPS) * norm_gain + norm_shift

def attend_block(source):
    queries, key_heads, values, segment_ids = source
    position = jnp.arange(SEQ)
    same_doc = (segment_ids[:, :, None] == segment_ids[:, None, :]) & (segment_ids[:, None, :] != 0)
    allowed = same_doc | (position[:, None] == position[None, :])[None]
    raw_scores = jnp.einsum('gqhd,gkhd->ghqk', queries, key_heads, precision=PRECISE) * HD ** (-0.5)
    scores = low_back(jnp.where(allowed[:, None], raw_scores, -1000000000.0))
    top_score = lax.optimization_barrier(jnp.max(scores, axis=-1, keepdims=True))
    exp_scores = jnp.exp(scores - top_score)
    soft_weights = exp_scores / lax.optimization_barrier(jnp.sum(exp_scores, axis=-1, keepdims=True))
    return jnp.einsum('ghqk,gkhd->gqhd', low(soft_weights), values, precision=PRECISE)

def forward(tokens, w_query, b_query, w_key, w_value, b_value, w_out, b_out, norm1_gain, norm1_shift, w_up, b_up, w_down, b_down, norm2_gain, norm2_shift, segments):
    queries = low(low_back(matmul(tokens, w_query) + b_query))
    key_heads = low(low_back(matmul(tokens, w_key)))
    values = low(low_back(matmul(tokens, w_value) + b_value))
    seq_count = TOKENS // SEQ
    group_size = math.gcd(seq_count, max(1, 4096 // SEQ))
    layout = (seq_count // group_size, group_size, SEQ, H, HD)
    attended = lax.map(jax.checkpoint(attend_block), (queries.reshape(layout), key_heads.reshape(layout), values.reshape(layout), segments.reshape(layout[:3])))
    attended = low(low_back(attended.reshape(TOKENS, D)))
    attn_out = low_back(matmul(attended, w_out) + b_out)
    hidden = layer_norm(tokens + attn_out, norm1_gain, norm1_shift)
    pre_act = low_back(matmul(low(hidden), w_up) + b_up)
    active = low(jax.nn.gelu(pre_act, approximate=False))
    fed = low_back(matmul(active, w_down) + b_down)
    return layer_norm(hidden + fed, norm2_gain, norm2_shift)

def reference(tokens, segments, w_query, b_query, w_key, w_value, b_value, w_out, b_out, norm1_gain, norm1_shift, w_up, b_up, w_down, b_down, norm2_gain, norm2_shift, cotangent):
    floats = tuple((argument.astype(jnp.float32) for argument in (tokens, w_query, b_query, w_key, w_value, b_value, w_out, b_out, norm1_gain, norm1_shift, w_up, b_up, w_down, b_down, norm2_gain, norm2_shift)))
    output, pullback = jax.vjp(lambda *params: forward(*params, segments), *floats)
    gradients = pullback(cotangent.astype(jnp.float32))
    return (output.astype(jnp.bfloat16), gradients[0].astype(jnp.bfloat16), gradients[1], gradients[2], gradients[3], gradients[4], gradients[5], gradients[6], gradients[7], gradients[8], gradients[9], gradients[10], gradients[11], gradients[12], gradients[13], gradients[14], gradients[15])
```

```python
import math

import jax
import jax.numpy as jnp
from jax import lax
from jax.experimental import pallas as pl
from jax.experimental.pallas import tpu as pltpu
from jax.sharding import PartitionSpec as P

HD = 64
SEQ = 1024
WIDTH = 1024
TOKENS = 32768
NORM_EPS = 1e-05
BF = jnp.bfloat16
F32 = jnp.float32
NEG = -1e30
QB = 256


def mm(a, b):
    return jnp.dot(a, b, preferred_element_type=F32)


def mm_t(a, b):
    return lax.dot_general(a, b, (((1,), (1,)), ((), ())), preferred_element_type=F32)


def tmm(a, b):
    return lax.dot_general(a, b, (((0,), (0,)), ((), ())), preferred_element_type=F32)


def gelu_exact(v):
    return jax.nn.gelu(v, approximate=False)


def attend_fwd_kernel(qkv_ref, seg_col_ref, seg_row_ref, o_ref, p_ref, linv_ref):
    lane = lax.broadcasted_iota(jnp.int32, (QB, 128), 1)
    seg_row = seg_row_ref[...]
    k = qkv_ref[:, 128:256]
    v = qkv_ref[:, 256:384]
    scale = HD ** (-0.5) * math.log2(math.e)
    for i in range(SEQ // QB):
        rows = slice(i * QB, (i + 1) * QB)
        q = qkv_ref[rows, 0:128]
        seg_col = seg_col_ref[rows, :]
        outs = []
        for h in range(2):
            mine = (lane < HD) if h == 0 else (lane >= HD)
            qm = jnp.where(mine, q, jnp.zeros_like(q))
            s = mm_t(qm, k)
            s = jnp.where(seg_col == seg_row, s * scale, NEG)
            top = jnp.max(s, axis=1, keepdims=True)
            p = jnp.exp2(s - top)
            total = jnp.sum(p, axis=1, keepdims=True)
            pb = p.astype(BF)
            p_ref[h, rows, :] = pb
            inv = 1.0 / total
            outs.append((mm(pb, v) * inv, jnp.broadcast_to(inv, (QB, 128))))
        o_ref[rows, :] = jnp.where(lane < HD, outs[0][0], outs[1][0]).astype(BF)
        linv_ref[rows, :] = jnp.where(lane < HD, outs[0][1], outs[1][1])


def attend_bwd_kernel(qkv_ref, do_ref, o_ref, linv_ref, p_ref, g_ref, ds_ref):
    lane = lax.broadcasted_iota(jnp.int32, (SEQ, 128), 1)
    q = qkv_ref[:, 0:128]
    k = qkv_ref[:, 128:256]
    v = qkv_ref[:, 256:384]
    scale = HD ** (-0.5)
    do = do_ref[...].astype(F32) * linv_ref[...]
    prod = do * o_ref[...].astype(F32)
    dob = do.astype(BF)
    qt = jnp.transpose(q.astype(F32)).astype(BF)
    dot_ = jnp.transpose(do).astype(BF)
    dq = []
    dkt = []
    dvt = []
    for h in range(2):
        mine = (lane < HD) if h == 0 else (lane >= HD)
        delta = jnp.sum(jnp.where(mine, prod, 0.0), axis=1, keepdims=True)
        dom = jnp.where(mine, dob, jnp.zeros_like(dob))
        for i in range(SEQ // QB):
            rows = slice(i * QB, (i + 1) * QB)
            dp = mm_t(dom[rows], v)
            ds = p_ref[h, rows, :].astype(F32) * (dp - delta[rows])
            ds_ref[h, rows, :] = ds.astype(BF)
        feats = slice(h * HD, (h + 1) * HD)
        dq.append(mm(ds_ref[h], k))
        dkt.append(mm(qt[feats], ds_ref[h]))
        dvt.append(mm(dot_[feats], p_ref[h]))
    g_ref[:, 0:128] = (jnp.where(lane < HD, dq[0], dq[1]) * scale).astype(BF)
    g_ref[:, 128:256] = (jnp.transpose(jnp.concatenate(dkt, 0)) * scale).astype(BF)
    g_ref[:, 256:384] = jnp.transpose(jnp.concatenate(dvt, 0)).astype(BF)


VMEM_LIMIT = 48 * 1024 * 1024


def attend_fwd(qkv, seg_col, seg_row):
    slots = qkv.shape[1] // 384
    return pl.pallas_call(
        attend_fwd_kernel,
        grid=(slots,),
        in_specs=[
            pl.BlockSpec((SEQ, 384), lambda j: (0, j)),
            pl.BlockSpec((SEQ, 1), lambda j: (0, 0)),
            pl.BlockSpec((1, SEQ), lambda j: (0, 0)),
        ],
        out_specs=[
            pl.BlockSpec((SEQ, 128), lambda j: (0, j)),
            pl.BlockSpec((2, SEQ, SEQ), lambda j: (j, 0, 0)),
            pl.BlockSpec((SEQ, 128), lambda j: (0, j)),
        ],
        out_shape=[
            jax.ShapeDtypeStruct((SEQ, slots * 128), BF),
            jax.ShapeDtypeStruct((slots * 2, SEQ, SEQ), BF),
            jax.ShapeDtypeStruct((SEQ, slots * 128), F32),
        ],
        compiler_params=pltpu.CompilerParams(vmem_limit_bytes=VMEM_LIMIT),
        cost_estimate=pl.CostEstimate(
            flops=slots * 2 * 4 * SEQ * SEQ * 256,
            bytes_accessed=slots * 5 * SEQ * SEQ,
            transcendentals=slots * 2 * SEQ * SEQ,
        ),
        name="attend_fwd",
    )(qkv, seg_col, seg_row)


def attend_bwd(qkv, do, o, linv, p):
    slots = qkv.shape[1] // 384
    return pl.pallas_call(
        attend_bwd_kernel,
        grid=(slots,),
        in_specs=[
            pl.BlockSpec((SEQ, 384), lambda j: (0, j)),
            pl.BlockSpec((SEQ, 128), lambda j: (0, j)),
            pl.BlockSpec((SEQ, 128), lambda j: (0, j)),
            pl.BlockSpec((SEQ, 128), lambda j: (0, j)),
            pl.BlockSpec((2, SEQ, SEQ), lambda j: (j, 0, 0)),
        ],
        out_specs=pl.BlockSpec((SEQ, 384), lambda j: (0, j)),
        out_shape=jax.ShapeDtypeStruct((SEQ, slots * 384), BF),
        scratch_shapes=[pltpu.VMEM((2, SEQ, SEQ), BF)],
        compiler_params=pltpu.CompilerParams(vmem_limit_bytes=VMEM_LIMIT),
        cost_estimate=pl.CostEstimate(
            flops=slots * 2 * 8 * SEQ * SEQ * 256,
            bytes_accessed=slots * 6 * SEQ * SEQ,
            transcendentals=0,
        ),
        name="attend_bwd",
    )(qkv, do, o, linv, p)


class Ring:
    def __init__(self):
        self.r = lax.axis_index("row")
        self.c = lax.axis_index("col")
        self.d = lax.axis_index("dp")
        self.rows = lax.axis_size("row")

    def shift(self, v, s):
        n = self.rows
        return lax.ppermute(v, "row", [(i, (i + s) % n) for i in range(n)])

    def core(self, v):
        return lax.ppermute(v, "dp", [(i, i ^ 1) for i in range(4)])

    def x(self, v):
        return lax.ppermute(v, "dp", [(i, i ^ 2) for i in range(4)])

    def y(self, v):
        return lax.ppermute(v, "col", [(0, 1), (1, 0)])

    def gather(self, piece, axis):
        parts = [piece]
        for _ in range(self.rows - 1):
            parts.append(self.shift(parts[-1], 1))
        own = jnp.concatenate(parts, axis)
        from_x, from_y = self.x(own), self.y(own)
        half = own.shape[0] // 2
        diag = jnp.concatenate([self.y(from_x[:half]), self.x(from_y[half:])], 0)
        first = [own, from_x, from_y, diag]
        other = [self.core(v) for v in first]
        return [first[0], other[0], first[1], other[1], first[2], other[2], first[3], other[3]]

    def scatter(self, blocks, cut):
        kept = [blocks[0], blocks[2], blocks[4], blocks[6]]
        sent = [blocks[1], blocks[3], blocks[5], blocks[7]]
        own, to_x, to_y, diag = [
            (a.astype(F32) + self.core(b).astype(F32)).astype(BF) for a, b in zip(kept, sent)
        ]
        half = own.shape[0] // 2
        via_y = self.y(diag[:half])
        via_x = self.x(diag[half:])
        to_x = jnp.concatenate([to_x[:half] + via_y, to_x[half:]], 0)
        to_y = jnp.concatenate([to_y[:half], to_y[half:] + via_x], 0)
        total = (own.astype(F32) + self.x(to_x).astype(F32) + self.y(to_y).astype(F32)).astype(BF)
        parts = cut(total)
        acc = parts[1]
        for s in range(1, self.rows):
            got = self.shift(acc, 1)
            acc = (parts[(s + 1) % self.rows].astype(F32) + got.astype(F32)).astype(BF)
        pair = jnp.stack([acc, self.core(acc)])
        quarters = jnp.concatenate([pair, self.x(pair)], 0)
        return self.absolute(quarters)

    def absolute(self, quarters):
        a = jnp.where(self.d % 2 == 1, quarters[jnp.array([1, 0, 3, 2])], quarters)
        return jnp.where(self.d // 2 == 1, jnp.concatenate([a[2:], a[:2]], 0), a)


def layer_norm(residual, gain, shift):
    mean = jnp.mean(residual, axis=1, keepdims=True)
    variance = jnp.mean(residual * residual, axis=1, keepdims=True) - mean * mean
    inv = lax.rsqrt(variance + NORM_EPS)
    normed = (residual - mean) * inv
    return normed * gain + shift, normed, inv


def layer_norm_back(grad, normed, inv, gain):
    g = grad * gain
    mean_g = jnp.mean(g, axis=1, keepdims=True)
    mean_gn = jnp.mean(g * normed, axis=1, keepdims=True)
    return inv * (g - mean_g - normed * mean_gn), jnp.sum(grad * normed, axis=0), jnp.sum(grad, axis=0)


def quarter(v, d, axis):
    n = v.shape[axis] // 4
    return lax.dynamic_slice_in_dim(v, d * n, n, axis)


def whole_sequences(
    tokens, segments, w_query, b_query, w_key, w_value, b_value, w_out, b_out, norm1_gain, norm1_shift,
    w_up, b_up, w_down, b_down, norm2_gain, norm2_shift, cotangent,
):
    ring = Ring()
    r, c, d = ring.r, ring.c, ring.d
    R, C = lax.axis_size("row"), lax.axis_size("col")
    feat = tokens.shape[1]

    def inward(block):
        parts = []
        for s in range(R):
            piece = lax.dynamic_slice_in_dim(block, ((r + s) % R) * SEQ, SEQ, 0)
            parts.append(piece if s == 0 else ring.shift(piece, s))
        return jnp.concatenate(parts, 1)

    def outward(rows):
        whole = jnp.zeros((R * SEQ, feat), rows.dtype)
        for s in range(R):
            piece = rows[:, s * feat : (s + 1) * feat]
            if s:
                piece = ring.shift(piece, -s)
            whole = lax.dynamic_update_slice_in_dim(whole, piece, ((r + s) % R) * SEQ, 0)
        return whole

    pairs = []
    for row in range(R):
        for col in range(C):
            n = col * R + row
            pairs.append((n, row * C + col))
    seg = lax.ppermute(segments, ("row", "col"), pairs)
    seg = lax.dynamic_slice_in_dim(seg, ((c * R + r) % C) * SEQ, SEQ, 0)
    ids = jnp.where(seg == 0, -1 - jnp.arange(SEQ, dtype=jnp.int32), seg)
    seg_col, seg_row = ids[:, None], ids[None, :]

    x = inward(tokens)
    qkv_piece = jnp.concatenate([quarter(w, d, 1) for w in (w_query, w_key, w_value)], 1)
    w_qkv = jnp.concatenate(ring.gather(qkv_piece, 0), 1)
    wo = jnp.concatenate(ring.gather(quarter(w_out, d, 0), 1), 0)
    wu = jnp.concatenate(ring.gather(quarter(w_up, d, 1), 0), 1)
    wd = jnp.concatenate(ring.gather(quarter(w_down, d, 0), 1), 0)
    cot = inward(cotangent)

    feat_vec = jnp.stack([b_out, norm1_gain, norm1_shift, b_down, norm2_gain, norm2_shift])
    feat_all = jnp.concatenate([feat_vec] + [ring.shift(feat_vec, s) for s in range(1, R)], 1).astype(F32)
    bo, g1, s1, bd, g2, s2 = [feat_all[i] for i in range(6)]
    hq = b_query.shape[0] // 4
    unit = b_up.shape[0] // 4
    slot_vec = jnp.concatenate(
        [b_query.reshape(4, hq), jnp.zeros((4, hq), BF), b_value.reshape(4, hq), b_up.reshape(4, unit)], 1
    )
    slot_vec = ring.absolute(slot_vec)
    slot_vec = jnp.concatenate([slot_vec, ring.y(slot_vec)], 0).astype(F32)
    b_qkv = slot_vec[:, : 3 * hq].reshape(-1)
    bu = slot_vec[:, 3 * hq :].reshape(-1)

    qkv = (mm(x, w_qkv) + b_qkv).astype(BF)
    att, prob, linv = attend_fwd(qkv, seg_col, seg_row)
    hidden, normed1, inv1 = layer_norm(x.astype(F32) + mm(att, wo) + bo, g1, s1)
    hidden_low = hidden.astype(BF)
    pre = mm(hidden_low, wu) + bu
    act = gelu_exact(pre).astype(BF)
    fed = mm(act, wd) + bd
    output, normed2, inv2 = layer_norm(hidden + fed, g2, s2)
    out_block = outward(output.astype(BF))

    grad_r2, d_g2, d_s2 = layer_norm_back(cot.astype(F32), normed2, inv2, g2)
    grad_fed = grad_r2.astype(BF)
    dwd = tmm(act, grad_fed).astype(BF)
    grad_act = mm_t(grad_fed, wd)
    _, slope = jax.vjp(gelu_exact, pre)
    grad_pre = slope(grad_act)[0].astype(BF)
    dwu = tmm(hidden_low, grad_pre).astype(BF)
    grad_hidden = mm_t(grad_pre, wu) + grad_r2
    grad_r1, d_g1, d_s1 = layer_norm_back(grad_hidden, normed1, inv1, g1)
    grad_attn = grad_r1.astype(BF)
    dwo = tmm(att, grad_attn).astype(BF)
    grad_att = mm_t(grad_attn, wo).astype(BF)
    g_qkv = attend_bwd(qkv, grad_att, att, linv, prob)
    dwqkv = tmm(x, g_qkv).astype(BF)
    x_grad = (mm_t(g_qkv, w_qkv) + grad_r1).astype(BF)
    x_grad_block = outward(x_grad)

    def rows_of(v, n=8):
        k = v.shape[0] // n
        return [v[i * k : (i + 1) * k] for i in range(n)]

    def cols_of(v, n=8):
        k = v.shape[1] // n
        return [v[:, i * k : (i + 1) * k] for i in range(n)]

    def cut_rows(v):
        return rows_of(v, R)

    def cut_cols(v):
        return cols_of(v, R)

    sum_down = ring.scatter(rows_of(dwd), cut_cols)
    sum_up = ring.scatter(cols_of(dwu), cut_rows)
    sum_out = ring.scatter(rows_of(dwo), cut_cols)
    sum_qkv = ring.scatter(cols_of(dwqkv), cut_rows)
    w_down_grad = sum_down.astype(F32).reshape(w_down.shape)
    w_out_grad = sum_out.astype(F32).reshape(w_out.shape)
    w_up_grad = sum_up.astype(F32).transpose(1, 0, 2).reshape(w_up.shape)
    sum_qkv = sum_qkv.astype(F32).transpose(1, 0, 2)
    wq_grad, wk_grad, wv_grad = [sum_qkv[:, :, i * hq : (i + 1) * hq].reshape(w_query.shape) for i in range(3)]

    g32 = g_qkv.astype(F32)
    slot_grad = jnp.concatenate(
        [
            jnp.sum(g32, axis=0).reshape(8, 3 * hq),
            jnp.sum(grad_pre.astype(F32), axis=0).reshape(8, unit),
        ],
        1,
    )
    feat_grad = jnp.stack(
        [jnp.sum(grad_attn.astype(F32), axis=0), d_g1, d_s1, jnp.sum(grad_fed.astype(F32), axis=0), d_g2, d_s2]
    )
    slot_grad = slot_grad[0::2] + ring.core(slot_grad[1::2])
    slot_grad = slot_grad[0::2] + ring.x(slot_grad[1::2])
    slot_grad = slot_grad[0] + ring.y(slot_grad[1])
    for s in (1, 2):
        slot_grad = slot_grad + lax.ppermute(slot_grad, "row", [(i, i ^ s) for i in range(R)])
    pair = jnp.stack([slot_grad, ring.core(slot_grad)])
    slot_grad = ring.absolute(jnp.concatenate([pair, ring.x(pair)], 0))
    bq_grad = slot_grad[:, :hq].reshape(-1)
    bv_grad = slot_grad[:, 2 * hq : 3 * hq].reshape(-1)
    bu_grad = slot_grad[:, 3 * hq :].reshape(-1)
    feat_grad = feat_grad + ring.core(feat_grad)
    feat_grad = feat_grad + ring.x(feat_grad)
    feat_grad = feat_grad + ring.y(feat_grad)
    own = feat_grad[:, :feat]
    for s in range(1, R):
        own = own + ring.shift(feat_grad[:, s * feat : (s + 1) * feat], -s)
    return (
        out_block, x_grad_block, wq_grad, bq_grad, wk_grad, wv_grad, bv_grad, w_out_grad, own[0], own[1], own[2],
        w_up_grad, bu_grad, w_down_grad, own[3], own[4], own[5],
    )


def tokens_cols(source):
    return lax.all_gather(source, "col", axis=0, tiled=True)


def tokens_rows(source):
    return lax.all_gather(source, "row", axis=0, tiled=True)


def product(row_piece, weight, flipped):
    if flipped:
        return lax.dot_general(
            row_piece, weight, (((1,), (1,)), ((), ())), preferred_element_type=jnp.float32
        )
    return jnp.dot(row_piece, weight, preferred_element_type=jnp.float32)


def outer_sum(left, right):
    return lax.dot_general(
        left, right, (((0,), (0,)), ((), ())), preferred_element_type=jnp.float32
    )


def settle_rows(gathered, weight, flipped, own_rows):

    def product_term(first_row, row_count):
        return product(gathered, weight, flipped)

    return lax.psum_scatter(
        product_term(jnp.int32(0), own_rows * lax.axis_size("row")),
        "row",
        scatter_dimension=0,
        tiled=True,
    )


def settle_cols(gathered, weight, flipped, own_rows):

    def product_term(first_row, row_count):
        return product(gathered, weight, flipped)

    return lax.psum_scatter(
        product_term(jnp.int32(0), own_rows * lax.axis_size("col")),
        "col",
        scatter_dimension=0,
        tiled=True,
    )


def row_sums(first_part, second_part):
    return lax.psum((jnp.sum(first_part, axis=1), jnp.sum(second_part, axis=1)), "row")


def norm_forward(residual, norm_gain, norm_shift):
    total_sum, square_sum = row_sums(residual, residual * residual)
    row_mean = (total_sum / WIDTH)[:, None]
    variance = (square_sum / WIDTH)[:, None] - row_mean * row_mean
    inv_std = lax.rsqrt(variance + NORM_EPS)
    normed = (residual - row_mean) * inv_std
    return (normed * norm_gain + norm_shift, normed, inv_std)


def norm_backward(grad_in, normed, inv_std, norm_gain):
    grad_norm = grad_in * norm_gain
    total_sum, cross_sum = row_sums(grad_norm, grad_norm * normed)
    grad_resid = inv_std * (grad_norm - total_sum[:, None] / WIDTH - normed * cross_sum[:, None] / WIDTH)
    return (grad_resid, jnp.sum(grad_in * normed, axis=0), jnp.sum(grad_in, axis=0))


def split_heads(array, seq_count):
    return array.reshape(seq_count, SEQ, array.shape[1] // HD, HD)


def pair_scores(queries, key_heads, segment_ids):
    position = jnp.arange(SEQ)
    same_doc = (segment_ids[:, None] == segment_ids[None, :]) & (segment_ids[None, :] != 0)
    allowed = same_doc | (position[:, None] == position[None, :])
    raw_scores = jnp.einsum(
        "qhd,khd->hqk", queries, key_heads, preferred_element_type=jnp.float32
    ) * HD ** (-0.5)
    return jnp.where(allowed[None], raw_scores, -1000000000.0)


def attend_forward(source):
    queries, key_heads, values, segment_ids = source
    scores = pair_scores(queries, key_heads, segment_ids)
    top_score = jnp.max(scores, axis=2, keepdims=True)
    exp_scores = jnp.exp(scores - top_score)
    total_sum = jnp.sum(exp_scores, axis=2, keepdims=True)
    soft_low = (exp_scores / total_sum).astype(jnp.bfloat16)
    attended = jnp.einsum("hqk,khd->qhd", soft_low, values, preferred_element_type=jnp.float32)
    return (attended.astype(jnp.bfloat16), (top_score + jnp.log(total_sum))[:, :, 0])


def attend_backward(source):
    queries, key_heads, values, segment_ids, grad_out, log_total = source
    scores = pair_scores(queries, key_heads, segment_ids)
    soft_weights = jnp.exp(scores - log_total[:, :, None])
    soft_low = soft_weights.astype(jnp.bfloat16)
    grad_values = jnp.einsum("hqk,qhd->khd", soft_low, grad_out, preferred_element_type=jnp.float32)
    grad_soft = jnp.einsum("qhd,khd->hqk", grad_out, values, preferred_element_type=jnp.float32)
    grad_scores = soft_weights * (
        grad_soft - jnp.sum(soft_weights * grad_soft, axis=2, keepdims=True)
    )
    grad_scores = grad_scores.astype(jnp.bfloat16)
    scale_factor = HD ** (-0.5)
    grad_queries = (
        jnp.einsum("hqk,khd->qhd", grad_scores, key_heads, preferred_element_type=jnp.float32)
        * scale_factor
    )
    grad_keys = (
        jnp.einsum("hqk,qhd->khd", grad_scores, queries, preferred_element_type=jnp.float32)
        * scale_factor
    )
    return (
        grad_queries.astype(jnp.bfloat16),
        grad_keys.astype(jnp.bfloat16),
        grad_values.astype(jnp.bfloat16),
    )


def split_heads_plan(
    tokens,
    segments,
    w_query,
    b_query,
    w_key,
    w_value,
    b_value,
    w_out,
    b_out,
    norm1_gain,
    norm1_shift,
    w_up,
    b_up,
    w_down,
    b_down,
    norm2_gain,
    norm2_shift,
    cotangent,
):
    rows_b = tokens.shape[0]
    rows_a = segments.shape[0]
    head_cols = w_query.shape[1]
    seq_count = rows_a // SEQ
    segment_seqs = segments.reshape(seq_count, SEQ)
    gathered_x = tokens_cols(tokens)
    stacked = jnp.concatenate([w_query, w_key, w_value], axis=1)
    projected = settle_rows(gathered_x, stacked, False, rows_a)
    queries = (projected[:, :head_cols] + b_query).astype(jnp.bfloat16)
    key_heads = projected[:, head_cols : 2 * head_cols].astype(jnp.bfloat16)
    values = (projected[:, 2 * head_cols :] + b_value).astype(jnp.bfloat16)
    query_seqs = split_heads(queries, seq_count)
    key_seqs = split_heads(key_heads, seq_count)
    value_seqs = split_heads(values, seq_count)
    attended, log_total = lax.map(attend_forward, (query_seqs, key_seqs, value_seqs, segment_seqs))
    attended = attended.reshape(rows_a, head_cols)
    gathered_o = tokens_rows(attended)
    attn_out = settle_cols(gathered_o, w_out, False, rows_b) + b_out
    hidden, normed1, inv_std1 = norm_forward(
        tokens.astype(jnp.float32) + attn_out, norm1_gain, norm1_shift
    )
    hidden_low = hidden.astype(jnp.bfloat16)
    gathered_h = tokens_cols(hidden_low)
    pre_act = settle_rows(gathered_h, w_up, False, rows_a) + b_up
    active = gelu_exact(pre_act).astype(jnp.bfloat16)
    gathered_a = tokens_rows(active)
    fed = settle_cols(gathered_a, w_down, False, rows_b) + b_down
    output, normed2, inv_std2 = norm_forward(hidden + fed, norm2_gain, norm2_shift)
    grad_r2, grad_gain2, grad_shift2 = norm_backward(
        cotangent.astype(jnp.float32), normed2, inv_std2, norm2_gain
    )
    grad_fed = grad_r2.astype(jnp.bfloat16)
    gathered_f = tokens_cols(grad_fed)
    grad_w_down = outer_sum(gathered_a, gathered_f)
    grad_active = settle_rows(gathered_f, w_down, True, rows_a)
    unused_out, slope_pull = jax.vjp(gelu_exact, pre_act)
    grad_pre = slope_pull(grad_active)[0].astype(jnp.bfloat16)
    gathered_p = tokens_rows(grad_pre)
    grad_w_up = outer_sum(gathered_h, gathered_p)
    grad_from_ff = settle_cols(gathered_p, w_up, True, rows_b)
    bias_up_part = jnp.sum(grad_pre.astype(jnp.float32), axis=0)
    bias_down_part = jnp.sum(grad_fed.astype(jnp.float32), axis=0)
    grad_r1, grad_gain1, grad_shift1 = norm_backward(
        grad_from_ff + grad_r2, normed1, inv_std1, norm1_gain
    )
    grad_attn = grad_r1.astype(jnp.bfloat16)
    gathered_d = tokens_cols(grad_attn)
    grad_w_out = outer_sum(gathered_o, gathered_d)
    grad_attended = settle_rows(gathered_d, w_out, True, rows_a).astype(jnp.bfloat16)
    grad_q, grad_k, grad_v = lax.map(
        attend_backward,
        (
            query_seqs,
            key_seqs,
            value_seqs,
            segment_seqs,
            split_heads(grad_attended, seq_count),
            log_total,
        ),
    )
    grad_q = grad_q.reshape(rows_a, head_cols)
    grad_k = grad_k.reshape(rows_a, head_cols)
    grad_v = grad_v.reshape(rows_a, head_cols)
    grad_proj = jnp.concatenate([grad_q, grad_k, grad_v], axis=1)
    gathered_g = tokens_rows(grad_proj)
    grad_stacked = outer_sum(gathered_x, gathered_g)
    tokens_grad = settle_cols(gathered_g, stacked, True, rows_b) + grad_r1
    bias_q, bias_v, bias_up = lax.psum(
        (
            jnp.sum(grad_q.astype(jnp.float32), axis=0),
            jnp.sum(grad_v.astype(jnp.float32), axis=0),
            bias_up_part,
        ),
        ("dp", "row"),
    )
    bias_out, bias_down, gain_one, shift_one, gain_two, shift_two = lax.psum(
        (
            jnp.sum(grad_attn.astype(jnp.float32), axis=0),
            bias_down_part,
            grad_gain1,
            grad_shift1,
            grad_gain2,
            grad_shift2,
        ),
        ("dp", "col"),
    )
    sum_stacked, sum_out, sum_up, sum_down = (
        lax.psum(grad_stacked.astype(jnp.bfloat16), "dp").astype(jnp.float32),
        lax.psum(grad_w_out.astype(jnp.bfloat16), "dp").astype(jnp.float32),
        lax.psum(grad_w_up.astype(jnp.bfloat16), "dp").astype(jnp.float32),
        lax.psum(grad_w_down.astype(jnp.bfloat16), "dp").astype(jnp.float32),
    )
    return (
        output.astype(jnp.bfloat16),
        tokens_grad.astype(jnp.bfloat16),
        sum_stacked[:, :head_cols],
        bias_q,
        sum_stacked[:, head_cols : 2 * head_cols],
        sum_stacked[:, 2 * head_cols :],
        bias_v,
        sum_out,
        bias_out,
        gain_one,
        shift_one,
        sum_up,
        bias_up,
        sum_down,
        bias_down,
        gain_two,
        shift_two,
    )


def solution(mesh):
    dp, rows, cols = (mesh.shape[name] for name in ("dp", "row", "col"))
    whole = TOKENS // SEQ == dp * rows * cols and dp == 4 and cols == 2
    plan = whole_sequences if whole else split_heads_plan
    placed = (
        P(("dp", "col"), "row"),
        P(("dp", "row")),
        P("row", "col"),
        P("col"),
        P("row", "col"),
        P("row", "col"),
        P("col"),
        P("col", "row"),
        P("row"),
        P("row"),
        P("row"),
        P("row", "col"),
        P("col"),
        P("col", "row"),
        P("row"),
        P("row"),
        P("row"),
        P(("dp", "col"), "row"),
    )
    return jax.shard_map(
        plan,
        mesh=mesh,
        in_specs=placed,
        out_specs=(
            P(("dp", "col"), "row"),
            P(("dp", "col"), "row"),
            P("row", "col"),
            P("col"),
            P("row", "col"),
            P("row", "col"),
            P("col"),
            P("col", "row"),
            P("row"),
            P("row"),
            P("row"),
            P("row", "col"),
            P("col"),
            P("col", "row"),
            P("row"),
            P("row"),
            P("row"),
        ),
        check_vma=False,
    )
```

```python
import math

import jax
import jax.numpy as jnp
from jax import lax
from jax.experimental import pallas as pl
from jax.experimental.pallas import tpu as pltpu
from jax.sharding import PartitionSpec as P

HD = 64
SEQ = 1024
WIDTH = 1024
TOKENS = 32768
NORM_EPS = 1e-05
BF = jnp.bfloat16
F32 = jnp.float32
NEG = -1e30
QB = 256


def mm(a, b):
    return jnp.dot(a, b, preferred_element_type=F32)


def mm_t(a, b):
    return lax.dot_general(a, b, (((1,), (1,)), ((), ())), preferred_element_type=F32)


def tmm(a, b):
    return lax.dot_general(a, b, (((0,), (0,)), ((), ())), preferred_element_type=F32)


def gelu_exact(v):
    return jax.nn.gelu(v, approximate=False)


def attend_rows(qkv_ref, seg_col_ref, seg_row, o_ref, p_ref, linv_ref, i):
    lane = lax.broadcasted_iota(jnp.int32, (QB, 128), 1)
    scale = HD ** (-0.5) * math.log2(math.e)
    rows = slice(i * QB, (i + 1) * QB)
    q = qkv_ref[rows, 0:128]
    k = qkv_ref[:, 128:256]
    v = qkv_ref[:, 256:384]
    seg_col = seg_col_ref[rows, :]
    outs = []
    for h in range(2):
        mine = (lane < HD) if h == 0 else (lane >= HD)
        qm = jnp.where(mine, q, jnp.zeros_like(q))
        s = mm_t(qm, k)
        s = jnp.where(seg_col == seg_row, s * scale, NEG)
        top = jnp.max(s, axis=1, keepdims=True)
        p = jnp.exp2(s - top)
        total = jnp.sum(p, axis=1, keepdims=True)
        pb = p.astype(BF)
        p_ref[h, rows, :] = pb
        inv = 1.0 / total
        outs.append((mm(pb, v) * inv, jnp.broadcast_to(inv, (QB, 128))))
    o_ref[rows, :] = jnp.where(lane < HD, outs[0][0], outs[1][0]).astype(BF)
    linv_ref[rows, :] = jnp.where(lane < HD, outs[0][1], outs[1][1])


def attend_fwd_kernel(
    x_ref, w_ref, b_ref, seg_col_ref, seg_row_ref, po, pu, pd,
    qkv_ref, o_ref, p_ref, linv_ref, wo, wu, wd, o_recv, o_sent, u_recv, u_sent, d_recv, d_sent,
):
    j = pl.program_id(0)
    peers = Peers()
    go = Gather(peers, po, wo, False, o_recv, o_sent, RING + NEAR + FAR)
    gu = Gather(peers, pu, wu, True, u_recv, u_sent, RING + NEAR)
    gd = Gather(peers, pd, wd, False, d_recv, d_sent, RING + DOWN_NEAR)
    every = (go, gu, gd)

    def hook(at, *stages):
        @pl.when(j == at)
        def _():
            for which, blocks in stages:
                for g in which:
                    g.relay(*blocks)

    @pl.when(j == 0)
    def _():
        peers.greet(ALL_PEERS)
        for g in every:
            g.start()

    seg_row = seg_row_ref[...]
    hook(1, ((go, gu), [(1, 0)]))
    hook(2, (every, [(0, 2), (0, 4)]))
    hook(3, ((go, gu), [(2, 0)]), ((go,), [(1, 2), (1, 4)]))
    hook(4, ((gu, gd), [(1, 2), (1, 4)]))
    hook(5, ((go, gu), [(3, 0)]))
    hook(6, (every, [(2, 2), (2, 4)]), ((go,), [(0, 6), (1, 6)]))
    hook(7, ((go,), [(3, 2), (3, 4)]))
    qkv_ref[...] = (mm(x_ref[...], w_ref[...]) + b_ref[...]).astype(BF)
    for i in range(SEQ // QB):
        if i == SEQ // QB // 2:
            hook(1, ((gd,), [(1, 0)]))
            hook(3, ((gd,), [(2, 0)]))
            hook(5, ((gd,), [(3, 0)]))
            hook(7, ((go,), [(2, 6), (3, 6)]), ((gu,), [(3, 2), (3, 4)]))
        attend_rows(qkv_ref, seg_col_ref, seg_row, o_ref, p_ref, linv_ref, i)

    @pl.when(j == 7)
    def _():
        for g in every:
            g.finish()


def attend_bwd_kernel(qkv_ref, do_ref, o_ref, linv_ref, p_ref, g_ref, ds_ref):
    lane = lax.broadcasted_iota(jnp.int32, (SEQ, 128), 1)
    q = qkv_ref[:, 0:128]
    k = qkv_ref[:, 128:256]
    v = qkv_ref[:, 256:384]
    scale = HD ** (-0.5)
    do = do_ref[...].astype(F32) * linv_ref[...]
    prod = do * o_ref[...].astype(F32)
    dob = do.astype(BF)
    qt = jnp.transpose(q.astype(F32)).astype(BF)
    dot_ = jnp.transpose(do).astype(BF)
    dq = []
    dkt = []
    dvt = []
    for h in range(2):
        mine = (lane < HD) if h == 0 else (lane >= HD)
        delta = jnp.sum(jnp.where(mine, prod, 0.0), axis=1, keepdims=True)
        dom = jnp.where(mine, dob, jnp.zeros_like(dob))
        for i in range(SEQ // QB):
            rows = slice(i * QB, (i + 1) * QB)
            dp = mm_t(dom[rows], v)
            ds = p_ref[h, rows, :].astype(F32) * (dp - delta[rows])
            ds_ref[h, rows, :] = ds.astype(BF)
        feats = slice(h * HD, (h + 1) * HD)
        dq.append(mm(ds_ref[h], k))
        dkt.append(mm(qt[feats], ds_ref[h]))
        dvt.append(mm(dot_[feats], p_ref[h]))
    g_ref[:, 0:128] = (jnp.where(lane < HD, dq[0], dq[1]) * scale).astype(BF)
    g_ref[:, 128:256] = (jnp.transpose(jnp.concatenate(dkt, 0)) * scale).astype(BF)
    g_ref[:, 256:384] = jnp.transpose(jnp.concatenate(dvt, 0)).astype(BF)


VMEM_LIMIT = 56 * 1024 * 1024


def attend_fwd(x, w_qkv, b_qkv, seg_col, seg_row, po, pu, pd):
    slots = w_qkv.shape[1] // 384
    whole = pl.BlockSpec(memory_space=pl.ANY)
    dma = pltpu.SemaphoreType.DMA
    return pl.pallas_call(
        attend_fwd_kernel,
        grid=(slots,),
        in_specs=[
            pl.BlockSpec((SEQ, x.shape[1]), lambda j: (0, 0)),
            pl.BlockSpec((x.shape[1], 384), lambda j: (0, j)),
            pl.BlockSpec((1, 384), lambda j: (0, j)),
            pl.BlockSpec((SEQ, 1), lambda j: (0, 0)),
            pl.BlockSpec((1, SEQ), lambda j: (0, 0)),
            whole,
            whole,
            whole,
        ],
        out_specs=[
            pl.BlockSpec((SEQ, 384), lambda j: (0, j)),
            pl.BlockSpec((SEQ, 128), lambda j: (0, j)),
            pl.BlockSpec((2, SEQ, SEQ), lambda j: (j, 0, 0)),
            pl.BlockSpec((SEQ, 128), lambda j: (0, j)),
            whole,
            whole,
            whole,
        ],
        out_shape=[
            jax.ShapeDtypeStruct((SEQ, slots * 384), BF),
            jax.ShapeDtypeStruct((SEQ, slots * 128), BF),
            jax.ShapeDtypeStruct((slots * 2, SEQ, SEQ), BF),
            jax.ShapeDtypeStruct((SEQ, slots * 128), F32),
            jax.ShapeDtypeStruct((8 * po.shape[0], 4 * po.shape[1]), BF),
            jax.ShapeDtypeStruct((4 * pu.shape[0], 8 * pu.shape[1]), BF),
            jax.ShapeDtypeStruct((8 * pd.shape[0], 4 * pd.shape[1]), BF),
        ],
        scratch_shapes=[dma((32,)), dma((32,))] * 3,
        compiler_params=pltpu.CompilerParams(vmem_limit_bytes=VMEM_LIMIT, collective_id=1, has_side_effects=True),
        cost_estimate=pl.CostEstimate(
            flops=slots * 2 * 4 * SEQ * SEQ * 256,
            bytes_accessed=slots * 5 * SEQ * SEQ,
            transcendentals=slots * 2 * SEQ * SEQ,
        ),
        name="attend_fwd",
    )(x, w_qkv, b_qkv, seg_col, seg_row, po, pu, pd)


def attend_bwd(qkv, do, o, linv, p):
    slots = qkv.shape[1] // 384
    return pl.pallas_call(
        attend_bwd_kernel,
        grid=(slots,),
        in_specs=[
            pl.BlockSpec((SEQ, 384), lambda j: (0, j)),
            pl.BlockSpec((SEQ, 128), lambda j: (0, j)),
            pl.BlockSpec((SEQ, 128), lambda j: (0, j)),
            pl.BlockSpec((SEQ, 128), lambda j: (0, j)),
            pl.BlockSpec((2, SEQ, SEQ), lambda j: (j, 0, 0)),
        ],
        out_specs=pl.BlockSpec((SEQ, 384), lambda j: (0, j)),
        out_shape=jax.ShapeDtypeStruct((SEQ, slots * 384), BF),
        scratch_shapes=[pltpu.VMEM((2, SEQ, SEQ), BF)],
        compiler_params=pltpu.CompilerParams(vmem_limit_bytes=VMEM_LIMIT),
        cost_estimate=pl.CostEstimate(
            flops=slots * 2 * 8 * SEQ * SEQ * 256,
            bytes_accessed=slots * 6 * SEQ * SEQ,
            transcendentals=0,
        ),
        name="attend_bwd",
    )(qkv, do, o, linv, p)


MESH = pl.DeviceIdType.MESH
ANY = pl.BlockSpec(memory_space=pl.ANY)
DMA = pltpu.SemaphoreType.DMA


class Peers:
    def __init__(self):
        self.r = lax.axis_index("row")
        d = lax.axis_index("dp")
        self.ids = {
            "core": {"dp": d + 1 - 2 * lax.rem(d, 2)},
            "x": {"dp": lax.rem(d + 2, 4)},
            "y": {"col": 1 - lax.axis_index("col")},
            1: {"row": lax.rem(self.r + 1, 4)},
            2: {"row": lax.rem(self.r + 2, 4)},
            3: {"row": lax.rem(self.r + 3, 4)},
        }

    def greet(self, names):
        barrier = pltpu.get_barrier_semaphore()
        for name in names:
            pl.semaphore_signal(barrier, inc=1, device_id=self.ids[name], device_id_type=MESH)
        pl.semaphore_wait(barrier, len(names))


def send(peers, name, src, dst, send_sem, recv_sem):
    return pltpu.make_async_remote_copy(
        src_ref=src, dst_ref=dst, send_sem=send_sem, recv_sem=recv_sem, device_id=peers.ids[name], device_id_type=MESH
    )


def near_edges(s):
    return [("x", s, 0, s, 2), ("y", s, 0, s, 4), ("core", s, 0, s, 1)]


def second_edges(s):
    return [("core", s, 2, s, 3), ("core", s, 4, s, 5)]


def far_edges(s):
    return [("y", s, 2, s, 6) if s % 2 == 0 else ("x", s, 4, s, 6), ("core", s, 6, s, 7)]


RING = [(1, s, 0, s + 1, 0) for s in range(3)]
NEAR = [e for s in range(4) for e in near_edges(s) + second_edges(s)]
FAR = [e for s in range(4) for e in far_edges(s)]
DOWN_NEAR = [e for s in range(3) for e in near_edges(s) + second_edges(s)] + [("core", 3, 0, 3, 1)]
DOWN_REST = [e for e in near_edges(3) if e[0] != "core"] + second_edges(3) + FAR


class Gather:
    def __init__(self, peers, piece, full, by_rows, recv, sent, edges):
        self.peers, self.piece, self.full, self.recv, self.sent = peers, piece, full, recv, sent
        self.by_rows = by_rows
        self.n = full.shape[1 if by_rows else 0] // 8
        self.m = full.shape[0 if by_rows else 1] // 4
        self.edges = edges
        self.waited = set()
        self.emitted = set()

    def blk(self, s, t):
        a = pl.ds(s * self.m, self.m)
        b = pl.ds(t * self.n, self.n)
        return self.full.at[a, b] if self.by_rows else self.full.at[b, a]

    def copy(self, at):
        name, s, t, s2, t2 = self.edges[at]
        src = self.piece if (s, t) == (0, 0) and self.piece is not None else self.blk(s, t)
        return send(self.peers, name, src, self.blk(s2, t2), self.sent.at[at], self.recv.at[at])

    def emit(self, s, t):
        for at, e in enumerate(self.edges):
            if e[1:3] == (s, t):
                assert at not in self.emitted
                self.emitted.add(at)
                self.copy(at).start()

    def arrived(self, s, t):
        for at, e in enumerate(self.edges):
            if e[3:5] == (s, t) and at not in self.waited:
                self.waited.add(at)
                self.copy(at).wait_recv()

    def relay(self, *blocks):
        for s, t in blocks:
            self.arrived(s, t)
            self.emit(s, t)

    def own(self):
        return pltpu.make_async_copy(self.piece, self.blk(0, 0), self.sent.at[len(self.edges)])

    def start(self):
        self.emit(0, 0)
        self.own().start()

    def finish(self):
        if self.piece is not None:
            self.own().wait()
        for at, e in enumerate(self.edges):
            if at not in self.waited:
                self.waited.add(at)
                self.copy(at).wait_recv()
        assert len(self.emitted) == len(self.edges)
        for at in range(len(self.edges)):
            self.copy(at).wait_send()


class Inward:
    def __init__(self, peers, block, rows, recv, sent):
        self.peers, self.block, self.rows, self.recv, self.sent = peers, block, rows, recv, sent

    def copy(self, s):
        r = lax.rem(self.peers.r + s, 4)
        src = self.block.at[pl.ds(pl.multiple_of(r * SEQ, SEQ), SEQ), :]
        f = self.block.shape[1]
        dst = self.rows.at[:, pl.ds(s * f, f)]
        if s == 0:
            return pltpu.make_async_copy(src, dst, self.sent.at[0])
        return send(self.peers, s, src, dst, self.sent.at[s], self.recv.at[s])

    def start(self):
        for s in (2, 1, 3, 0):
            self.copy(s).start()

    def finish(self):
        self.copy(0).wait()
        for s in (1, 2, 3):
            self.copy(s).wait()


ALL_PEERS = ("core", "x", "y", 1, 2, 3)


def first_kernel(tokens, piece, x, w, g_recv, g_sent, i_recv, i_sent):
    peers = Peers()
    peers.greet(ALL_PEERS)
    g = Gather(peers, piece, w, True, g_recv, g_sent, RING + NEAR + FAR)
    a = Inward(peers, tokens, x, i_recv, i_sent)
    g.start()
    a.start()
    for s in (1, 2, 3):
        g.relay((s, 0), (s - 1, 2), (s - 1, 4))
    g.relay((3, 2), (3, 4))
    for s in range(4):
        g.relay((s, 6))
    g.finish()
    a.finish()


def first(tokens, piece):
    return pl.pallas_call(
        first_kernel,
        in_specs=[ANY, ANY],
        out_specs=[ANY, ANY],
        out_shape=[
            jax.ShapeDtypeStruct((SEQ, 4 * tokens.shape[1]), BF),
            jax.ShapeDtypeStruct((4 * piece.shape[0], 8 * piece.shape[1]), BF),
        ],
        scratch_shapes=[DMA((32,)), DMA((32,)), DMA((4,)), DMA((4,))],
        compiler_params=pltpu.CompilerParams(collective_id=0, has_side_effects=True),
        name="first",
    )(tokens, piece)


RB = 128


def norm_rows(v):
    mean = jnp.mean(v, axis=1, keepdims=True)
    variance = jnp.mean(v * v, axis=1, keepdims=True) - mean * mean
    inv = lax.rsqrt(variance + NORM_EPS)
    return (v - mean) * inv, inv


def norm_rows_back(g, normed, inv):
    mean_g = jnp.mean(g, axis=1, keepdims=True)
    mean_gn = jnp.mean(g * normed, axis=1, keepdims=True)
    return inv * (g - mean_g - normed * mean_gn)


def gelu_and_slope(v):
    z = jnp.abs(v) * (0.5 ** 0.5)
    t = 1.0 / (1.0 + 0.3275911 * z)
    poly = t * (0.254829592 + t * (-0.284496736 + t * (1.421413741 + t * (-1.453152027 + t * 1.061405429))))
    bell = jnp.exp2(z * z * -math.log2(math.e))
    tail = 0.5 * poly * bell
    cdf = jnp.where(v >= 0, 1.0 - tail, tail)
    return v * cdf, cdf + v * bell * (1.0 / math.sqrt(2.0 * math.pi))


def row_blocks(body, n=RB):
    def run(i, carry):
        body(pl.ds(pl.multiple_of(i * n, n), n))
        return carry

    lax.fori_loop(0, SEQ // n, run, 0)


def ff_fwd_kernel(
    x_ref, att_ref, wo_ref, vec_ref, bu_ref, cot, wu_in, wd_in,
    wu, wd, act_ref, slope_ref, hlow_ref, normed1_ref, inv1_ref, out_ref, r2_ref, vg_ref,
    acc, wu_buf, wd_buf, cot_buf, buf_sem, u_recv, u_sent, d_recv, d_sent, i_recv, i_sent,
):
    j = pl.program_id(0)
    peers = Peers()
    gu = Gather(peers, None, wu, True, u_recv, u_sent, FAR)
    gd = Gather(peers, None, wd, False, d_recv, d_sent, DOWN_REST)
    inward = Inward(peers, cot, cot_buf, i_recv, i_sent)
    n = wu_buf.shape[2]

    def fetch(t, slot):
        cols = pl.ds(pl.multiple_of(t * n, n), n)
        return (
            pltpu.make_async_copy(wu.at[:, cols], wu_buf.at[slot], buf_sem.at[0, slot]),
            pltpu.make_async_copy(wd.at[cols, :], wd_buf.at[slot], buf_sem.at[1, slot]),
        )

    @pl.when(j == 0)
    def _():
        peers.greet(ALL_PEERS)
        for t in range(2):
            for c in fetch(t, t):
                c.start()
        gd.emit(3, 0)
        for s in range(3):
            gu.emit(s, 2 if s % 2 == 0 else 4)
            gd.emit(s, 2 if s % 2 == 0 else 4)
        gu.emit(3, 4)
        inward.start()

        def body(rows):
            v = x_ref[rows, :].astype(F32) + mm(att_ref[rows, :], wo_ref[...]) + vec_ref[0:1, :]
            normed, inv = norm_rows(v)
            normed1_ref[rows, :] = normed
            inv1_ref[rows, :] = jnp.broadcast_to(inv, (RB, 128))
            hlow_ref[rows, :] = (normed * vec_ref[1:2, :] + vec_ref[2:3, :]).astype(BF)

        row_blocks(body)
        acc[...] = jnp.zeros_like(acc)
        gd.relay((3, 2), (3, 4))

    @pl.when(j == 1)
    def _():
        gd.arrived(3, 3)
        for s in range(4):
            gu.relay((s, 6))

    @pl.when(j == 2)
    def _():
        gd.arrived(3, 5)

    @pl.when(j == 4)
    def _():
        for s in range(4):
            gd.relay((s, 6))

    @pl.when(j == 5)
    def _():
        for s in range(4):
            gu.arrived(s, 7)
            gd.arrived(s, 7)

    slot = lax.rem(j, 2)
    for c in fetch(j, slot):
        c.wait()
    w_up = wu_buf.at[slot]
    w_down = wd_buf.at[slot]
    bias = bu_ref[...]
    for i in range(SEQ // 256):
        rows = slice(i * 256, (i + 1) * 256)
        act, slope = gelu_and_slope(mm(hlow_ref[rows, :], w_up[...]) + bias)
        act = act.astype(BF)
        act_ref[rows, :] = act
        slope_ref[rows, :] = slope.astype(BF)
        acc[rows, :] += mm(act, w_down[...])

    @pl.when(j < 6)
    def _():
        for c in fetch(j + 2, slot):
            c.start()

    @pl.when(j == 7)
    def _():
        inward.finish()
        vg_ref[...] = jnp.zeros_like(vg_ref)

        def body(rows):
            hidden = normed1_ref[rows, :] * vec_ref[1:2, :] + vec_ref[2:3, :]
            normed, inv = norm_rows(hidden + (acc[rows, :] + vec_ref[3:4, :]))
            out_ref[rows, :] = (normed * vec_ref[4:5, :] + vec_ref[5:6, :]).astype(BF)
            c = cot_buf[rows, :].astype(F32)
            r2 = norm_rows_back(c * vec_ref[4:5, :], normed, inv)
            r2_ref[rows, :] = r2
            vg_ref[0:1, :] += jnp.sum(c * normed, axis=0, keepdims=True)
            vg_ref[1:2, :] += jnp.sum(c, axis=0, keepdims=True)
            vg_ref[2:3, :] += jnp.sum(r2.astype(BF).astype(F32), axis=0, keepdims=True)

        row_blocks(body)
        gu.finish()
        gd.finish()


ONCE = pl.Buffered(1)


def const(*shape):
    return pl.BlockSpec(shape, lambda j: (0,) * len(shape), pipeline_mode=ONCE)


def ff_fwd(x, att, wo, vec, bu, cot, wu, wd):
    width, units = wu.shape
    n = units // 8
    return pl.pallas_call(
        ff_fwd_kernel,
        grid=(8,),
        in_specs=[
            const(SEQ, width),
            const(SEQ, width),
            const(width, width),
            const(8, width),
            pl.BlockSpec((1, n), lambda j: (0, j)),
            ANY,
            ANY,
            ANY,
        ],
        out_specs=[
            ANY,
            ANY,
            pl.BlockSpec((SEQ, n), lambda j: (0, j)),
            pl.BlockSpec((SEQ, n), lambda j: (0, j)),
            const(SEQ, width),
            const(SEQ, width),
            const(SEQ, 128),
            const(SEQ, width),
            const(SEQ, width),
            const(8, width),
        ],
        out_shape=[
            jax.ShapeDtypeStruct(wu.shape, BF),
            jax.ShapeDtypeStruct(wd.shape, BF),
            jax.ShapeDtypeStruct((SEQ, units), BF),
            jax.ShapeDtypeStruct((SEQ, units), BF),
            jax.ShapeDtypeStruct((SEQ, width), BF),
            jax.ShapeDtypeStruct((SEQ, width), F32),
            jax.ShapeDtypeStruct((SEQ, 128), F32),
            jax.ShapeDtypeStruct((SEQ, width), BF),
            jax.ShapeDtypeStruct((SEQ, width), F32),
            jax.ShapeDtypeStruct((8, width), F32),
        ],
        input_output_aliases={6: 0, 7: 1},
        scratch_shapes=[
            pltpu.VMEM((SEQ, width), F32),
            pltpu.VMEM((2, width, n), BF),
            pltpu.VMEM((2, n, width), BF),
            pltpu.VMEM((SEQ, width), BF),
            DMA((2, 2)),
            DMA((32,)),
            DMA((32,)),
            DMA((32,)),
            DMA((32,)),
            DMA((4,)),
            DMA((4,)),
        ],
        compiler_params=pltpu.CompilerParams(vmem_limit_bytes=VMEM_LIMIT, collective_id=2, has_side_effects=True),
        name="ff_fwd",
    )(x, att, wo, vec, bu, cot, wu, wd)


class Outward:
    def __init__(self, peers, rows, block, recv, sent):
        self.peers, self.rows, self.block, self.recv, self.sent = peers, rows, block, recv, sent

    def copy(self, s):
        f = self.block.shape[1]
        src = self.rows.at[:, pl.ds(s * f, f)]
        dst = self.block.at[pl.ds(pl.multiple_of(self.peers.r * SEQ, SEQ), SEQ), :]
        if s == 0:
            return pltpu.make_async_copy(src, dst, self.sent.at[0])
        return send(self.peers, 4 - s, src, dst, self.sent.at[s], self.recv.at[s])

    def start(self):
        for s in (2, 1, 3, 0):
            self.copy(s).start()

    def finish(self):
        self.copy(0).wait()
        for s in (1, 2, 3):
            self.copy(s).wait()


def ff_bwd_kernel(
    r2_ref, hlow_ref, wu_ref, wd_ref, act_ref, slope_ref, normed1_ref, inv1_ref, vec_ref, out,
    out_block, dwu_ref, dwd_ref, r1_ref, gattn_ref, vg_ref, bu_ref,
    gfed, gp, hlow_t, o_recv, o_sent,
):
    j = pl.program_id(0)
    peers = Peers()
    outward = Outward(peers, out, out_block, o_recv, o_sent)

    @pl.when(j == 0)
    def _():
        peers.greet((1, 2, 3))
        outward.start()

        def body(rows):
            gfed[rows, :] = r2_ref[rows, :].astype(BF)

        row_blocks(body)
        r1_ref[...] = r2_ref[...]
        for i in range(SEQ // 256):
            rows = slice(i * 256, (i + 1) * 256)
            hlow_t[:, rows] = jnp.transpose(hlow_ref[rows, :])

    bsum = jnp.zeros((1, bu_ref.shape[1]), F32)
    for i in range(SEQ // 256):
        rows = slice(i * 256, (i + 1) * 256)
        g = (mm_t(gfed[rows, :], wd_ref[...]) * slope_ref[rows, :].astype(F32)).astype(BF)
        gp[rows, :] = g
        bsum += jnp.sum(g.astype(F32), axis=0, keepdims=True)
    bu_ref[...] = jnp.broadcast_to(bsum, bu_ref.shape)
    dwd_ref[...] = tmm(act_ref[...], gfed[...]).astype(BF)
    dwu_ref[...] = mm(hlow_t[...], gp[...]).astype(BF)
    r1_ref[...] += mm_t(gp[...], wu_ref[...])

    @pl.when(j == 7)
    def _():
        vg_ref[...] = jnp.zeros_like(vg_ref)

        def body(rows):
            gh = r1_ref[rows, :]
            normed = normed1_ref[rows, :]
            r1 = norm_rows_back(gh * vec_ref[1:2, :], normed, inv1_ref[rows, 0:1])
            r1_ref[rows, :] = r1
            low = r1.astype(BF)
            gattn_ref[rows, :] = low
            vg_ref[0:1, :] += jnp.sum(gh * normed, axis=0, keepdims=True)
            vg_ref[1:2, :] += jnp.sum(gh, axis=0, keepdims=True)
            vg_ref[2:3, :] += jnp.sum(low.astype(F32), axis=0, keepdims=True)

        row_blocks(body)
        outward.finish()


def ff_bwd(r2, hlow, wu, wd, act, slope, normed1, inv1, vec, out):
    width, units = wu.shape
    n = units // 8
    return pl.pallas_call(
        ff_bwd_kernel,
        grid=(8,),
        in_specs=[
            const(SEQ, width),
            const(SEQ, width),
            pl.BlockSpec((width, n), lambda j: (0, j)),
            pl.BlockSpec((n, width), lambda j: (j, 0)),
            pl.BlockSpec((SEQ, n), lambda j: (0, j)),
            pl.BlockSpec((SEQ, n), lambda j: (0, j)),
            const(SEQ, width),
            const(SEQ, 128),
            const(8, width),
            ANY,
        ],
        out_specs=[
            ANY,
            pl.BlockSpec((width, n), lambda j: (0, j)),
            pl.BlockSpec((n, width), lambda j: (j, 0)),
            const(SEQ, width),
            const(SEQ, width),
            const(8, width),
            pl.BlockSpec((8, n), lambda j: (0, j)),
        ],
        out_shape=[
            jax.ShapeDtypeStruct((4 * SEQ, width // 4), BF),
            jax.ShapeDtypeStruct((width, units), BF),
            jax.ShapeDtypeStruct((units, width), BF),
            jax.ShapeDtypeStruct((SEQ, width), F32),
            jax.ShapeDtypeStruct((SEQ, width), BF),
            jax.ShapeDtypeStruct((8, width), F32),
            jax.ShapeDtypeStruct((8, units), F32),
        ],
        scratch_shapes=[
            pltpu.VMEM((SEQ, width), BF),
            pltpu.VMEM((SEQ, n), BF),
            pltpu.VMEM((width, SEQ), BF),
            DMA((4,)),
            DMA((4,)),
        ],
        compiler_params=pltpu.CompilerParams(vmem_limit_bytes=VMEM_LIMIT, collective_id=3, has_side_effects=True),
        name="ff_bwd",
    )(r2, hlow, wu, wd, act, slope, normed1, inv1, vec, out)


class Ring:
    def __init__(self):
        self.r = lax.axis_index("row")
        self.c = lax.axis_index("col")
        self.d = lax.axis_index("dp")
        self.rows = lax.axis_size("row")

    def shift(self, v, s):
        n = self.rows
        return lax.ppermute(v, "row", [(i, (i + s) % n) for i in range(n)])

    def core(self, v):
        return lax.ppermute(v, "dp", [(i, i ^ 1) for i in range(4)])

    def x(self, v):
        return lax.ppermute(v, "dp", [(i, i ^ 2) for i in range(4)])

    def y(self, v):
        return lax.ppermute(v, "col", [(0, 1), (1, 0)])

    def gather(self, piece, axis):
        parts = [piece]
        for _ in range(self.rows - 1):
            parts.append(self.shift(parts[-1], 1))
        own = jnp.concatenate(parts, axis)
        from_x, from_y = self.x(own), self.y(own)
        half = own.shape[0] // 2
        diag = jnp.concatenate([self.y(from_x[:half]), self.x(from_y[half:])], 0)
        first = [own, from_x, from_y, diag]
        other = [self.core(v) for v in first]
        return [first[0], other[0], first[1], other[1], first[2], other[2], first[3], other[3]]

    def scatter(self, blocks, cut):
        kept = [blocks[0], blocks[2], blocks[4], blocks[6]]
        sent = [blocks[1], blocks[3], blocks[5], blocks[7]]
        own, to_x, to_y, diag = [
            (a.astype(F32) + self.core(b).astype(F32)).astype(BF) for a, b in zip(kept, sent)
        ]
        half = own.shape[0] // 2
        via_y = self.y(diag[:half])
        via_x = self.x(diag[half:])
        to_x = jnp.concatenate([to_x[:half] + via_y, to_x[half:]], 0)
        to_y = jnp.concatenate([to_y[:half], to_y[half:] + via_x], 0)
        total = (own.astype(F32) + self.x(to_x).astype(F32) + self.y(to_y).astype(F32)).astype(BF)
        parts = cut(total)
        acc = parts[1]
        for s in range(1, self.rows):
            got = self.shift(acc, 1)
            acc = (parts[(s + 1) % self.rows].astype(F32) + got.astype(F32)).astype(BF)
        pair = jnp.stack([acc, self.core(acc)])
        quarters = jnp.concatenate([pair, self.x(pair)], 0)
        return self.absolute(quarters)

    def absolute(self, quarters):
        a = jnp.where(self.d % 2 == 1, quarters[jnp.array([1, 0, 3, 2])], quarters)
        return jnp.where(self.d // 2 == 1, jnp.concatenate([a[2:], a[:2]], 0), a)


def quarter(v, d, axis):
    n = v.shape[axis] // 4
    return lax.dynamic_slice_in_dim(v, d * n, n, axis)


def whole_sequences(
    tokens, segments, w_query, b_query, w_key, w_value, b_value, w_out, b_out, norm1_gain, norm1_shift,
    w_up, b_up, w_down, b_down, norm2_gain, norm2_shift, cotangent,
):
    ring = Ring()
    r, c, d = ring.r, ring.c, ring.d
    R, C = lax.axis_size("row"), lax.axis_size("col")
    feat = tokens.shape[1]

    def outward(rows):
        whole = jnp.zeros((R * SEQ, feat), rows.dtype)
        for s in range(R):
            piece = rows[:, s * feat : (s + 1) * feat]
            if s:
                piece = ring.shift(piece, -s)
            whole = lax.dynamic_update_slice_in_dim(whole, piece, ((r + s) % R) * SEQ, 0)
        return whole

    pairs = []
    for row in range(R):
        for col in range(C):
            n = col * R + row
            pairs.append((n, row * C + col))
    seg = lax.ppermute(segments, ("row", "col"), pairs)
    seg = lax.dynamic_slice_in_dim(seg, ((c * R + r) % C) * SEQ, SEQ, 0)
    ids = jnp.where(seg == 0, -1 - jnp.arange(SEQ, dtype=jnp.int32), seg)
    seg_col, seg_row = ids[:, None], ids[None, :]

    qkv_piece = jnp.concatenate([quarter(w, d, 1) for w in (w_query, w_key, w_value)], 1)
    x, w_qkv = first(tokens, qkv_piece)

    feat_vec = jnp.stack([b_out, norm1_gain, norm1_shift, b_down, norm2_gain, norm2_shift, b_out, b_out])
    feat_all = jnp.concatenate([feat_vec] + [ring.shift(feat_vec, s) for s in range(1, R)], 1).astype(F32)
    hq = b_query.shape[0] // 4
    unit = b_up.shape[0] // 4
    slot_vec = jnp.concatenate(
        [b_query.reshape(4, hq), jnp.zeros((4, hq), BF), b_value.reshape(4, hq), b_up.reshape(4, unit)], 1
    )
    slot_vec = ring.absolute(slot_vec)
    slot_vec = jnp.concatenate([slot_vec, ring.y(slot_vec)], 0).astype(F32)
    b_qkv = slot_vec[:, : 3 * hq].reshape(1, -1)
    bu = slot_vec[:, 3 * hq :].reshape(1, -1)

    qkv, att, prob, linv, wo, wu, wd = attend_fwd(
        x, w_qkv, b_qkv, seg_col, seg_row, quarter(w_out, d, 0), quarter(w_up, d, 1), quarter(w_down, d, 0)
    )
    wu, wd, act, slope, hidden_low, normed1, inv1, output, grad_r2, vg2 = ff_fwd(
        x, att, wo, feat_all, bu, cotangent, wu, wd
    )

    out_block, dwu, dwd, grad_r1, grad_attn, vg1, bu_part = ff_bwd(
        grad_r2, hidden_low, wu, wd, act, slope, normed1, inv1, feat_all, output
    )
    dwo = tmm(att, grad_attn).astype(BF)
    grad_att = mm_t(grad_attn, wo).astype(BF)
    g_qkv = attend_bwd(qkv, grad_att, att, linv, prob)
    dwqkv = tmm(x, g_qkv).astype(BF)
    x_grad = (mm_t(g_qkv, w_qkv) + grad_r1).astype(BF)
    x_grad_block = outward(x_grad)

    def rows_of(v, n=8):
        k = v.shape[0] // n
        return [v[i * k : (i + 1) * k] for i in range(n)]

    def cols_of(v, n=8):
        k = v.shape[1] // n
        return [v[:, i * k : (i + 1) * k] for i in range(n)]

    def cut_rows(v):
        return rows_of(v, R)

    def cut_cols(v):
        return cols_of(v, R)

    sum_down = ring.scatter(rows_of(dwd), cut_cols)
    sum_up = ring.scatter(cols_of(dwu), cut_rows)
    sum_out = ring.scatter(rows_of(dwo), cut_cols)
    sum_qkv = ring.scatter(cols_of(dwqkv), cut_rows)
    w_down_grad = sum_down.astype(F32).reshape(w_down.shape)
    w_out_grad = sum_out.astype(F32).reshape(w_out.shape)
    w_up_grad = sum_up.astype(F32).transpose(1, 0, 2).reshape(w_up.shape)
    sum_qkv = sum_qkv.astype(F32).transpose(1, 0, 2)
    wq_grad, wk_grad, wv_grad = [sum_qkv[:, :, i * hq : (i + 1) * hq].reshape(w_query.shape) for i in range(3)]

    g32 = g_qkv.astype(F32)
    slot_grad = jnp.concatenate(
        [
            jnp.sum(g32, axis=0).reshape(8, 3 * hq),
            bu_part[0].reshape(8, unit),
        ],
        1,
    )
    feat_grad = jnp.stack([vg1[2], vg1[0], vg1[1], vg2[2], vg2[0], vg2[1]])
    slot_grad = slot_grad[0::2] + ring.core(slot_grad[1::2])
    slot_grad = slot_grad[0::2] + ring.x(slot_grad[1::2])
    slot_grad = slot_grad[0] + ring.y(slot_grad[1])
    for s in (1, 2):
        slot_grad = slot_grad + lax.ppermute(slot_grad, "row", [(i, i ^ s) for i in range(R)])
    pair = jnp.stack([slot_grad, ring.core(slot_grad)])
    slot_grad = ring.absolute(jnp.concatenate([pair, ring.x(pair)], 0))
    bq_grad = slot_grad[:, :hq].reshape(-1)
    bv_grad = slot_grad[:, 2 * hq : 3 * hq].reshape(-1)
    bu_grad = slot_grad[:, 3 * hq :].reshape(-1)
    feat_grad = feat_grad + ring.core(feat_grad)
    feat_grad = feat_grad + ring.x(feat_grad)
    feat_grad = feat_grad + ring.y(feat_grad)
    own = feat_grad[:, :feat]
    for s in range(1, R):
        own = own + ring.shift(feat_grad[:, s * feat : (s + 1) * feat], -s)
    return (
        out_block, x_grad_block, wq_grad, bq_grad, wk_grad, wv_grad, bv_grad, w_out_grad, own[0], own[1], own[2],
        w_up_grad, bu_grad, w_down_grad, own[3], own[4], own[5],
    )


def tokens_cols(source):
    return lax.all_gather(source, "col", axis=0, tiled=True)


def tokens_rows(source):
    return lax.all_gather(source, "row", axis=0, tiled=True)


def product(row_piece, weight, flipped):
    if flipped:
        return lax.dot_general(
            row_piece, weight, (((1,), (1,)), ((), ())), preferred_element_type=jnp.float32
        )
    return jnp.dot(row_piece, weight, preferred_element_type=jnp.float32)


def outer_sum(left, right):
    return lax.dot_general(
        left, right, (((0,), (0,)), ((), ())), preferred_element_type=jnp.float32
    )


def settle_rows(gathered, weight, flipped, own_rows):

    def product_term(first_row, row_count):
        return product(gathered, weight, flipped)

    return lax.psum_scatter(
        product_term(jnp.int32(0), own_rows * lax.axis_size("row")),
        "row",
        scatter_dimension=0,
        tiled=True,
    )


def settle_cols(gathered, weight, flipped, own_rows):

    def product_term(first_row, row_count):
        return product(gathered, weight, flipped)

    return lax.psum_scatter(
        product_term(jnp.int32(0), own_rows * lax.axis_size("col")),
        "col",
        scatter_dimension=0,
        tiled=True,
    )


def row_sums(first_part, second_part):
    return lax.psum((jnp.sum(first_part, axis=1), jnp.sum(second_part, axis=1)), "row")


def norm_forward(residual, norm_gain, norm_shift):
    total_sum, square_sum = row_sums(residual, residual * residual)
    row_mean = (total_sum / WIDTH)[:, None]
    variance = (square_sum / WIDTH)[:, None] - row_mean * row_mean
    inv_std = lax.rsqrt(variance + NORM_EPS)
    normed = (residual - row_mean) * inv_std
    return (normed * norm_gain + norm_shift, normed, inv_std)


def norm_backward(grad_in, normed, inv_std, norm_gain):
    grad_norm = grad_in * norm_gain
    total_sum, cross_sum = row_sums(grad_norm, grad_norm * normed)
    grad_resid = inv_std * (grad_norm - total_sum[:, None] / WIDTH - normed * cross_sum[:, None] / WIDTH)
    return (grad_resid, jnp.sum(grad_in * normed, axis=0), jnp.sum(grad_in, axis=0))


def split_heads(array, seq_count):
    return array.reshape(seq_count, SEQ, array.shape[1] // HD, HD)


def pair_scores(queries, key_heads, segment_ids):
    position = jnp.arange(SEQ)
    same_doc = (segment_ids[:, None] == segment_ids[None, :]) & (segment_ids[None, :] != 0)
    allowed = same_doc | (position[:, None] == position[None, :])
    raw_scores = jnp.einsum(
        "qhd,khd->hqk", queries, key_heads, preferred_element_type=jnp.float32
    ) * HD ** (-0.5)
    return jnp.where(allowed[None], raw_scores, -1000000000.0)


def attend_forward(source):
    queries, key_heads, values, segment_ids = source
    scores = pair_scores(queries, key_heads, segment_ids)
    top_score = jnp.max(scores, axis=2, keepdims=True)
    exp_scores = jnp.exp(scores - top_score)
    total_sum = jnp.sum(exp_scores, axis=2, keepdims=True)
    soft_low = (exp_scores / total_sum).astype(jnp.bfloat16)
    attended = jnp.einsum("hqk,khd->qhd", soft_low, values, preferred_element_type=jnp.float32)
    return (attended.astype(jnp.bfloat16), (top_score + jnp.log(total_sum))[:, :, 0])


def attend_backward(source):
    queries, key_heads, values, segment_ids, grad_out, log_total = source
    scores = pair_scores(queries, key_heads, segment_ids)
    soft_weights = jnp.exp(scores - log_total[:, :, None])
    soft_low = soft_weights.astype(jnp.bfloat16)
    grad_values = jnp.einsum("hqk,qhd->khd", soft_low, grad_out, preferred_element_type=jnp.float32)
    grad_soft = jnp.einsum("qhd,khd->hqk", grad_out, values, preferred_element_type=jnp.float32)
    grad_scores = soft_weights * (
        grad_soft - jnp.sum(soft_weights * grad_soft, axis=2, keepdims=True)
    )
    grad_scores = grad_scores.astype(jnp.bfloat16)
    scale_factor = HD ** (-0.5)
    grad_queries = (
        jnp.einsum("hqk,khd->qhd", grad_scores, key_heads, preferred_element_type=jnp.float32)
        * scale_factor
    )
    grad_keys = (
        jnp.einsum("hqk,qhd->khd", grad_scores, queries, preferred_element_type=jnp.float32)
        * scale_factor
    )
    return (
        grad_queries.astype(jnp.bfloat16),
        grad_keys.astype(jnp.bfloat16),
        grad_values.astype(jnp.bfloat16),
    )


def split_heads_plan(
    tokens,
    segments,
    w_query,
    b_query,
    w_key,
    w_value,
    b_value,
    w_out,
    b_out,
    norm1_gain,
    norm1_shift,
    w_up,
    b_up,
    w_down,
    b_down,
    norm2_gain,
    norm2_shift,
    cotangent,
):
    rows_b = tokens.shape[0]
    rows_a = segments.shape[0]
    head_cols = w_query.shape[1]
    seq_count = rows_a // SEQ
    segment_seqs = segments.reshape(seq_count, SEQ)
    gathered_x = tokens_cols(tokens)
    stacked = jnp.concatenate([w_query, w_key, w_value], axis=1)
    projected = settle_rows(gathered_x, stacked, False, rows_a)
    queries = (projected[:, :head_cols] + b_query).astype(jnp.bfloat16)
    key_heads = projected[:, head_cols : 2 * head_cols].astype(jnp.bfloat16)
    values = (projected[:, 2 * head_cols :] + b_value).astype(jnp.bfloat16)
    query_seqs = split_heads(queries, seq_count)
    key_seqs = split_heads(key_heads, seq_count)
    value_seqs = split_heads(values, seq_count)
    attended, log_total = lax.map(attend_forward, (query_seqs, key_seqs, value_seqs, segment_seqs))
    attended = attended.reshape(rows_a, head_cols)
    gathered_o = tokens_rows(attended)
    attn_out = settle_cols(gathered_o, w_out, False, rows_b) + b_out
    hidden, normed1, inv_std1 = norm_forward(
        tokens.astype(jnp.float32) + attn_out, norm1_gain, norm1_shift
    )
    hidden_low = hidden.astype(jnp.bfloat16)
    gathered_h = tokens_cols(hidden_low)
    pre_act = settle_rows(gathered_h, w_up, False, rows_a) + b_up
    active = gelu_exact(pre_act).astype(jnp.bfloat16)
    gathered_a = tokens_rows(active)
    fed = settle_cols(gathered_a, w_down, False, rows_b) + b_down
    output, normed2, inv_std2 = norm_forward(hidden + fed, norm2_gain, norm2_shift)
    grad_r2, grad_gain2, grad_shift2 = norm_backward(
        cotangent.astype(jnp.float32), normed2, inv_std2, norm2_gain
    )
    grad_fed = grad_r2.astype(jnp.bfloat16)
    gathered_f = tokens_cols(grad_fed)
    grad_w_down = outer_sum(gathered_a, gathered_f)
    grad_active = settle_rows(gathered_f, w_down, True, rows_a)
    unused_out, slope_pull = jax.vjp(gelu_exact, pre_act)
    grad_pre = slope_pull(grad_active)[0].astype(jnp.bfloat16)
    gathered_p = tokens_rows(grad_pre)
    grad_w_up = outer_sum(gathered_h, gathered_p)
    grad_from_ff = settle_cols(gathered_p, w_up, True, rows_b)
    bias_up_part = jnp.sum(grad_pre.astype(jnp.float32), axis=0)
    bias_down_part = jnp.sum(grad_fed.astype(jnp.float32), axis=0)
    grad_r1, grad_gain1, grad_shift1 = norm_backward(
        grad_from_ff + grad_r2, normed1, inv_std1, norm1_gain
    )
    grad_attn = grad_r1.astype(jnp.bfloat16)
    gathered_d = tokens_cols(grad_attn)
    grad_w_out = outer_sum(gathered_o, gathered_d)
    grad_attended = settle_rows(gathered_d, w_out, True, rows_a).astype(jnp.bfloat16)
    grad_q, grad_k, grad_v = lax.map(
        attend_backward,
        (
            query_seqs,
            key_seqs,
            value_seqs,
            segment_seqs,
            split_heads(grad_attended, seq_count),
            log_total,
        ),
    )
    grad_q = grad_q.reshape(rows_a, head_cols)
    grad_k = grad_k.reshape(rows_a, head_cols)
    grad_v = grad_v.reshape(rows_a, head_cols)
    grad_proj = jnp.concatenate([grad_q, grad_k, grad_v], axis=1)
    gathered_g = tokens_rows(grad_proj)
    grad_stacked = outer_sum(gathered_x, gathered_g)
    tokens_grad = settle_cols(gathered_g, stacked, True, rows_b) + grad_r1
    bias_q, bias_v, bias_up = lax.psum(
        (
            jnp.sum(grad_q.astype(jnp.float32), axis=0),
            jnp.sum(grad_v.astype(jnp.float32), axis=0),
            bias_up_part,
        ),
        ("dp", "row"),
    )
    bias_out, bias_down, gain_one, shift_one, gain_two, shift_two = lax.psum(
        (
            jnp.sum(grad_attn.astype(jnp.float32), axis=0),
            bias_down_part,
            grad_gain1,
            grad_shift1,
            grad_gain2,
            grad_shift2,
        ),
        ("dp", "col"),
    )
    sum_stacked, sum_out, sum_up, sum_down = (
        lax.psum(grad_stacked.astype(jnp.bfloat16), "dp").astype(jnp.float32),
        lax.psum(grad_w_out.astype(jnp.bfloat16), "dp").astype(jnp.float32),
        lax.psum(grad_w_up.astype(jnp.bfloat16), "dp").astype(jnp.float32),
        lax.psum(grad_w_down.astype(jnp.bfloat16), "dp").astype(jnp.float32),
    )
    return (
        output.astype(jnp.bfloat16),
        tokens_grad.astype(jnp.bfloat16),
        sum_stacked[:, :head_cols],
        bias_q,
        sum_stacked[:, head_cols : 2 * head_cols],
        sum_stacked[:, 2 * head_cols :],
        bias_v,
        sum_out,
        bias_out,
        gain_one,
        shift_one,
        sum_up,
        bias_up,
        sum_down,
        bias_down,
        gain_two,
        shift_two,
    )


def solution(mesh):
    dp, rows, cols = (mesh.shape[name] for name in ("dp", "row", "col"))
    whole = TOKENS // SEQ == dp * rows * cols and dp == 4 and cols == 2
    plan = whole_sequences if whole else split_heads_plan
    placed = (
        P(("dp", "col"), "row"),
        P(("dp", "row")),
        P("row", "col"),
        P("col"),
        P("row", "col"),
        P("row", "col"),
        P("col"),
        P("col", "row"),
        P("row"),
        P("row"),
        P("row"),
        P("row", "col"),
        P("col"),
        P("col", "row"),
        P("row"),
        P("row"),
        P("row"),
        P(("dp", "col"), "row"),
    )
    return jax.shard_map(
        plan,
        mesh=mesh,
        in_specs=placed,
        out_specs=(
            P(("dp", "col"), "row"),
            P(("dp", "col"), "row"),
            P("row", "col"),
            P("col"),
            P("row", "col"),
            P("row", "col"),
            P("col"),
            P("col", "row"),
            P("row"),
            P("row"),
            P("row"),
            P("row", "col"),
            P("col"),
            P("col", "row"),
            P("row"),
            P("row"),
            P("row"),
        ),
        check_vma=False,
    )
```

```python
import math

import jax
import jax.numpy as jnp
from jax import lax
from jax.experimental import pallas as pl
from jax.experimental.pallas import tpu as pltpu
from jax.sharding import PartitionSpec as P

HD = 64
SEQ = 1024
WIDTH = 1024
TOKENS = 32768
NORM_EPS = 1e-05
BF = jnp.bfloat16
F32 = jnp.float32
NEG = -1e30
QB = 256


def mm(a, b):
    return jnp.dot(a, b, preferred_element_type=F32)


def mm_t(a, b):
    return lax.dot_general(a, b, (((1,), (1,)), ((), ())), preferred_element_type=F32)


def tmm(a, b):
    return lax.dot_general(a, b, (((0,), (0,)), ((), ())), preferred_element_type=F32)


def gelu_exact(v):
    return jax.nn.gelu(v, approximate=False)


def attend_rows(qkv_ref, seg_col_ref, seg_row, o_ref, p_ref, linv_ref, i):
    lane = lax.broadcasted_iota(jnp.int32, (QB, 128), 1)
    scale = HD ** (-0.5) * math.log2(math.e)
    rows = slice(i * QB, (i + 1) * QB)
    q = qkv_ref[rows, 0:128]
    k = qkv_ref[:, 128:256]
    v = qkv_ref[:, 256:384]
    seg_col = seg_col_ref[rows, :]
    outs = []
    for h in range(2):
        mine = (lane < HD) if h == 0 else (lane >= HD)
        qm = jnp.where(mine, q, jnp.zeros_like(q))
        s = mm_t(qm, k)
        s = jnp.where(seg_col == seg_row, s * scale, NEG)
        top = jnp.max(s, axis=1, keepdims=True)
        p = jnp.exp2(s - top)
        total = jnp.sum(p, axis=1, keepdims=True)
        pb = p.astype(BF)
        p_ref[h, rows, :] = pb
        inv = 1.0 / total
        outs.append((mm(pb, v) * inv, jnp.broadcast_to(inv, (QB, 128))))
    o_ref[rows, :] = jnp.where(lane < HD, outs[0][0], outs[1][0]).astype(BF)
    linv_ref[rows, :] = jnp.where(lane < HD, outs[0][1], outs[1][1])


def attend_fwd_kernel(
    x_ref, w_ref, b_ref, seg_col_ref, seg_row_ref, po, pu, pd,
    qkv_ref, o_ref, p_ref, linv_ref, wo, wu, wd, o_recv, o_sent, u_recv, u_sent, d_recv, d_sent,
):
    j = pl.program_id(0)
    peers = Peers()
    go = Gather(peers, po, wo, False, o_recv, o_sent, RING + NEAR + FAR)
    gu = Gather(peers, pu, wu, True, u_recv, u_sent, RING + NEAR)
    gd = Gather(peers, pd, wd, False, d_recv, d_sent, RING + DOWN_NEAR)
    every = (go, gu, gd)

    def hook(at, *stages):
        @pl.when(j == at)
        def _():
            for which, blocks in stages:
                for g in which:
                    g.relay(*blocks)

    @pl.when(j == 0)
    def _():
        peers.greet(ALL_PEERS)
        for g in every:
            g.start()

    seg_row = seg_row_ref[...]
    hook(1, ((go, gu), [(1, 0)]))
    hook(2, (every, [(0, 2), (0, 4)]))
    hook(3, ((go, gu), [(2, 0)]), ((go,), [(1, 2), (1, 4)]))
    hook(4, ((gu, gd), [(1, 2), (1, 4)]))
    hook(5, ((go, gu), [(3, 0)]))
    hook(6, (every, [(2, 2), (2, 4)]), ((go,), [(0, 6), (1, 6)]))
    hook(7, ((go,), [(3, 2), (3, 4)]))
    qkv_ref[...] = (mm(x_ref[...], w_ref[...]) + b_ref[...]).astype(BF)
    for i in range(SEQ // QB):
        if i == SEQ // QB // 2:
            hook(1, ((gd,), [(1, 0)]))
            hook(3, ((gd,), [(2, 0)]))
            hook(5, ((gd,), [(3, 0)]))
            hook(7, ((go,), [(2, 6), (3, 6)]), ((gu,), [(3, 2), (3, 4)]))
        attend_rows(qkv_ref, seg_col_ref, seg_row, o_ref, p_ref, linv_ref, i)

    @pl.when(j == 7)
    def _():
        for g in every:
            g.finish()


VMEM_LIMIT = 56 * 1024 * 1024


def attend_fwd(x, w_qkv, b_qkv, seg_col, seg_row, po, pu, pd):
    slots = w_qkv.shape[1] // 384
    whole = pl.BlockSpec(memory_space=pl.ANY)
    dma = pltpu.SemaphoreType.DMA
    return pl.pallas_call(
        attend_fwd_kernel,
        grid=(slots,),
        in_specs=[
            pl.BlockSpec((SEQ, x.shape[1]), lambda j: (0, 0)),
            pl.BlockSpec((x.shape[1], 384), lambda j: (0, j)),
            pl.BlockSpec((1, 384), lambda j: (0, j)),
            pl.BlockSpec((SEQ, 1), lambda j: (0, 0)),
            pl.BlockSpec((1, SEQ), lambda j: (0, 0)),
            whole,
            whole,
            whole,
        ],
        out_specs=[
            pl.BlockSpec((SEQ, 384), lambda j: (0, j)),
            pl.BlockSpec((SEQ, 128), lambda j: (0, j)),
            pl.BlockSpec((2, SEQ, SEQ), lambda j: (j, 0, 0)),
            pl.BlockSpec((SEQ, 128), lambda j: (0, j)),
            whole,
            whole,
            whole,
        ],
        out_shape=[
            jax.ShapeDtypeStruct((SEQ, slots * 384), BF),
            jax.ShapeDtypeStruct((SEQ, slots * 128), BF),
            jax.ShapeDtypeStruct((slots * 2, SEQ, SEQ), BF),
            jax.ShapeDtypeStruct((SEQ, slots * 128), F32),
            jax.ShapeDtypeStruct((8 * po.shape[0], 4 * po.shape[1]), BF),
            jax.ShapeDtypeStruct((4 * pu.shape[0], 8 * pu.shape[1]), BF),
            jax.ShapeDtypeStruct((8 * pd.shape[0], 4 * pd.shape[1]), BF),
        ],
        scratch_shapes=[dma((32,)), dma((32,))] * 3,
        compiler_params=pltpu.CompilerParams(vmem_limit_bytes=VMEM_LIMIT, collective_id=1, has_side_effects=True),
        cost_estimate=pl.CostEstimate(
            flops=slots * 2 * 4 * SEQ * SEQ * 256,
            bytes_accessed=slots * 5 * SEQ * SEQ,
            transcendentals=slots * 2 * SEQ * SEQ,
        ),
        name="attend_fwd",
    )(x, w_qkv, b_qkv, seg_col, seg_row, po, pu, pd)


MESH = pl.DeviceIdType.MESH
ANY = pl.BlockSpec(memory_space=pl.ANY)
DMA = pltpu.SemaphoreType.DMA


class Peers:
    def __init__(self):
        self.r = lax.axis_index("row")
        d = lax.axis_index("dp")
        self.ids = {
            "core": {"dp": d + 1 - 2 * lax.rem(d, 2)},
            "x": {"dp": lax.rem(d + 2, 4)},
            "y": {"col": 1 - lax.axis_index("col")},
            1: {"row": lax.rem(self.r + 1, 4)},
            2: {"row": lax.rem(self.r + 2, 4)},
            3: {"row": lax.rem(self.r + 3, 4)},
        }

    def greet(self, names):
        barrier = pltpu.get_barrier_semaphore()
        for name in names:
            pl.semaphore_signal(barrier, inc=1, device_id=self.ids[name], device_id_type=MESH)
        pl.semaphore_wait(barrier, len(names))


def send(peers, name, src, dst, send_sem, recv_sem):
    return pltpu.make_async_remote_copy(
        src_ref=src, dst_ref=dst, send_sem=send_sem, recv_sem=recv_sem, device_id=peers.ids[name], device_id_type=MESH
    )


def near_edges(s):
    return [("x", s, 0, s, 2), ("y", s, 0, s, 4), ("core", s, 0, s, 1)]


def second_edges(s):
    return [("core", s, 2, s, 3), ("core", s, 4, s, 5)]


def far_edges(s):
    return [("y", s, 2, s, 6) if s % 2 == 0 else ("x", s, 4, s, 6), ("core", s, 6, s, 7)]


RING = [(1, s, 0, s + 1, 0) for s in range(3)]
NEAR = [e for s in range(4) for e in near_edges(s) + second_edges(s)]
FAR = [e for s in range(4) for e in far_edges(s)]
DOWN_NEAR = [e for s in range(3) for e in near_edges(s) + second_edges(s)] + [("core", 3, 0, 3, 1)]
DOWN_REST = [e for e in near_edges(3) if e[0] != "core"] + second_edges(3) + FAR


class Gather:
    def __init__(self, peers, piece, full, by_rows, recv, sent, edges):
        self.peers, self.piece, self.full, self.recv, self.sent = peers, piece, full, recv, sent
        self.by_rows = by_rows
        self.n = full.shape[1 if by_rows else 0] // 8
        self.m = full.shape[0 if by_rows else 1] // 4
        self.edges = edges
        self.waited = set()
        self.emitted = set()

    def blk(self, s, t):
        a = pl.ds(s * self.m, self.m)
        b = pl.ds(t * self.n, self.n)
        return self.full.at[a, b] if self.by_rows else self.full.at[b, a]

    def copy(self, at):
        name, s, t, s2, t2 = self.edges[at]
        src = self.piece if (s, t) == (0, 0) and self.piece is not None else self.blk(s, t)
        return send(self.peers, name, src, self.blk(s2, t2), self.sent.at[at], self.recv.at[at])

    def emit(self, s, t):
        for at, e in enumerate(self.edges):
            if e[1:3] == (s, t):
                assert at not in self.emitted
                self.emitted.add(at)
                self.copy(at).start()

    def arrived(self, s, t):
        for at, e in enumerate(self.edges):
            if e[3:5] == (s, t) and at not in self.waited:
                self.waited.add(at)
                self.copy(at).wait_recv()

    def relay(self, *blocks):
        for s, t in blocks:
            self.arrived(s, t)
            self.emit(s, t)

    def own(self):
        return pltpu.make_async_copy(self.piece, self.blk(0, 0), self.sent.at[len(self.edges)])

    def start(self):
        self.emit(0, 0)
        self.own().start()

    def finish(self):
        if self.piece is not None:
            self.own().wait()
        for at, e in enumerate(self.edges):
            if at not in self.waited:
                self.waited.add(at)
                self.copy(at).wait_recv()
        assert len(self.emitted) == len(self.edges)
        for at in range(len(self.edges)):
            self.copy(at).wait_send()


class Inward:
    def __init__(self, peers, block, rows, recv, sent):
        self.peers, self.block, self.rows, self.recv, self.sent = peers, block, rows, recv, sent

    def copy(self, s):
        r = lax.rem(self.peers.r + s, 4)
        src = self.block.at[pl.ds(pl.multiple_of(r * SEQ, SEQ), SEQ), :]
        f = self.block.shape[1]
        dst = self.rows.at[:, pl.ds(s * f, f)]
        if s == 0:
            return pltpu.make_async_copy(src, dst, self.sent.at[0])
        return send(self.peers, s, src, dst, self.sent.at[s], self.recv.at[s])

    def start(self):
        for s in (2, 1, 3, 0):
            self.copy(s).start()

    def finish(self):
        self.copy(0).wait()
        for s in (1, 2, 3):
            self.copy(s).wait()


ALL_PEERS = ("core", "x", "y", 1, 2, 3)


def first_kernel(tokens, piece, x, w, g_recv, g_sent, i_recv, i_sent):
    peers = Peers()
    peers.greet(ALL_PEERS)
    g = Gather(peers, piece, w, True, g_recv, g_sent, RING + NEAR + FAR)
    a = Inward(peers, tokens, x, i_recv, i_sent)
    g.start()
    a.start()
    for s in (1, 2, 3):
        g.relay((s, 0), (s - 1, 2), (s - 1, 4))
    g.relay((3, 2), (3, 4))
    for s in range(4):
        g.relay((s, 6))
    g.finish()
    a.finish()


def first(tokens, piece):
    return pl.pallas_call(
        first_kernel,
        in_specs=[ANY, ANY],
        out_specs=[ANY, ANY],
        out_shape=[
            jax.ShapeDtypeStruct((SEQ, 4 * tokens.shape[1]), BF),
            jax.ShapeDtypeStruct((4 * piece.shape[0], 8 * piece.shape[1]), BF),
        ],
        scratch_shapes=[DMA((32,)), DMA((32,)), DMA((4,)), DMA((4,))],
        compiler_params=pltpu.CompilerParams(collective_id=0, has_side_effects=True),
        name="first",
    )(tokens, piece)


RB = 128


def norm_rows(v):
    mean = jnp.mean(v, axis=1, keepdims=True)
    variance = jnp.mean(v * v, axis=1, keepdims=True) - mean * mean
    inv = lax.rsqrt(variance + NORM_EPS)
    return (v - mean) * inv, inv


def norm_rows_back(g, normed, inv):
    mean_g = jnp.mean(g, axis=1, keepdims=True)
    mean_gn = jnp.mean(g * normed, axis=1, keepdims=True)
    return inv * (g - mean_g - normed * mean_gn)


def gelu_and_slope(v):
    z = jnp.abs(v) * (0.5 ** 0.5)
    t = 1.0 / (1.0 + 0.3275911 * z)
    poly = t * (0.254829592 + t * (-0.284496736 + t * (1.421413741 + t * (-1.453152027 + t * 1.061405429))))
    bell = jnp.exp2(z * z * -math.log2(math.e))
    tail = 0.5 * poly * bell
    cdf = jnp.where(v >= 0, 1.0 - tail, tail)
    return v * cdf, cdf + v * bell * (1.0 / math.sqrt(2.0 * math.pi))


def row_blocks(body, n=RB):
    def run(i, carry):
        body(pl.ds(pl.multiple_of(i * n, n), n))
        return carry

    lax.fori_loop(0, SEQ // n, run, 0)


def ff_fwd_kernel(
    x_ref, att_ref, wo_ref, vec_ref, bu_ref, cot, wu_in, wd_in,
    wu, wd, act_ref, slope_ref, hlow_ref, normed1_ref, inv1_ref, out_ref, r2_ref, vg_ref,
    acc, wu_buf, wd_buf, cot_buf, buf_sem, u_recv, u_sent, d_recv, d_sent, i_recv, i_sent,
):
    j = pl.program_id(0)
    peers = Peers()
    gu = Gather(peers, None, wu, True, u_recv, u_sent, FAR)
    gd = Gather(peers, None, wd, False, d_recv, d_sent, DOWN_REST)
    inward = Inward(peers, cot, cot_buf, i_recv, i_sent)
    n = wu_buf.shape[2]

    def fetch(t, slot):
        cols = pl.ds(pl.multiple_of(t * n, n), n)
        return (
            pltpu.make_async_copy(wu.at[:, cols], wu_buf.at[slot], buf_sem.at[0, slot]),
            pltpu.make_async_copy(wd.at[cols, :], wd_buf.at[slot], buf_sem.at[1, slot]),
        )

    @pl.when(j == 0)
    def _():
        peers.greet(ALL_PEERS)
        for t in range(2):
            for c in fetch(t, t):
                c.start()
        gd.emit(3, 0)
        for s in range(3):
            gu.emit(s, 2 if s % 2 == 0 else 4)
            gd.emit(s, 2 if s % 2 == 0 else 4)
        gu.emit(3, 4)
        inward.start()

        def body(rows):
            v = x_ref[rows, :].astype(F32) + mm(att_ref[rows, :], wo_ref[...]) + vec_ref[0:1, :]
            normed, inv = norm_rows(v)
            normed1_ref[rows, :] = normed
            inv1_ref[rows, :] = jnp.broadcast_to(inv, (RB, 128))
            hlow_ref[rows, :] = (normed * vec_ref[1:2, :] + vec_ref[2:3, :]).astype(BF)

        row_blocks(body)
        acc[...] = jnp.zeros_like(acc)
        gd.relay((3, 2), (3, 4))

    @pl.when(j == 1)
    def _():
        gd.arrived(3, 3)
        for s in range(4):
            gu.relay((s, 6))

    @pl.when(j == 2)
    def _():
        gd.arrived(3, 5)

    @pl.when(j == 4)
    def _():
        for s in range(4):
            gd.relay((s, 6))

    @pl.when(j == 5)
    def _():
        for s in range(4):
            gu.arrived(s, 7)
            gd.arrived(s, 7)

    slot = lax.rem(j, 2)
    for c in fetch(j, slot):
        c.wait()
    w_up = wu_buf.at[slot]
    w_down = wd_buf.at[slot]
    bias = bu_ref[...]
    for i in range(SEQ // 256):
        rows = slice(i * 256, (i + 1) * 256)
        act, slope = gelu_and_slope(mm(hlow_ref[rows, :], w_up[...]) + bias)
        act = act.astype(BF)
        act_ref[rows, :] = act
        slope_ref[rows, :] = slope.astype(BF)
        acc[rows, :] += mm(act, w_down[...])

    @pl.when(j < 6)
    def _():
        for c in fetch(j + 2, slot):
            c.start()

    @pl.when(j == 7)
    def _():
        inward.finish()
        vg_ref[...] = jnp.zeros_like(vg_ref)

        def body(rows):
            hidden = normed1_ref[rows, :] * vec_ref[1:2, :] + vec_ref[2:3, :]
            normed, inv = norm_rows(hidden + (acc[rows, :] + vec_ref[3:4, :]))
            out_ref[rows, :] = (normed * vec_ref[4:5, :] + vec_ref[5:6, :]).astype(BF)
            c = cot_buf[rows, :].astype(F32)
            r2 = norm_rows_back(c * vec_ref[4:5, :], normed, inv)
            r2_ref[rows, :] = r2
            vg_ref[0:1, :] += jnp.sum(c * normed, axis=0, keepdims=True)
            vg_ref[1:2, :] += jnp.sum(c, axis=0, keepdims=True)
            vg_ref[2:3, :] += jnp.sum(r2.astype(BF).astype(F32), axis=0, keepdims=True)

        row_blocks(body)
        gu.finish()
        gd.finish()


ONCE = pl.Buffered(1)


def const(*shape):
    return pl.BlockSpec(shape, lambda j: (0,) * len(shape), pipeline_mode=ONCE)


def ff_fwd(x, att, wo, vec, bu, cot, wu, wd):
    width, units = wu.shape
    n = units // 8
    return pl.pallas_call(
        ff_fwd_kernel,
        grid=(8,),
        in_specs=[
            const(SEQ, width),
            const(SEQ, width),
            const(width, width),
            const(8, width),
            pl.BlockSpec((1, n), lambda j: (0, j)),
            ANY,
            ANY,
            ANY,
        ],
        out_specs=[
            ANY,
            ANY,
            pl.BlockSpec((SEQ, n), lambda j: (0, j)),
            pl.BlockSpec((SEQ, n), lambda j: (0, j)),
            const(SEQ, width),
            const(SEQ, width),
            const(SEQ, 128),
            const(SEQ, width),
            const(SEQ, width),
            const(8, width),
        ],
        out_shape=[
            jax.ShapeDtypeStruct(wu.shape, BF),
            jax.ShapeDtypeStruct(wd.shape, BF),
            jax.ShapeDtypeStruct((SEQ, units), BF),
            jax.ShapeDtypeStruct((SEQ, units), BF),
            jax.ShapeDtypeStruct((SEQ, width), BF),
            jax.ShapeDtypeStruct((SEQ, width), F32),
            jax.ShapeDtypeStruct((SEQ, 128), F32),
            jax.ShapeDtypeStruct((SEQ, width), BF),
            jax.ShapeDtypeStruct((SEQ, width), F32),
            jax.ShapeDtypeStruct((8, width), F32),
        ],
        input_output_aliases={6: 0, 7: 1},
        scratch_shapes=[
            pltpu.VMEM((SEQ, width), F32),
            pltpu.VMEM((2, width, n), BF),
            pltpu.VMEM((2, n, width), BF),
            pltpu.VMEM((SEQ, width), BF),
            DMA((2, 2)),
            DMA((32,)),
            DMA((32,)),
            DMA((32,)),
            DMA((32,)),
            DMA((4,)),
            DMA((4,)),
        ],
        compiler_params=pltpu.CompilerParams(vmem_limit_bytes=VMEM_LIMIT, collective_id=2, has_side_effects=True),
        name="ff_fwd",
    )(x, att, wo, vec, bu, cot, wu, wd)


ORDER = (7, 6, 1, 3, 5, 0, 2, 4)


def slot_at(j):
    return jnp.where(j < 2, 7 - j, jnp.where(j < 5, 2 * j - 3, 2 * j - 10))


def sum_rows(dst, *srcs):
    n = dst.shape[0]
    step = min(n, 64)

    def run(i, carry):
        rows = pl.ds(pl.multiple_of(i * step, step), step)
        total = srcs[0][rows, :].astype(F32)
        for src in srcs[1:]:
            total += src[rows, :].astype(F32)
        dst[rows, :] = total.astype(BF)
        return carry

    lax.fori_loop(0, n // step, run, 0)


class Fold:
    SCRATCH = 12

    @staticmethod
    def scratch(a, b):
        return [
            pltpu.VMEM((2, a, b), BF),
            pltpu.VMEM((4, a, b), BF),
            pltpu.VMEM((a, b), BF),
            pltpu.VMEM((2, a // 2, b), BF),
            DMA((12,)),
        ]

    def __init__(self, peers, stage, land, corner, land_corner, sems):
        self.peers, self.stage, self.land, self.corner, self.land_corner, self.sems = (
            peers, stage, land, corner, land_corner, sems,
        )
        self.half = corner.shape[0] // 2

    def to_core(self, p):
        k = (ORDER[p] - 1) // 2
        return send(self.peers, "core", self.stage.at[p % 2], self.land.at[k], self.sems.at[4 + k], self.sems.at[k])

    def to_side(self, h):
        src = self.corner.at[pl.ds(h * self.half, self.half), :]
        return send(self.peers, "xy"[1 - h], src, self.land_corner.at[h], self.sems.at[10 + h], self.sems.at[8 + h])

    def before(self, j):
        for p in (2, 4, 5, 6):
            @pl.when(j == p)
            def _(p=p):
                self.to_core(p - 2).wait_send()

    def from_core(self, t):
        k = t // 2
        self.to_core(ORDER.index(t + 1)).wait_recv()
        return self.land.at[k]

    def after(self, j, out):
        for p, t in enumerate(ORDER):
            @pl.when(j == p)
            def _(p=p, t=t):
                mine = self.stage.at[p % 2]
                if t % 2 == 1:
                    self.to_core(p).start()
                    return
                theirs = self.from_core(t)
                if t == 6:
                    sum_rows(self.corner, mine, theirs)
                    self.to_side(0).start()
                    self.to_side(1).start()
                    return
                if t == 0:
                    sum_rows(out, mine, theirs)
                    return
                h = t // 2 - 1
                self.to_side(h).wait_recv()
                for q in range(2):
                    rows = pl.ds(q * self.half, self.half)
                    more = (self.land_corner.at[h],) if q == h else ()
                    sum_rows(out.at[rows, :], mine.at[rows, :], theirs.at[rows, :], *more)

    def finish(self):
        self.to_side(0).wait_send()
        self.to_side(1).wait_send()


class Cross:
    def __init__(self, peers, kept, own, land_x, land_y, sems):
        self.peers, self.kept, self.own, self.land_x, self.land_y, self.sems = peers, kept, own, land_x, land_y, sems

    def copies(self):
        s = self.sems
        return (
            send(self.peers, "x", self.kept.at[1], self.land_x, s.at[0], s.at[1]),
            send(self.peers, "y", self.kept.at[2], self.land_y, s.at[2], s.at[3]),
            pltpu.make_async_copy(self.kept.at[0], self.own, s.at[4]),
        )

    def start(self):
        for c in self.copies():
            c.start()

    def finish(self, out):
        for c in self.copies():
            c.wait()
        sum_rows(out, self.own, self.land_x, self.land_y)


class Deal:
    def __init__(self, peers, total, by_rows, land, sems):
        self.peers, self.total, self.by_rows, self.land, self.sems = peers, total, by_rows, land, sems

    def part(self, s):
        n = self.total.shape[0 if self.by_rows else 1] // 4
        return self.total.at[pl.ds(s * n, n), :] if self.by_rows else self.total.at[:, pl.ds(s * n, n)]

    def copy(self, s):
        return send(self.peers, 4 - s, self.part(s), self.land.at[s - 1], self.sems.at[2 + s], self.sems.at[s - 1])

    def start(self):
        for s in (2, 1, 3):
            self.copy(s).start()

    def finish(self, out):
        for s in (1, 2, 3):
            self.copy(s).wait()
        sum_rows(out, self.part(0), self.land.at[0], self.land.at[1], self.land.at[2])


class Spread:
    def __init__(self, peers, own, place, sems):
        d = lax.axis_index("dp")
        self.peers, self.own, self.sems, self.here = peers, own, sems, place(d)
        self.from_x = place(lax.rem(d + 2, 4))

    def local(self):
        return pltpu.make_async_copy(self.own, self.here, self.sems.at[6])

    def copies(self):
        s = self.sems
        return (
            send(self.peers, "x", self.own, self.here, s.at[0], s.at[1]),
            send(self.peers, "core", self.own, self.here, s.at[2], s.at[3]),
            send(self.peers, "core", self.from_x, self.from_x, s.at[4], s.at[5]),
        )

    def start(self):
        to_x, to_core, _ = self.copies()
        to_x.start()
        to_core.start()
        self.local().start()

    def relay(self):
        to_x, _, on = self.copies()
        to_x.wait_recv()
        on.start()

    def finish(self):
        to_x, to_core, on = self.copies()
        to_x.wait_send()
        to_core.wait()
        on.wait()
        self.local().wait()


class Outward:
    def __init__(self, peers, rows, block, sems, parts=(2, 1, 3, 0)):
        self.peers, self.rows, self.block, self.sems, self.parts = peers, rows, block, sems, parts

    def copy(self, s):
        f = self.block.shape[1]
        src = self.rows.at[:, pl.ds(s * f, f)]
        dst = self.block.at[pl.ds(pl.multiple_of(self.peers.r * SEQ, SEQ), SEQ), :]
        if s == 0:
            return pltpu.make_async_copy(src, dst, self.sems.at[0])
        return send(self.peers, 4 - s, src, dst, self.sems.at[s], self.sems.at[4 + s])

    def start(self):
        for s in self.parts:
            self.copy(s).start()

    def finish(self):
        for s in self.parts:
            self.copy(s).wait()


def ff_down_bwd_kernel(
    r2_ref, wd_ref, act_ref, slope_ref, out, out_block, gp_ref, bu_ref, kept_ref,
    gfed, stage, land, corner, land_corner, f_sems, o_sems,
):
    j = pl.program_id(0)
    peers = Peers()
    outward = Outward(peers, out, out_block, o_sems, (2, 0))
    fold = Fold(peers, stage, land, corner, land_corner, f_sems)

    @pl.when(j == 0)
    def _():
        peers.greet(ALL_PEERS)
        outward.start()

        def body(rows):
            gfed[rows, :] = r2_ref[rows, :].astype(BF)

        row_blocks(body)

    bsum = jnp.zeros((1, bu_ref.shape[1]), F32)
    for i in range(SEQ // 256):
        rows = slice(i * 256, (i + 1) * 256)
        g = (mm_t(gfed[rows, :], wd_ref[...]) * slope_ref[rows, :].astype(F32)).astype(BF)
        gp_ref[rows, :] = g
        bsum += jnp.sum(g.astype(F32), axis=0, keepdims=True)
    bu_ref[...] = jnp.broadcast_to(bsum, bu_ref.shape)
    fold.before(j)
    stage[lax.rem(j, 2)] = tmm(act_ref[...], gfed[...]).astype(BF)
    fold.after(j, kept_ref.at[0])

    @pl.when(j == 7)
    def _():
        fold.finish()
        outward.finish()


def kept_spec(a, b):
    return pl.BlockSpec((1, a, b), lambda j: (jnp.maximum(j - 5, 0), 0, 0))


def ff_down_bwd(r2, wd, act, slope, out):
    units, width = wd.shape
    n = units // 8
    return pl.pallas_call(
        ff_down_bwd_kernel,
        grid=(8,),
        in_specs=[
            const(SEQ, width),
            pl.BlockSpec((n, width), lambda j: (slot_at(j), 0)),
            pl.BlockSpec((SEQ, n), lambda j: (0, slot_at(j))),
            pl.BlockSpec((SEQ, n), lambda j: (0, slot_at(j))),
            ANY,
        ],
        out_specs=[
            ANY,
            pl.BlockSpec((SEQ, n), lambda j: (0, slot_at(j))),
            pl.BlockSpec((8, n), lambda j: (0, slot_at(j))),
            kept_spec(n, width),
        ],
        out_shape=[
            jax.ShapeDtypeStruct((4 * SEQ, width // 4), BF),
            jax.ShapeDtypeStruct((SEQ, units), BF),
            jax.ShapeDtypeStruct((8, units), F32),
            jax.ShapeDtypeStruct((3, n, width), BF),
        ],
        scratch_shapes=[pltpu.VMEM((SEQ, width), BF), *Fold.scratch(n, width), DMA((8,))],
        compiler_params=pltpu.CompilerParams(vmem_limit_bytes=VMEM_LIMIT, collective_id=3, has_side_effects=True),
        name="ff_down_bwd",
    )(r2, wd, act, slope, out)


def ff_up_bwd_kernel(
    r2_ref, hlow_ref, gp_ref, wu_ref, normed1_ref, inv1_ref, vec_ref, out, out_block_in, kept_d,
    out_block, r1_ref, gattn_ref, vg_ref, kept_ref, own_ref,
    hlow_t, stage, land, corner, land_corner, f_sems, own_d, land_x, land_y, c_sems, o_sems,
):
    j = pl.program_id(0)
    peers = Peers()
    outward = Outward(peers, out, out_block, o_sems, (1, 3))
    fold = Fold(peers, stage, land, corner, land_corner, f_sems)
    cross = Cross(peers, kept_d, own_d, land_x, land_y, c_sems)

    @pl.when(j == 0)
    def _():
        peers.greet(ALL_PEERS)
        cross.start()
        outward.start()
        r1_ref[...] = r2_ref[...]
        for i in range(SEQ // 256):
            rows = slice(i * 256, (i + 1) * 256)
            hlow_t[:, rows] = jnp.transpose(hlow_ref[rows, :])

    fold.before(j)
    stage[lax.rem(j, 2)] = mm(hlow_t[...], gp_ref[...]).astype(BF)
    fold.after(j, kept_ref.at[0])
    r1_ref[...] += mm_t(gp_ref[...], wu_ref[...])

    @pl.when(j == 7)
    def _():
        vg_ref[...] = jnp.zeros_like(vg_ref)

        def body(rows):
            gh = r1_ref[rows, :]
            normed = normed1_ref[rows, :]
            r1 = norm_rows_back(gh * vec_ref[1:2, :], normed, inv1_ref[rows, 0:1])
            r1_ref[rows, :] = r1
            low = r1.astype(BF)
            gattn_ref[rows, :] = low
            vg_ref[0:1, :] += jnp.sum(gh * normed, axis=0, keepdims=True)
            vg_ref[1:2, :] += jnp.sum(gh, axis=0, keepdims=True)
            vg_ref[2:3, :] += jnp.sum(low.astype(F32), axis=0, keepdims=True)

        row_blocks(body)
        cross.finish(own_ref)
        fold.finish()
        outward.finish()


def ff_up_bwd(r2, hlow, gp, wu, normed1, inv1, vec, out, out_block, kept_d):
    width, units = wu.shape
    n = units // 8
    return pl.pallas_call(
        ff_up_bwd_kernel,
        grid=(8,),
        in_specs=[
            const(SEQ, width),
            const(SEQ, width),
            pl.BlockSpec((SEQ, n), lambda j: (0, slot_at(j))),
            pl.BlockSpec((width, n), lambda j: (0, slot_at(j))),
            const(SEQ, width),
            const(SEQ, 128),
            const(8, width),
            ANY,
            ANY,
            ANY,
        ],
        out_specs=[
            ANY,
            const(SEQ, width),
            const(SEQ, width),
            const(8, width),
            kept_spec(width, n),
            const(n, width),
        ],
        out_shape=[
            jax.ShapeDtypeStruct(out_block.shape, BF),
            jax.ShapeDtypeStruct((SEQ, width), F32),
            jax.ShapeDtypeStruct((SEQ, width), BF),
            jax.ShapeDtypeStruct((8, width), F32),
            jax.ShapeDtypeStruct((3, width, n), BF),
            jax.ShapeDtypeStruct((n, width), BF),
        ],
        input_output_aliases={8: 0},
        scratch_shapes=[
            pltpu.VMEM((width, SEQ), BF),
            *Fold.scratch(width, n),
            pltpu.VMEM((n, width), BF),
            pltpu.VMEM((n, width), BF),
            pltpu.VMEM((n, width), BF),
            DMA((5,)),
            DMA((8,)),
        ],
        compiler_params=pltpu.CompilerParams(vmem_limit_bytes=VMEM_LIMIT, collective_id=4, has_side_effects=True),
        name="ff_up_bwd",
    )(r2, hlow, gp, wu, normed1, inv1, vec, out, out_block, kept_d)


def attend_bwd_kernel(
    gattn_ref, wo_ref, att_ref, qkv_ref, linv_ref, p_ref, x_ref, w_ref, r1, tot_d, kept_u,
    xg_ref, gsum_ref, kept_q, kept_o, down_ref, up_ref,
    x_t, acc, ds_ref, g_ref, a_sem,
    q_stage, q_land, q_corner, q_land_corner, q_sems, o_stage, o_land, o_corner, o_land_corner, o_sems,
    zd_land, zd_sems, own_u, land_x, land_y, c_sems, tot_u, zu_land, zu_sems,
):
    j = pl.program_id(0)
    peers = Peers()
    fold_q = Fold(peers, q_stage, q_land, q_corner, q_land_corner, q_sems)
    fold_o = Fold(peers, o_stage, o_land, o_corner, o_land_corner, o_sems)
    deal_d = Deal(peers, tot_d, False, zd_land, zd_sems)
    cross_u = Cross(peers, kept_u, own_u, land_x, land_y, c_sems)
    deal_u = Deal(peers, tot_u, True, zu_land, zu_sems)
    load = pltpu.make_async_copy(r1, acc, a_sem)

    @pl.when(j == 0)
    def _():
        peers.greet(ALL_PEERS)
        load.start()
        cross_u.start()
        deal_d.start()
        for i in range(SEQ // 256):
            rows = slice(i * 256, (i + 1) * 256)
            x_t[:, rows] = jnp.transpose(x_ref[rows, :])
        load.wait()

    @pl.when(j == 4)
    def _():
        cross_u.finish(tot_u)
        deal_u.start()
        deal_d.finish(down_ref)

    lane = lax.broadcasted_iota(jnp.int32, (SEQ, 128), 1)
    scale = HD ** (-0.5)
    fold_o.before(j)
    fold_q.before(j)
    o_stage[lax.rem(j, 2)] = tmm(att_ref[...], gattn_ref[...]).astype(BF)
    fold_o.after(j, kept_o.at[0])
    q = qkv_ref[:, 0:128]
    k = qkv_ref[:, 128:256]
    v = qkv_ref[:, 256:384]
    do = mm_t(gattn_ref[...], wo_ref[...]).astype(BF).astype(F32) * linv_ref[...]
    prod = do * att_ref[...].astype(F32)
    dob = do.astype(BF)
    q_t = jnp.transpose(q)
    do_t = jnp.transpose(dob)
    dq, dk_t, dv_t = [], [], []
    for h in range(2):
        mine = (lane < HD) if h == 0 else (lane >= HD)
        delta = jnp.sum(jnp.where(mine, prod, 0.0), axis=1, keepdims=True)
        dom = jnp.where(mine, dob, jnp.zeros_like(dob))
        for i in range(SEQ // QB):
            rows = slice(i * QB, (i + 1) * QB)
            dp = mm_t(dom[rows], v)
            ds_ref[h, rows, :] = (p_ref[h, rows, :].astype(F32) * (dp - delta[rows])).astype(BF)
        feats = slice(h * HD, (h + 1) * HD)
        dq.append(mm(ds_ref[h], k))
        dk_t.append(mm(q_t[feats], ds_ref[h]))
        dv_t.append(mm(do_t[feats], p_ref[h]))
    g_ref[:, 0:128] = (jnp.where(lane < HD, dq[0], dq[1]) * scale).astype(BF)
    g_ref[:, 128:256] = (jnp.transpose(jnp.concatenate(dk_t, 0)) * scale).astype(BF)
    g_ref[:, 256:384] = jnp.transpose(jnp.concatenate(dv_t, 0)).astype(BF)
    gsum_ref[...] = jnp.broadcast_to(jnp.sum(g_ref[...].astype(F32), axis=0, keepdims=True), gsum_ref.shape)
    q_stage[lax.rem(j, 2)] = mm(x_t[...], g_ref[...]).astype(BF)
    fold_q.after(j, kept_q.at[0])
    acc[...] += mm_t(g_ref[...], w_ref[...])

    @pl.when(j == 7)
    def _():
        def body(rows):
            xg_ref[rows, :] = acc[rows, :].astype(BF)

        row_blocks(body)
        deal_u.finish(up_ref)
        fold_o.finish()
        fold_q.finish()


def attend_bwd(gattn, wo, att, qkv, linv, p, x, w_qkv, r1, tot_d, kept_u):
    width = x.shape[1]
    heads = 128
    n = tot_d.shape[0]
    return pl.pallas_call(
        attend_bwd_kernel,
        grid=(8,),
        in_specs=[
            const(SEQ, width),
            pl.BlockSpec((heads, width), lambda j: (slot_at(j), 0)),
            pl.BlockSpec((SEQ, heads), lambda j: (0, slot_at(j))),
            pl.BlockSpec((SEQ, 3 * heads), lambda j: (0, slot_at(j))),
            pl.BlockSpec((SEQ, heads), lambda j: (0, slot_at(j))),
            pl.BlockSpec((2, SEQ, SEQ), lambda j: (slot_at(j), 0, 0)),
            const(SEQ, width),
            pl.BlockSpec((width, 3 * heads), lambda j: (0, slot_at(j))),
            ANY,
            const(n, width),
            ANY,
        ],
        out_specs=[
            const(SEQ, width),
            pl.BlockSpec((8, 3 * heads), lambda j: (0, slot_at(j))),
            kept_spec(width, 3 * heads),
            kept_spec(heads, width),
            const(n, width // 4),
            const(width // 4, n),
        ],
        out_shape=[
            jax.ShapeDtypeStruct((SEQ, width), BF),
            jax.ShapeDtypeStruct((8, 24 * heads), F32),
            jax.ShapeDtypeStruct((3, width, 3 * heads), BF),
            jax.ShapeDtypeStruct((3, heads, width), BF),
            jax.ShapeDtypeStruct((n, width // 4), BF),
            jax.ShapeDtypeStruct((width // 4, n), BF),
        ],
        scratch_shapes=[
            pltpu.VMEM((width, SEQ), BF),
            pltpu.VMEM((SEQ, width), F32),
            pltpu.VMEM((2, SEQ, SEQ), BF),
            pltpu.VMEM((SEQ, 3 * heads), BF),
            DMA,
            *Fold.scratch(width, 3 * heads),
            *Fold.scratch(heads, width),
            pltpu.VMEM((3, n, width // 4), BF),
            DMA((6,)),
            pltpu.VMEM((width, n), BF),
            pltpu.VMEM((width, n), BF),
            pltpu.VMEM((width, n), BF),
            DMA((5,)),
            pltpu.VMEM((width, n), BF),
            pltpu.VMEM((3, width // 4, n), BF),
            DMA((6,)),
        ],
        compiler_params=pltpu.CompilerParams(vmem_limit_bytes=VMEM_LIMIT, collective_id=5, has_side_effects=True),
        name="attend_bwd",
    )(gattn, wo, att, qkv, linv, p, x, w_qkv, r1, tot_d, kept_u)


def last_kernel(
    xg, kept_q, kept_o, own_d, own_u, vec_ref,
    x_block, gq, go, gd, gu, slot_out, feat_ref,
    q_own, q_x, q_y, q_c, q_tot, q_land, q_z, q_sum, o_own, o_x, o_y, o_c, o_tot, o_land, o_z, o_sum,
    v1, v2, v3, l1, l2, l3, l4, v_own, v_sems, out_sems, s_sems,
):
    peers = Peers()
    peers.greet(ALL_PEERS)
    outward = Outward(peers, xg, x_block, out_sems)
    cross_q = Cross(peers, kept_q, q_own, q_x, q_y, q_c)
    cross_o = Cross(peers, kept_o, o_own, o_x, o_y, o_c)
    deal_q = Deal(peers, q_tot, True, q_land, q_z)
    deal_o = Deal(peers, o_tot, False, o_land, o_z)

    def rows_at(ref):
        n = ref.shape[0] // 4
        return lambda q: ref.at[pl.ds(pl.multiple_of(q * n, n), n), :]

    def cols_at(ref, first, n):
        return lambda q: ref.at[:, pl.ds(pl.multiple_of(first + q * n, n), n)]

    heads = q_sum.shape[1] // 3
    units = own_u.shape[1]
    spread_d = Spread(peers, own_d, rows_at(gd), s_sems.at[0])
    spread_u = Spread(peers, own_u, cols_at(gu, 0, units), s_sems.at[1])
    spread_o = Spread(peers, o_sum, rows_at(go), s_sems.at[2])
    spread_q = [
        Spread(peers, q_sum.at[:, pl.ds(i * heads, heads)], cols_at(gq, 4 * i * heads, heads), s_sems.at[3 + i])
        for i in range(3)
    ]
    spread_v = Spread(peers, v_own, lambda q: slot_out.at[q], s_sems.at[6])

    to_core = send(peers, "core", vec_ref.at[pl.ds(4, 12)], l1, v_sems.at[0], v_sems.at[1])
    to_x = send(peers, "x", v1.at[pl.ds(2, 10)], l2, v_sems.at[2], v_sems.at[3])
    to_y = send(peers, "y", v2.at[pl.ds(1, 11)], l3, v_sems.at[4], v_sems.at[5])
    to_rows = []
    for i in (1, 2, 3):
        to_rows.append(send(peers, i, v3.at[0], l4.at[i - 1, 0], v_sems.at[6 + 4 * i], v_sems.at[7 + 4 * i]))
        src = v3.at[pl.ds(4 + 2 * (4 - i), 2)]
        to_rows.append(send(peers, i, src, l4.at[i - 1, pl.ds(1, 2)], v_sems.at[8 + 4 * i], v_sems.at[9 + 4 * i]))

    to_core.start()
    cross_o.start()
    cross_q.start()
    spread_d.start()
    spread_u.start()
    outward.start()

    to_core.wait()
    v1[0:4] = vec_ref[0:4] + l1[8:12]
    v1[4:12] = vec_ref[4:12] + l1[0:8]
    to_x.start()
    to_x.wait()
    v2[0:2] = v1[0:2] + l2[0:2]
    v2[4:12] = v1[4:12] + l2[2:10]
    v2[2:4] = v1[2:4]
    to_y.start()
    cross_o.finish(o_tot)
    deal_o.start()
    to_y.wait()
    v3[0:1] = v2[0:1] + l3[0:1]
    v3[4:12] = v2[4:12] + l3[3:11]
    for c in to_rows:
        c.start()
    cross_q.finish(q_tot)
    deal_q.start()
    for c in to_rows:
        c.wait()
    v_own[...] = v3[0] + l4[0, 0] + l4[1, 0] + l4[2, 0]
    feat_ref[...] = v3[4:6] + l4[0, 1:3] + l4[1, 1:3] + l4[2, 1:3]
    spread_v.start()
    spread_d.relay()
    spread_u.relay()
    deal_o.finish(o_sum)
    spread_o.start()
    spread_v.relay()
    deal_q.finish(q_sum)
    for sp in spread_q:
        sp.start()
    spread_o.relay()
    for sp in spread_q:
        sp.relay()
    for sp in (spread_d, spread_u, spread_o, spread_v, *spread_q):
        sp.finish()
    outward.finish()


def last(xg, kept_q, kept_o, own_d, own_u, vec):
    width = xg.shape[1]
    part = width // 4
    n = own_d.shape[0]
    heads = kept_o.shape[1]
    vmem = pl.BlockSpec(memory_space=pltpu.VMEM)

    def bufs(a, b, by_rows):
        piece = (a // 4, b) if by_rows else (a, b // 4)
        return [
            pltpu.VMEM((a, b), BF),
            pltpu.VMEM((a, b), BF),
            pltpu.VMEM((a, b), BF),
            DMA((5,)),
            pltpu.VMEM((a, b), BF),
            pltpu.VMEM((3, *piece), BF),
            DMA((6,)),
            pltpu.VMEM(piece, BF),
        ]

    return pl.pallas_call(
        last_kernel,
        in_specs=[ANY, ANY, ANY, ANY, ANY, vmem],
        out_specs=[ANY, ANY, ANY, ANY, ANY, ANY, vmem],
        out_shape=[
            jax.ShapeDtypeStruct((4 * SEQ, part), BF),
            jax.ShapeDtypeStruct((part, 12 * heads), BF),
            jax.ShapeDtypeStruct((4 * heads, part), BF),
            jax.ShapeDtypeStruct((4 * n, part), BF),
            jax.ShapeDtypeStruct((part, 4 * n), BF),
            jax.ShapeDtypeStruct((4, 8, 128), F32),
            jax.ShapeDtypeStruct((2, 8, 128), F32),
        ],
        scratch_shapes=[
            *bufs(width, 3 * heads, True),
            *bufs(heads, width, False),
            pltpu.VMEM((12, 8, 128), F32),
            pltpu.VMEM((12, 8, 128), F32),
            pltpu.VMEM((12, 8, 128), F32),
            pltpu.VMEM((12, 8, 128), F32),
            pltpu.VMEM((10, 8, 128), F32),
            pltpu.VMEM((11, 8, 128), F32),
            pltpu.VMEM((3, 3, 8, 128), F32),
            pltpu.VMEM((8, 128), F32),
            DMA((24,)),
            DMA((8,)),
            DMA((7, 7)),
        ],
        compiler_params=pltpu.CompilerParams(vmem_limit_bytes=VMEM_LIMIT, collective_id=6, has_side_effects=True),
        name="last",
    )(xg, kept_q, kept_o, own_d, own_u, vec)


class Ring:
    def __init__(self):
        self.r = lax.axis_index("row")
        self.c = lax.axis_index("col")
        self.d = lax.axis_index("dp")
        self.rows = lax.axis_size("row")

    def shift(self, v, s):
        n = self.rows
        return lax.ppermute(v, "row", [(i, (i + s) % n) for i in range(n)])

    def y(self, v):
        return lax.ppermute(v, "col", [(0, 1), (1, 0)])

    def absolute(self, quarters):
        a = jnp.where(self.d % 2 == 1, quarters[jnp.array([1, 0, 3, 2])], quarters)
        return jnp.where(self.d // 2 == 1, jnp.concatenate([a[2:], a[:2]], 0), a)


def quarter(v, d, axis):
    n = v.shape[axis] // 4
    return lax.dynamic_slice_in_dim(v, d * n, n, axis)


def whole_sequences(
    tokens, segments, w_query, b_query, w_key, w_value, b_value, w_out, b_out, norm1_gain, norm1_shift,
    w_up, b_up, w_down, b_down, norm2_gain, norm2_shift, cotangent,
):
    ring = Ring()
    r, c, d = ring.r, ring.c, ring.d
    R, C = lax.axis_size("row"), lax.axis_size("col")
    feat = tokens.shape[1]

    pairs = []
    for row in range(R):
        for col in range(C):
            n = col * R + row
            pairs.append((n, row * C + col))
    seg = lax.ppermute(segments, ("row", "col"), pairs)
    seg = lax.dynamic_slice_in_dim(seg, ((c * R + r) % C) * SEQ, SEQ, 0)
    ids = jnp.where(seg == 0, -1 - jnp.arange(SEQ, dtype=jnp.int32), seg)
    seg_col, seg_row = ids[:, None], ids[None, :]

    qkv_piece = jnp.concatenate([quarter(w, d, 1) for w in (w_query, w_key, w_value)], 1)
    x, w_qkv = first(tokens, qkv_piece)

    feat_vec = jnp.stack([b_out, norm1_gain, norm1_shift, b_down, norm2_gain, norm2_shift, b_out, b_out])
    feat_all = jnp.concatenate([feat_vec] + [ring.shift(feat_vec, s) for s in range(1, R)], 1).astype(F32)
    hq = b_query.shape[0] // 4
    unit = b_up.shape[0] // 4
    slot_vec = jnp.concatenate(
        [b_query.reshape(4, hq), jnp.zeros((4, hq), BF), b_value.reshape(4, hq), b_up.reshape(4, unit)], 1
    )
    slot_vec = ring.absolute(slot_vec)
    slot_vec = jnp.concatenate([slot_vec, ring.y(slot_vec)], 0).astype(F32)
    b_qkv = slot_vec[:, : 3 * hq].reshape(1, -1)
    bu = slot_vec[:, 3 * hq :].reshape(1, -1)

    qkv, att, prob, linv, wo, wu, wd = attend_fwd(
        x, w_qkv, b_qkv, seg_col, seg_row, quarter(w_out, d, 0), quarter(w_up, d, 1), quarter(w_down, d, 0)
    )
    wu, wd, act, slope, hidden_low, normed1, inv1, output, grad_r2, vg2 = ff_fwd(
        x, att, wo, feat_all, bu, cotangent, wu, wd
    )

    out_block, grad_pre, bu_part, kept_d = ff_down_bwd(grad_r2, wd, act, slope, output)
    out_block, grad_r1, grad_attn, vg1, kept_u, tot_d = ff_up_bwd(
        grad_r2, hidden_low, grad_pre, wu, normed1, inv1, feat_all, output, out_block, kept_d
    )
    x_grad, g_part, kept_q, kept_o, own_d, own_u = attend_bwd(
        grad_attn, wo, att, qkv, linv, prob, x, w_qkv, grad_r1, tot_d, kept_u
    )

    slot_grad = jnp.concatenate([g_part[0].reshape(8, 3 * hq), bu_part[0].reshape(8, unit)], 1)
    slot_grad = jnp.pad(slot_grad, ((0, 0), (0, 1024 - slot_grad.shape[1]))).reshape(8, 8, 128)
    feat_grad = jnp.stack([vg1[2], vg1[0], vg1[1], vg2[2], vg2[0], vg2[1]])
    feat_grad = feat_grad.reshape(6, R, feat).transpose(1, 0, 2).reshape(R, 6 * feat)
    feat_grad = jnp.pad(feat_grad, ((0, 0), (0, 2048 - 6 * feat))).reshape(8, 8, 128)
    pick = [slot_grad[t : t + 1] for t in (0, 4, 2, 6)]
    tiles = jnp.concatenate(pick + [feat_grad] + [slot_grad[t : t + 1] for t in (1, 5, 3, 7)], 0)

    x_grad_block, gq, go, gd, gu, slot_sum, own = last(x_grad, kept_q, kept_o, own_d, own_u, tiles)
    wq_grad, wk_grad, wv_grad = [gq[:, i * 4 * hq : (i + 1) * 4 * hq].astype(F32) for i in range(3)]
    w_out_grad, w_up_grad, w_down_grad = go.astype(F32), gu.astype(F32), gd.astype(F32)
    slot_sum = slot_sum.reshape(4, 1024)
    bq_grad = slot_sum[:, :hq].reshape(-1)
    bv_grad = slot_sum[:, 2 * hq : 3 * hq].reshape(-1)
    bu_grad = slot_sum[:, 3 * hq : 3 * hq + unit].reshape(-1)
    own = own.reshape(-1)[: 6 * feat].reshape(6, feat)
    return (
        out_block, x_grad_block, wq_grad, bq_grad, wk_grad, wv_grad, bv_grad, w_out_grad, own[0], own[1], own[2],
        w_up_grad, bu_grad, w_down_grad, own[3], own[4], own[5],
    )


def tokens_cols(source):
    return lax.all_gather(source, "col", axis=0, tiled=True)


def tokens_rows(source):
    return lax.all_gather(source, "row", axis=0, tiled=True)


def product(row_piece, weight, flipped):
    if flipped:
        return lax.dot_general(
            row_piece, weight, (((1,), (1,)), ((), ())), preferred_element_type=jnp.float32
        )
    return jnp.dot(row_piece, weight, preferred_element_type=jnp.float32)


def outer_sum(left, right):
    return lax.dot_general(
        left, right, (((0,), (0,)), ((), ())), preferred_element_type=jnp.float32
    )


def settle_rows(gathered, weight, flipped, own_rows):

    def product_term(first_row, row_count):
        return product(gathered, weight, flipped)

    return lax.psum_scatter(
        product_term(jnp.int32(0), own_rows * lax.axis_size("row")),
        "row",
        scatter_dimension=0,
        tiled=True,
    )


def settle_cols(gathered, weight, flipped, own_rows):

    def product_term(first_row, row_count):
        return product(gathered, weight, flipped)

    return lax.psum_scatter(
        product_term(jnp.int32(0), own_rows * lax.axis_size("col")),
        "col",
        scatter_dimension=0,
        tiled=True,
    )


def row_sums(first_part, second_part):
    return lax.psum((jnp.sum(first_part, axis=1), jnp.sum(second_part, axis=1)), "row")


def norm_forward(residual, norm_gain, norm_shift):
    total_sum, square_sum = row_sums(residual, residual * residual)
    row_mean = (total_sum / WIDTH)[:, None]
    variance = (square_sum / WIDTH)[:, None] - row_mean * row_mean
    inv_std = lax.rsqrt(variance + NORM_EPS)
    normed = (residual - row_mean) * inv_std
    return (normed * norm_gain + norm_shift, normed, inv_std)


def norm_backward(grad_in, normed, inv_std, norm_gain):
    grad_norm = grad_in * norm_gain
    total_sum, cross_sum = row_sums(grad_norm, grad_norm * normed)
    grad_resid = inv_std * (grad_norm - total_sum[:, None] / WIDTH - normed * cross_sum[:, None] / WIDTH)
    return (grad_resid, jnp.sum(grad_in * normed, axis=0), jnp.sum(grad_in, axis=0))


def split_heads(array, seq_count):
    return array.reshape(seq_count, SEQ, array.shape[1] // HD, HD)


def pair_scores(queries, key_heads, segment_ids):
    position = jnp.arange(SEQ)
    same_doc = (segment_ids[:, None] == segment_ids[None, :]) & (segment_ids[None, :] != 0)
    allowed = same_doc | (position[:, None] == position[None, :])
    raw_scores = jnp.einsum(
        "qhd,khd->hqk", queries, key_heads, preferred_element_type=jnp.float32
    ) * HD ** (-0.5)
    return jnp.where(allowed[None], raw_scores, -1000000000.0)


def attend_forward(source):
    queries, key_heads, values, segment_ids = source
    scores = pair_scores(queries, key_heads, segment_ids)
    top_score = jnp.max(scores, axis=2, keepdims=True)
    exp_scores = jnp.exp(scores - top_score)
    total_sum = jnp.sum(exp_scores, axis=2, keepdims=True)
    soft_low = (exp_scores / total_sum).astype(jnp.bfloat16)
    attended = jnp.einsum("hqk,khd->qhd", soft_low, values, preferred_element_type=jnp.float32)
    return (attended.astype(jnp.bfloat16), (top_score + jnp.log(total_sum))[:, :, 0])


def attend_backward(source):
    queries, key_heads, values, segment_ids, grad_out, log_total = source
    scores = pair_scores(queries, key_heads, segment_ids)
    soft_weights = jnp.exp(scores - log_total[:, :, None])
    soft_low = soft_weights.astype(jnp.bfloat16)
    grad_values = jnp.einsum("hqk,qhd->khd", soft_low, grad_out, preferred_element_type=jnp.float32)
    grad_soft = jnp.einsum("qhd,khd->hqk", grad_out, values, preferred_element_type=jnp.float32)
    grad_scores = soft_weights * (
        grad_soft - jnp.sum(soft_weights * grad_soft, axis=2, keepdims=True)
    )
    grad_scores = grad_scores.astype(jnp.bfloat16)
    scale_factor = HD ** (-0.5)
    grad_queries = (
        jnp.einsum("hqk,khd->qhd", grad_scores, key_heads, preferred_element_type=jnp.float32)
        * scale_factor
    )
    grad_keys = (
        jnp.einsum("hqk,qhd->khd", grad_scores, queries, preferred_element_type=jnp.float32)
        * scale_factor
    )
    return (
        grad_queries.astype(jnp.bfloat16),
        grad_keys.astype(jnp.bfloat16),
        grad_values.astype(jnp.bfloat16),
    )


def split_heads_plan(
    tokens,
    segments,
    w_query,
    b_query,
    w_key,
    w_value,
    b_value,
    w_out,
    b_out,
    norm1_gain,
    norm1_shift,
    w_up,
    b_up,
    w_down,
    b_down,
    norm2_gain,
    norm2_shift,
    cotangent,
):
    rows_b = tokens.shape[0]
    rows_a = segments.shape[0]
    head_cols = w_query.shape[1]
    seq_count = rows_a // SEQ
    segment_seqs = segments.reshape(seq_count, SEQ)
    gathered_x = tokens_cols(tokens)
    stacked = jnp.concatenate([w_query, w_key, w_value], axis=1)
    projected = settle_rows(gathered_x, stacked, False, rows_a)
    queries = (projected[:, :head_cols] + b_query).astype(jnp.bfloat16)
    key_heads = projected[:, head_cols : 2 * head_cols].astype(jnp.bfloat16)
    values = (projected[:, 2 * head_cols :] + b_value).astype(jnp.bfloat16)
    query_seqs = split_heads(queries, seq_count)
    key_seqs = split_heads(key_heads, seq_count)
    value_seqs = split_heads(values, seq_count)
    attended, log_total = lax.map(attend_forward, (query_seqs, key_seqs, value_seqs, segment_seqs))
    attended = attended.reshape(rows_a, head_cols)
    gathered_o = tokens_rows(attended)
    attn_out = settle_cols(gathered_o, w_out, False, rows_b) + b_out
    hidden, normed1, inv_std1 = norm_forward(
        tokens.astype(jnp.float32) + attn_out, norm1_gain, norm1_shift
    )
    hidden_low = hidden.astype(jnp.bfloat16)
    gathered_h = tokens_cols(hidden_low)
    pre_act = settle_rows(gathered_h, w_up, False, rows_a) + b_up
    active = gelu_exact(pre_act).astype(jnp.bfloat16)
    gathered_a = tokens_rows(active)
    fed = settle_cols(gathered_a, w_down, False, rows_b) + b_down
    output, normed2, inv_std2 = norm_forward(hidden + fed, norm2_gain, norm2_shift)
    grad_r2, grad_gain2, grad_shift2 = norm_backward(
        cotangent.astype(jnp.float32), normed2, inv_std2, norm2_gain
    )
    grad_fed = grad_r2.astype(jnp.bfloat16)
    gathered_f = tokens_cols(grad_fed)
    grad_w_down = outer_sum(gathered_a, gathered_f)
    grad_active = settle_rows(gathered_f, w_down, True, rows_a)
    unused_out, slope_pull = jax.vjp(gelu_exact, pre_act)
    grad_pre = slope_pull(grad_active)[0].astype(jnp.bfloat16)
    gathered_p = tokens_rows(grad_pre)
    grad_w_up = outer_sum(gathered_h, gathered_p)
    grad_from_ff = settle_cols(gathered_p, w_up, True, rows_b)
    bias_up_part = jnp.sum(grad_pre.astype(jnp.float32), axis=0)
    bias_down_part = jnp.sum(grad_fed.astype(jnp.float32), axis=0)
    grad_r1, grad_gain1, grad_shift1 = norm_backward(
        grad_from_ff + grad_r2, normed1, inv_std1, norm1_gain
    )
    grad_attn = grad_r1.astype(jnp.bfloat16)
    gathered_d = tokens_cols(grad_attn)
    grad_w_out = outer_sum(gathered_o, gathered_d)
    grad_attended = settle_rows(gathered_d, w_out, True, rows_a).astype(jnp.bfloat16)
    grad_q, grad_k, grad_v = lax.map(
        attend_backward,
        (
            query_seqs,
            key_seqs,
            value_seqs,
            segment_seqs,
            split_heads(grad_attended, seq_count),
            log_total,
        ),
    )
    grad_q = grad_q.reshape(rows_a, head_cols)
    grad_k = grad_k.reshape(rows_a, head_cols)
    grad_v = grad_v.reshape(rows_a, head_cols)
    grad_proj = jnp.concatenate([grad_q, grad_k, grad_v], axis=1)
    gathered_g = tokens_rows(grad_proj)
    grad_stacked = outer_sum(gathered_x, gathered_g)
    tokens_grad = settle_cols(gathered_g, stacked, True, rows_b) + grad_r1
    bias_q, bias_v, bias_up = lax.psum(
        (
            jnp.sum(grad_q.astype(jnp.float32), axis=0),
            jnp.sum(grad_v.astype(jnp.float32), axis=0),
            bias_up_part,
        ),
        ("dp", "row"),
    )
    bias_out, bias_down, gain_one, shift_one, gain_two, shift_two = lax.psum(
        (
            jnp.sum(grad_attn.astype(jnp.float32), axis=0),
            bias_down_part,
            grad_gain1,
            grad_shift1,
            grad_gain2,
            grad_shift2,
        ),
        ("dp", "col"),
    )
    sum_stacked, sum_out, sum_up, sum_down = (
        lax.psum(grad_stacked.astype(jnp.bfloat16), "dp").astype(jnp.float32),
        lax.psum(grad_w_out.astype(jnp.bfloat16), "dp").astype(jnp.float32),
        lax.psum(grad_w_up.astype(jnp.bfloat16), "dp").astype(jnp.float32),
        lax.psum(grad_w_down.astype(jnp.bfloat16), "dp").astype(jnp.float32),
    )
    return (
        output.astype(jnp.bfloat16),
        tokens_grad.astype(jnp.bfloat16),
        sum_stacked[:, :head_cols],
        bias_q,
        sum_stacked[:, head_cols : 2 * head_cols],
        sum_stacked[:, 2 * head_cols :],
        bias_v,
        sum_out,
        bias_out,
        gain_one,
        shift_one,
        sum_up,
        bias_up,
        sum_down,
        bias_down,
        gain_two,
        shift_two,
    )


def solution(mesh):
    dp, rows, cols = (mesh.shape[name] for name in ("dp", "row", "col"))
    whole = TOKENS // SEQ == dp * rows * cols and dp == 4 and cols == 2
    plan = whole_sequences if whole else split_heads_plan
    placed = (
        P(("dp", "col"), "row"),
        P(("dp", "row")),
        P("row", "col"),
        P("col"),
        P("row", "col"),
        P("row", "col"),
        P("col"),
        P("col", "row"),
        P("row"),
        P("row"),
        P("row"),
        P("row", "col"),
        P("col"),
        P("col", "row"),
        P("row"),
        P("row"),
        P("row"),
        P(("dp", "col"), "row"),
    )
    return jax.shard_map(
        plan,
        mesh=mesh,
        in_specs=placed,
        out_specs=(
            P(("dp", "col"), "row"),
            P(("dp", "col"), "row"),
            P("row", "col"),
            P("col"),
            P("row", "col"),
            P("row", "col"),
            P("col"),
            P("col", "row"),
            P("row"),
            P("row"),
            P("row"),
            P("row", "col"),
            P("col"),
            P("col", "row"),
            P("row"),
            P("row"),
            P("row"),
        ),
        check_vma=False,
    )
```

```python
import math

import jax
import jax.numpy as jnp
from jax import lax
from jax.experimental import pallas as pl
from jax.experimental.pallas import tpu as pltpu
from jax.sharding import PartitionSpec as P

HD = 64
SEQ = 1024
WIDTH = 1024
TOKENS = 32768
NORM_EPS = 1e-05
BF = jnp.bfloat16
F32 = jnp.float32
NEG = -1e30
QB = 256
VMEM_LIMIT = 56 * 1024 * 1024
MESH = pl.DeviceIdType.MESH
ANY = pl.BlockSpec(memory_space=pl.ANY)
DMA = pltpu.SemaphoreType.DMA
ONCE = pl.Buffered(1)


def const(*shape):
    return pl.BlockSpec(shape, lambda j: (0,) * len(shape), pipeline_mode=ONCE)


def mm(a, b):
    return jnp.dot(a, b, preferred_element_type=F32)


def mm_t(a, b):
    return lax.dot_general(a, b, (((1,), (1,)), ((), ())), preferred_element_type=F32)


def tmm(a, b):
    return lax.dot_general(a, b, (((0,), (0,)), ((), ())), preferred_element_type=F32)


def gelu_exact(v):
    return jax.nn.gelu(v, approximate=False)


def attend_rows(qkv_ref, seg_col_ref, seg_row, o_ref, p_ref, linv_ref, i):
    lane = lax.broadcasted_iota(jnp.int32, (QB, 128), 1)
    scale = HD ** (-0.5) * math.log2(math.e)
    rows = slice(i * QB, (i + 1) * QB)
    q = qkv_ref[rows, 0:128]
    k = qkv_ref[:, 128:256]
    v = qkv_ref[:, 256:384]
    seg_col = seg_col_ref[rows, 0:1]
    outs = []
    for h in range(2):
        mine = (lane < HD) if h == 0 else (lane >= HD)
        qm = jnp.where(mine, q, jnp.zeros_like(q))
        s = mm_t(qm, k)
        s = jnp.where(seg_col == seg_row, s * scale, NEG)
        top = jnp.max(s, axis=1, keepdims=True)
        p = jnp.exp2(s - top)
        total = jnp.sum(p, axis=1, keepdims=True)
        pb = p.astype(BF)
        p_ref[h, rows, :] = pb
        inv = 1.0 / total
        outs.append((mm(pb, v) * inv, jnp.broadcast_to(inv, (QB, 128))))
    o_ref[rows, :] = jnp.where(lane < HD, outs[0][0], outs[1][0]).astype(BF)
    linv_ref[rows, :] = jnp.where(lane < HD, outs[0][1], outs[1][1])


def attend_fwd_kernel(
    x_ref, w_ref, b_ref, seg_ref, cot, wo_in, wu_in, wd_in,
    qkv_ref, o_ref, p_ref, linv_ref, wo, wu, wd, cot_first,
    seg_col_ref, seg_row_ref, cot_own, i_sems, o_recv, o_sent, u_recv, u_sent, d_recv, d_sent,
):
    j = pl.program_id(0)
    peers = Peers()
    go = Gather(peers, None, wo, False, o_recv, o_sent, RING + LATER_NEAR + FAR)
    gu = Gather(peers, None, wu, True, u_recv, u_sent, RING + LATER_NEAR)
    gd = Gather(peers, None, wd, False, d_recv, d_sent, RING + DOWN_NEAR)
    every = (go, gu, gd)
    inward = Inward(peers, cot, cot_first, cot_own, i_sems, (0,))

    plan = {
        8: ((go, (1, 0)), (gu, (1, 0))),
        12: ((gd, (1, 0)), (go, (1, 2), (1, 4), (2, 0)), (gu, (1, 2), (1, 4))),
        16: ((gu, (2, 0)), (go, (0, 6), (1, 6)), (gd, (1, 2), (1, 4))),
        20: ((gd, (2, 0)), (go, (2, 2), (2, 4), (3, 0)), (gu, (2, 2), (2, 4))),
        25: ((gu, (3, 0)), (go, (2, 6), (3, 2), (3, 4)), (gd, (2, 2), (2, 4))),
        29: ((gd, (3, 0)), (gu, (3, 2), (3, 4)), (go, (3, 6))),
    }

    def hook(i):
        for at, work in plan.items():
            if at % 4 == i:
                @pl.when(j == at // 4)
                def _(at=at, work=work):
                    for g, *blocks in work:
                        g.relay(*blocks)
                    if at == 20:
                        inward.settle()
                        inward.start(0)

    @pl.when(j == 0)
    def _():
        peers.hello(ALL_PEERS)
        inward.load()
        tile = seg_ref[4 * peers.c + peers.r]
        for i in range(8):
            row = tile[i : i + 1, :]
            at = lax.broadcasted_iota(jnp.int32, (1, 128), 1) + i * 128
            row = jnp.where(row == 0, -1 - at, row)
            seg_row_ref[:, i * 128 : (i + 1) * 128] = row
            seg_col_ref[i * 128 : (i + 1) * 128, :] = jnp.transpose(jnp.broadcast_to(row, (128, 128)))

    qkv_ref[...] = (mm(x_ref[...], w_ref[...]) + b_ref[0, :, 0:384]).astype(BF)
    @pl.when(j == 0)
    def _():
        peers.meet(ALL_PEERS)
        for g in every:
            g.emit(0, 0)
        go.emit(0, 2)

    seg_row = seg_row_ref[...]
    for i in range(SEQ // QB):
        hook(i)
        attend_rows(qkv_ref, seg_col_ref, seg_row, o_ref, p_ref, linv_ref, i)

    @pl.when(j == 7)
    def _():
        for g in every:
            g.finish()
        inward.finish()


def attend_fwd(x, w_qkv, b_slot, seg, cot, wo, wu, wd):
    slots = w_qkv.shape[1] // 384
    return pl.pallas_call(
        attend_fwd_kernel,
        grid=(slots,),
        in_specs=[
            const(SEQ, x.shape[1]),
            pl.BlockSpec((x.shape[1], 384), lambda j: (0, j)),
            pl.BlockSpec((1, 1, b_slot.shape[2]), lambda j: (j, 0, 0)),
            const(8, 8, 128),
            ANY,
            ANY,
            ANY,
            ANY,
        ],
        out_specs=[
            pl.BlockSpec((SEQ, 384), lambda j: (0, j)),
            pl.BlockSpec((SEQ, 128), lambda j: (0, j)),
            pl.BlockSpec((2, SEQ, SEQ), lambda j: (j, 0, 0)),
            pl.BlockSpec((SEQ, 128), lambda j: (0, j)),
            ANY,
            ANY,
            ANY,
            ANY,
        ],
        out_shape=[
            jax.ShapeDtypeStruct((SEQ, slots * 384), BF),
            jax.ShapeDtypeStruct((SEQ, slots * 128), BF),
            jax.ShapeDtypeStruct((slots * 2, SEQ, SEQ), BF),
            jax.ShapeDtypeStruct((SEQ, slots * 128), F32),
            jax.ShapeDtypeStruct(wo.shape, BF),
            jax.ShapeDtypeStruct(wu.shape, BF),
            jax.ShapeDtypeStruct(wd.shape, BF),
            jax.ShapeDtypeStruct((SEQ // CHUNKS, x.shape[1]), BF),
        ],
        input_output_aliases={5: 4, 6: 5, 7: 6},
        scratch_shapes=[
            pltpu.VMEM((SEQ, 128), jnp.int32),
            pltpu.VMEM((1, SEQ), jnp.int32),
            pltpu.VMEM((SEQ // CHUNKS, cot.shape[1]), BF),
            sems_of_exchange(),
            *[DMA((32,))] * 6,
        ],
        compiler_params=pltpu.CompilerParams(vmem_limit_bytes=VMEM_LIMIT, collective_id=1, has_side_effects=True),
        name="attend_fwd",
    )(x, w_qkv, b_slot, seg, cot, wo, wu, wd)


class Peers:
    def __init__(self):
        self.r = lax.axis_index("row")
        self.c = lax.axis_index("col")
        self.d = d = lax.axis_index("dp")
        self.ids = {
            "core": {"dp": d + 1 - 2 * lax.rem(d, 2)},
            "x": {"dp": lax.rem(d + 2, 4)},
            "y": {"col": 1 - self.c},
            1: {"row": lax.rem(self.r + 1, 4)},
            2: {"row": lax.rem(self.r + 2, 4)},
            3: {"row": lax.rem(self.r + 3, 4)},
        }

    def hello(self, names):
        barrier = pltpu.get_barrier_semaphore()
        for name in names:
            pl.semaphore_signal(barrier, inc=1, device_id=self.ids[name], device_id_type=MESH)

    def meet(self, names):
        pl.semaphore_wait(pltpu.get_barrier_semaphore(), len(names))


def send(peers, name, src, dst, send_sem, recv_sem):
    return pltpu.make_async_remote_copy(
        src_ref=src, dst_ref=dst, send_sem=send_sem, recv_sem=recv_sem, device_id=peers.ids[name], device_id_type=MESH
    )


def near_edges(s):
    return [("x", s, 0, s, 2), ("y", s, 0, s, 4), ("core", s, 0, s, 1)]


def second_edges(s):
    return [("core", s, 2, s, 3), ("core", s, 4, s, 5)]


def far_edges(s):
    return [("y", s, 2, s, 6) if s % 2 == 0 else ("x", s, 4, s, 6), ("core", s, 6, s, 7)]


RING = [(1, s, 0, s + 1, 0) for s in range(3)]
NEAR = [e for s in range(4) for e in near_edges(s) + second_edges(s)]
FAR = [e for s in range(4) for e in far_edges(s)]
OWN_BLOCK = near_edges(0) + second_edges(0)
LATER_NEAR = [e for e in NEAR if e[1] > 0]
DOWN_NEAR = [e for e in LATER_NEAR if e[1] < 3] + [("core", 3, 0, 3, 1)]
DOWN_REST = [e for e in near_edges(3) if e[0] != "core"] + second_edges(3) + FAR


class Gather:
    def __init__(self, peers, piece, full, by_rows, recv, sent, edges):
        self.peers, self.piece, self.full, self.recv, self.sent = peers, piece, full, recv, sent
        self.by_rows = by_rows
        self.n = full.shape[1 if by_rows else 0] // 8
        self.m = full.shape[0 if by_rows else 1] // 4
        self.edges = edges
        self.waited = set()
        self.emitted = set()

    def blk(self, s, t):
        a = pl.ds(s * self.m, self.m)
        b = pl.ds(t * self.n, self.n)
        return self.full.at[a, b] if self.by_rows else self.full.at[b, a]

    def copy(self, at):
        name, s, t, s2, t2 = self.edges[at]
        src = self.piece if (s, t) == (0, 0) and self.piece is not None else self.blk(s, t)
        return send(self.peers, name, src, self.blk(s2, t2), self.sent.at[at], self.recv.at[at])

    def emit(self, s, t):
        for at, e in enumerate(self.edges):
            if e[1:3] == (s, t):
                assert at not in self.emitted
                self.emitted.add(at)
                self.copy(at).start()

    def emit_own_slot(self, s):
        for at, e in enumerate(self.edges):
            if e[1:3] == (s, 0):
                self.emitted.add(at)
                self.copy(at).start()

    def arrived(self, s, t):
        for at, e in enumerate(self.edges):
            if e[3:5] == (s, t) and at not in self.waited:
                self.waited.add(at)
                self.copy(at).wait_recv()

    def relay(self, *blocks):
        for s, t in blocks:
            self.arrived(s, t)
            self.emit(s, t)

    def own(self):
        return pltpu.make_async_copy(self.piece, self.blk(0, 0), self.sent.at[len(self.edges)])

    def start(self):
        self.emit(0, 0)
        self.own().start()

    def finish(self):
        if self.piece is not None:
            self.own().wait()
        for at, e in enumerate(self.edges):
            if at not in self.waited:
                self.waited.add(at)
                self.copy(at).wait_recv()
        assert len(self.emitted) == len(self.edges)
        for at in range(len(self.edges)):
            self.copy(at).wait_send()


class Line:
    WAVES = ((3, 2, 1), (1, 3, 2), (1, 3, 2), (1, 2, 3))

    def __init__(self, peers, gather, sems):
        self.peers, self.gather, self.sems = peers, gather, sems

    def copy(self, up, s):
        s2 = s + 1 if up else (s - 1 if s else 3)
        g = self.gather
        src = g.piece if s == 0 else g.blk(s, 0)
        return send(
            self.peers, 1 if up else 3, src, g.blk(s2, 0), self.sems.at[(0 if up else 4) + s], self.sems.at[7 + s2]
        )

    def each(self, what):
        r = self.peers.r
        for s in range(3):
            @pl.when((r >= s) & (r < 3))
            def _(s=s):
                what(self.copy(True, s))
        for s in (0, 3, 2):
            @pl.when((r > 0) & (r <= (3 if s == 0 else s - 1)))
            def _(s=s):
                what(self.copy(False, s))

    def start(self):
        r = self.peers.r

        @pl.when(r < 3)
        def _():
            self.copy(True, 0).start()

        @pl.when(r > 0)
        def _():
            self.copy(False, 0).start()

    def wave(self, k):
        for row, order in enumerate(self.WAVES):
            s = order[k]

            @pl.when(self.peers.r == row)
            def _(row=row, s=s):
                self.copy(True, s - 1).wait_recv()
                below = row >= s
                if below and row < 3:
                    self.copy(True, s).start()
                if not below and row > 0:
                    self.copy(False, s).start()
                self.gather.emit_own_slot(s)

    def finish(self):
        self.each(lambda c: c.wait_send())


CHUNKS = 4


def sems_of_exchange():
    return DMA((2, 4, CHUNKS))


class Inward:
    def __init__(self, peers, block, rows, buf, sems, chunks=range(CHUNKS)):
        self.peers, self.block, self.rows, self.buf, self.sems, self.chunks = peers, block, rows, buf, sems, chunks
        self.n = SEQ // CHUNKS

    def ends(self, s, first, count):
        r = lax.rem(self.peers.r + s, 4)
        f = self.block.shape[1]
        src = self.block.at[pl.ds(pl.multiple_of(r * SEQ + first * self.n, self.n), count * self.n), :]
        at = first if self.rows.shape[0] == SEQ else first - self.chunks[0]
        return src, self.rows.at[pl.ds(at * self.n, count * self.n), pl.ds(s * f, f)]

    def copy(self, s, k):
        return send(self.peers, s, *self.ends(s, k, 1), self.sems.at[0, s, k], self.sems.at[1, s, k])

    def own(self):
        src, dst = self.ends(0, self.chunks[0], len(self.chunks))
        return (
            pltpu.make_async_copy(src, self.buf, self.sems.at[0, 0, 0]),
            pltpu.make_async_copy(self.buf, dst, self.sems.at[1, 0, 0]),
        )

    def start(self, *chunks):
        for k in chunks:
            for s in (2, 1, 3):
                self.copy(s, k).start()

    def load(self):
        self.own()[0].start()

    def settle(self):
        self.own()[0].wait()
        self.own()[1].start()

    def finish(self):
        self.own()[1].wait()
        for k in self.chunks:
            for s in (1, 2, 3):
                self.copy(s, k).wait()


ALL_PEERS = ("core", "x", "y", 1, 2, 3)


def first_kernel(
    tokens, segments, w_query, w_key, w_value, w_out, w_up, w_down,
    vectors,
    x, w, wo, wu, wd, feat_out, slot_out, seg_out,
    pq, po, pu, pd, rows_buf, feat, slot, l_sems, q_recv, q_sent, o_recv, o_sent, u_recv, u_sent, d_recv, d_sent,
    i_sems, v_sems, z_sems,
):
    peers = Peers()
    r, d = peers.r, peers.d

    def own_cols(ref):
        n = ref.shape[1] // 4
        return ref.at[:, pl.ds(pl.multiple_of(d * n, n), n)]

    def own_rows(ref):
        n = ref.shape[0] // 4
        return ref.at[pl.ds(pl.multiple_of(d * n, n), n), :]

    peers.hello(ALL_PEERS)
    heads = w_query.shape[1] // 4
    loads = [
        pltpu.make_async_copy(own_cols(ref), pq.at[:, pl.ds(i * heads, heads)], l_sems.at[i])
        for i, ref in enumerate((w_query, w_key, w_value))
    ]
    loads += [
        pltpu.make_async_copy(own_rows(w_out), po, l_sems.at[3]),
        pltpu.make_async_copy(own_cols(w_up), pu, l_sems.at[4]),
        pltpu.make_async_copy(own_rows(w_down), pd, l_sems.at[5]),
    ]
    for c in loads:
        c.start()
    feat[...] = jnp.zeros_like(feat)
    f = feat.shape[1]
    for i in range(6):
        feat[i : i + 1, :] = vectors[:, i * f : (i + 1) * f]
    units = slot.shape[2] - 3 * heads
    at_q, at_v, at_u = 6 * f, 6 * f + 4 * heads, 6 * f + 8 * heads

    def quarter(first, n, q):
        return vectors[:, pl.ds(pl.multiple_of(first + q * n, 128), n)]

    for t in range(4):
        q = d
        if t % 2:
            q = q + 1 - 2 * lax.rem(q, 2)
        if t // 2:
            q = lax.rem(q + 2, 4)
        slot[t, :, 0:heads] = quarter(at_q, heads, q)
        slot[t, :, heads : 2 * heads] = jnp.zeros((1, heads), F32)
        slot[t, :, 2 * heads : 3 * heads] = quarter(at_v, heads, q)
        slot[t, :, 3 * heads :] = quarter(at_u, units, q)
    for c in loads:
        c.wait()

    gq = Gather(peers, pq, w, True, q_recv, q_sent, NEAR + FAR)
    line = Line(peers, gq, z_sems)
    go = Gather(peers, po, wo, False, o_recv, o_sent, OWN_BLOCK)
    gu = Gather(peers, pu, wu, True, u_recv, u_sent, OWN_BLOCK)
    gd = Gather(peers, pd, wd, False, d_recv, d_sent, OWN_BLOCK)
    later = (go, gu, gd)
    inward = Inward(peers, tokens, x, rows_buf, i_sems)
    inward.load()
    here = seg_out.at[pl.ds(2 * r, 2)]
    small = [
        pltpu.make_async_copy(feat, feat_out.at[:, pl.ds(0, f)], v_sems.at[0]),
        pltpu.make_async_copy(slot, slot_out.at[pl.ds(0, 4)], v_sems.at[1]),
        pltpu.make_async_copy(segments, here, v_sems.at[2]),
        send(peers, "y", slot, slot_out.at[pl.ds(4, 4)], v_sems.at[3], v_sems.at[4]),
    ]
    for i in (1, 2, 3):
        small.append(send(peers, i, feat, feat_out.at[:, pl.ds(i * f, f)], v_sems.at[3 + 2 * i], v_sems.at[4 + 2 * i]))
        small.append(send(peers, i, segments, here, v_sems.at[9 + 2 * i], v_sems.at[10 + 2 * i]))

    peers.meet(ALL_PEERS)
    line.start()
    gq.start()
    for c in small:
        c.start()
    for g in later:
        g.start()
    line.wave(0)
    inward.settle()
    gq.relay((0, 2), (0, 4))
    line.wave(1)
    for g in later:
        g.relay((0, 2), (0, 4))
    line.wave(2)
    inward.start(*inward.chunks)
    for s in (1, 2, 3):
        gq.relay((s, 2), (s, 4))
    for s in range(4):
        gq.relay((s, 6))
    for c in small:
        c.wait()
    for g in (gq, *later):
        g.finish()
    line.finish()
    inward.finish()


def first(tokens, segments, weights, vectors):
    w_query, _, _, w_out, w_up, w_down = weights
    width = 4 * tokens.shape[1]
    heads = w_query.shape[1] // 4
    units = w_up.shape[1] // 4
    vmem = pl.BlockSpec(memory_space=pltpu.VMEM)
    return pl.pallas_call(
        first_kernel,
        in_specs=[ANY, vmem] + [ANY] * 6 + [vmem],
        out_specs=[ANY] * 8,
        out_shape=[
            jax.ShapeDtypeStruct((SEQ, width), BF),
            jax.ShapeDtypeStruct((width, 24 * heads), BF),
            jax.ShapeDtypeStruct((8 * heads, width), BF),
            jax.ShapeDtypeStruct((width, 8 * units), BF),
            jax.ShapeDtypeStruct((8 * units, width), BF),
            jax.ShapeDtypeStruct((8, width), F32),
            jax.ShapeDtypeStruct((8, 1, 3 * heads + units), F32),
            jax.ShapeDtypeStruct((8, 8, 128), jnp.int32),
        ],
        scratch_shapes=[
            pltpu.VMEM((width // 4, 3 * heads), BF),
            pltpu.VMEM((heads, width // 4), BF),
            pltpu.VMEM((width // 4, units), BF),
            pltpu.VMEM((units, width // 4), BF),
            pltpu.VMEM((SEQ, width // 4), BF),
            pltpu.VMEM((8, width // 4), F32),
            pltpu.VMEM((4, 1, 3 * heads + units), F32),
            DMA((6,)),
            *[DMA((32,))] * 8,
            sems_of_exchange(),
            DMA((20,)),
            DMA((11,)),
        ],
        compiler_params=pltpu.CompilerParams(vmem_limit_bytes=VMEM_LIMIT, collective_id=0, has_side_effects=True),
        name="first",
    )(tokens, segments, *weights, vectors)


RB = 128


def norm_rows(v):
    mean = jnp.mean(v, axis=1, keepdims=True)
    variance = jnp.mean(v * v, axis=1, keepdims=True) - mean * mean
    inv = lax.rsqrt(variance + NORM_EPS)
    return (v - mean) * inv, inv


def norm_rows_back(g, normed, inv):
    mean_g = jnp.mean(g, axis=1, keepdims=True)
    mean_gn = jnp.mean(g * normed, axis=1, keepdims=True)
    return inv * (g - mean_g - normed * mean_gn)


def gelu_and_slope(v):
    z = jnp.abs(v) * (0.5 ** 0.5)
    t = 1.0 / (1.0 + 0.3275911 * z)
    poly = t * (0.254829592 + t * (-0.284496736 + t * (1.421413741 + t * (-1.453152027 + t * 1.061405429))))
    bell = jnp.exp2(z * z * -math.log2(math.e))
    tail = 0.5 * poly * bell
    cdf = jnp.where(v >= 0, 1.0 - tail, tail)
    return v * cdf, cdf + v * bell * (1.0 / math.sqrt(2.0 * math.pi))


def row_blocks(body, n=RB):
    def run(i, carry):
        body(pl.ds(pl.multiple_of(i * n, n), n))
        return carry

    lax.fori_loop(0, SEQ // n, run, 0)


def ff_fwd_kernel(
    x_ref, att_ref, wo_ref, vec_ref, b_ref, cot, cot_first, wu_in, wd_in,
    wu, wd, act_ref, slope_ref, hlow_ref, normed1_ref, inv1_ref, out_ref, r2_ref, vg_ref,
    acc, wu_buf, wd_buf, cot_buf, cot_own, buf_sem, u_recv, u_sent, d_recv, d_sent, i_sems, c_sem,
):
    j = pl.program_id(0)
    peers = Peers()
    gu = Gather(peers, None, wu, True, u_recv, u_sent, FAR)
    gd = Gather(peers, None, wd, False, d_recv, d_sent, DOWN_REST)
    inward = Inward(peers, cot, cot_buf, cot_own, i_sems, range(1, CHUNKS))
    early = pltpu.make_async_copy(cot_first, cot_buf.at[pl.ds(0, SEQ // CHUNKS), :], c_sem)
    n = wu_buf.shape[2]

    def fetch(t, slot):
        cols = pl.ds(pl.multiple_of(t * n, n), n)
        return (
            pltpu.make_async_copy(wu.at[:, cols], wu_buf.at[slot], buf_sem.at[0, slot]),
            pltpu.make_async_copy(wd.at[cols, :], wd_buf.at[slot], buf_sem.at[1, slot]),
        )

    @pl.when(j == 0)
    def _():
        peers.hello(ALL_PEERS)
        for t in range(2):
            for c in fetch(t, t):
                c.start()
        early.start()
        inward.load()
        acc[...] = jnp.zeros_like(acc)
        peers.meet(ALL_PEERS)
        gd.emit(3, 0)
        for s in (0, 1, 2):
            gu.emit(s, 2 if s % 2 == 0 else 4)
            gd.emit(s, 2 if s % 2 == 0 else 4)
        gu.emit(3, 4)
        inward.start(*inward.chunks)

        def body(rows):
            v = x_ref[rows, :].astype(F32) + mm(att_ref[rows, :], wo_ref[...]) + vec_ref[0:1, :]
            normed, inv = norm_rows(v)
            normed1_ref[rows, :] = normed
            inv1_ref[rows, :] = jnp.broadcast_to(inv, (RB, 128))
            hlow_ref[rows, :] = (normed * vec_ref[1:2, :] + vec_ref[2:3, :]).astype(BF)

        row_blocks(body)
        gd.relay((3, 2), (3, 4))

    @pl.when(j == 1)
    def _():
        gd.arrived(3, 3)
        inward.settle()

    @pl.when(j == 2)
    def _():
        gd.arrived(3, 5)

    @pl.when(j == 4)
    def _():
        for g in (gu, gd):
            g.relay((0, 6), (1, 6), (2, 6), (3, 6))

    @pl.when(j == 5)
    def _():
        for s in range(4):
            gu.arrived(s, 7)
            gd.arrived(s, 7)

    slot = lax.rem(j, 2)
    for c in fetch(j, slot):
        c.wait()
    w_up = wu_buf.at[slot]
    w_down = wd_buf.at[slot]
    bias = b_ref[0, :, 384:]
    for i in range(SEQ // 256):
        rows = slice(i * 256, (i + 1) * 256)
        act, slope = gelu_and_slope(mm(hlow_ref[rows, :], w_up[...]) + bias)
        act = act.astype(BF)
        act_ref[rows, :] = act
        slope_ref[rows, :] = slope.astype(BF)
        acc[rows, :] += mm(act, w_down[...])

    @pl.when(j < 6)
    def _():
        for c in fetch(j + 2, slot):
            c.start()

    @pl.when(j == 7)
    def _():
        inward.finish()
        early.wait()
        vg_ref[...] = jnp.zeros_like(vg_ref)

        def body(rows):
            hidden = normed1_ref[rows, :] * vec_ref[1:2, :] + vec_ref[2:3, :]
            normed, inv = norm_rows(hidden + (acc[rows, :] + vec_ref[3:4, :]))
            out_ref[rows, :] = (normed * vec_ref[4:5, :] + vec_ref[5:6, :]).astype(BF)
            c = cot_buf[rows, :].astype(F32)
            r2 = norm_rows_back(c * vec_ref[4:5, :], normed, inv)
            r2_ref[rows, :] = r2
            vg_ref[0:1, :] += jnp.sum(c * normed, axis=0, keepdims=True)
            vg_ref[1:2, :] += jnp.sum(c, axis=0, keepdims=True)
            vg_ref[2:3, :] += jnp.sum(r2.astype(BF).astype(F32), axis=0, keepdims=True)

        row_blocks(body)
        gu.finish()
        gd.finish()


def ff_fwd(x, att, wo, vec, bu, cot, cot_first, wu, wd):
    width, units = wu.shape
    n = units // 8
    return pl.pallas_call(
        ff_fwd_kernel,
        grid=(8,),
        in_specs=[
            const(SEQ, width),
            const(SEQ, width),
            const(width, width),
            const(8, width),
            pl.BlockSpec((1, 1, bu.shape[2]), lambda j: (j, 0, 0)),
            ANY,
            ANY,
            ANY,
            ANY,
        ],
        out_specs=[
            ANY,
            ANY,
            pl.BlockSpec((SEQ, n), lambda j: (0, j)),
            pl.BlockSpec((SEQ, n), lambda j: (0, j)),
            const(SEQ, width),
            const(SEQ, width),
            const(SEQ, 128),
            const(SEQ, width),
            const(SEQ, width),
            const(8, width),
        ],
        out_shape=[
            jax.ShapeDtypeStruct(wu.shape, BF),
            jax.ShapeDtypeStruct(wd.shape, BF),
            jax.ShapeDtypeStruct((SEQ, units), BF),
            jax.ShapeDtypeStruct((SEQ, units), BF),
            jax.ShapeDtypeStruct((SEQ, width), BF),
            jax.ShapeDtypeStruct((SEQ, width), F32),
            jax.ShapeDtypeStruct((SEQ, 128), F32),
            jax.ShapeDtypeStruct((SEQ, width), BF),
            jax.ShapeDtypeStruct((SEQ, width), F32),
            jax.ShapeDtypeStruct((8, width), F32),
        ],
        input_output_aliases={7: 0, 8: 1},
        scratch_shapes=[
            pltpu.VMEM((SEQ, width), F32),
            pltpu.VMEM((2, width, n), BF),
            pltpu.VMEM((2, n, width), BF),
            pltpu.VMEM((SEQ, width), BF),
            pltpu.VMEM((SEQ - SEQ // CHUNKS, width // 4), BF),
            DMA((2, 2)),
            DMA((32,)),
            DMA((32,)),
            DMA((32,)),
            DMA((32,)),
            sems_of_exchange(),
            DMA,
        ],
        compiler_params=pltpu.CompilerParams(vmem_limit_bytes=VMEM_LIMIT, collective_id=2, has_side_effects=True),
        name="ff_fwd",
    )(x, att, wo, vec, bu, cot, cot_first, wu, wd)


ORDER = (7, 6, 1, 3, 5, 0, 2, 4)
PAIRS = (7, 6, 3, 2, 5, 4, 1, 0)


def slot_at(j):
    return jnp.where(j < 2, 7 - j, jnp.where(j < 5, 2 * j - 3, 2 * j - 10))


def pair_at(j):
    return jnp.where(j < 2, 7 - j, jnp.where(j < 4, 5 - j, jnp.where(j < 6, 9 - j, 7 - j)))


def sum_rows(dst, *srcs):
    n = dst.shape[0]
    step = min(n, 64)

    def run(i, carry):
        rows = pl.ds(pl.multiple_of(i * step, step), step)
        total = srcs[0][rows, :].astype(F32)
        for src in srcs[1:]:
            total += src[rows, :].astype(F32)
        dst[rows, :] = total.astype(BF)
        return carry

    lax.fori_loop(0, n // step, run, 0)


class Fold:
    @staticmethod
    def scratch(a, b):
        return [
            pltpu.VMEM((2, a, b), BF),
            pltpu.VMEM((4, a, b), BF),
            pltpu.VMEM((a, b), BF),
            pltpu.VMEM((2, a // 2, b), BF),
            DMA((12,)),
        ]

    def __init__(self, peers, order, stage, land, corner, land_corner, sems):
        self.peers, self.order, self.stage, self.land, self.corner, self.land_corner, self.sems = (
            peers, order, stage, land, corner, land_corner, sems,
        )
        self.half = corner.shape[0] // 2

    def to_core(self, p):
        k = (self.order[p] - 1) // 2
        return send(self.peers, "core", self.stage.at[p % 2], self.land.at[k], self.sems.at[4 + k], self.sems.at[k])

    def to_side(self, h):
        src = self.corner.at[pl.ds(h * self.half, self.half), :]
        return send(self.peers, "xy"[1 - h], src, self.land_corner.at[h], self.sems.at[10 + h], self.sems.at[8 + h])

    def before(self, j):
        for p in range(2, 8):
            if self.order[p - 2] % 2 == 0:
                continue

            @pl.when(j == p)
            def _(p=p):
                self.to_core(p - 2).wait_send()

    def from_core(self, t):
        k = t // 2
        self.to_core(self.order.index(t + 1)).wait_recv()
        return self.land.at[k]

    def after(self, j, outs):
        for p, t in enumerate(self.order):
            @pl.when(j == p)
            def _(p=p, t=t):
                mine = self.stage.at[p % 2]
                if t % 2 == 1:
                    self.to_core(p).start()
                    return
                theirs = self.from_core(t)
                if t == 6:
                    sum_rows(self.corner, mine, theirs)
                    self.to_side(0).start()
                    self.to_side(1).start()
                    return
                out = outs[t]
                if t == 0:
                    sum_rows(out, mine, theirs)
                    return
                h = t // 2 - 1
                self.to_side(h).wait_recv()
                for q in range(2):
                    rows = pl.ds(q * self.half, self.half)
                    more = (self.land_corner.at[h],) if q == h else ()
                    sum_rows(out.at[rows, :], mine.at[rows, :], theirs.at[rows, :], *more)

    def finish(self):
        for p in (6, 7):
            if self.order[p] % 2:
                self.to_core(p).wait_send()
        self.to_side(0).wait_send()
        self.to_side(1).wait_send()


class Cross:
    def __init__(self, peers, for_x, for_y, land_x, land_y, sems, cuts=1):
        self.peers, self.sems, self.cuts = peers, sems, cuts
        self.ends = {"x": (for_x, land_x), "y": (for_y, land_y)}
        self.n = land_x.shape[0] // cuts

    def copy(self, way, h=0):
        src, dst = self.ends[way]
        rows = pl.ds(h * self.n, self.n)
        at = 4 * h + 2 * "xy".index(way)
        return send(self.peers, way, src.at[rows, :], dst.at[rows, :], self.sems.at[at], self.sems.at[at + 1])

    def start(self, ways="xy", h=0):
        for way in ways:
            self.copy(way, h).start()

    def finish(self, own, out):
        for h in range(self.cuts):
            for way in "xy":
                self.copy(way, h).wait()
        sum_rows(out, own, self.ends["x"][1], self.ends["y"][1])


class Whole:
    @staticmethod
    def scratch(a, b):
        return [
            pltpu.VMEM((8 * a, b), BF),
            pltpu.VMEM((4, a, b), BF),
            pltpu.VMEM((4, a, b), BF),
            pltpu.VMEM((2, a // 2, b), BF),
            pltpu.VMEM((a, b), BF),
            pltpu.VMEM((a, b), BF),
            DMA((12,)),
            DMA((4,)),
        ]

    def __init__(self, peers, total, land, kept, land_corner, land_x, land_y, sems, c_sems):
        self.peers, self.total, self.land, self.kept, self.land_corner, self.sems = (
            peers, total, land, kept, land_corner, sems,
        )
        self.a = land.shape[1]
        self.half = self.a // 2
        self.cross = Cross(peers, kept.at[1], kept.at[2], land_x, land_y, c_sems)

    def block(self, t):
        return self.total.at[pl.ds(t * self.a, self.a), :]

    def to_core(self, k):
        return send(
            self.peers, "core", self.block(2 * k + 1), self.land.at[k], self.sems.at[4 + k], self.sems.at[k]
        )

    def to_side(self, h):
        src = self.kept.at[3, pl.ds(h * self.half, self.half), :]
        return send(self.peers, "xy"[1 - h], src, self.land_corner.at[h], self.sems.at[10 + h], self.sems.at[8 + h])

    def start(self):
        for k in (3, 1, 2, 0):
            self.to_core(k).start()

    def corner(self):
        for k in (3, 1, 2, 0):
            self.to_core(k).wait_recv()
            sum_rows(self.kept.at[k], self.block(2 * k), self.land.at[k])
            if k == 3:
                self.to_side(0).start()
                self.to_side(1).start()

    def sides(self):
        for h in range(2):
            self.to_side(h).wait_recv()
            rows = pl.ds(h * self.half, self.half)
            mine = self.kept.at[1 + h, rows, :]
            sum_rows(mine, mine, self.land_corner.at[h])
        self.cross.start()

    def finish(self, out):
        self.cross.finish(self.kept.at[0], out)
        for k in range(4):
            self.to_core(k).wait_send()
        for h in range(2):
            self.to_side(h).wait_send()


class Deal:
    def __init__(self, peers, total, by_rows, land, sems):
        self.peers, self.total, self.by_rows, self.land, self.sems = peers, total, by_rows, land, sems

    def part(self, s):
        n = self.total.shape[0 if self.by_rows else 1] // 4
        return self.total.at[pl.ds(s * n, n), :] if self.by_rows else self.total.at[:, pl.ds(s * n, n)]

    def copy(self, s):
        return send(self.peers, 4 - s, self.part(s), self.land.at[s - 1], self.sems.at[2 + s], self.sems.at[s - 1])

    def start(self):
        for s in (2, 1, 3):
            self.copy(s).start()

    def finish(self, out):
        for s in (1, 2, 3):
            self.copy(s).wait()
        sum_rows(out, self.part(0), self.land.at[0], self.land.at[1], self.land.at[2])


class LineDeal:
    def __init__(self, peers, total, by_rows, land, tmp, sems):
        self.peers, self.land, self.tmp, self.sems = peers, land, tmp, sems
        self.part = Deal(peers, total, by_rows, None, None).part

    def copy(self, up, b, row, src):
        go = (b - row if up else row - b) - 1
        at = (0 if up else 3) + go
        return send(
            self.peers, 1 if up else 3, src, self.land.at[0 if up else 1, go], self.sems.at[at], self.sems.at[6 + at]
        )

    def slot(self, b, row):
        return (row - b) % 4

    def first(self, up, b, row):
        return self.copy(up, b, row, self.part(self.slot(b, row)))

    def pass_on(self, up, b, row):
        go = (b - row if up else row - b) - 1
        tmp = self.tmp.at[0 if up else 1, go]
        return self.copy(up, b, row, tmp), tmp

    def got(self, up, b, row):
        go = b - row if up else row - b
        at = (0 if up else 3) + go
        land = self.land.at[0 if up else 1, go]
        send(self.peers, 1 if up else 3, land, land, self.sems.at[at], self.sems.at[6 + at]).wait_recv()
        return land

    STEPS = (((1, True, 3), (1, True, 2), (2, False, 0), (2, False, 1)), ((2, True, 3), (1, False, 0)))
    STARTS = ((0, True, 3), (0, True, 2), (0, True, 1), (3, False, 0), (3, False, 1), (3, False, 2))

    def when(self, row, run):
        pl.when(self.peers.r == row)(run)

    def start(self):
        for row, up, b in self.STARTS:
            self.when(row, lambda up=up, b=b, row=row: self.first(up, b, row).start())

    def step(self, k):
        for row, up, b in self.STEPS[k]:
            def run(row=row, up=up, b=b):
                land = self.got(up, b, row)
                copy, tmp = self.pass_on(up, b, row)
                sum_rows(tmp, land, self.part(self.slot(b, row)))
                copy.start()

            self.when(row, run)

    def finish(self, out):
        for row in range(4):
            def run(row=row):
                lands = []
                if row > 0:
                    lands.append(self.got(True, row, row))
                if row < 3:
                    lands.append(self.got(False, row, row))
                sum_rows(out, self.part(0), *lands)

            self.when(row, run)
        for row, up, b in self.STARTS:
            self.when(row, lambda up=up, b=b, row=row: self.first(up, b, row).wait_send())
        for moves in self.STEPS:
            for row, up, b in moves:
                self.when(row, lambda up=up, b=b, row=row: self.pass_on(up, b, row)[0].wait_send())


class Spread:
    def __init__(self, peers, own, place, sems):
        d = lax.axis_index("dp")
        self.peers, self.own, self.sems, self.here = peers, own, sems, place(d)
        self.from_x = place(lax.rem(d + 2, 4))

    def local(self):
        return pltpu.make_async_copy(self.own, self.here, self.sems.at[6])

    def copies(self):
        s = self.sems
        return (
            send(self.peers, "x", self.own, self.here, s.at[0], s.at[1]),
            send(self.peers, "core", self.own, self.here, s.at[2], s.at[3]),
            send(self.peers, "core", self.from_x, self.from_x, s.at[4], s.at[5]),
        )

    def start(self):
        to_x, to_core, _ = self.copies()
        to_x.start()
        to_core.start()
        self.local().start()

    def relay(self):
        to_x, _, on = self.copies()
        to_x.wait_recv()
        on.start()

    def finish(self):
        to_x, to_core, on = self.copies()
        to_x.wait_send()
        to_core.wait()
        on.wait()
        self.local().wait()


class Outward:
    def __init__(self, peers, rows, block, buf, sems, parts=(2, 1, 3, 0)):
        self.peers, self.rows, self.block, self.buf, self.sems = peers, rows, block, buf, sems
        self.away = [s for s in parts if s]
        self.stays = 0 in parts
        self.n = SEQ // CHUNKS

    def ends(self, s, first, count):
        f = self.block.shape[1]
        mine = pl.ds(pl.multiple_of(self.peers.r * SEQ + first * self.n, self.n), count * self.n)
        return self.rows.at[pl.ds(first * self.n, count * self.n), pl.ds(s * f, f)], self.block.at[mine, :]

    def copy(self, s, k):
        return send(self.peers, 4 - s, *self.ends(s, k, 1), self.sems.at[0, s, k], self.sems.at[1, s, k])

    def load(self):
        return pltpu.make_async_copy(self.ends(0, 0, CHUNKS)[0], self.buf, self.sems.at[0, 0, 0])

    def store(self):
        src, dst = self.ends(0, 0, CHUNKS)
        return pltpu.make_async_copy(src if self.buf is None else self.buf, dst, self.sems.at[1, 0, 0])

    def start(self, *chunks):
        for k in chunks:
            for s in self.away:
                self.copy(s, k).start()

    def settle(self):
        self.load().wait()
        self.store().start()

    def finish(self):
        if self.stays:
            self.store().wait()
        for k in range(CHUNKS):
            for s in self.away:
                self.copy(s, k).wait()


def ff_down_bwd_kernel(
    r2_ref, wd_ref, act_ref, slope_ref, out, out_block, gp_ref, bu_ref, kept_ref,
    gfed, out_own, stage, land, corner, land_corner, f_sems, o_sems,
):
    j = pl.program_id(0)
    peers = Peers()
    outward = Outward(peers, out, out_block, out_own, o_sems, (2, 0))
    fold = Fold(peers, ORDER, stage, land, corner, land_corner, f_sems)

    @pl.when(j == 0)
    def _():
        peers.hello(ALL_PEERS)
        outward.load().start()

        def body(rows):
            gfed[rows, :] = r2_ref[rows, :].astype(BF)

        row_blocks(body)
        peers.meet(ALL_PEERS)
        outward.start(*range(CHUNKS))

    bsum = jnp.zeros((1, bu_ref.shape[2]), F32)
    for i in range(SEQ // 256):
        rows = slice(i * 256, (i + 1) * 256)
        g = (mm_t(gfed[rows, :], wd_ref[...]) * slope_ref[rows, :].astype(F32)).astype(BF)
        gp_ref[rows, :] = g
        bsum += jnp.sum(g.astype(F32), axis=0, keepdims=True)
    bu_ref[0] = bsum
    fold.before(j)
    stage[lax.rem(j, 2)] = tmm(act_ref[...], gfed[...]).astype(BF)
    fold.after(j, {t: kept_ref.at[0] for t in (0, 2, 4)})

    @pl.when(j == 1)
    def _():
        outward.settle()

    @pl.when(j == 7)
    def _():
        fold.finish()
        outward.finish()


def kept_spec(a, b):
    return pl.BlockSpec((1, a, b), lambda j: (jnp.maximum(j - 5, 0), 0, 0))


def ff_down_bwd(r2, wd, act, slope, out):
    units, width = wd.shape
    n = units // 8
    return pl.pallas_call(
        ff_down_bwd_kernel,
        grid=(8,),
        in_specs=[
            const(SEQ, width),
            pl.BlockSpec((n, width), lambda j: (slot_at(j), 0)),
            pl.BlockSpec((SEQ, n), lambda j: (0, slot_at(j))),
            pl.BlockSpec((SEQ, n), lambda j: (0, slot_at(j))),
            ANY,
        ],
        out_specs=[
            ANY,
            pl.BlockSpec((SEQ, n), lambda j: (0, slot_at(j))),
            pl.BlockSpec((1, 1, n), lambda j: (slot_at(j), 0, 0)),
            kept_spec(n, width),
        ],
        out_shape=[
            jax.ShapeDtypeStruct((4 * SEQ, width // 4), BF),
            jax.ShapeDtypeStruct((SEQ, units), BF),
            jax.ShapeDtypeStruct((8, 1, n), F32),
            jax.ShapeDtypeStruct((3, n, width), BF),
        ],
        scratch_shapes=[
            pltpu.VMEM((SEQ, width), BF),
            pltpu.VMEM((SEQ, width // 4), BF),
            *Fold.scratch(n, width),
            sems_of_exchange(),
        ],
        compiler_params=pltpu.CompilerParams(vmem_limit_bytes=VMEM_LIMIT, collective_id=3, has_side_effects=True),
        name="ff_down_bwd",
    )(r2, wd, act, slope, out)


def ff_up_bwd_kernel(
    r2_ref, hlow_ref, gp_ref, wu_ref, normed1_ref, inv1_ref, vec_ref, out, out_block_in, kept_d,
    out_block, r1_ref, gattn_ref, vg_ref, kept_ref, own_ref,
    hlow_t, stage, land, corner, land_corner, f_sems, own_d, land_x, land_y, c_sems, o_sems,
):
    j = pl.program_id(0)
    peers = Peers()
    outward = Outward(peers, out, out_block, None, o_sems, (1, 3))
    fold = Fold(peers, ORDER, stage, land, corner, land_corner, f_sems)
    cross = Cross(peers, kept_d.at[1], kept_d.at[2], land_x, land_y, c_sems, 2)
    load = pltpu.make_async_copy(kept_d.at[0], own_d, c_sems.at[8])

    @pl.when(j == 0)
    def _():
        peers.hello(ALL_PEERS)
        load.start()
        r1_ref[...] = r2_ref[...]
        for i in range(SEQ // 256):
            rows = slice(i * 256, (i + 1) * 256)
            hlow_t[:, rows] = jnp.transpose(hlow_ref[rows, :])
        peers.meet(ALL_PEERS)
        cross.start()
        outward.start(*range(CHUNKS))

    fold.before(j)
    stage[lax.rem(j, 2)] = mm(hlow_t[...], gp_ref[...]).astype(BF)
    fold.after(j, {t: kept_ref.at[0] for t in (0, 2, 4)})

    @pl.when(j == 1)
    def _():
        cross.start(h=1)

    r1_ref[...] += mm_t(gp_ref[...], wu_ref[...])

    @pl.when(j == 7)
    def _():
        vg_ref[...] = jnp.zeros_like(vg_ref)

        def body(rows):
            gh = r1_ref[rows, :]
            normed = normed1_ref[rows, :]
            r1 = norm_rows_back(gh * vec_ref[1:2, :], normed, inv1_ref[rows, 0:1])
            r1_ref[rows, :] = r1
            low = r1.astype(BF)
            gattn_ref[rows, :] = low
            vg_ref[0:1, :] += jnp.sum(gh * normed, axis=0, keepdims=True)
            vg_ref[1:2, :] += jnp.sum(gh, axis=0, keepdims=True)
            vg_ref[2:3, :] += jnp.sum(low.astype(F32), axis=0, keepdims=True)

        row_blocks(body)
        load.wait()
        cross.finish(own_d, own_ref)
        fold.finish()
        outward.finish()


def ff_up_bwd(r2, hlow, gp, wu, normed1, inv1, vec, out, out_block, kept_d):
    width, units = wu.shape
    n = units // 8
    return pl.pallas_call(
        ff_up_bwd_kernel,
        grid=(8,),
        in_specs=[
            const(SEQ, width),
            const(SEQ, width),
            pl.BlockSpec((SEQ, n), lambda j: (0, slot_at(j))),
            pl.BlockSpec((width, n), lambda j: (0, slot_at(j))),
            const(SEQ, width),
            const(SEQ, 128),
            const(8, width),
            ANY,
            ANY,
            ANY,
        ],
        out_specs=[
            ANY,
            const(SEQ, width),
            const(SEQ, width),
            const(8, width),
            kept_spec(width, n),
            const(n, width),
        ],
        out_shape=[
            jax.ShapeDtypeStruct(out_block.shape, BF),
            jax.ShapeDtypeStruct((SEQ, width), F32),
            jax.ShapeDtypeStruct((SEQ, width), BF),
            jax.ShapeDtypeStruct((8, width), F32),
            jax.ShapeDtypeStruct((3, width, n), BF),
            jax.ShapeDtypeStruct((n, width), BF),
        ],
        input_output_aliases={8: 0},
        scratch_shapes=[
            pltpu.VMEM((width, SEQ), BF),
            *Fold.scratch(width, n),
            pltpu.VMEM((n, width), BF),
            pltpu.VMEM((n, width), BF),
            pltpu.VMEM((n, width), BF),
            DMA((9,)),
            sems_of_exchange(),
        ],
        compiler_params=pltpu.CompilerParams(vmem_limit_bytes=VMEM_LIMIT, collective_id=4, has_side_effects=True),
        name="ff_up_bwd",
    )(r2, hlow, gp, wu, normed1, inv1, vec, out, out_block, kept_d)


def attend_bwd_kernel(
    gattn_ref, wo_ref, att_ref, qkv_ref, linv_ref, p_ref, x_ref, att_all, tot_d, kept_u,
    g_ref, gsum_ref, tot_q, tot_o, down_ref, up_ref,
    x_t, ds_ref,
    q_stage, q_land, q_corner, q_land_corner, q_sems,
    q_kept, q_x, q_y, q_c, o_total, o_land, o_kept, o_land_corner, o_x, o_y, o_sems, o_c,
    zd_land, zd_sems, own_u, land_x, land_y, c_sems, tot_u, zu_land, zu_sems,
):
    j = pl.program_id(0)
    peers = Peers()
    fold_q = Fold(peers, PAIRS, q_stage, q_land, q_corner, q_land_corner, q_sems)
    whole_o = Whole(peers, o_total, o_land, o_kept, o_land_corner, o_x, o_y, o_sems, o_c)
    cross_q = Cross(peers, q_kept.at[1], q_kept.at[2], q_x, q_y, q_c)
    deal_d = Deal(peers, tot_d, False, zd_land, zd_sems)
    cross_u = Cross(peers, kept_u.at[1], kept_u.at[2], land_x, land_y, c_sems)
    deal_u = Deal(peers, tot_u, True, zu_land, zu_sems)
    load_u = pltpu.make_async_copy(kept_u.at[0], own_u, c_sems.at[4])

    @pl.when(j == 0)
    def _():
        load_u.start()
        peers.hello(ALL_PEERS)
        for i in range(SEQ // 256):
            rows = slice(i * 256, (i + 1) * 256)
            x_t[:, rows] = jnp.transpose(x_ref[rows, :])
        load_u.wait()
        peers.meet(ALL_PEERS)
        cross_u.start()
        deal_d.start()
        o_total[...] = tmm(att_all[...], gattn_ref[...]).astype(BF)
        whole_o.start()

    @pl.when(j == 1)
    def _():
        whole_o.corner()

    @pl.when(j == 3)
    def _():
        whole_o.sides()

    @pl.when(j == 6)
    def _():
        whole_o.finish(tot_o)

    @pl.when(j == 4)
    def _():
        cross_u.finish(own_u, tot_u)
        deal_u.start()
        deal_d.finish(down_ref)

    lane = lax.broadcasted_iota(jnp.int32, (SEQ, 128), 1)
    scale = HD ** (-0.5)
    fold_q.before(j)
    q = qkv_ref[:, 0:128]
    k = qkv_ref[:, 128:256]
    v = qkv_ref[:, 256:384]
    do = mm_t(gattn_ref[...], wo_ref[...]).astype(BF).astype(F32) * linv_ref[...]
    prod = do * att_ref[...].astype(F32)
    dob = do.astype(BF)
    q_t = jnp.transpose(q)
    do_t = jnp.transpose(dob)
    dq, dk_t, dv_t = [], [], []
    for h in range(2):
        mine = (lane < HD) if h == 0 else (lane >= HD)
        delta = jnp.sum(jnp.where(mine, prod, 0.0), axis=1, keepdims=True)
        dom = jnp.where(mine, dob, jnp.zeros_like(dob))
        for i in range(SEQ // QB):
            rows = slice(i * QB, (i + 1) * QB)
            dp = mm_t(dom[rows], v)
            ds_ref[h, rows, :] = (p_ref[h, rows, :].astype(F32) * (dp - delta[rows])).astype(BF)
        feats = slice(h * HD, (h + 1) * HD)
        dq.append(mm(ds_ref[h], k))
        dk_t.append(mm(q_t[feats], ds_ref[h]))
        dv_t.append(mm(do_t[feats], p_ref[h]))
    g_ref[:, 0:128] = (jnp.where(lane < HD, dq[0], dq[1]) * scale).astype(BF)
    g_ref[:, 128:256] = (jnp.transpose(jnp.concatenate(dk_t, 0)) * scale).astype(BF)
    g_ref[:, 256:384] = jnp.transpose(jnp.concatenate(dv_t, 0)).astype(BF)
    gsum_ref[0] = jnp.sum(g_ref[...].astype(F32), axis=0, keepdims=True)
    q_stage[lax.rem(j, 2)] = mm(x_t[...], g_ref[...]).astype(BF)
    fold_q.after(j, {t: q_kept.at[t // 2] for t in (0, 2, 4)})

    @pl.when(j == PAIRS.index(2))
    def _():
        cross_q.start("x")

    @pl.when(j == PAIRS.index(4))
    def _():
        cross_q.start("y")

    @pl.when(j == 7)
    def _():
        deal_u.finish(up_ref)
        fold_q.finish()
        cross_q.finish(q_kept.at[0], tot_q)


def attend_bwd(gattn, wo, att, qkv, linv, p, x, tot_d, kept_u):
    width = x.shape[1]
    heads = 128
    n = tot_d.shape[0]
    return pl.pallas_call(
        attend_bwd_kernel,
        grid=(8,),
        in_specs=[
            const(SEQ, width),
            pl.BlockSpec((heads, width), lambda j: (pair_at(j), 0)),
            pl.BlockSpec((SEQ, heads), lambda j: (0, pair_at(j))),
            pl.BlockSpec((SEQ, 3 * heads), lambda j: (0, pair_at(j))),
            pl.BlockSpec((SEQ, heads), lambda j: (0, pair_at(j))),
            pl.BlockSpec((2, SEQ, SEQ), lambda j: (pair_at(j), 0, 0)),
            const(SEQ, width),
            const(SEQ, width),
            const(n, width),
            ANY,
        ],
        out_specs=[
            pl.BlockSpec((SEQ, 3 * heads), lambda j: (0, pair_at(j))),
            pl.BlockSpec((1, 1, 3 * heads), lambda j: (pair_at(j), 0, 0)),
            const(width, 3 * heads),
            const(heads, width),
            const(n, width // 4),
            const(width // 4, n),
        ],
        out_shape=[
            jax.ShapeDtypeStruct((SEQ, 24 * heads), BF),
            jax.ShapeDtypeStruct((8, 1, 3 * heads), F32),
            jax.ShapeDtypeStruct((width, 3 * heads), BF),
            jax.ShapeDtypeStruct((heads, width), BF),
            jax.ShapeDtypeStruct((n, width // 4), BF),
            jax.ShapeDtypeStruct((width // 4, n), BF),
        ],
        scratch_shapes=[
            pltpu.VMEM((width, SEQ), BF),
            pltpu.VMEM((2, SEQ, SEQ), BF),
            *Fold.scratch(width, 3 * heads),
            pltpu.VMEM((3, width, 3 * heads), BF),
            pltpu.VMEM((width, 3 * heads), BF),
            pltpu.VMEM((width, 3 * heads), BF),
            DMA((4,)),
            *Whole.scratch(heads, width),
            pltpu.VMEM((3, n, width // 4), BF),
            DMA((6,)),
            pltpu.VMEM((width, n), BF),
            pltpu.VMEM((width, n), BF),
            pltpu.VMEM((width, n), BF),
            DMA((5,)),
            pltpu.VMEM((width, n), BF),
            pltpu.VMEM((3, width // 4, n), BF),
            DMA((6,)),
        ],
        compiler_params=pltpu.CompilerParams(vmem_limit_bytes=VMEM_LIMIT, collective_id=5, has_side_effects=True),
        name="attend_bwd",
    )(gattn, wo, att, qkv, linv, p, x, att, tot_d, kept_u)


def last_kernel(
    tot_q, tot_o, own_d, own_u, g_part, u_part, vec1, vec2, g, w, r1,
    x_block, gq, go, gd, gu, slot_out, feat_ref,
    g_buf, w_buf, acc, xg, ld_sems,
    q_land, q_tmp, q_z, q_sum, o_land, o_tmp, o_z, o_sum,
    vec_ref, v1, v2, v3, l1, l2, l3, l4, v_own, v_sems, out_sems, s_sems,
):
    peers = Peers()
    outward = Outward(peers, xg, x_block, None, out_sems)
    deal_q = LineDeal(peers, tot_q, True, q_land, q_tmp, q_z)
    deal_o = LineDeal(peers, tot_o, False, o_land, o_tmp, o_z)
    loads = (
        pltpu.make_async_copy(w, w_buf, ld_sems.at[0]),
        pltpu.make_async_copy(g, g_buf, ld_sems.at[1]),
        pltpu.make_async_copy(r1, acc, ld_sems.at[2]),
    )
    peers.hello(ALL_PEERS)
    for c in loads:
        c.start()

    def products(k):
        rows = slice(k * (SEQ // CHUNKS), (k + 1) * (SEQ // CHUNKS))
        xg[rows, :] = (mm_t(g_buf[rows, :], w_buf[...]) + acc[rows, :]).astype(BF)
        outward.start(k)

    vec_ref[...] = jnp.zeros_like(vec_ref)
    heads3, units = g_part.shape[2], u_part.shape[2]
    for k, t in enumerate((0, 4, 2, 6, 1, 5, 3, 7)):
        k = k if k < 4 else k + 8
        for i in range(heads3 // 128):
            vec_ref[k, i : i + 1, :] = g_part[t, :, i * 128 : (i + 1) * 128]
        for i in range(units // 128):
            at = heads3 // 128 + i
            vec_ref[k, at : at + 1, :] = u_part[t, :, i * 128 : (i + 1) * 128]
    f = vec1.shape[1] // 4
    rows = [(vec1, 2), (vec1, 0), (vec1, 1), (vec2, 2), (vec2, 0), (vec2, 1)]
    for k in range(4):
        for v, (ref, row) in enumerate(rows):
            for i in range(f // 128):
                at = v * (f // 128) + i
                first = k * f + i * 128
                vec_ref[4 + 2 * k + at // 8, at % 8 : at % 8 + 1, :] = ref[row : row + 1, first : first + 128]

    def rows_at(ref):
        n = ref.shape[0] // 4
        return lambda q: ref.at[pl.ds(pl.multiple_of(q * n, n), n), :]

    def cols_at(ref, first, n):
        return lambda q: ref.at[:, pl.ds(pl.multiple_of(first + q * n, n), n)]

    heads = q_sum.shape[1] // 3
    units = own_u.shape[1]
    spread_d = Spread(peers, own_d, rows_at(gd), s_sems.at[0])
    spread_u = Spread(peers, own_u, cols_at(gu, 0, units), s_sems.at[1])
    spread_o = Spread(peers, o_sum, rows_at(go), s_sems.at[2])
    spread_q = [
        Spread(peers, q_sum.at[:, pl.ds(i * heads, heads)], cols_at(gq, 4 * i * heads, heads), s_sems.at[3 + i])
        for i in range(3)
    ]
    spread_v = Spread(peers, v_own, lambda q: slot_out.at[q], s_sems.at[6])

    to_core = send(peers, "core", vec_ref.at[pl.ds(4, 12)], l1, v_sems.at[0], v_sems.at[1])
    to_x = send(peers, "x", v1.at[pl.ds(2, 10)], l2, v_sems.at[2], v_sems.at[3])
    to_y = send(peers, "y", v2.at[pl.ds(1, 11)], l3, v_sems.at[4], v_sems.at[5])
    to_rows = []
    for i in (1, 2, 3):
        to_rows.append(send(peers, i, v3.at[0], l4.at[i - 1, 0], v_sems.at[6 + 4 * i], v_sems.at[7 + 4 * i]))
        src = v3.at[pl.ds(4 + 2 * (4 - i), 2)]
        to_rows.append(send(peers, i, src, l4.at[i - 1, pl.ds(1, 2)], v_sems.at[8 + 4 * i], v_sems.at[9 + 4 * i]))

    peers.meet(ALL_PEERS)
    deal_o.start()
    deal_q.start()
    to_core.start()
    spread_d.start()
    spread_u.start()
    for c in loads:
        c.wait()
    products(0)
    deal_o.step(0)
    deal_q.step(0)
    products(1)
    to_core.wait()
    v1[0:4] = vec_ref[0:4] + l1[8:12]
    v1[4:12] = vec_ref[4:12] + l1[0:8]
    to_x.start()
    deal_o.step(1)
    deal_q.step(1)
    products(2)
    products(3)
    outward.store().start()
    to_x.wait()
    v2[0:2] = v1[0:2] + l2[0:2]
    v2[4:12] = v1[4:12] + l2[2:10]
    v2[2:4] = v1[2:4]
    to_y.start()
    spread_d.relay()
    spread_u.relay()
    deal_o.finish(o_sum)
    spread_o.start()
    deal_q.finish(q_sum)
    for sp in spread_q:
        sp.start()
    to_y.wait()
    v3[0:1] = v2[0:1] + l3[0:1]
    v3[4:12] = v2[4:12] + l3[3:11]
    for c in to_rows:
        c.start()
    spread_o.relay()
    for sp in spread_q:
        sp.relay()
    for c in to_rows:
        c.wait()
    v_own[...] = v3[0] + l4[0, 0] + l4[1, 0] + l4[2, 0]
    feat_ref[...] = v3[4:6] + l4[0, 1:3] + l4[1, 1:3] + l4[2, 1:3]
    spread_v.start()
    spread_v.relay()
    for sp in (spread_d, spread_u, spread_o, spread_v, *spread_q):
        sp.finish()
    outward.finish()


def last(tot_q, tot_o, own_d, own_u, g_part, u_part, vec1, vec2, g, w, r1):
    width = r1.shape[1]
    part = width // 4
    n = own_d.shape[0]
    heads = tot_o.shape[0]
    vmem = pl.BlockSpec(memory_space=pltpu.VMEM)

    def bufs(a, b, by_rows):
        piece = (a // 4, b) if by_rows else (a, b // 4)
        return [pltpu.VMEM((2, 3, *piece), BF), pltpu.VMEM((2, 2, *piece), BF), DMA((12,)), pltpu.VMEM(piece, BF)]

    return pl.pallas_call(
        last_kernel,
        in_specs=[vmem] * 8 + [ANY] * 3,
        out_specs=[ANY, ANY, ANY, ANY, ANY, ANY, vmem],
        out_shape=[
            jax.ShapeDtypeStruct((4 * SEQ, part), BF),
            jax.ShapeDtypeStruct((part, 12 * heads), BF),
            jax.ShapeDtypeStruct((4 * heads, part), BF),
            jax.ShapeDtypeStruct((4 * n, part), BF),
            jax.ShapeDtypeStruct((part, 4 * n), BF),
            jax.ShapeDtypeStruct((4, 8, 128), F32),
            jax.ShapeDtypeStruct((2, 8, 128), F32),
        ],
        scratch_shapes=[
            pltpu.VMEM((SEQ, 24 * heads), BF),
            pltpu.VMEM((width, 24 * heads), BF),
            pltpu.VMEM((SEQ, width), F32),
            pltpu.VMEM((SEQ, width), BF),
            DMA((3,)),
            *bufs(width, 3 * heads, True),
            *bufs(heads, width, False),
            pltpu.VMEM((16, 8, 128), F32),
            pltpu.VMEM((12, 8, 128), F32),
            pltpu.VMEM((12, 8, 128), F32),
            pltpu.VMEM((12, 8, 128), F32),
            pltpu.VMEM((12, 8, 128), F32),
            pltpu.VMEM((10, 8, 128), F32),
            pltpu.VMEM((11, 8, 128), F32),
            pltpu.VMEM((3, 3, 8, 128), F32),
            pltpu.VMEM((8, 128), F32),
            DMA((24,)),
            sems_of_exchange(),
            DMA((7, 7)),
        ],
        compiler_params=pltpu.CompilerParams(vmem_limit_bytes=VMEM_LIMIT, collective_id=6, has_side_effects=True),
        name="last",
    )(tot_q, tot_o, own_d, own_u, g_part, u_part, vec1, vec2, g, w, r1)


def whole_sequences(
    tokens, segments, w_query, b_query, w_key, w_value, b_value, w_out, b_out, norm1_gain, norm1_shift,
    w_up, b_up, w_down, b_down, norm2_gain, norm2_shift, cotangent,
):
    R = lax.axis_size("row")
    feat = tokens.shape[1]
    hq = b_query.shape[0] // 4
    unit = b_up.shape[0] // 4
    vectors = (b_out, norm1_gain, norm1_shift, b_down, norm2_gain, norm2_shift, b_query, b_value, b_up)
    vectors = jnp.concatenate(vectors).astype(F32).reshape(1, -1)
    x, w_qkv, wo, wu, wd, feat_all, b_slot, seg = first(
        tokens,
        segments.reshape(2, 8, 128),
        (w_query, w_key, w_value, w_out, w_up, w_down),
        vectors,
    )

    qkv, att, prob, linv, wo, wu, wd, cot_first = attend_fwd(x, w_qkv, b_slot, seg, cotangent, wo, wu, wd)
    wu, wd, act, slope, hidden_low, normed1, inv1, output, grad_r2, vg2 = ff_fwd(
        x, att, wo, feat_all, b_slot, cotangent, cot_first, wu, wd
    )

    out_block, grad_pre, bu_part, kept_d = ff_down_bwd(grad_r2, wd, act, slope, output)
    out_block, grad_r1, grad_attn, vg1, kept_u, tot_d = ff_up_bwd(
        grad_r2, hidden_low, grad_pre, wu, normed1, inv1, feat_all, output, out_block, kept_d
    )
    g_qkv, g_part, tot_q, tot_o, own_d, own_u = attend_bwd(
        grad_attn, wo, att, qkv, linv, prob, x, tot_d, kept_u
    )

    x_grad_block, gq, go, gd, gu, slot_sum, own = last(
        tot_q, tot_o, own_d, own_u, g_part, bu_part, vg1, vg2, g_qkv, w_qkv, grad_r1
    )
    wq_grad, wk_grad, wv_grad = [gq[:, i * 4 * hq : (i + 1) * 4 * hq].astype(F32) for i in range(3)]
    w_out_grad, w_up_grad, w_down_grad = go.astype(F32), gu.astype(F32), gd.astype(F32)
    slot_sum = slot_sum.reshape(4, 1024)
    bq_grad = slot_sum[:, :hq].reshape(-1)
    bv_grad = slot_sum[:, 2 * hq : 3 * hq].reshape(-1)
    bu_grad = slot_sum[:, 3 * hq : 3 * hq + unit].reshape(-1)
    own = own.reshape(-1)[: 6 * feat].reshape(6, feat)
    return (
        out_block, x_grad_block, wq_grad, bq_grad, wk_grad, wv_grad, bv_grad, w_out_grad, own[0], own[1], own[2],
        w_up_grad, bu_grad, w_down_grad, own[3], own[4], own[5],
    )


def tokens_cols(source):
    return lax.all_gather(source, "col", axis=0, tiled=True)


def tokens_rows(source):
    return lax.all_gather(source, "row", axis=0, tiled=True)


def product(row_piece, weight, flipped):
    if flipped:
        return lax.dot_general(
            row_piece, weight, (((1,), (1,)), ((), ())), preferred_element_type=jnp.float32
        )
    return jnp.dot(row_piece, weight, preferred_element_type=jnp.float32)


def outer_sum(left, right):
    return lax.dot_general(
        left, right, (((0,), (0,)), ((), ())), preferred_element_type=jnp.float32
    )


def settle_rows(gathered, weight, flipped, own_rows):

    def product_term(first_row, row_count):
        return product(gathered, weight, flipped)

    return lax.psum_scatter(
        product_term(jnp.int32(0), own_rows * lax.axis_size("row")),
        "row",
        scatter_dimension=0,
        tiled=True,
    )


def settle_cols(gathered, weight, flipped, own_rows):

    def product_term(first_row, row_count):
        return product(gathered, weight, flipped)

    return lax.psum_scatter(
        product_term(jnp.int32(0), own_rows * lax.axis_size("col")),
        "col",
        scatter_dimension=0,
        tiled=True,
    )


def row_sums(first_part, second_part):
    return lax.psum((jnp.sum(first_part, axis=1), jnp.sum(second_part, axis=1)), "row")


def norm_forward(residual, norm_gain, norm_shift):
    total_sum, square_sum = row_sums(residual, residual * residual)
    row_mean = (total_sum / WIDTH)[:, None]
    variance = (square_sum / WIDTH)[:, None] - row_mean * row_mean
    inv_std = lax.rsqrt(variance + NORM_EPS)
    normed = (residual - row_mean) * inv_std
    return (normed * norm_gain + norm_shift, normed, inv_std)


def norm_backward(grad_in, normed, inv_std, norm_gain):
    grad_norm = grad_in * norm_gain
    total_sum, cross_sum = row_sums(grad_norm, grad_norm * normed)
    grad_resid = inv_std * (grad_norm - total_sum[:, None] / WIDTH - normed * cross_sum[:, None] / WIDTH)
    return (grad_resid, jnp.sum(grad_in * normed, axis=0), jnp.sum(grad_in, axis=0))


def split_heads(array, seq_count):
    return array.reshape(seq_count, SEQ, array.shape[1] // HD, HD)


def pair_scores(queries, key_heads, segment_ids):
    position = jnp.arange(SEQ)
    same_doc = (segment_ids[:, None] == segment_ids[None, :]) & (segment_ids[None, :] != 0)
    allowed = same_doc | (position[:, None] == position[None, :])
    raw_scores = jnp.einsum(
        "qhd,khd->hqk", queries, key_heads, preferred_element_type=jnp.float32
    ) * HD ** (-0.5)
    return jnp.where(allowed[None], raw_scores, -1000000000.0)


def attend_forward(source):
    queries, key_heads, values, segment_ids = source
    scores = pair_scores(queries, key_heads, segment_ids)
    top_score = jnp.max(scores, axis=2, keepdims=True)
    exp_scores = jnp.exp(scores - top_score)
    total_sum = jnp.sum(exp_scores, axis=2, keepdims=True)
    soft_low = (exp_scores / total_sum).astype(jnp.bfloat16)
    attended = jnp.einsum("hqk,khd->qhd", soft_low, values, preferred_element_type=jnp.float32)
    return (attended.astype(jnp.bfloat16), (top_score + jnp.log(total_sum))[:, :, 0])


def attend_backward(source):
    queries, key_heads, values, segment_ids, grad_out, log_total = source
    scores = pair_scores(queries, key_heads, segment_ids)
    soft_weights = jnp.exp(scores - log_total[:, :, None])
    soft_low = soft_weights.astype(jnp.bfloat16)
    grad_values = jnp.einsum("hqk,qhd->khd", soft_low, grad_out, preferred_element_type=jnp.float32)
    grad_soft = jnp.einsum("qhd,khd->hqk", grad_out, values, preferred_element_type=jnp.float32)
    grad_scores = soft_weights * (
        grad_soft - jnp.sum(soft_weights * grad_soft, axis=2, keepdims=True)
    )
    grad_scores = grad_scores.astype(jnp.bfloat16)
    scale_factor = HD ** (-0.5)
    grad_queries = (
        jnp.einsum("hqk,khd->qhd", grad_scores, key_heads, preferred_element_type=jnp.float32)
        * scale_factor
    )
    grad_keys = (
        jnp.einsum("hqk,qhd->khd", grad_scores, queries, preferred_element_type=jnp.float32)
        * scale_factor
    )
    return (
        grad_queries.astype(jnp.bfloat16),
        grad_keys.astype(jnp.bfloat16),
        grad_values.astype(jnp.bfloat16),
    )


def split_heads_plan(
    tokens,
    segments,
    w_query,
    b_query,
    w_key,
    w_value,
    b_value,
    w_out,
    b_out,
    norm1_gain,
    norm1_shift,
    w_up,
    b_up,
    w_down,
    b_down,
    norm2_gain,
    norm2_shift,
    cotangent,
):
    rows_b = tokens.shape[0]
    rows_a = segments.shape[0]
    head_cols = w_query.shape[1]
    seq_count = rows_a // SEQ
    segment_seqs = segments.reshape(seq_count, SEQ)
    gathered_x = tokens_cols(tokens)
    stacked = jnp.concatenate([w_query, w_key, w_value], axis=1)
    projected = settle_rows(gathered_x, stacked, False, rows_a)
    queries = (projected[:, :head_cols] + b_query).astype(jnp.bfloat16)
    key_heads = projected[:, head_cols : 2 * head_cols].astype(jnp.bfloat16)
    values = (projected[:, 2 * head_cols :] + b_value).astype(jnp.bfloat16)
    query_seqs = split_heads(queries, seq_count)
    key_seqs = split_heads(key_heads, seq_count)
    value_seqs = split_heads(values, seq_count)
    attended, log_total = lax.map(attend_forward, (query_seqs, key_seqs, value_seqs, segment_seqs))
    attended = attended.reshape(rows_a, head_cols)
    gathered_o = tokens_rows(attended)
    attn_out = settle_cols(gathered_o, w_out, False, rows_b) + b_out
    hidden, normed1, inv_std1 = norm_forward(
        tokens.astype(jnp.float32) + attn_out, norm1_gain, norm1_shift
    )
    hidden_low = hidden.astype(jnp.bfloat16)
    gathered_h = tokens_cols(hidden_low)
    pre_act = settle_rows(gathered_h, w_up, False, rows_a) + b_up
    active = gelu_exact(pre_act).astype(jnp.bfloat16)
    gathered_a = tokens_rows(active)
    fed = settle_cols(gathered_a, w_down, False, rows_b) + b_down
    output, normed2, inv_std2 = norm_forward(hidden + fed, norm2_gain, norm2_shift)
    grad_r2, grad_gain2, grad_shift2 = norm_backward(
        cotangent.astype(jnp.float32), normed2, inv_std2, norm2_gain
    )
    grad_fed = grad_r2.astype(jnp.bfloat16)
    gathered_f = tokens_cols(grad_fed)
    grad_w_down = outer_sum(gathered_a, gathered_f)
    grad_active = settle_rows(gathered_f, w_down, True, rows_a)
    unused_out, slope_pull = jax.vjp(gelu_exact, pre_act)
    grad_pre = slope_pull(grad_active)[0].astype(jnp.bfloat16)
    gathered_p = tokens_rows(grad_pre)
    grad_w_up = outer_sum(gathered_h, gathered_p)
    grad_from_ff = settle_cols(gathered_p, w_up, True, rows_b)
    bias_up_part = jnp.sum(grad_pre.astype(jnp.float32), axis=0)
    bias_down_part = jnp.sum(grad_fed.astype(jnp.float32), axis=0)
    grad_r1, grad_gain1, grad_shift1 = norm_backward(
        grad_from_ff + grad_r2, normed1, inv_std1, norm1_gain
    )
    grad_attn = grad_r1.astype(jnp.bfloat16)
    gathered_d = tokens_cols(grad_attn)
    grad_w_out = outer_sum(gathered_o, gathered_d)
    grad_attended = settle_rows(gathered_d, w_out, True, rows_a).astype(jnp.bfloat16)
    grad_q, grad_k, grad_v = lax.map(
        attend_backward,
        (
            query_seqs,
            key_seqs,
            value_seqs,
            segment_seqs,
            split_heads(grad_attended, seq_count),
            log_total,
        ),
    )
    grad_q = grad_q.reshape(rows_a, head_cols)
    grad_k = grad_k.reshape(rows_a, head_cols)
    grad_v = grad_v.reshape(rows_a, head_cols)
    grad_proj = jnp.concatenate([grad_q, grad_k, grad_v], axis=1)
    gathered_g = tokens_rows(grad_proj)
    grad_stacked = outer_sum(gathered_x, gathered_g)
    tokens_grad = settle_cols(gathered_g, stacked, True, rows_b) + grad_r1
    bias_q, bias_v, bias_up = lax.psum(
        (
            jnp.sum(grad_q.astype(jnp.float32), axis=0),
            jnp.sum(grad_v.astype(jnp.float32), axis=0),
            bias_up_part,
        ),
        ("dp", "row"),
    )
    bias_out, bias_down, gain_one, shift_one, gain_two, shift_two = lax.psum(
        (
            jnp.sum(grad_attn.astype(jnp.float32), axis=0),
            bias_down_part,
            grad_gain1,
            grad_shift1,
            grad_gain2,
            grad_shift2,
        ),
        ("dp", "col"),
    )
    sum_stacked, sum_out, sum_up, sum_down = (
        lax.psum(grad_stacked.astype(jnp.bfloat16), "dp").astype(jnp.float32),
        lax.psum(grad_w_out.astype(jnp.bfloat16), "dp").astype(jnp.float32),
        lax.psum(grad_w_up.astype(jnp.bfloat16), "dp").astype(jnp.float32),
        lax.psum(grad_w_down.astype(jnp.bfloat16), "dp").astype(jnp.float32),
    )
    return (
        output.astype(jnp.bfloat16),
        tokens_grad.astype(jnp.bfloat16),
        sum_stacked[:, :head_cols],
        bias_q,
        sum_stacked[:, head_cols : 2 * head_cols],
        sum_stacked[:, 2 * head_cols :],
        bias_v,
        sum_out,
        bias_out,
        gain_one,
        shift_one,
        sum_up,
        bias_up,
        sum_down,
        bias_down,
        gain_two,
        shift_two,
    )


def solution(mesh):
    dp, rows, cols = (mesh.shape[name] for name in ("dp", "row", "col"))
    whole = TOKENS // SEQ == dp * rows * cols and dp == 4 and cols == 2
    plan = whole_sequences if whole else split_heads_plan
    placed = (
        P(("dp", "col"), "row"),
        P(("dp", "row")),
        P("row", "col"),
        P("col"),
        P("row", "col"),
        P("row", "col"),
        P("col"),
        P("col", "row"),
        P("row"),
        P("row"),
        P("row"),
        P("row", "col"),
        P("col"),
        P("col", "row"),
        P("row"),
        P("row"),
        P("row"),
        P(("dp", "col"), "row"),
    )
    return jax.shard_map(
        plan,
        mesh=mesh,
        in_specs=placed,
        out_specs=(
            P(("dp", "col"), "row"),
            P(("dp", "col"), "row"),
            P("row", "col"),
            P("col"),
            P("row", "col"),
            P("row", "col"),
            P("col"),
            P("col", "row"),
            P("row"),
            P("row"),
            P("row"),
            P("row", "col"),
            P("col"),
            P("col", "row"),
            P("row"),
            P("row"),
            P("row"),
        ),
        check_vma=False,
    )
```

```python
import math

import jax
import jax.numpy as jnp
from jax import lax
from jax.experimental import pallas as pl
from jax.experimental.pallas import tpu as pltpu
from jax.sharding import PartitionSpec as P

HD = 64
SEQ = 1024
WIDTH = 1024
TOKENS = 32768
NORM_EPS = 1e-05
BF = jnp.bfloat16
F32 = jnp.float32
NEG = -1e30
QB = 256
VMEM_LIMIT = 56 * 1024 * 1024
MESH = pl.DeviceIdType.MESH
ANY = pl.BlockSpec(memory_space=pl.ANY)
DMA = pltpu.SemaphoreType.DMA
ONCE = pl.Buffered(1)


def const(*shape):
    return pl.BlockSpec(shape, lambda j: (0,) * len(shape), pipeline_mode=ONCE)


def mm(a, b):
    return jnp.dot(a, b, preferred_element_type=F32)


def mm_t(a, b):
    return lax.dot_general(a, b, (((1,), (1,)), ((), ())), preferred_element_type=F32)


def tmm(a, b):
    return lax.dot_general(a, b, (((0,), (0,)), ((), ())), preferred_element_type=F32)


def gelu_exact(v):
    return jax.nn.gelu(v, approximate=False)


def attend_rows(qkv_ref, seg_col_ref, seg_row, o_ref, p_ref, linv_ref, hook):
    lane = lax.broadcasted_iota(jnp.int32, (QB, 128), 1)
    scale = HD ** (-0.5) * math.log2(math.e)
    k = qkv_ref[:, 128:256]
    v = qkv_ref[:, 256:384]
    units = [(i, h) for i in range(SEQ // QB) for h in range(2)]

    def scores(i, h):
        q = qkv_ref[i * QB : (i + 1) * QB, 0:128]
        mine = (lane < HD) if h == 0 else (lane >= HD)
        return mm_t(jnp.where(mine, q, jnp.zeros_like(q)), k)

    ahead = scores(*units[0])
    outs = []
    for at, (i, h) in enumerate(units):
        rows = slice(i * QB, (i + 1) * QB)
        if h == 0:
            hook(i)
        s = ahead
        if at + 1 < len(units):
            ahead = scores(*units[at + 1])
        s = jnp.where(seg_col_ref[rows, 0:1] == seg_row, s * scale, NEG)
        top = jnp.max(s, axis=1, keepdims=True)
        p = jnp.exp2(s - top)
        total = jnp.sum(p, axis=1, keepdims=True)
        pb = p.astype(BF)
        p_ref[h, rows, :] = pb
        inv = 1.0 / total
        outs.append((mm(pb, v) * inv, jnp.broadcast_to(inv, (QB, 128))))
        if h == 1:
            o_ref[rows, :] = jnp.where(lane < HD, outs[0][0], outs[1][0]).astype(BF)
            linv_ref[rows, :] = jnp.where(lane < HD, outs[0][1], outs[1][1])
            outs = []


def attend_fwd_kernel(
    x_ref, w_ref, b_ref, seg_ref, cot, wo_in, wu_in, wd_in,
    qkv_ref, o_ref, p_ref, linv_ref, wo, wu, wd, cot_first,
    x_buf, seg_col_ref, seg_row_ref, cot_own, i_sems, o_recv, o_sent, u_recv, u_sent, d_recv, d_sent,
):
    j = pl.program_id(0)
    peers = Peers()
    go = Gather(peers, None, wo, False, o_recv, o_sent, RING + LATER_NEAR + FAR)
    gu = Gather(peers, None, wu, True, u_recv, u_sent, RING + LATER_NEAR + far_edges(0))
    gd = Gather(peers, None, wd, False, d_recv, d_sent, RING + DOWN_NEAR + far_edges(0, 1))
    every = (go, gu, gd)
    inward = Inward(peers, cot, cot_first, cot_own, i_sems, (0,))

    plan = {
        8: ((go, (1, 0)), (gu, (1, 0))),
        10: ((gu, (0, 6)), (gd, (0, 6))),
        12: ((gd, (1, 0)), (go, (1, 2), (1, 4), (2, 0)), (gu, (1, 2), (1, 4))),
        16: ((gu, (2, 0)), (go, (0, 6), (1, 6)), (gd, (1, 2), (1, 4))),
        20: ((gd, (2, 0)), (go, (2, 2), (2, 4), (3, 0)), (gu, (2, 2), (2, 4))),
        25: ((gu, (3, 0)), (go, (2, 6), (3, 2), (3, 4)), (gd, (2, 2), (2, 4))),
        29: ((gd, (3, 0)), (gu, (3, 2), (3, 4)), (go, (3, 6))),
    }

    def hook(i):
        for at, work in plan.items():
            if at % 4 == i:
                @pl.when(j == at // 4)
                def _(at=at, work=work):
                    for g, *blocks in work:
                        g.relay(*blocks)
                    if at == 20:
                        inward.settle()
                        inward.start(0)

    @pl.when(j == 0)
    def _():
        peers.hello(ALL_PEERS)
        inward.load()
        f = x_ref.shape[2]
        for s in range(4):
            x_buf[:, s * f : (s + 1) * f] = x_ref[s]
        tile = seg_ref[4 * peers.c + peers.r]
        for i in range(8):
            row = tile[i : i + 1, :]
            at = lax.broadcasted_iota(jnp.int32, (1, 128), 1) + i * 128
            row = jnp.where(row == 0, -1 - at, row)
            seg_row_ref[:, i * 128 : (i + 1) * 128] = row
            seg_col_ref[i * 128 : (i + 1) * 128, :] = jnp.transpose(jnp.broadcast_to(row, (128, 128)))

    qkv_ref[...] = (mm(x_buf[...], w_ref[...]) + b_ref[0, :, 0:384]).astype(BF)
    @pl.when(j == 0)
    def _():
        peers.meet(ALL_PEERS)
        for g in every:
            g.emit(0, 0)
        go.emit(0, 2)
        gu.emit(0, 2)
        gd.emit(0, 4)

    seg_row = seg_row_ref[...]
    attend_rows(qkv_ref, seg_col_ref, seg_row, o_ref, p_ref, linv_ref, hook)

    @pl.when(j == 7)
    def _():
        for g in every:
            g.finish()
        inward.finish()


def attend_fwd(x, w_qkv, b_slot, seg, cot, wo, wu, wd):
    slots = w_qkv.shape[1] // 384
    return pl.pallas_call(
        attend_fwd_kernel,
        grid=(slots,),
        in_specs=[
            const(*x.shape),
            pl.BlockSpec((w_qkv.shape[0], 384), lambda j: (0, j)),
            pl.BlockSpec((1, 1, b_slot.shape[2]), lambda j: (j, 0, 0)),
            const(8, 8, 128),
            ANY,
            ANY,
            ANY,
            ANY,
        ],
        out_specs=[
            pl.BlockSpec((SEQ, 384), lambda j: (0, j)),
            pl.BlockSpec((SEQ, 128), lambda j: (0, j)),
            pl.BlockSpec((2, SEQ, SEQ), lambda j: (j, 0, 0)),
            pl.BlockSpec((SEQ, 128), lambda j: (0, j)),
            ANY,
            ANY,
            ANY,
            ANY,
        ],
        out_shape=[
            jax.ShapeDtypeStruct((SEQ, slots * 384), BF),
            jax.ShapeDtypeStruct((SEQ, slots * 128), BF),
            jax.ShapeDtypeStruct((slots * 2, SEQ, SEQ), BF),
            jax.ShapeDtypeStruct((SEQ, slots * 128), F32),
            jax.ShapeDtypeStruct(wo.shape, BF),
            jax.ShapeDtypeStruct(wu.shape, BF),
            jax.ShapeDtypeStruct(wd.shape, BF),
            jax.ShapeDtypeStruct((SEQ // CHUNKS, w_qkv.shape[0]), BF),
        ],
        input_output_aliases={5: 4, 6: 5, 7: 6},
        scratch_shapes=[
            pltpu.VMEM((SEQ, w_qkv.shape[0]), BF),
            pltpu.VMEM((SEQ, 128), jnp.int32),
            pltpu.VMEM((1, SEQ), jnp.int32),
            pltpu.VMEM((SEQ // CHUNKS, cot.shape[1]), BF),
            sems_of_exchange(),
            *[DMA((32,))] * 6,
        ],
        compiler_params=pltpu.CompilerParams(vmem_limit_bytes=VMEM_LIMIT, collective_id=1, has_side_effects=True),
        name="attend_fwd",
    )(x, w_qkv, b_slot, seg, cot, wo, wu, wd)


class Peers:
    def __init__(self):
        self.r = lax.axis_index("row")
        self.c = lax.axis_index("col")
        self.d = d = lax.axis_index("dp")
        self.ids = {
            "core": {"dp": d + 1 - 2 * lax.rem(d, 2)},
            "x": {"dp": lax.rem(d + 2, 4)},
            "y": {"col": 1 - self.c},
            1: {"row": lax.rem(self.r + 1, 4)},
            2: {"row": lax.rem(self.r + 2, 4)},
            3: {"row": lax.rem(self.r + 3, 4)},
        }

    def hello(self, names):
        barrier = pltpu.get_barrier_semaphore()
        for name in names:
            pl.semaphore_signal(barrier, inc=1, device_id=self.ids[name], device_id_type=MESH)

    def meet(self, names):
        pl.semaphore_wait(pltpu.get_barrier_semaphore(), len(names))


def send(peers, name, src, dst, send_sem, recv_sem):
    return pltpu.make_async_remote_copy(
        src_ref=src, dst_ref=dst, send_sem=send_sem, recv_sem=recv_sem, device_id=peers.ids[name], device_id_type=MESH
    )


def near_edges(s):
    return [("x", s, 0, s, 2), ("y", s, 0, s, 4), ("core", s, 0, s, 1)]


def second_edges(s):
    return [("core", s, 2, s, 3), ("core", s, 4, s, 5)]


def far_edges(s, flip=0):
    return [("y", s, 2, s, 6) if (s + flip) % 2 == 0 else ("x", s, 4, s, 6), ("core", s, 6, s, 7)]


def emit_far(gather, s, flip=0):
    gather.emit(s, 2 if (s + flip) % 2 == 0 else 4)


RING = [(1, s, 0, s + 1, 0) for s in range(3)]
NEAR = [e for s in range(4) for e in near_edges(s) + second_edges(s)]
FAR = [e for s in range(4) for e in far_edges(s)]
OWN_BLOCK = near_edges(0) + second_edges(0)
LATER_NEAR = [e for e in NEAR if e[1] > 0]
UP_FAR = [e for s in (1, 2, 3) for e in far_edges(s)]
DOWN_FAR = [e for s in (1, 2, 3) for e in far_edges(s, 1)]
DOWN_NEAR = [e for e in LATER_NEAR if e[1] < 3] + [("core", 3, 0, 3, 1)]
DOWN_REST = [e for e in near_edges(3) if e[0] != "core"] + second_edges(3) + DOWN_FAR


class Gather:
    def __init__(self, peers, piece, full, by_rows, recv, sent, edges):
        self.peers, self.piece, self.full, self.recv, self.sent = peers, piece, full, recv, sent
        self.by_rows = by_rows
        self.n = full.shape[1 if by_rows else 0] // 8
        self.m = full.shape[0 if by_rows else 1] // 4
        self.edges = edges
        self.waited = set()
        self.emitted = set()

    def blk(self, s, t):
        a = pl.ds(s * self.m, self.m)
        b = pl.ds(t * self.n, self.n)
        return self.full.at[a, b] if self.by_rows else self.full.at[b, a]

    def copy(self, at):
        name, s, t, s2, t2 = self.edges[at]
        src = self.piece if (s, t) == (0, 0) and self.piece is not None else self.blk(s, t)
        return send(self.peers, name, src, self.blk(s2, t2), self.sent.at[at], self.recv.at[at])

    def emit(self, s, t):
        for at, e in enumerate(self.edges):
            if e[1:3] == (s, t):
                assert at not in self.emitted
                self.emitted.add(at)
                self.copy(at).start()

    def emit_own_slot(self, s):
        for at, e in enumerate(self.edges):
            if e[1:3] == (s, 0):
                self.emitted.add(at)
                self.copy(at).start()

    def arrived(self, s, t):
        for at, e in enumerate(self.edges):
            if e[3:5] == (s, t) and at not in self.waited:
                self.waited.add(at)
                self.copy(at).wait_recv()

    def relay(self, *blocks):
        for s, t in blocks:
            self.arrived(s, t)
            self.emit(s, t)

    def own(self):
        return pltpu.make_async_copy(self.piece, self.blk(0, 0), self.sent.at[len(self.edges)])

    def start(self):
        self.emit(0, 0)
        self.own().start()

    def finish(self):
        if self.piece is not None:
            self.own().wait()
        for at, e in enumerate(self.edges):
            if at not in self.waited:
                self.waited.add(at)
                self.copy(at).wait_recv()
        assert len(self.emitted) == len(self.edges)
        for at in range(len(self.edges)):
            self.copy(at).wait_send()


class Line:
    WAVES = ((3, 2, 1), (1, 3, 2), (1, 3, 2), (1, 2, 3))

    def __init__(self, peers, gather, sems):
        self.peers, self.gather, self.sems = peers, gather, sems

    def copy(self, up, s):
        s2 = s + 1 if up else (s - 1 if s else 3)
        g = self.gather
        src = g.piece if s == 0 else g.blk(s, 0)
        return send(
            self.peers, 1 if up else 3, src, g.blk(s2, 0), self.sems.at[(0 if up else 4) + s], self.sems.at[7 + s2]
        )

    def each(self, what):
        r = self.peers.r
        for s in range(3):
            @pl.when((r >= s) & (r < 3))
            def _(s=s):
                what(self.copy(True, s))
        for s in (0, 3, 2):
            @pl.when((r > 0) & (r <= (3 if s == 0 else s - 1)))
            def _(s=s):
                what(self.copy(False, s))

    def start(self):
        r = self.peers.r

        @pl.when(r < 3)
        def _():
            self.copy(True, 0).start()

        @pl.when(r > 0)
        def _():
            self.copy(False, 0).start()

    def wave(self, k):
        for row, order in enumerate(self.WAVES):
            s = order[k]

            @pl.when(self.peers.r == row)
            def _(row=row, s=s):
                self.copy(True, s - 1).wait_recv()
                below = row >= s
                if below and row < 3:
                    self.copy(True, s).start()
                if not below and row > 0:
                    self.copy(False, s).start()
                self.gather.emit_own_slot(s)

    def finish(self):
        self.each(lambda c: c.wait_send())


CHUNKS = 4
FINE = 8


def sems_of_exchange(cuts=CHUNKS):
    return DMA((2, 4, cuts))


class Inward:
    def __init__(self, peers, block, rows, buf, sems, chunks=range(CHUNKS), cuts=CHUNKS):
        self.peers, self.block, self.rows, self.buf, self.sems, self.chunks = peers, block, rows, buf, sems, chunks
        self.n = SEQ // cuts

    def ends(self, s, first, count):
        r = lax.rem(self.peers.r + s, 4)
        f = self.block.shape[1]
        src = self.block.at[pl.ds(pl.multiple_of(r * SEQ + first * self.n, self.n), count * self.n), :]
        at = first if self.rows.shape[-2] == SEQ else first - self.chunks[0]
        rows = pl.ds(at * self.n, count * self.n)
        return src, self.rows.at[s, rows, :] if len(self.rows.shape) == 3 else self.rows.at[rows, pl.ds(s * f, f)]

    def copy(self, s, k):
        return send(self.peers, s, *self.ends(s, k, 1), self.sems.at[0, s, k], self.sems.at[1, s, k])

    def own(self):
        src, dst = self.ends(0, self.chunks[0], len(self.chunks))
        return (
            pltpu.make_async_copy(src, self.buf, self.sems.at[0, 0, 0]),
            pltpu.make_async_copy(self.buf, dst, self.sems.at[1, 0, 0]),
        )

    def start(self, *chunks):
        for k in chunks:
            for s in (2, 1, 3):
                self.copy(s, k).start()

    def load(self):
        self.own()[0].start()

    def settle(self):
        self.own()[0].wait()
        self.own()[1].start()

    def finish(self):
        self.own()[1].wait()
        for k in self.chunks:
            for s in (1, 2, 3):
                self.copy(s, k).wait()


ALL_PEERS = ("core", "x", "y", 1, 2, 3)


def first_kernel(
    tokens, segments, w_query, w_key, w_value, w_out, w_up, w_down,
    vectors,
    x, w, wo, wu, wd, feat_out, slot_out, seg_out,
    pq, po, pu, pd, rows_buf, feat, slot, l_sems, q_recv, q_sent, o_recv, o_sent, u_recv, u_sent, d_recv, d_sent,
    i_sems, v_sems, z_sems,
):
    peers = Peers()
    r, d = peers.r, peers.d

    def own_cols(ref):
        n = ref.shape[1] // 4
        return ref.at[:, pl.ds(pl.multiple_of(d * n, n), n)]

    def own_rows(ref):
        n = ref.shape[0] // 4
        return ref.at[pl.ds(pl.multiple_of(d * n, n), n), :]

    peers.hello(ALL_PEERS)
    heads = w_query.shape[1] // 4
    loads = [
        pltpu.make_async_copy(own_cols(ref), pq.at[:, pl.ds(i * heads, heads)], l_sems.at[i])
        for i, ref in enumerate((w_query, w_key, w_value))
    ]
    loads += [
        pltpu.make_async_copy(own_rows(w_out), po, l_sems.at[3]),
        pltpu.make_async_copy(own_cols(w_up), pu, l_sems.at[4]),
        pltpu.make_async_copy(own_rows(w_down), pd, l_sems.at[5]),
    ]
    for c in loads:
        c.start()
    feat[...] = jnp.zeros_like(feat)
    f = feat.shape[1]
    for i in range(6):
        feat[i : i + 1, :] = vectors[:, i * f : (i + 1) * f]
    units = slot.shape[2] - 3 * heads
    at_q, at_v, at_u = 6 * f, 6 * f + 4 * heads, 6 * f + 8 * heads

    def quarter(first, n, q):
        return vectors[:, pl.ds(pl.multiple_of(first + q * n, 128), n)]

    for t in range(4):
        q = d
        if t % 2:
            q = q + 1 - 2 * lax.rem(q, 2)
        if t // 2:
            q = lax.rem(q + 2, 4)
        slot[t, :, 0:heads] = quarter(at_q, heads, q)
        slot[t, :, heads : 2 * heads] = jnp.zeros((1, heads), F32)
        slot[t, :, 2 * heads : 3 * heads] = quarter(at_v, heads, q)
        slot[t, :, 3 * heads :] = quarter(at_u, units, q)
    for c in loads:
        c.wait()

    gq = Gather(peers, pq, w, True, q_recv, q_sent, NEAR + FAR)
    line = Line(peers, gq, z_sems)
    go = Gather(peers, po, wo, False, o_recv, o_sent, OWN_BLOCK)
    gu = Gather(peers, pu, wu, True, u_recv, u_sent, OWN_BLOCK)
    gd = Gather(peers, pd, wd, False, d_recv, d_sent, OWN_BLOCK)
    later = (go, gu, gd)
    inward = Inward(peers, tokens, x, rows_buf, i_sems, range(FINE), FINE)
    inward.load()
    here = seg_out.at[pl.ds(2 * r, 2)]
    small = [
        pltpu.make_async_copy(feat, feat_out.at[:, pl.ds(0, f)], v_sems.at[0]),
        pltpu.make_async_copy(slot, slot_out.at[pl.ds(0, 4)], v_sems.at[1]),
        pltpu.make_async_copy(segments, here, v_sems.at[2]),
        send(peers, "y", slot, slot_out.at[pl.ds(4, 4)], v_sems.at[3], v_sems.at[4]),
    ]
    for i in (1, 2, 3):
        small.append(send(peers, i, feat, feat_out.at[:, pl.ds(i * f, f)], v_sems.at[3 + 2 * i], v_sems.at[4 + 2 * i]))
        small.append(send(peers, i, segments, here, v_sems.at[9 + 2 * i], v_sems.at[10 + 2 * i]))

    peers.meet(ALL_PEERS)
    line.start()
    gq.start()
    for c in small:
        c.start()
    for g in later:
        g.start()
    inward.start(0)
    line.wave(0)
    inward.start(1)
    inward.settle()
    gq.relay((0, 2), (0, 4))
    line.wave(1)
    inward.start(2)
    for g in later:
        g.relay((0, 2), (0, 4))
    line.wave(2)
    inward.start(*range(3, FINE))
    for s in (1, 2, 3):
        gq.relay((s, 2), (s, 4))
    for s in range(4):
        gq.relay((s, 6))
    for c in small:
        c.wait()
    for g in (gq, *later):
        g.finish()
    line.finish()
    inward.finish()


def first(tokens, segments, weights, vectors):
    w_query, _, _, w_out, w_up, w_down = weights
    width = 4 * tokens.shape[1]
    heads = w_query.shape[1] // 4
    units = w_up.shape[1] // 4
    vmem = pl.BlockSpec(memory_space=pltpu.VMEM)
    return pl.pallas_call(
        first_kernel,
        in_specs=[ANY, vmem] + [ANY] * 6 + [vmem],
        out_specs=[ANY] * 8,
        out_shape=[
            jax.ShapeDtypeStruct((4, SEQ, width // 4), BF),
            jax.ShapeDtypeStruct((width, 24 * heads), BF),
            jax.ShapeDtypeStruct((8 * heads, width), BF),
            jax.ShapeDtypeStruct((width, 8 * units), BF),
            jax.ShapeDtypeStruct((8 * units, width), BF),
            jax.ShapeDtypeStruct((8, width), F32),
            jax.ShapeDtypeStruct((8, 1, 3 * heads + units), F32),
            jax.ShapeDtypeStruct((8, 8, 128), jnp.int32),
        ],
        scratch_shapes=[
            pltpu.VMEM((width // 4, 3 * heads), BF),
            pltpu.VMEM((heads, width // 4), BF),
            pltpu.VMEM((width // 4, units), BF),
            pltpu.VMEM((units, width // 4), BF),
            pltpu.VMEM((SEQ, width // 4), BF),
            pltpu.VMEM((8, width // 4), F32),
            pltpu.VMEM((4, 1, 3 * heads + units), F32),
            DMA((6,)),
            *[DMA((32,))] * 8,
            sems_of_exchange(FINE),
            DMA((20,)),
            DMA((11,)),
        ],
        compiler_params=pltpu.CompilerParams(vmem_limit_bytes=VMEM_LIMIT, collective_id=0, has_side_effects=True),
        name="first",
    )(tokens, segments, *weights, vectors)


RB = 256


def norm_rows(v):
    mean = jnp.mean(v, axis=1, keepdims=True)
    variance = jnp.mean(v * v, axis=1, keepdims=True) - mean * mean
    inv = lax.rsqrt(variance + NORM_EPS)
    return (v - mean) * inv, inv


def norm_rows_back(g, normed, inv):
    mean_g = jnp.mean(g, axis=1, keepdims=True)
    mean_gn = jnp.mean(g * normed, axis=1, keepdims=True)
    return inv * (g - mean_g - normed * mean_gn)


def gelu_and_slope(v):
    z = jnp.abs(v) * (0.5 ** 0.5)
    t = 1.0 / (1.0 + 0.3275911 * z)
    poly = t * (0.254829592 + t * (-0.284496736 + t * (1.421413741 + t * (-1.453152027 + t * 1.061405429))))
    bell = jnp.exp2(z * z * -math.log2(math.e))
    tail = 0.5 * poly * bell
    cdf = jnp.where(v >= 0, 1.0 - tail, tail)
    return v * cdf, cdf + v * bell * (1.0 / math.sqrt(2.0 * math.pi))


def row_blocks(body, n=RB):
    def run(i, carry):
        body(pl.ds(pl.multiple_of(i * n, n), n))
        return carry

    lax.fori_loop(0, SEQ // n, run, 0)


def ff_fwd_kernel(
    x_ref, att_ref, wo_ref, vec_ref, b_ref, cot, cot_first, wu_in, wd_in,
    wu, wd, act_ref, slope_ref, hlow_ref, normed1_ref, inv1_ref, out_ref, r2_ref, vg_ref,
    acc, wu_buf, wd_buf, cot_buf, cot_own, buf_sem, u_recv, u_sent, d_recv, d_sent, i_sems, c_sem,
):
    j = pl.program_id(0)
    peers = Peers()
    gu = Gather(peers, None, wu, True, u_recv, u_sent, UP_FAR)
    gd = Gather(peers, None, wd, False, d_recv, d_sent, DOWN_REST)
    inward = Inward(peers, cot, cot_buf, cot_own, i_sems, range(1, CHUNKS))
    early = pltpu.make_async_copy(cot_first, cot_buf.at[pl.ds(0, SEQ // CHUNKS), :], c_sem)
    n = wu_buf.shape[2]

    def fetch(t, slot):
        cols = pl.ds(pl.multiple_of(t * n, n), n)
        return (
            pltpu.make_async_copy(wu.at[:, cols], wu_buf.at[slot], buf_sem.at[0, slot]),
            pltpu.make_async_copy(wd.at[cols, :], wd_buf.at[slot], buf_sem.at[1, slot]),
        )

    @pl.when(j == 0)
    def _():
        peers.hello(ALL_PEERS)
        for t in range(2):
            for c in fetch(t, t):
                c.start()
        early.start()
        inward.load()
        acc[...] = jnp.zeros_like(acc)
        peers.meet(ALL_PEERS)
        gd.emit(3, 0)
        for s in (1, 2):
            emit_far(gu, s)
            emit_far(gd, s, 1)
        emit_far(gu, 3)
        inward.start(*inward.chunks)

        def body(rows):
            x = jnp.concatenate([x_ref[s, rows, :] for s in range(4)], 1)
            v = x.astype(F32) + mm(att_ref[rows, :], wo_ref[...]) + vec_ref[0:1, :]
            normed, inv = norm_rows(v)
            normed1_ref[rows, :] = normed
            inv1_ref[rows, :] = jnp.broadcast_to(inv, (RB, 128))
            hlow_ref[rows, :] = (normed * vec_ref[1:2, :] + vec_ref[2:3, :]).astype(BF)

        row_blocks(body)
        gd.relay((3, 2), (3, 4))

    @pl.when(j == 1)
    def _():
        gd.arrived(3, 3)
        inward.settle()

    @pl.when(j == 2)
    def _():
        gd.arrived(3, 5)

    @pl.when(j == 4)
    def _():
        for g in (gu, gd):
            g.relay((1, 6), (2, 6), (3, 6))

    @pl.when(j == 5)
    def _():
        for s in (1, 2, 3):
            gu.arrived(s, 7)
            gd.arrived(s, 7)

    slot = lax.rem(j, 2)
    for c in fetch(j, slot):
        c.wait()
    w_up = wu_buf.at[slot]
    w_down = wd_buf.at[slot]
    bias = b_ref[0, :, 384:]
    for i in range(SEQ // 512):
        rows = slice(i * 512, (i + 1) * 512)
        act, slope = gelu_and_slope(mm(hlow_ref[rows, :], w_up[...]) + bias)
        act = act.astype(BF)
        act_ref[rows, :] = act
        slope_ref[rows, :] = slope.astype(BF)
        acc[rows, :] += mm(act, w_down[...])

    @pl.when(j < 6)
    def _():
        for c in fetch(j + 2, slot):
            c.start()

    @pl.when(j == 7)
    def _():
        inward.finish()
        early.wait()
        vg_ref[...] = jnp.zeros_like(vg_ref)

        def body(rows):
            hidden = normed1_ref[rows, :] * vec_ref[1:2, :] + vec_ref[2:3, :]
            normed, inv = norm_rows(hidden + (acc[rows, :] + vec_ref[3:4, :]))
            out_ref[rows, :] = (normed * vec_ref[4:5, :] + vec_ref[5:6, :]).astype(BF)
            c = cot_buf[rows, :].astype(F32)
            r2 = norm_rows_back(c * vec_ref[4:5, :], normed, inv)
            r2_ref[rows, :] = r2
            vg_ref[0:1, :] += jnp.sum(c * normed, axis=0, keepdims=True)
            vg_ref[1:2, :] += jnp.sum(c, axis=0, keepdims=True)
            vg_ref[2:3, :] += jnp.sum(r2.astype(BF).astype(F32), axis=0, keepdims=True)

        row_blocks(body)
        gu.finish()
        gd.finish()


def ff_fwd(x, att, wo, vec, bu, cot, cot_first, wu, wd):
    width, units = wu.shape
    n = units // 8
    return pl.pallas_call(
        ff_fwd_kernel,
        grid=(8,),
        in_specs=[
            const(*x.shape),
            const(SEQ, width),
            const(width, width),
            const(8, width),
            pl.BlockSpec((1, 1, bu.shape[2]), lambda j: (j, 0, 0)),
            ANY,
            ANY,
            ANY,
            ANY,
        ],
        out_specs=[
            ANY,
            ANY,
            pl.BlockSpec((SEQ, n), lambda j: (0, j)),
            pl.BlockSpec((SEQ, n), lambda j: (0, j)),
            const(SEQ, width),
            const(SEQ, width),
            const(SEQ, 128),
            const(SEQ, width),
            const(SEQ, width),
            const(8, width),
        ],
        out_shape=[
            jax.ShapeDtypeStruct(wu.shape, BF),
            jax.ShapeDtypeStruct(wd.shape, BF),
            jax.ShapeDtypeStruct((SEQ, units), BF),
            jax.ShapeDtypeStruct((SEQ, units), BF),
            jax.ShapeDtypeStruct((SEQ, width), BF),
            jax.ShapeDtypeStruct((SEQ, width), F32),
            jax.ShapeDtypeStruct((SEQ, 128), F32),
            jax.ShapeDtypeStruct((SEQ, width), BF),
            jax.ShapeDtypeStruct((SEQ, width), F32),
            jax.ShapeDtypeStruct((8, width), F32),
        ],
        input_output_aliases={7: 0, 8: 1},
        scratch_shapes=[
            pltpu.VMEM((SEQ, width), F32),
            pltpu.VMEM((2, width, n), BF),
            pltpu.VMEM((2, n, width), BF),
            pltpu.VMEM((SEQ, width), BF),
            pltpu.VMEM((SEQ - SEQ // CHUNKS, width // 4), BF),
            DMA((2, 2)),
            DMA((32,)),
            DMA((32,)),
            DMA((32,)),
            DMA((32,)),
            sems_of_exchange(),
            DMA,
        ],
        compiler_params=pltpu.CompilerParams(vmem_limit_bytes=VMEM_LIMIT, collective_id=2, has_side_effects=True),
        name="ff_fwd",
    )(x, att, wo, vec, bu, cot, cot_first, wu, wd)


ORDER = (7, 6, 1, 3, 5, 0, 2, 4)
PAIRS = (7, 6, 3, 2, 5, 4, 1, 0)


def slot_at(j):
    return jnp.where(j < 2, 7 - j, jnp.where(j < 5, 2 * j - 3, 2 * j - 10))


def pair_at(j):
    return jnp.where(j < 2, 7 - j, jnp.where(j < 4, 5 - j, jnp.where(j < 6, 9 - j, 7 - j)))


def sum_rows(dst, *srcs):
    n = dst.shape[0]
    step = min(n, 64)

    def run(i, carry):
        rows = pl.ds(pl.multiple_of(i * step, step), step)
        total = srcs[0][rows, :].astype(F32)
        for src in srcs[1:]:
            total += src[rows, :].astype(F32)
        dst[rows, :] = total.astype(BF)
        return carry

    lax.fori_loop(0, n // step, run, 0)


class Fold:
    @staticmethod
    def scratch(a, b):
        return [
            pltpu.VMEM((2, a, b), BF),
            pltpu.VMEM((4, a, b), BF),
            pltpu.VMEM((a, b), BF),
            pltpu.VMEM((2, a // 2, b), BF),
            DMA((12,)),
        ]

    def __init__(self, peers, order, stage, land, corner, land_corner, sems):
        self.peers, self.order, self.stage, self.land, self.corner, self.land_corner, self.sems = (
            peers, order, stage, land, corner, land_corner, sems,
        )
        self.half = corner.shape[0] // 2

    def to_core(self, p):
        k = (self.order[p] - 1) // 2
        return send(self.peers, "core", self.stage.at[p % 2], self.land.at[k], self.sems.at[4 + k], self.sems.at[k])

    def to_side(self, h):
        src = self.corner.at[pl.ds(h * self.half, self.half), :]
        return send(self.peers, "xy"[1 - h], src, self.land_corner.at[h], self.sems.at[10 + h], self.sems.at[8 + h])

    def before(self, j):
        for p in range(2, 8):
            if self.order[p - 2] % 2 == 0:
                continue

            @pl.when(j == p)
            def _(p=p):
                self.to_core(p - 2).wait_send()

    def from_core(self, t):
        k = t // 2
        self.to_core(self.order.index(t + 1)).wait_recv()
        return self.land.at[k]

    def after(self, j, outs):
        for p, t in enumerate(self.order):
            @pl.when(j == p)
            def _(p=p, t=t):
                mine = self.stage.at[p % 2]
                if t % 2 == 1:
                    self.to_core(p).start()
                    return
                theirs = self.from_core(t)
                if t == 6:
                    sum_rows(self.corner, mine, theirs)
                    self.to_side(0).start()
                    self.to_side(1).start()
                    return
                out = outs[t]
                if t == 0:
                    sum_rows(out, mine, theirs)
                    return
                h = t // 2 - 1
                self.to_side(h).wait_recv()
                for q in range(2):
                    rows = pl.ds(q * self.half, self.half)
                    more = (self.land_corner.at[h],) if q == h else ()
                    sum_rows(out.at[rows, :], mine.at[rows, :], theirs.at[rows, :], *more)

    def finish(self):
        for p in (6, 7):
            if self.order[p] % 2:
                self.to_core(p).wait_send()
        self.to_side(0).wait_send()
        self.to_side(1).wait_send()


class Cross:
    def __init__(self, peers, for_x, for_y, land_x, land_y, sems, cuts=1):
        self.peers, self.sems, self.cuts = peers, sems, cuts
        self.ends = {"x": (for_x, land_x), "y": (for_y, land_y)}
        self.n = land_x.shape[0] // cuts

    def copy(self, way, h=0):
        src, dst = self.ends[way]
        rows = pl.ds(h * self.n, self.n)
        at = 4 * h + 2 * "xy".index(way)
        return send(self.peers, way, src.at[rows, :], dst.at[rows, :], self.sems.at[at], self.sems.at[at + 1])

    def start(self, ways="xy", h=0):
        for way in ways:
            self.copy(way, h).start()

    def finish(self, own, out):
        for h in range(self.cuts):
            for way in "xy":
                self.copy(way, h).wait()
        sum_rows(out, own, self.ends["x"][1], self.ends["y"][1])


class Whole:
    @staticmethod
    def scratch(a, b):
        return [
            pltpu.VMEM((8 * a, b), BF),
            pltpu.VMEM((4, a, b), BF),
            pltpu.VMEM((4, a, b), BF),
            pltpu.VMEM((2, a // 2, b), BF),
            pltpu.VMEM((a, b), BF),
            pltpu.VMEM((a, b), BF),
            DMA((12,)),
            DMA((4,)),
        ]

    def __init__(self, peers, total, land, kept, land_corner, land_x, land_y, sems, c_sems):
        self.peers, self.total, self.land, self.kept, self.land_corner, self.sems = (
            peers, total, land, kept, land_corner, sems,
        )
        self.a = land.shape[1]
        self.half = self.a // 2
        self.cross = Cross(peers, kept.at[1], kept.at[2], land_x, land_y, c_sems)

    def block(self, t):
        return self.total.at[pl.ds(t * self.a, self.a), :]

    def to_core(self, k):
        return send(
            self.peers, "core", self.block(2 * k + 1), self.land.at[k], self.sems.at[4 + k], self.sems.at[k]
        )

    def to_side(self, h):
        src = self.kept.at[3, pl.ds(h * self.half, self.half), :]
        return send(self.peers, "xy"[1 - h], src, self.land_corner.at[h], self.sems.at[10 + h], self.sems.at[8 + h])

    def start(self):
        for k in (3, 1, 2, 0):
            self.to_core(k).start()

    def corner(self):
        for k in (3, 1, 2, 0):
            self.to_core(k).wait_recv()
            sum_rows(self.kept.at[k], self.block(2 * k), self.land.at[k])
            if k == 3:
                self.to_side(0).start()
                self.to_side(1).start()

    def sides(self):
        for h in range(2):
            self.to_side(h).wait_recv()
            rows = pl.ds(h * self.half, self.half)
            mine = self.kept.at[1 + h, rows, :]
            sum_rows(mine, mine, self.land_corner.at[h])
        self.cross.start()

    def finish(self, out):
        self.cross.finish(self.kept.at[0], out)
        for k in range(4):
            self.to_core(k).wait_send()
        for h in range(2):
            self.to_side(h).wait_send()


class Deal:
    def __init__(self, peers, total, by_rows, land, sems):
        self.peers, self.total, self.by_rows, self.land, self.sems = peers, total, by_rows, land, sems

    def part(self, s):
        n = self.total.shape[0 if self.by_rows else 1] // 4
        return self.total.at[pl.ds(s * n, n), :] if self.by_rows else self.total.at[:, pl.ds(s * n, n)]

    def copy(self, s):
        return send(self.peers, 4 - s, self.part(s), self.land.at[s - 1], self.sems.at[2 + s], self.sems.at[s - 1])

    def start(self):
        for s in (2, 1, 3):
            self.copy(s).start()

    def finish(self, out):
        for s in (1, 2, 3):
            self.copy(s).wait()
        sum_rows(out, self.part(0), self.land.at[0], self.land.at[1], self.land.at[2])


class LineDeal:
    def __init__(self, peers, total, by_rows, land, tmp, sems):
        self.peers, self.land, self.tmp, self.sems = peers, land, tmp, sems
        self.part = Deal(peers, total, by_rows, None, None).part

    def copy(self, up, b, row, src):
        go = (b - row if up else row - b) - 1
        at = (0 if up else 3) + go
        return send(
            self.peers, 1 if up else 3, src, self.land.at[0 if up else 1, go], self.sems.at[at], self.sems.at[6 + at]
        )

    def slot(self, b, row):
        return (row - b) % 4

    def first(self, up, b, row):
        return self.copy(up, b, row, self.part(self.slot(b, row)))

    def pass_on(self, up, b, row):
        go = (b - row if up else row - b) - 1
        tmp = self.tmp.at[0 if up else 1, go]
        return self.copy(up, b, row, tmp), tmp

    def got(self, up, b, row):
        go = b - row if up else row - b
        at = (0 if up else 3) + go
        land = self.land.at[0 if up else 1, go]
        send(self.peers, 1 if up else 3, land, land, self.sems.at[at], self.sems.at[6 + at]).wait_recv()
        return land

    STEPS = (((1, True, 3), (1, True, 2), (2, False, 0), (2, False, 1)), ((2, True, 3), (1, False, 0)))
    STARTS = ((0, True, 3), (0, True, 2), (0, True, 1), (3, False, 0), (3, False, 1), (3, False, 2))

    def when(self, row, run):
        pl.when(self.peers.r == row)(run)

    def start(self):
        for row, up, b in self.STARTS:
            self.when(row, lambda up=up, b=b, row=row: self.first(up, b, row).start())

    def step(self, k):
        for row, up, b in self.STEPS[k]:
            def run(row=row, up=up, b=b):
                land = self.got(up, b, row)
                copy, tmp = self.pass_on(up, b, row)
                sum_rows(tmp, land, self.part(self.slot(b, row)))
                copy.start()

            self.when(row, run)

    def finish(self, out):
        for row in range(4):
            def run(row=row):
                lands = []
                if row > 0:
                    lands.append(self.got(True, row, row))
                if row < 3:
                    lands.append(self.got(False, row, row))
                sum_rows(out, self.part(0), *lands)

            self.when(row, run)
        for row, up, b in self.STARTS:
            self.when(row, lambda up=up, b=b, row=row: self.first(up, b, row).wait_send())
        for moves in self.STEPS:
            for row, up, b in moves:
                self.when(row, lambda up=up, b=b, row=row: self.pass_on(up, b, row)[0].wait_send())


class Spread:
    def __init__(self, peers, own, place, sems):
        d = lax.axis_index("dp")
        self.peers, self.own, self.sems, self.here = peers, own, sems, place(d)
        self.from_x = place(lax.rem(d + 2, 4))

    def local(self):
        return pltpu.make_async_copy(self.own, self.here, self.sems.at[6])

    def copies(self):
        s = self.sems
        return (
            send(self.peers, "x", self.own, self.here, s.at[0], s.at[1]),
            send(self.peers, "core", self.own, self.here, s.at[2], s.at[3]),
            send(self.peers, "core", self.from_x, self.from_x, s.at[4], s.at[5]),
        )

    def start(self):
        to_x, to_core, _ = self.copies()
        to_x.start()
        to_core.start()
        self.local().start()

    def relay(self):
        to_x, _, on = self.copies()
        to_x.wait_recv()
        on.start()

    def finish(self):
        to_x, to_core, on = self.copies()
        to_x.wait_send()
        to_core.wait()
        on.wait()
        self.local().wait()


class Outward:
    def __init__(self, peers, rows, block, buf, sems, parts=(2, 1, 3, 0)):
        self.peers, self.rows, self.block, self.buf, self.sems = peers, rows, block, buf, sems
        self.away = [s for s in parts if s]
        self.stays = 0 in parts
        self.n = SEQ // CHUNKS

    def ends(self, s, first, count):
        f = self.block.shape[1]
        mine = pl.ds(pl.multiple_of(self.peers.r * SEQ + first * self.n, self.n), count * self.n)
        return self.rows.at[pl.ds(first * self.n, count * self.n), pl.ds(s * f, f)], self.block.at[mine, :]

    def copy(self, s, k):
        return send(self.peers, 4 - s, *self.ends(s, k, 1), self.sems.at[0, s, k], self.sems.at[1, s, k])

    def load(self):
        return pltpu.make_async_copy(self.ends(0, 0, CHUNKS)[0], self.buf, self.sems.at[0, 0, 0])

    def store(self):
        src, dst = self.ends(0, 0, CHUNKS)
        return pltpu.make_async_copy(src if self.buf is None else self.buf, dst, self.sems.at[1, 0, 0])

    def start(self, *chunks):
        for k in chunks:
            for s in self.away:
                self.copy(s, k).start()

    def settle(self):
        self.load().wait()
        self.store().start()

    def finish(self):
        if self.stays:
            self.store().wait()
        for k in range(CHUNKS):
            for s in self.away:
                self.copy(s, k).wait()


def ff_down_bwd_kernel(
    r2_ref, wd_ref, act_ref, slope_ref, out, out_block, gp_ref, bu_ref, kept_ref,
    gfed, out_own, stage, land, corner, land_corner, f_sems, o_sems,
):
    j = pl.program_id(0)
    peers = Peers()
    outward = Outward(peers, out, out_block, out_own, o_sems, (2, 0))
    fold = Fold(peers, ORDER, stage, land, corner, land_corner, f_sems)

    @pl.when(j == 0)
    def _():
        peers.hello(ALL_PEERS)
        outward.load().start()

        def body(rows):
            gfed[rows, :] = r2_ref[rows, :].astype(BF)

        row_blocks(body)
        peers.meet(ALL_PEERS)
        outward.start(*range(CHUNKS))

    bsum = jnp.zeros((1, bu_ref.shape[2]), F32)
    for i in range(SEQ // 256):
        rows = slice(i * 256, (i + 1) * 256)
        g = (mm_t(gfed[rows, :], wd_ref[...]) * slope_ref[rows, :].astype(F32)).astype(BF)
        gp_ref[rows, :] = g
        bsum += jnp.sum(g.astype(F32), axis=0, keepdims=True)
    bu_ref[0] = bsum
    fold.before(j)
    stage[lax.rem(j, 2)] = tmm(act_ref[...], gfed[...]).astype(BF)
    fold.after(j, {t: kept_ref.at[0] for t in (0, 2, 4)})

    @pl.when(j == 1)
    def _():
        outward.settle()

    @pl.when(j == 7)
    def _():
        fold.finish()
        outward.finish()


def kept_spec(a, b):
    return pl.BlockSpec((1, a, b), lambda j: (jnp.maximum(j - 5, 0), 0, 0))


def ff_down_bwd(r2, wd, act, slope, out):
    units, width = wd.shape
    n = units // 8
    return pl.pallas_call(
        ff_down_bwd_kernel,
        grid=(8,),
        in_specs=[
            const(SEQ, width),
            pl.BlockSpec((n, width), lambda j: (slot_at(j), 0)),
            pl.BlockSpec((SEQ, n), lambda j: (0, slot_at(j))),
            pl.BlockSpec((SEQ, n), lambda j: (0, slot_at(j))),
            ANY,
        ],
        out_specs=[
            ANY,
            pl.BlockSpec((SEQ, n), lambda j: (0, slot_at(j))),
            pl.BlockSpec((1, 1, n), lambda j: (slot_at(j), 0, 0)),
            kept_spec(n, width),
        ],
        out_shape=[
            jax.ShapeDtypeStruct((4 * SEQ, width // 4), BF),
            jax.ShapeDtypeStruct((SEQ, units), BF),
            jax.ShapeDtypeStruct((8, 1, n), F32),
            jax.ShapeDtypeStruct((3, n, width), BF),
        ],
        scratch_shapes=[
            pltpu.VMEM((SEQ, width), BF),
            pltpu.VMEM((SEQ, width // 4), BF),
            *Fold.scratch(n, width),
            sems_of_exchange(),
        ],
        compiler_params=pltpu.CompilerParams(vmem_limit_bytes=VMEM_LIMIT, collective_id=3, has_side_effects=True),
        name="ff_down_bwd",
    )(r2, wd, act, slope, out)


def ff_up_bwd_kernel(
    r2_ref, hlow_ref, gp_ref, wu_ref, normed1_ref, inv1_ref, vec_ref, out, out_block_in, kept_d,
    out_block, r1_ref, gattn_ref, vg_ref, kept_ref, own_ref,
    hlow_t, stage, land, corner, land_corner, f_sems, own_d, land_x, land_y, c_sems, o_sems,
):
    j = pl.program_id(0)
    peers = Peers()
    outward = Outward(peers, out, out_block, None, o_sems, (1, 3))
    fold = Fold(peers, ORDER, stage, land, corner, land_corner, f_sems)
    cross = Cross(peers, kept_d.at[1], kept_d.at[2], land_x, land_y, c_sems, 2)
    load = pltpu.make_async_copy(kept_d.at[0], own_d, c_sems.at[8])

    @pl.when(j == 0)
    def _():
        peers.hello(ALL_PEERS)
        load.start()
        r1_ref[...] = r2_ref[...]
        for i in range(SEQ // 256):
            rows = slice(i * 256, (i + 1) * 256)
            hlow_t[:, rows] = jnp.transpose(hlow_ref[rows, :])
        peers.meet(ALL_PEERS)
        cross.start()
        outward.start(*range(CHUNKS))

    fold.before(j)
    stage[lax.rem(j, 2)] = mm(hlow_t[...], gp_ref[...]).astype(BF)
    fold.after(j, {t: kept_ref.at[0] for t in (0, 2, 4)})

    @pl.when(j == 1)
    def _():
        cross.start(h=1)

    r1_ref[...] += mm_t(gp_ref[...], wu_ref[...])

    @pl.when(j == 7)
    def _():
        vg_ref[...] = jnp.zeros_like(vg_ref)

        def body(rows):
            gh = r1_ref[rows, :]
            normed = normed1_ref[rows, :]
            r1 = norm_rows_back(gh * vec_ref[1:2, :], normed, inv1_ref[rows, 0:1])
            r1_ref[rows, :] = r1
            low = r1.astype(BF)
            gattn_ref[rows, :] = low
            vg_ref[0:1, :] += jnp.sum(gh * normed, axis=0, keepdims=True)
            vg_ref[1:2, :] += jnp.sum(gh, axis=0, keepdims=True)
            vg_ref[2:3, :] += jnp.sum(low.astype(F32), axis=0, keepdims=True)

        row_blocks(body)
        load.wait()
        cross.finish(own_d, own_ref)
        fold.finish()
        outward.finish()


def ff_up_bwd(r2, hlow, gp, wu, normed1, inv1, vec, out, out_block, kept_d):
    width, units = wu.shape
    n = units // 8
    return pl.pallas_call(
        ff_up_bwd_kernel,
        grid=(8,),
        in_specs=[
            const(SEQ, width),
            const(SEQ, width),
            pl.BlockSpec((SEQ, n), lambda j: (0, slot_at(j))),
            pl.BlockSpec((width, n), lambda j: (0, slot_at(j))),
            const(SEQ, width),
            const(SEQ, 128),
            const(8, width),
            ANY,
            ANY,
            ANY,
        ],
        out_specs=[
            ANY,
            const(SEQ, width),
            const(SEQ, width),
            const(8, width),
            kept_spec(width, n),
            const(n, width),
        ],
        out_shape=[
            jax.ShapeDtypeStruct(out_block.shape, BF),
            jax.ShapeDtypeStruct((SEQ, width), F32),
            jax.ShapeDtypeStruct((SEQ, width), BF),
            jax.ShapeDtypeStruct((8, width), F32),
            jax.ShapeDtypeStruct((3, width, n), BF),
            jax.ShapeDtypeStruct((n, width), BF),
        ],
        input_output_aliases={8: 0},
        scratch_shapes=[
            pltpu.VMEM((width, SEQ), BF),
            *Fold.scratch(width, n),
            pltpu.VMEM((n, width), BF),
            pltpu.VMEM((n, width), BF),
            pltpu.VMEM((n, width), BF),
            DMA((9,)),
            sems_of_exchange(),
        ],
        compiler_params=pltpu.CompilerParams(vmem_limit_bytes=VMEM_LIMIT, collective_id=4, has_side_effects=True),
        name="ff_up_bwd",
    )(r2, hlow, gp, wu, normed1, inv1, vec, out, out_block, kept_d)


def attend_bwd_kernel(
    gattn_ref, wo_ref, att_ref, qkv_ref, linv_ref, p_ref, x_ref, att_all, tot_d, kept_u,
    g_ref, gsum_ref, tot_q, tot_o, down_ref, up_ref,
    x_t, ds_ref,
    q_stage, q_land, q_corner, q_land_corner, q_sems,
    q_kept, q_x, q_y, q_c, o_total, o_land, o_kept, o_land_corner, o_x, o_y, o_sems, o_c,
    zd_land, zd_sems, own_u, land_x, land_y, c_sems, tot_u, zu_land, zu_sems,
):
    j = pl.program_id(0)
    peers = Peers()
    fold_q = Fold(peers, PAIRS, q_stage, q_land, q_corner, q_land_corner, q_sems)
    whole_o = Whole(peers, o_total, o_land, o_kept, o_land_corner, o_x, o_y, o_sems, o_c)
    cross_q = Cross(peers, q_kept.at[1], q_kept.at[2], q_x, q_y, q_c)
    deal_d = Deal(peers, tot_d, False, zd_land, zd_sems)
    cross_u = Cross(peers, kept_u.at[1], kept_u.at[2], land_x, land_y, c_sems)
    deal_u = Deal(peers, tot_u, True, zu_land, zu_sems)
    load_u = pltpu.make_async_copy(kept_u.at[0], own_u, c_sems.at[4])

    @pl.when(j == 0)
    def _():
        load_u.start()
        peers.hello(ALL_PEERS)
        f = x_ref.shape[2]
        for s in range(4):
            x_t[s * f : (s + 1) * f, :] = jnp.transpose(x_ref[s])
        load_u.wait()
        peers.meet(ALL_PEERS)
        cross_u.start()
        deal_d.start()
        o_total[...] = tmm(att_all[...], gattn_ref[...]).astype(BF)
        whole_o.start()

    @pl.when(j == 1)
    def _():
        whole_o.corner()

    @pl.when(j == 3)
    def _():
        whole_o.sides()

    @pl.when(j == 6)
    def _():
        whole_o.finish(tot_o)

    @pl.when(j == 4)
    def _():
        cross_u.finish(own_u, tot_u)
        deal_u.start()
        deal_d.finish(down_ref)

    lane = lax.broadcasted_iota(jnp.int32, (SEQ, 128), 1)
    scale = HD ** (-0.5)
    fold_q.before(j)
    q = qkv_ref[:, 0:128]
    k = qkv_ref[:, 128:256]
    v = qkv_ref[:, 256:384]
    do = mm_t(gattn_ref[...], wo_ref[...]).astype(BF).astype(F32) * linv_ref[...]
    prod = do * att_ref[...].astype(F32)
    dob = do.astype(BF)
    q_t = jnp.transpose(q)
    k_t = jnp.transpose(k)
    do_t = jnp.transpose(dob)
    dq_t, dk_t, dv_t = [], [], []
    for h in range(2):
        mine = (lane < HD) if h == 0 else (lane >= HD)
        delta = jnp.sum(jnp.where(mine, prod, 0.0), axis=1, keepdims=True)
        dom = jnp.where(mine, dob, jnp.zeros_like(dob))
        for i in range(SEQ // QB):
            rows = slice(i * QB, (i + 1) * QB)
            dp = mm_t(dom[rows], v)
            ds_ref[h, rows, :] = (p_ref[h, rows, :].astype(F32) * (dp - delta[rows])).astype(BF)
        feats = slice(h * HD, (h + 1) * HD)
        dq_t.append(mm_t(k_t[feats], ds_ref[h]))
        dk_t.append(mm(q_t[feats], ds_ref[h]))
        dv_t.append(mm(do_t[feats], p_ref[h]))
    g_ref[:, 0:128] = (jnp.transpose(jnp.concatenate(dq_t, 0)) * scale).astype(BF)
    g_ref[:, 128:256] = (jnp.transpose(jnp.concatenate(dk_t, 0)) * scale).astype(BF)
    g_ref[:, 256:384] = jnp.transpose(jnp.concatenate(dv_t, 0)).astype(BF)
    gsum_ref[0] = jnp.sum(g_ref[...].astype(F32), axis=0, keepdims=True)
    q_stage[lax.rem(j, 2)] = mm(x_t[...], g_ref[...]).astype(BF)
    fold_q.after(j, {t: q_kept.at[t // 2] for t in (0, 2, 4)})

    @pl.when(j == PAIRS.index(2))
    def _():
        cross_q.start("x")

    @pl.when(j == PAIRS.index(4))
    def _():
        cross_q.start("y")

    @pl.when(j == 7)
    def _():
        deal_u.finish(up_ref)
        fold_q.finish()
        cross_q.finish(q_kept.at[0], tot_q)


def attend_bwd(gattn, wo, att, qkv, linv, p, x, tot_d, kept_u):
    width = wo.shape[1]
    heads = 128
    n = tot_d.shape[0]
    return pl.pallas_call(
        attend_bwd_kernel,
        grid=(8,),
        in_specs=[
            const(SEQ, width),
            pl.BlockSpec((heads, width), lambda j: (pair_at(j), 0)),
            pl.BlockSpec((SEQ, heads), lambda j: (0, pair_at(j))),
            pl.BlockSpec((SEQ, 3 * heads), lambda j: (0, pair_at(j))),
            pl.BlockSpec((SEQ, heads), lambda j: (0, pair_at(j))),
            pl.BlockSpec((2, SEQ, SEQ), lambda j: (pair_at(j), 0, 0)),
            const(*x.shape),
            const(SEQ, width),
            const(n, width),
            ANY,
        ],
        out_specs=[
            pl.BlockSpec((SEQ, 3 * heads), lambda j: (0, pair_at(j))),
            pl.BlockSpec((1, 1, 3 * heads), lambda j: (pair_at(j), 0, 0)),
            const(width, 3 * heads),
            const(heads, width),
            const(n, width // 4),
            const(width // 4, n),
        ],
        out_shape=[
            jax.ShapeDtypeStruct((SEQ, 24 * heads), BF),
            jax.ShapeDtypeStruct((8, 1, 3 * heads), F32),
            jax.ShapeDtypeStruct((width, 3 * heads), BF),
            jax.ShapeDtypeStruct((heads, width), BF),
            jax.ShapeDtypeStruct((n, width // 4), BF),
            jax.ShapeDtypeStruct((width // 4, n), BF),
        ],
        scratch_shapes=[
            pltpu.VMEM((width, SEQ), BF),
            pltpu.VMEM((2, SEQ, SEQ), BF),
            *Fold.scratch(width, 3 * heads),
            pltpu.VMEM((3, width, 3 * heads), BF),
            pltpu.VMEM((width, 3 * heads), BF),
            pltpu.VMEM((width, 3 * heads), BF),
            DMA((4,)),
            *Whole.scratch(heads, width),
            pltpu.VMEM((3, n, width // 4), BF),
            DMA((6,)),
            pltpu.VMEM((width, n), BF),
            pltpu.VMEM((width, n), BF),
            pltpu.VMEM((width, n), BF),
            DMA((5,)),
            pltpu.VMEM((width, n), BF),
            pltpu.VMEM((3, width // 4, n), BF),
            DMA((6,)),
        ],
        compiler_params=pltpu.CompilerParams(vmem_limit_bytes=VMEM_LIMIT, collective_id=5, has_side_effects=True),
        name="attend_bwd",
    )(gattn, wo, att, qkv, linv, p, x, att, tot_d, kept_u)


def last_kernel(
    tot_q, tot_o, own_d, own_u, g_part, u_part, vec1, vec2, g, w, r1,
    x_block, gq, go, gd, gu, slot_out, feat_ref,
    g_buf, w_buf, acc, xg, ld_sems,
    q_land, q_tmp, q_z, q_sum, o_land, o_tmp, o_z, o_sum,
    vec_ref, v1, v2, v3, l1, l2, l3, l4, v_own, v_sems, out_sems, s_sems,
):
    peers = Peers()
    outward = Outward(peers, xg, x_block, None, out_sems)
    deal_q = LineDeal(peers, tot_q, True, q_land, q_tmp, q_z)
    deal_o = LineDeal(peers, tot_o, False, o_land, o_tmp, o_z)
    loads = (
        pltpu.make_async_copy(w, w_buf, ld_sems.at[0]),
        pltpu.make_async_copy(g, g_buf, ld_sems.at[1]),
        pltpu.make_async_copy(r1, acc, ld_sems.at[2]),
    )
    peers.hello(ALL_PEERS)
    for c in loads:
        c.start()

    def products(k):
        rows = slice(k * (SEQ // CHUNKS), (k + 1) * (SEQ // CHUNKS))
        xg[rows, :] = (mm_t(g_buf[rows, :], w_buf[...]) + acc[rows, :]).astype(BF)
        outward.start(k)

    vec_ref[...] = jnp.zeros_like(vec_ref)
    heads3, units = g_part.shape[2], u_part.shape[2]
    for k, t in enumerate((0, 4, 2, 6, 1, 5, 3, 7)):
        k = k if k < 4 else k + 8
        for i in range(heads3 // 128):
            vec_ref[k, i : i + 1, :] = g_part[t, :, i * 128 : (i + 1) * 128]
        for i in range(units // 128):
            at = heads3 // 128 + i
            vec_ref[k, at : at + 1, :] = u_part[t, :, i * 128 : (i + 1) * 128]
    f = vec1.shape[1] // 4
    rows = [(vec1, 2), (vec1, 0), (vec1, 1), (vec2, 2), (vec2, 0), (vec2, 1)]
    for k in range(4):
        for v, (ref, row) in enumerate(rows):
            for i in range(f // 128):
                at = v * (f // 128) + i
                first = k * f + i * 128
                vec_ref[4 + 2 * k + at // 8, at % 8 : at % 8 + 1, :] = ref[row : row + 1, first : first + 128]

    def rows_at(ref):
        n = ref.shape[0] // 4
        return lambda q: ref.at[pl.ds(pl.multiple_of(q * n, n), n), :]

    def cols_at(ref, first, n):
        return lambda q: ref.at[:, pl.ds(pl.multiple_of(first + q * n, n), n)]

    heads = q_sum.shape[1] // 3
    units = own_u.shape[1]
    spread_d = Spread(peers, own_d, rows_at(gd), s_sems.at[0])
    spread_u = Spread(peers, own_u, cols_at(gu, 0, units), s_sems.at[1])
    spread_o = Spread(peers, o_sum, rows_at(go), s_sems.at[2])
    spread_q = [
        Spread(peers, q_sum.at[:, pl.ds(i * heads, heads)], cols_at(gq, 4 * i * heads, heads), s_sems.at[3 + i])
        for i in range(3)
    ]
    spread_v = Spread(peers, v_own, lambda q: slot_out.at[q], s_sems.at[6])

    to_core = send(peers, "core", vec_ref.at[pl.ds(4, 12)], l1, v_sems.at[0], v_sems.at[1])
    to_x = send(peers, "x", v1.at[pl.ds(2, 10)], l2, v_sems.at[2], v_sems.at[3])
    to_y = send(peers, "y", v2.at[pl.ds(1, 11)], l3, v_sems.at[4], v_sems.at[5])
    to_rows = []
    for i in (1, 2, 3):
        to_rows.append(send(peers, i, v3.at[0], l4.at[i - 1, 0], v_sems.at[6 + 4 * i], v_sems.at[7 + 4 * i]))
        src = v3.at[pl.ds(4 + 2 * (4 - i), 2)]
        to_rows.append(send(peers, i, src, l4.at[i - 1, pl.ds(1, 2)], v_sems.at[8 + 4 * i], v_sems.at[9 + 4 * i]))

    peers.meet(ALL_PEERS)
    deal_o.start()
    deal_q.start()
    to_core.start()
    spread_d.start()
    spread_u.start()
    for c in loads:
        c.wait()
    products(0)
    deal_o.step(0)
    deal_q.step(0)
    products(1)
    to_core.wait()
    v1[0:4] = vec_ref[0:4] + l1[8:12]
    v1[4:12] = vec_ref[4:12] + l1[0:8]
    to_x.start()
    deal_o.step(1)
    deal_q.step(1)
    products(2)
    products(3)
    outward.store().start()
    to_x.wait()
    v2[0:2] = v1[0:2] + l2[0:2]
    v2[4:12] = v1[4:12] + l2[2:10]
    v2[2:4] = v1[2:4]
    to_y.start()
    spread_d.relay()
    spread_u.relay()
    deal_o.finish(o_sum)
    spread_o.start()
    deal_q.finish(q_sum)
    for sp in spread_q:
        sp.start()
    to_y.wait()
    v3[0:1] = v2[0:1] + l3[0:1]
    v3[4:12] = v2[4:12] + l3[3:11]
    for c in to_rows:
        c.start()
    spread_o.relay()
    for sp in spread_q:
        sp.relay()
    for c in to_rows:
        c.wait()
    v_own[...] = v3[0] + l4[0, 0] + l4[1, 0] + l4[2, 0]
    feat_ref[...] = v3[4:6] + l4[0, 1:3] + l4[1, 1:3] + l4[2, 1:3]
    spread_v.start()
    spread_v.relay()
    for sp in (spread_d, spread_u, spread_o, spread_v, *spread_q):
        sp.finish()
    outward.finish()


def last(tot_q, tot_o, own_d, own_u, g_part, u_part, vec1, vec2, g, w, r1):
    width = r1.shape[1]
    part = width // 4
    n = own_d.shape[0]
    heads = tot_o.shape[0]
    vmem = pl.BlockSpec(memory_space=pltpu.VMEM)

    def bufs(a, b, by_rows):
        piece = (a // 4, b) if by_rows else (a, b // 4)
        return [pltpu.VMEM((2, 3, *piece), BF), pltpu.VMEM((2, 2, *piece), BF), DMA((12,)), pltpu.VMEM(piece, BF)]

    return pl.pallas_call(
        last_kernel,
        in_specs=[vmem] * 8 + [ANY] * 3,
        out_specs=[ANY, ANY, ANY, ANY, ANY, ANY, vmem],
        out_shape=[
            jax.ShapeDtypeStruct((4 * SEQ, part), BF),
            jax.ShapeDtypeStruct((part, 12 * heads), BF),
            jax.ShapeDtypeStruct((4 * heads, part), BF),
            jax.ShapeDtypeStruct((4 * n, part), BF),
            jax.ShapeDtypeStruct((part, 4 * n), BF),
            jax.ShapeDtypeStruct((4, 8, 128), F32),
            jax.ShapeDtypeStruct((2, 8, 128), F32),
        ],
        scratch_shapes=[
            pltpu.VMEM((SEQ, 24 * heads), BF),
            pltpu.VMEM((width, 24 * heads), BF),
            pltpu.VMEM((SEQ, width), F32),
            pltpu.VMEM((SEQ, width), BF),
            DMA((3,)),
            *bufs(width, 3 * heads, True),
            *bufs(heads, width, False),
            pltpu.VMEM((16, 8, 128), F32),
            pltpu.VMEM((12, 8, 128), F32),
            pltpu.VMEM((12, 8, 128), F32),
            pltpu.VMEM((12, 8, 128), F32),
            pltpu.VMEM((12, 8, 128), F32),
            pltpu.VMEM((10, 8, 128), F32),
            pltpu.VMEM((11, 8, 128), F32),
            pltpu.VMEM((3, 3, 8, 128), F32),
            pltpu.VMEM((8, 128), F32),
            DMA((24,)),
            sems_of_exchange(),
            DMA((7, 7)),
        ],
        compiler_params=pltpu.CompilerParams(vmem_limit_bytes=VMEM_LIMIT, collective_id=6, has_side_effects=True),
        name="last",
    )(tot_q, tot_o, own_d, own_u, g_part, u_part, vec1, vec2, g, w, r1)


def whole_sequences(
    tokens, segments, w_query, b_query, w_key, w_value, b_value, w_out, b_out, norm1_gain, norm1_shift,
    w_up, b_up, w_down, b_down, norm2_gain, norm2_shift, cotangent,
):
    R = lax.axis_size("row")
    feat = tokens.shape[1]
    hq = b_query.shape[0] // 4
    unit = b_up.shape[0] // 4
    vectors = (b_out, norm1_gain, norm1_shift, b_down, norm2_gain, norm2_shift, b_query, b_value, b_up)
    size = sum(v.shape[0] for v in vectors)
    first_at, packed = 0, 0.0
    for v in vectors:
        packed += jnp.pad(v.astype(F32), (first_at, size - first_at - v.shape[0]))
        first_at += v.shape[0]
    vectors = packed.reshape(1, -1)
    x, w_qkv, wo, wu, wd, feat_all, b_slot, seg = first(
        tokens,
        segments.reshape(2, 8, 128),
        (w_query, w_key, w_value, w_out, w_up, w_down),
        vectors,
    )

    qkv, att, prob, linv, wo, wu, wd, cot_first = attend_fwd(x, w_qkv, b_slot, seg, cotangent, wo, wu, wd)
    wu, wd, act, slope, hidden_low, normed1, inv1, output, grad_r2, vg2 = ff_fwd(
        x, att, wo, feat_all, b_slot, cotangent, cot_first, wu, wd
    )

    out_block, grad_pre, bu_part, kept_d = ff_down_bwd(grad_r2, wd, act, slope, output)
    out_block, grad_r1, grad_attn, vg1, kept_u, tot_d = ff_up_bwd(
        grad_r2, hidden_low, grad_pre, wu, normed1, inv1, feat_all, output, out_block, kept_d
    )
    g_qkv, g_part, tot_q, tot_o, own_d, own_u = attend_bwd(
        grad_attn, wo, att, qkv, linv, prob, x, tot_d, kept_u
    )

    x_grad_block, gq, go, gd, gu, slot_sum, own = last(
        tot_q, tot_o, own_d, own_u, g_part, bu_part, vg1, vg2, g_qkv, w_qkv, grad_r1
    )
    wq_grad, wk_grad, wv_grad = [gq[:, i * 4 * hq : (i + 1) * 4 * hq].astype(F32) for i in range(3)]
    w_out_grad, w_up_grad, w_down_grad = go.astype(F32), gu.astype(F32), gd.astype(F32)
    slot_sum = slot_sum.reshape(4, 1024)
    bq_grad = slot_sum[:, :hq].reshape(-1)
    bv_grad = slot_sum[:, 2 * hq : 3 * hq].reshape(-1)
    bu_grad = slot_sum[:, 3 * hq : 3 * hq + unit].reshape(-1)
    own = own.reshape(-1)[: 6 * feat].reshape(6, feat)
    return (
        out_block, x_grad_block, wq_grad, bq_grad, wk_grad, wv_grad, bv_grad, w_out_grad, own[0], own[1], own[2],
        w_up_grad, bu_grad, w_down_grad, own[3], own[4], own[5],
    )


def tokens_cols(source):
    return lax.all_gather(source, "col", axis=0, tiled=True)


def tokens_rows(source):
    return lax.all_gather(source, "row", axis=0, tiled=True)


def product(row_piece, weight, flipped):
    if flipped:
        return lax.dot_general(
            row_piece, weight, (((1,), (1,)), ((), ())), preferred_element_type=jnp.float32
        )
    return jnp.dot(row_piece, weight, preferred_element_type=jnp.float32)


def outer_sum(left, right):
    return lax.dot_general(
        left, right, (((0,), (0,)), ((), ())), preferred_element_type=jnp.float32
    )


def settle_rows(gathered, weight, flipped, own_rows):

    def product_term(first_row, row_count):
        return product(gathered, weight, flipped)

    return lax.psum_scatter(
        product_term(jnp.int32(0), own_rows * lax.axis_size("row")),
        "row",
        scatter_dimension=0,
        tiled=True,
    )


def settle_cols(gathered, weight, flipped, own_rows):

    def product_term(first_row, row_count):
        return product(gathered, weight, flipped)

    return lax.psum_scatter(
        product_term(jnp.int32(0), own_rows * lax.axis_size("col")),
        "col",
        scatter_dimension=0,
        tiled=True,
    )


def row_sums(first_part, second_part):
    return lax.psum((jnp.sum(first_part, axis=1), jnp.sum(second_part, axis=1)), "row")


def norm_forward(residual, norm_gain, norm_shift):
    total_sum, square_sum = row_sums(residual, residual * residual)
    row_mean = (total_sum / WIDTH)[:, None]
    variance = (square_sum / WIDTH)[:, None] - row_mean * row_mean
    inv_std = lax.rsqrt(variance + NORM_EPS)
    normed = (residual - row_mean) * inv_std
    return (normed * norm_gain + norm_shift, normed, inv_std)


def norm_backward(grad_in, normed, inv_std, norm_gain):
    grad_norm = grad_in * norm_gain
    total_sum, cross_sum = row_sums(grad_norm, grad_norm * normed)
    grad_resid = inv_std * (grad_norm - total_sum[:, None] / WIDTH - normed * cross_sum[:, None] / WIDTH)
    return (grad_resid, jnp.sum(grad_in * normed, axis=0), jnp.sum(grad_in, axis=0))


def split_heads(array, seq_count):
    return array.reshape(seq_count, SEQ, array.shape[1] // HD, HD)


def pair_scores(queries, key_heads, segment_ids):
    position = jnp.arange(SEQ)
    same_doc = (segment_ids[:, None] == segment_ids[None, :]) & (segment_ids[None, :] != 0)
    allowed = same_doc | (position[:, None] == position[None, :])
    raw_scores = jnp.einsum(
        "qhd,khd->hqk", queries, key_heads, preferred_element_type=jnp.float32
    ) * HD ** (-0.5)
    return jnp.where(allowed[None], raw_scores, -1000000000.0)


def attend_forward(source):
    queries, key_heads, values, segment_ids = source
    scores = pair_scores(queries, key_heads, segment_ids)
    top_score = jnp.max(scores, axis=2, keepdims=True)
    exp_scores = jnp.exp(scores - top_score)
    total_sum = jnp.sum(exp_scores, axis=2, keepdims=True)
    soft_low = (exp_scores / total_sum).astype(jnp.bfloat16)
    attended = jnp.einsum("hqk,khd->qhd", soft_low, values, preferred_element_type=jnp.float32)
    return (attended.astype(jnp.bfloat16), (top_score + jnp.log(total_sum))[:, :, 0])


def attend_backward(source):
    queries, key_heads, values, segment_ids, grad_out, log_total = source
    scores = pair_scores(queries, key_heads, segment_ids)
    soft_weights = jnp.exp(scores - log_total[:, :, None])
    soft_low = soft_weights.astype(jnp.bfloat16)
    grad_values = jnp.einsum("hqk,qhd->khd", soft_low, grad_out, preferred_element_type=jnp.float32)
    grad_soft = jnp.einsum("qhd,khd->hqk", grad_out, values, preferred_element_type=jnp.float32)
    grad_scores = soft_weights * (
        grad_soft - jnp.sum(soft_weights * grad_soft, axis=2, keepdims=True)
    )
    grad_scores = grad_scores.astype(jnp.bfloat16)
    scale_factor = HD ** (-0.5)
    grad_queries = (
        jnp.einsum("hqk,khd->qhd", grad_scores, key_heads, preferred_element_type=jnp.float32)
        * scale_factor
    )
    grad_keys = (
        jnp.einsum("hqk,qhd->khd", grad_scores, queries, preferred_element_type=jnp.float32)
        * scale_factor
    )
    return (
        grad_queries.astype(jnp.bfloat16),
        grad_keys.astype(jnp.bfloat16),
        grad_values.astype(jnp.bfloat16),
    )


def split_heads_plan(
    tokens,
    segments,
    w_query,
    b_query,
    w_key,
    w_value,
    b_value,
    w_out,
    b_out,
    norm1_gain,
    norm1_shift,
    w_up,
    b_up,
    w_down,
    b_down,
    norm2_gain,
    norm2_shift,
    cotangent,
):
    rows_b = tokens.shape[0]
    rows_a = segments.shape[0]
    head_cols = w_query.shape[1]
    seq_count = rows_a // SEQ
    segment_seqs = segments.reshape(seq_count, SEQ)
    gathered_x = tokens_cols(tokens)
    stacked = jnp.concatenate([w_query, w_key, w_value], axis=1)
    projected = settle_rows(gathered_x, stacked, False, rows_a)
    queries = (projected[:, :head_cols] + b_query).astype(jnp.bfloat16)
    key_heads = projected[:, head_cols : 2 * head_cols].astype(jnp.bfloat16)
    values = (projected[:, 2 * head_cols :] + b_value).astype(jnp.bfloat16)
    query_seqs = split_heads(queries, seq_count)
    key_seqs = split_heads(key_heads, seq_count)
    value_seqs = split_heads(values, seq_count)
    attended, log_total = lax.map(attend_forward, (query_seqs, key_seqs, value_seqs, segment_seqs))
    attended = attended.reshape(rows_a, head_cols)
    gathered_o = tokens_rows(attended)
    attn_out = settle_cols(gathered_o, w_out, False, rows_b) + b_out
    hidden, normed1, inv_std1 = norm_forward(
        tokens.astype(jnp.float32) + attn_out, norm1_gain, norm1_shift
    )
    hidden_low = hidden.astype(jnp.bfloat16)
    gathered_h = tokens_cols(hidden_low)
    pre_act = settle_rows(gathered_h, w_up, False, rows_a) + b_up
    active = gelu_exact(pre_act).astype(jnp.bfloat16)
    gathered_a = tokens_rows(active)
    fed = settle_cols(gathered_a, w_down, False, rows_b) + b_down
    output, normed2, inv_std2 = norm_forward(hidden + fed, norm2_gain, norm2_shift)
    grad_r2, grad_gain2, grad_shift2 = norm_backward(
        cotangent.astype(jnp.float32), normed2, inv_std2, norm2_gain
    )
    grad_fed = grad_r2.astype(jnp.bfloat16)
    gathered_f = tokens_cols(grad_fed)
    grad_w_down = outer_sum(gathered_a, gathered_f)
    grad_active = settle_rows(gathered_f, w_down, True, rows_a)
    unused_out, slope_pull = jax.vjp(gelu_exact, pre_act)
    grad_pre = slope_pull(grad_active)[0].astype(jnp.bfloat16)
    gathered_p = tokens_rows(grad_pre)
    grad_w_up = outer_sum(gathered_h, gathered_p)
    grad_from_ff = settle_cols(gathered_p, w_up, True, rows_b)
    bias_up_part = jnp.sum(grad_pre.astype(jnp.float32), axis=0)
    bias_down_part = jnp.sum(grad_fed.astype(jnp.float32), axis=0)
    grad_r1, grad_gain1, grad_shift1 = norm_backward(
        grad_from_ff + grad_r2, normed1, inv_std1, norm1_gain
    )
    grad_attn = grad_r1.astype(jnp.bfloat16)
    gathered_d = tokens_cols(grad_attn)
    grad_w_out = outer_sum(gathered_o, gathered_d)
    grad_attended = settle_rows(gathered_d, w_out, True, rows_a).astype(jnp.bfloat16)
    grad_q, grad_k, grad_v = lax.map(
        attend_backward,
        (
            query_seqs,
            key_seqs,
            value_seqs,
            segment_seqs,
            split_heads(grad_attended, seq_count),
            log_total,
        ),
    )
    grad_q = grad_q.reshape(rows_a, head_cols)
    grad_k = grad_k.reshape(rows_a, head_cols)
    grad_v = grad_v.reshape(rows_a, head_cols)
    grad_proj = jnp.concatenate([grad_q, grad_k, grad_v], axis=1)
    gathered_g = tokens_rows(grad_proj)
    grad_stacked = outer_sum(gathered_x, gathered_g)
    tokens_grad = settle_cols(gathered_g, stacked, True, rows_b) + grad_r1
    bias_q, bias_v, bias_up = lax.psum(
        (
            jnp.sum(grad_q.astype(jnp.float32), axis=0),
            jnp.sum(grad_v.astype(jnp.float32), axis=0),
            bias_up_part,
        ),
        ("dp", "row"),
    )
    bias_out, bias_down, gain_one, shift_one, gain_two, shift_two = lax.psum(
        (
            jnp.sum(grad_attn.astype(jnp.float32), axis=0),
            bias_down_part,
            grad_gain1,
            grad_shift1,
            grad_gain2,
            grad_shift2,
        ),
        ("dp", "col"),
    )
    sum_stacked, sum_out, sum_up, sum_down = (
        lax.psum(grad_stacked.astype(jnp.bfloat16), "dp").astype(jnp.float32),
        lax.psum(grad_w_out.astype(jnp.bfloat16), "dp").astype(jnp.float32),
        lax.psum(grad_w_up.astype(jnp.bfloat16), "dp").astype(jnp.float32),
        lax.psum(grad_w_down.astype(jnp.bfloat16), "dp").astype(jnp.float32),
    )
    return (
        output.astype(jnp.bfloat16),
        tokens_grad.astype(jnp.bfloat16),
        sum_stacked[:, :head_cols],
        bias_q,
        sum_stacked[:, head_cols : 2 * head_cols],
        sum_stacked[:, 2 * head_cols :],
        bias_v,
        sum_out,
        bias_out,
        gain_one,
        shift_one,
        sum_up,
        bias_up,
        sum_down,
        bias_down,
        gain_two,
        shift_two,
    )


def solution(mesh):
    dp, rows, cols = (mesh.shape[name] for name in ("dp", "row", "col"))
    whole = TOKENS // SEQ == dp * rows * cols and dp == 4 and cols == 2
    plan = whole_sequences if whole else split_heads_plan
    placed = (
        P(("dp", "col"), "row"),
        P(("dp", "row")),
        P("row", "col"),
        P("col"),
        P("row", "col"),
        P("row", "col"),
        P("col"),
        P("col", "row"),
        P("row"),
        P("row"),
        P("row"),
        P("row", "col"),
        P("col"),
        P("col", "row"),
        P("row"),
        P("row"),
        P("row"),
        P(("dp", "col"), "row"),
    )
    return jax.shard_map(
        plan,
        mesh=mesh,
        in_specs=placed,
        out_specs=(
            P(("dp", "col"), "row"),
            P(("dp", "col"), "row"),
            P("row", "col"),
            P("col"),
            P("row", "col"),
            P("row", "col"),
            P("col"),
            P("col", "row"),
            P("row"),
            P("row"),
            P("row"),
            P("row", "col"),
            P("col"),
            P("col", "row"),
            P("row"),
            P("row"),
            P("row"),
        ),
        check_vma=False,
    )
```

```python
import math

import jax
import jax.numpy as jnp
from jax import lax
from jax.experimental import pallas as pl
from jax.experimental.pallas import tpu as pltpu
from jax.sharding import PartitionSpec as P

HD = 64
SEQ = 1024
WIDTH = 1024
TOKENS = 32768
NORM_EPS = 1e-05
BF = jnp.bfloat16
F32 = jnp.float32
NEG = -1e30
QB = 256
VMEM_LIMIT = 56 * 1024 * 1024
MESH = pl.DeviceIdType.MESH
ANY = pl.BlockSpec(memory_space=pl.ANY)
DMA = pltpu.SemaphoreType.DMA
ONCE = pl.Buffered(1)


def const(*shape):
    return pl.BlockSpec(shape, lambda j: (0,) * len(shape), pipeline_mode=ONCE)


def mm(a, b):
    return jnp.dot(a, b, preferred_element_type=F32)


def mm_t(a, b):
    return lax.dot_general(a, b, (((1,), (1,)), ((), ())), preferred_element_type=F32)


def tmm(a, b):
    return lax.dot_general(a, b, (((0,), (0,)), ((), ())), preferred_element_type=F32)


def gelu_exact(v):
    return jax.nn.gelu(v, approximate=False)


def attend_rows(qkv_ref, seg_col_ref, seg_row, o_ref, p_ref, linv_ref):
    lane = lax.broadcasted_iota(jnp.int32, (QB, 128), 1)
    scale = HD ** (-0.5) * math.log2(math.e)
    k = qkv_ref[:, 128:256]
    v = qkv_ref[:, 256:384]
    units = [(i, h) for i in range(SEQ // QB) for h in range(2)]

    def scores(i, h):
        q = qkv_ref[i * QB : (i + 1) * QB, 0:128]
        mine = (lane < HD) if h == 0 else (lane >= HD)
        return mm_t(jnp.where(mine, q, jnp.zeros_like(q)), k)

    ahead = scores(*units[0])
    outs = []
    for at, (i, h) in enumerate(units):
        rows = slice(i * QB, (i + 1) * QB)
        s = ahead
        if at + 1 < len(units):
            ahead = scores(*units[at + 1])
        s = jnp.where(seg_col_ref[rows, 0:1] == seg_row, s * scale, NEG)
        top = jnp.max(s, axis=1, keepdims=True)
        p = jnp.exp2(s - top)
        total = jnp.sum(p, axis=1, keepdims=True)
        pb = p.astype(BF)
        p_ref[h, rows, :] = pb
        inv = 1.0 / total
        outs.append((mm(pb, v) * inv, jnp.broadcast_to(inv, (QB, 128))))
        if h == 1:
            o_ref[rows, :] = jnp.where(lane < HD, outs[0][0], outs[1][0]).astype(BF)
            linv_ref[rows, :] = jnp.where(lane < HD, outs[0][1], outs[1][1])
            outs = []


def attend_fwd_kernel(
    x_ref, w_ref, b_ref, seg_ref, cot, wo_in, wu_in, wd_in,
    qkv_ref, o_ref, p_ref, linv_ref, x_t, wo, wu, wd, cot_first,
    x_buf, seg_col_ref, seg_row_ref, cot_own, i_sems, o_recv, o_sent, u_recv, u_sent, d_recv, d_sent,
):
    j = pl.program_id(0)
    peers = Peers()
    go = Gather(peers, None, wo, False, o_recv, o_sent, RING + LATER_NEAR + FAR)
    gu = Gather(peers, None, wu, True, u_recv, u_sent, RING + LATER_NEAR + far_edges(0))
    gd = Gather(peers, None, wd, False, d_recv, d_sent, RING + DOWN_NEAR + far_edges(0, 1))
    every = (go, gu, gd)
    inward = Inward(peers, cot, cot_first, cot_own, i_sems, (0,))

    plan = {
        2: ((go, (1, 0)), (gu, (1, 0)), (gu, (0, 6)), (gd, (0, 6))),
        3: ((gd, (1, 0)), (go, (1, 2), (1, 4), (2, 0))),
        4: ((gu, (1, 2), (1, 4), (2, 0)), (go, (0, 6), (1, 6))),
        5: ((gd, (1, 2), (1, 4), (2, 0)), (go, (2, 2), (2, 4), (3, 0))),
        6: ((gu, (2, 2), (2, 4)), (gu, (3, 0))),
        7: ((gd, (2, 2), (2, 4)), (go, (2, 6), (3, 2), (3, 4))),
        8: ((gd, (3, 0)), (gu, (3, 2), (3, 4)), (go, (3, 6))),
    }

    def relay(step):
        for g, *blocks in plan[step]:
            g.relay(*blocks)

    @pl.when(j == 0)
    def _():
        peers.hello(ALL_PEERS)
        inward.load()
        f = x_ref.shape[2]
        for s in range(4):
            x_buf[:, s * f : (s + 1) * f] = x_ref[s]
        tile = seg_ref[4 * peers.c + peers.r]
        for i in range(8):
            row = tile[i : i + 1, :]
            at = lax.broadcasted_iota(jnp.int32, (1, 128), 1) + i * 128
            row = jnp.where(row == 0, -1 - at, row)
            seg_row_ref[:, i * 128 : (i + 1) * 128] = row
            seg_col_ref[i * 128 : (i + 1) * 128, :] = jnp.transpose(jnp.broadcast_to(row, (128, 128)))

    qkv_ref[...] = (mm(x_buf[...], w_ref[...]) + b_ref[0, :, 0:384]).astype(BF)
    @pl.when(j == 0)
    def _():
        peers.meet(ALL_PEERS)
        for g in every:
            g.emit(0, 0)
        go.emit(0, 2)
        gu.emit(0, 2)
        gd.emit(0, 4)

    for at in range(2, 8):
        @pl.when(j == at)
        def _(at=at):
            relay(at)
            if at == 5:
                inward.settle()
                inward.start(0)

    seg_row = seg_row_ref[...]
    attend_rows(qkv_ref, seg_col_ref, seg_row, o_ref, p_ref, linv_ref)

    @pl.when(j == 7)
    def _():
        f = x_ref.shape[2]
        for s in range(4):
            x_t[s * f : (s + 1) * f, :] = jnp.transpose(x_ref[s])
        relay(8)
        for g in every:
            g.finish()
        inward.finish()


def attend_fwd(x, w_qkv, b_slot, seg, cot, wo, wu, wd):
    slots = w_qkv.shape[1] // 384
    return pl.pallas_call(
        attend_fwd_kernel,
        grid=(slots,),
        in_specs=[
            const(*x.shape),
            pl.BlockSpec((w_qkv.shape[0], 384), lambda j: (0, j)),
            pl.BlockSpec((1, 1, b_slot.shape[2]), lambda j: (j, 0, 0)),
            const(8, 8, 128),
            ANY,
            ANY,
            ANY,
            ANY,
        ],
        out_specs=[
            pl.BlockSpec((SEQ, 384), lambda j: (0, j)),
            pl.BlockSpec((SEQ, 128), lambda j: (0, j)),
            pl.BlockSpec((2, SEQ, SEQ), lambda j: (j, 0, 0)),
            pl.BlockSpec((SEQ, 128), lambda j: (0, j)),
            const(w_qkv.shape[0], SEQ),
            ANY,
            ANY,
            ANY,
            ANY,
        ],
        out_shape=[
            jax.ShapeDtypeStruct((SEQ, slots * 384), BF),
            jax.ShapeDtypeStruct((SEQ, slots * 128), BF),
            jax.ShapeDtypeStruct((slots * 2, SEQ, SEQ), BF),
            jax.ShapeDtypeStruct((SEQ, slots * 128), F32),
            jax.ShapeDtypeStruct((w_qkv.shape[0], SEQ), BF),
            jax.ShapeDtypeStruct(wo.shape, BF),
            jax.ShapeDtypeStruct(wu.shape, BF),
            jax.ShapeDtypeStruct(wd.shape, BF),
            jax.ShapeDtypeStruct((SEQ // CHUNKS, w_qkv.shape[0]), BF),
        ],
        input_output_aliases={5: 5, 6: 6, 7: 7},
        scratch_shapes=[
            pltpu.VMEM((SEQ, w_qkv.shape[0]), BF),
            pltpu.VMEM((SEQ, 128), jnp.int32),
            pltpu.VMEM((1, SEQ), jnp.int32),
            pltpu.VMEM((SEQ // CHUNKS, cot.shape[1]), BF),
            sems_of_exchange(),
            *[DMA((32,))] * 6,
        ],
        compiler_params=pltpu.CompilerParams(vmem_limit_bytes=VMEM_LIMIT, collective_id=1, has_side_effects=True),
        name="attend_fwd",
    )(x, w_qkv, b_slot, seg, cot, wo, wu, wd)


class Peers:
    def __init__(self):
        self.r = lax.axis_index("row")
        self.c = lax.axis_index("col")
        self.d = d = lax.axis_index("dp")
        self.ids = {
            "core": {"dp": d + 1 - 2 * lax.rem(d, 2)},
            "x": {"dp": lax.rem(d + 2, 4)},
            "y": {"col": 1 - self.c},
            1: {"row": lax.rem(self.r + 1, 4)},
            2: {"row": lax.rem(self.r + 2, 4)},
            3: {"row": lax.rem(self.r + 3, 4)},
        }

    def hello(self, names):
        barrier = pltpu.get_barrier_semaphore()
        for name in names:
            pl.semaphore_signal(barrier, inc=1, device_id=self.ids[name], device_id_type=MESH)

    def meet(self, names):
        pl.semaphore_wait(pltpu.get_barrier_semaphore(), len(names))


def send(peers, name, src, dst, send_sem, recv_sem):
    return pltpu.make_async_remote_copy(
        src_ref=src, dst_ref=dst, send_sem=send_sem, recv_sem=recv_sem, device_id=peers.ids[name], device_id_type=MESH
    )


def near_edges(s):
    return [("x", s, 0, s, 2), ("y", s, 0, s, 4), ("core", s, 0, s, 1)]


def second_edges(s):
    return [("core", s, 2, s, 3), ("core", s, 4, s, 5)]


def far_edges(s, flip=0):
    return [("y", s, 2, s, 6) if (s + flip) % 2 == 0 else ("x", s, 4, s, 6), ("core", s, 6, s, 7)]


def emit_far(gather, s, flip=0):
    gather.emit(s, 2 if (s + flip) % 2 == 0 else 4)


RING = [(1, s, 0, s + 1, 0) for s in range(3)]
NEAR = [e for s in range(4) for e in near_edges(s) + second_edges(s)]
FAR = [e for s in range(4) for e in far_edges(s)]
OWN_BLOCK = near_edges(0) + second_edges(0)
LATER_NEAR = [e for e in NEAR if e[1] > 0]
UP_FAR = [e for s in (1, 2, 3) for e in far_edges(s)]
DOWN_FAR = [e for s in (1, 2, 3) for e in far_edges(s, 1)]
DOWN_NEAR = [e for e in LATER_NEAR if e[1] < 3] + [("core", 3, 0, 3, 1)]
DOWN_REST = [e for e in near_edges(3) if e[0] != "core"] + second_edges(3) + DOWN_FAR


class Gather:
    def __init__(self, peers, piece, full, by_rows, recv, sent, edges):
        self.peers, self.piece, self.full, self.recv, self.sent = peers, piece, full, recv, sent
        self.by_rows = by_rows
        self.n = full.shape[1 if by_rows else 0] // 8
        self.m = full.shape[0 if by_rows else 1] // 4
        self.edges = edges
        self.waited = set()
        self.emitted = set()

    def blk(self, s, t):
        a = pl.ds(s * self.m, self.m)
        b = pl.ds(t * self.n, self.n)
        return self.full.at[a, b] if self.by_rows else self.full.at[b, a]

    def copy(self, at):
        name, s, t, s2, t2 = self.edges[at]
        src = self.piece if (s, t) == (0, 0) and self.piece is not None else self.blk(s, t)
        return send(self.peers, name, src, self.blk(s2, t2), self.sent.at[at], self.recv.at[at])

    def emit(self, s, t):
        for at, e in enumerate(self.edges):
            if e[1:3] == (s, t):
                assert at not in self.emitted
                self.emitted.add(at)
                self.copy(at).start()

    def emit_own_slot(self, s):
        for at, e in enumerate(self.edges):
            if e[1:3] == (s, 0):
                self.emitted.add(at)
                self.copy(at).start()

    def arrived(self, s, t):
        for at, e in enumerate(self.edges):
            if e[3:5] == (s, t) and at not in self.waited:
                self.waited.add(at)
                self.copy(at).wait_recv()

    def relay(self, *blocks):
        for s, t in blocks:
            self.arrived(s, t)
            self.emit(s, t)

    def own(self):
        return pltpu.make_async_copy(self.piece, self.blk(0, 0), self.sent.at[len(self.edges)])

    def start(self):
        self.emit(0, 0)
        self.own().start()

    def finish(self):
        if self.piece is not None:
            self.own().wait()
        for at, e in enumerate(self.edges):
            if at not in self.waited:
                self.waited.add(at)
                self.copy(at).wait_recv()
        assert len(self.emitted) == len(self.edges)
        for at in range(len(self.edges)):
            self.copy(at).wait_send()


class Line:
    WAVES = ((3, 2, 1), (1, 3, 2), (1, 3, 2), (1, 2, 3))

    def __init__(self, peers, gather, sems):
        self.peers, self.gather, self.sems = peers, gather, sems

    def copy(self, up, s):
        s2 = s + 1 if up else (s - 1 if s else 3)
        g = self.gather
        src = g.piece if s == 0 else g.blk(s, 0)
        return send(
            self.peers, 1 if up else 3, src, g.blk(s2, 0), self.sems.at[(0 if up else 4) + s], self.sems.at[7 + s2]
        )

    def each(self, what):
        r = self.peers.r
        for s in range(3):
            @pl.when((r >= s) & (r < 3))
            def _(s=s):
                what(self.copy(True, s))
        for s in (0, 3, 2):
            @pl.when((r > 0) & (r <= (3 if s == 0 else s - 1)))
            def _(s=s):
                what(self.copy(False, s))

    def start(self):
        r = self.peers.r

        @pl.when(r < 3)
        def _():
            self.copy(True, 0).start()

        @pl.when(r > 0)
        def _():
            self.copy(False, 0).start()

    def wave(self, k):
        for row, order in enumerate(self.WAVES):
            s = order[k]

            @pl.when(self.peers.r == row)
            def _(row=row, s=s):
                self.copy(True, s - 1).wait_recv()
                below = row >= s
                if below and row < 3:
                    self.copy(True, s).start()
                if not below and row > 0:
                    self.copy(False, s).start()
                self.gather.emit_own_slot(s)

    def finish(self):
        self.each(lambda c: c.wait_send())


CHUNKS = 4
FINE = 8


def sems_of_exchange(cuts=CHUNKS):
    return DMA((2, 4, cuts))


class Inward:
    def __init__(self, peers, block, rows, buf, sems, chunks=range(CHUNKS), cuts=CHUNKS):
        self.peers, self.block, self.rows, self.buf, self.sems, self.chunks = peers, block, rows, buf, sems, chunks
        self.n = SEQ // cuts

    def ends(self, s, first, count):
        r = lax.rem(self.peers.r + s, 4)
        f = self.block.shape[1]
        src = self.block.at[pl.ds(pl.multiple_of(r * SEQ + first * self.n, self.n), count * self.n), :]
        at = first if self.rows.shape[-2] == SEQ else first - self.chunks[0]
        rows = pl.ds(at * self.n, count * self.n)
        return src, self.rows.at[s, rows, :] if len(self.rows.shape) == 3 else self.rows.at[rows, pl.ds(s * f, f)]

    def copy(self, s, k):
        return send(self.peers, s, *self.ends(s, k, 1), self.sems.at[0, s, k], self.sems.at[1, s, k])

    def own(self):
        src, dst = self.ends(0, self.chunks[0], len(self.chunks))
        return (
            pltpu.make_async_copy(src, self.buf, self.sems.at[0, 0, 0]),
            pltpu.make_async_copy(self.buf, dst, self.sems.at[1, 0, 0]),
        )

    def start(self, *chunks):
        for k in chunks:
            for s in (2, 1, 3):
                self.copy(s, k).start()

    def load(self):
        self.own()[0].start()

    def settle(self):
        self.own()[0].wait()
        self.own()[1].start()

    def finish(self):
        self.own()[1].wait()
        for k in self.chunks:
            for s in (1, 2, 3):
                self.copy(s, k).wait()


ALL_PEERS = ("core", "x", "y", 1, 2, 3)


def first_kernel(
    tokens, segments, w_query, w_key, w_value, w_out, w_up, w_down,
    vectors,
    x, w, wo, wu, wd, feat_out, slot_out, seg_out,
    pq, po, pu, pd, rows_buf, feat, slot, l_sems, q_recv, q_sent, o_recv, o_sent, u_recv, u_sent, d_recv, d_sent,
    i_sems, v_sems, z_sems,
):
    peers = Peers()
    r, d = peers.r, peers.d

    def own_cols(ref):
        n = ref.shape[1] // 4
        return ref.at[:, pl.ds(pl.multiple_of(d * n, n), n)]

    def own_rows(ref):
        n = ref.shape[0] // 4
        return ref.at[pl.ds(pl.multiple_of(d * n, n), n), :]

    peers.hello(ALL_PEERS)
    heads = w_query.shape[1] // 4
    loads = [
        pltpu.make_async_copy(own_cols(ref), pq.at[:, pl.ds(i * heads, heads)], l_sems.at[i])
        for i, ref in enumerate((w_query, w_key, w_value))
    ]
    loads += [
        pltpu.make_async_copy(own_rows(w_out), po, l_sems.at[3]),
        pltpu.make_async_copy(own_cols(w_up), pu, l_sems.at[4]),
        pltpu.make_async_copy(own_rows(w_down), pd, l_sems.at[5]),
    ]
    for c in loads:
        c.start()
    feat[...] = jnp.zeros_like(feat)
    f = feat.shape[1]
    for i in range(6):
        feat[i : i + 1, :] = vectors[:, i * f : (i + 1) * f]
    units = slot.shape[2] - 3 * heads
    at_q, at_v, at_u = 6 * f, 6 * f + 4 * heads, 6 * f + 8 * heads

    def quarter(first, n, q):
        return vectors[:, pl.ds(pl.multiple_of(first + q * n, 128), n)]

    for t in range(4):
        q = d
        if t % 2:
            q = q + 1 - 2 * lax.rem(q, 2)
        if t // 2:
            q = lax.rem(q + 2, 4)
        slot[t, :, 0:heads] = quarter(at_q, heads, q)
        slot[t, :, heads : 2 * heads] = jnp.zeros((1, heads), F32)
        slot[t, :, 2 * heads : 3 * heads] = quarter(at_v, heads, q)
        slot[t, :, 3 * heads :] = quarter(at_u, units, q)
    for c in loads:
        c.wait()

    gq = Gather(peers, pq, w, True, q_recv, q_sent, NEAR + FAR)
    line = Line(peers, gq, z_sems)
    go = Gather(peers, po, wo, False, o_recv, o_sent, OWN_BLOCK)
    gu = Gather(peers, pu, wu, True, u_recv, u_sent, OWN_BLOCK)
    gd = Gather(peers, pd, wd, False, d_recv, d_sent, OWN_BLOCK)
    later = (go, gu, gd)
    inward = Inward(peers, tokens, x, rows_buf, i_sems, range(FINE), FINE)
    inward.load()
    here = seg_out.at[pl.ds(2 * r, 2)]
    small = [
        pltpu.make_async_copy(feat, feat_out.at[:, pl.ds(0, f)], v_sems.at[0]),
        pltpu.make_async_copy(slot, slot_out.at[pl.ds(0, 4)], v_sems.at[1]),
        pltpu.make_async_copy(segments, here, v_sems.at[2]),
        send(peers, "y", slot, slot_out.at[pl.ds(4, 4)], v_sems.at[3], v_sems.at[4]),
    ]
    for i in (1, 2, 3):
        small.append(send(peers, i, feat, feat_out.at[:, pl.ds(i * f, f)], v_sems.at[3 + 2 * i], v_sems.at[4 + 2 * i]))
        small.append(send(peers, i, segments, here, v_sems.at[9 + 2 * i], v_sems.at[10 + 2 * i]))

    peers.meet(ALL_PEERS)
    line.start()
    gq.start()
    for c in small:
        c.start()
    for g in later:
        g.start()
    inward.start(0)
    line.wave(0)
    inward.start(1)
    inward.settle()
    gq.relay((0, 2), (0, 4))
    line.wave(1)
    inward.start(2)
    for g in later:
        g.relay((0, 2), (0, 4))
    line.wave(2)
    inward.start(*range(3, FINE))
    for s in (1, 2, 3):
        gq.relay((s, 2), (s, 4))
    for s in range(4):
        gq.relay((s, 6))
    for c in small:
        c.wait()
    for g in (gq, *later):
        g.finish()
    line.finish()
    inward.finish()


def first(tokens, segments, weights, vectors):
    w_query, _, _, w_out, w_up, w_down = weights
    width = 4 * tokens.shape[1]
    heads = w_query.shape[1] // 4
    units = w_up.shape[1] // 4
    vmem = pl.BlockSpec(memory_space=pltpu.VMEM)
    return pl.pallas_call(
        first_kernel,
        in_specs=[ANY, vmem] + [ANY] * 6 + [vmem],
        out_specs=[ANY] * 8,
        out_shape=[
            jax.ShapeDtypeStruct((4, SEQ, width // 4), BF),
            jax.ShapeDtypeStruct((width, 24 * heads), BF),
            jax.ShapeDtypeStruct((8 * heads, width), BF),
            jax.ShapeDtypeStruct((width, 8 * units), BF),
            jax.ShapeDtypeStruct((8 * units, width), BF),
            jax.ShapeDtypeStruct((8, width), F32),
            jax.ShapeDtypeStruct((8, 1, 3 * heads + units), F32),
            jax.ShapeDtypeStruct((8, 8, 128), jnp.int32),
        ],
        scratch_shapes=[
            pltpu.VMEM((width // 4, 3 * heads), BF),
            pltpu.VMEM((heads, width // 4), BF),
            pltpu.VMEM((width // 4, units), BF),
            pltpu.VMEM((units, width // 4), BF),
            pltpu.VMEM((SEQ, width // 4), BF),
            pltpu.VMEM((8, width // 4), F32),
            pltpu.VMEM((4, 1, 3 * heads + units), F32),
            DMA((6,)),
            *[DMA((32,))] * 8,
            sems_of_exchange(FINE),
            DMA((20,)),
            DMA((11,)),
        ],
        compiler_params=pltpu.CompilerParams(vmem_limit_bytes=VMEM_LIMIT, collective_id=0, has_side_effects=True),
        name="first",
    )(tokens, segments, *weights, vectors)


RB = 256


def norm_rows(v):
    mean = jnp.mean(v, axis=1, keepdims=True)
    variance = jnp.mean(v * v, axis=1, keepdims=True) - mean * mean
    inv = lax.rsqrt(variance + NORM_EPS)
    return (v - mean) * inv, inv


def norm_rows_back(g, normed, inv):
    mean_g = jnp.mean(g, axis=1, keepdims=True)
    mean_gn = jnp.mean(g * normed, axis=1, keepdims=True)
    return inv * (g - mean_g - normed * mean_gn)


def gelu_and_slope(v):
    t = 1.0 / (1.0 + (0.3275911 * 0.5 ** 0.5) * jnp.abs(v))
    half = (0.127414796, -0.142248368, 0.7107068705, -0.7265760135, 0.5307027145)
    poly = t * (half[0] + t * (half[1] + t * (half[2] + t * (half[3] + t * half[4]))))
    bell = jnp.exp2(v * v * (-0.5 * math.log2(math.e)))
    tail = poly * bell
    cdf = jnp.where(v >= 0, 1.0 - tail, tail)
    return v * cdf, cdf + v * bell * (1.0 / math.sqrt(2.0 * math.pi))


def row_blocks(body, n=RB):
    def run(i, carry):
        body(pl.ds(pl.multiple_of(i * n, n), n))
        return carry

    lax.fori_loop(0, SEQ // n, run, 0)


def ff_fwd_kernel(
    x_ref, att_ref, wo_ref, vec_ref, b_ref, cot, cot_first, wu_in, wd_in,
    wu, wd, act_ref, slope_ref, hlow_ref, normed1_ref, inv1_ref, out_ref, r2_ref, vg_ref,
    acc, wu_buf, wd_buf, cot_buf, cot_own, buf_sem, u_recv, u_sent, d_recv, d_sent, i_sems, c_sem,
):
    j = pl.program_id(0)
    peers = Peers()
    gu = Gather(peers, None, wu, True, u_recv, u_sent, UP_FAR)
    gd = Gather(peers, None, wd, False, d_recv, d_sent, DOWN_REST)
    inward = Inward(peers, cot, cot_buf, cot_own, i_sems, range(1, CHUNKS))
    early = pltpu.make_async_copy(cot_first, cot_buf.at[pl.ds(0, SEQ // CHUNKS), :], c_sem)
    n = wu_buf.shape[2]

    def fetch(t, slot):
        cols = pl.ds(pl.multiple_of(t * n, n), n)
        return (
            pltpu.make_async_copy(wu.at[:, cols], wu_buf.at[slot], buf_sem.at[0, slot]),
            pltpu.make_async_copy(wd.at[cols, :], wd_buf.at[slot], buf_sem.at[1, slot]),
        )

    @pl.when(j == 0)
    def _():
        peers.hello(ALL_PEERS)
        for t in range(2):
            for c in fetch(t, t):
                c.start()
        early.start()
        inward.load()
        acc[...] = jnp.zeros_like(acc)
        peers.meet(ALL_PEERS)
        gd.emit(3, 0)
        for s in (1, 2):
            emit_far(gu, s)
            emit_far(gd, s, 1)
        emit_far(gu, 3)
        inward.start(*inward.chunks)

        def body(rows):
            x = jnp.concatenate([x_ref[s, rows, :] for s in range(4)], 1)
            v = x.astype(F32) + mm(att_ref[rows, :], wo_ref[...]) + vec_ref[0:1, :]
            normed, inv = norm_rows(v)
            normed1_ref[rows, :] = normed
            inv1_ref[rows, :] = jnp.broadcast_to(inv, (RB, 128))
            hlow_ref[rows, :] = (normed * vec_ref[1:2, :] + vec_ref[2:3, :]).astype(BF)

        row_blocks(body)
        gd.relay((3, 2), (3, 4))

    @pl.when(j == 1)
    def _():
        gd.arrived(3, 3)
        inward.settle()

    @pl.when(j == 2)
    def _():
        gd.arrived(3, 5)

    @pl.when(j == 4)
    def _():
        for g in (gu, gd):
            g.relay((1, 6), (2, 6), (3, 6))

    @pl.when(j == 5)
    def _():
        for s in (1, 2, 3):
            gu.arrived(s, 7)
            gd.arrived(s, 7)

    slot = lax.rem(j, 2)
    for c in fetch(j, slot):
        c.wait()
    w_up = wu_buf.at[slot]
    w_down = wd_buf.at[slot]
    bias = b_ref[0, :, 384:]
    for i in range(SEQ // 512):
        rows = slice(i * 512, (i + 1) * 512)
        act, slope = gelu_and_slope(mm(hlow_ref[rows, :], w_up[...]) + bias)
        act = act.astype(BF)
        act_ref[rows, :] = act
        slope_ref[rows, :] = slope.astype(BF)
        acc[rows, :] += mm(act, w_down[...])

    @pl.when(j < 6)
    def _():
        for c in fetch(j + 2, slot):
            c.start()

    @pl.when(j == 7)
    def _():
        inward.finish()
        early.wait()
        vg_ref[...] = jnp.zeros_like(vg_ref)

        def body(rows):
            hidden = normed1_ref[rows, :] * vec_ref[1:2, :] + vec_ref[2:3, :]
            normed, inv = norm_rows(hidden + (acc[rows, :] + vec_ref[3:4, :]))
            out_ref[rows, :] = (normed * vec_ref[4:5, :] + vec_ref[5:6, :]).astype(BF)
            c = cot_buf[rows, :].astype(F32)
            r2 = norm_rows_back(c * vec_ref[4:5, :], normed, inv)
            r2_ref[rows, :] = r2
            vg_ref[0:1, :] += jnp.sum(c * normed, axis=0, keepdims=True)
            vg_ref[1:2, :] += jnp.sum(c, axis=0, keepdims=True)
            vg_ref[2:3, :] += jnp.sum(r2.astype(BF).astype(F32), axis=0, keepdims=True)

        row_blocks(body)
        gu.finish()
        gd.finish()


def ff_fwd(x, att, wo, vec, bu, cot, cot_first, wu, wd):
    width, units = wu.shape
    n = units // 8
    return pl.pallas_call(
        ff_fwd_kernel,
        grid=(8,),
        in_specs=[
            const(*x.shape),
            const(SEQ, width),
            const(width, width),
            const(8, width),
            pl.BlockSpec((1, 1, bu.shape[2]), lambda j: (j, 0, 0)),
            ANY,
            ANY,
            ANY,
            ANY,
        ],
        out_specs=[
            ANY,
            ANY,
            pl.BlockSpec((SEQ, n), lambda j: (0, j)),
            pl.BlockSpec((SEQ, n), lambda j: (0, j)),
            const(SEQ, width),
            const(SEQ, width),
            const(SEQ, 128),
            const(SEQ, width),
            const(SEQ, width),
            const(8, width),
        ],
        out_shape=[
            jax.ShapeDtypeStruct(wu.shape, BF),
            jax.ShapeDtypeStruct(wd.shape, BF),
            jax.ShapeDtypeStruct((SEQ, units), BF),
            jax.ShapeDtypeStruct((SEQ, units), BF),
            jax.ShapeDtypeStruct((SEQ, width), BF),
            jax.ShapeDtypeStruct((SEQ, width), F32),
            jax.ShapeDtypeStruct((SEQ, 128), F32),
            jax.ShapeDtypeStruct((SEQ, width), BF),
            jax.ShapeDtypeStruct((SEQ, width), F32),
            jax.ShapeDtypeStruct((8, width), F32),
        ],
        input_output_aliases={7: 0, 8: 1},
        scratch_shapes=[
            pltpu.VMEM((SEQ, width), F32),
            pltpu.VMEM((2, width, n), BF),
            pltpu.VMEM((2, n, width), BF),
            pltpu.VMEM((SEQ, width), BF),
            pltpu.VMEM((SEQ - SEQ // CHUNKS, width // 4), BF),
            DMA((2, 2)),
            DMA((32,)),
            DMA((32,)),
            DMA((32,)),
            DMA((32,)),
            sems_of_exchange(),
            DMA,
        ],
        compiler_params=pltpu.CompilerParams(vmem_limit_bytes=VMEM_LIMIT, collective_id=2, has_side_effects=True),
        name="ff_fwd",
    )(x, att, wo, vec, bu, cot, cot_first, wu, wd)


ORDER = (7, 6, 1, 3, 5, 0, 2, 4)
PAIRS = (7, 6, 3, 2, 5, 4, 1, 0)


def slot_at(j):
    return jnp.where(j < 2, 7 - j, jnp.where(j < 5, 2 * j - 3, 2 * j - 10))


def pair_at(j):
    return jnp.where(j < 2, 7 - j, jnp.where(j < 4, 5 - j, jnp.where(j < 6, 9 - j, 7 - j)))


def sum_rows(dst, *srcs):
    n = dst.shape[0]
    step = min(n, 64)

    def run(i, carry):
        rows = pl.ds(pl.multiple_of(i * step, step), step)
        total = srcs[0][rows, :].astype(F32)
        for src in srcs[1:]:
            total += src[rows, :].astype(F32)
        dst[rows, :] = total.astype(BF)
        return carry

    lax.fori_loop(0, n // step, run, 0)


class Fold:
    @staticmethod
    def scratch(a, b):
        return [
            pltpu.VMEM((2, a, b), BF),
            pltpu.VMEM((4, a, b), BF),
            pltpu.VMEM((a, b), BF),
            pltpu.VMEM((2, a // 2, b), BF),
            DMA((12,)),
        ]

    def __init__(self, peers, order, stage, land, corner, land_corner, sems):
        self.peers, self.order, self.stage, self.land, self.corner, self.land_corner, self.sems = (
            peers, order, stage, land, corner, land_corner, sems,
        )
        self.half = corner.shape[0] // 2

    def to_core(self, p):
        k = (self.order[p] - 1) // 2
        return send(self.peers, "core", self.stage.at[p % 2], self.land.at[k], self.sems.at[4 + k], self.sems.at[k])

    def to_side(self, h):
        src = self.corner.at[pl.ds(h * self.half, self.half), :]
        return send(self.peers, "xy"[1 - h], src, self.land_corner.at[h], self.sems.at[10 + h], self.sems.at[8 + h])

    def before(self, j):
        for p in range(2, 8):
            if self.order[p - 2] % 2 == 0:
                continue

            @pl.when(j == p)
            def _(p=p):
                self.to_core(p - 2).wait_send()

    def from_core(self, t):
        k = t // 2
        self.to_core(self.order.index(t + 1)).wait_recv()
        return self.land.at[k]

    def after(self, j, outs):
        for p, t in enumerate(self.order):
            @pl.when(j == p)
            def _(p=p, t=t):
                mine = self.stage.at[p % 2]
                if t % 2 == 1:
                    self.to_core(p).start()
                    return
                theirs = self.from_core(t)
                if t == 6:
                    sum_rows(self.corner, mine, theirs)
                    self.to_side(0).start()
                    self.to_side(1).start()
                    return
                out = outs[t]
                if t == 0:
                    sum_rows(out, mine, theirs)
                    return
                h = t // 2 - 1
                self.to_side(h).wait_recv()
                for q in range(2):
                    rows = pl.ds(q * self.half, self.half)
                    more = (self.land_corner.at[h],) if q == h else ()
                    sum_rows(out.at[rows, :], mine.at[rows, :], theirs.at[rows, :], *more)

    def finish(self):
        for p in (6, 7):
            if self.order[p] % 2:
                self.to_core(p).wait_send()
        self.to_side(0).wait_send()
        self.to_side(1).wait_send()


class Cross:
    def __init__(self, peers, for_x, for_y, land_x, land_y, sems, cuts=1):
        self.peers, self.sems, self.cuts = peers, sems, cuts
        self.ends = {"x": (for_x, land_x), "y": (for_y, land_y)}
        self.n = land_x.shape[0] // cuts

    def copy(self, way, h=0):
        src, dst = self.ends[way]
        rows = pl.ds(h * self.n, self.n)
        at = 4 * h + 2 * "xy".index(way)
        return send(self.peers, way, src.at[rows, :], dst.at[rows, :], self.sems.at[at], self.sems.at[at + 1])

    def start(self, ways="xy", h=0):
        for way in ways:
            self.copy(way, h).start()

    def finish(self, own, out):
        for h in range(self.cuts):
            for way in "xy":
                self.copy(way, h).wait()
        sum_rows(out, own, self.ends["x"][1], self.ends["y"][1])


class Whole:
    @staticmethod
    def scratch(a, b):
        return [
            pltpu.VMEM((8 * a, b), BF),
            pltpu.VMEM((4, a, b), BF),
            pltpu.VMEM((4, a, b), BF),
            pltpu.VMEM((2, a // 2, b), BF),
            pltpu.VMEM((a, b), BF),
            pltpu.VMEM((a, b), BF),
            DMA((12,)),
            DMA((4,)),
        ]

    def __init__(self, peers, total, land, kept, land_corner, land_x, land_y, sems, c_sems):
        self.peers, self.total, self.land, self.kept, self.land_corner, self.sems = (
            peers, total, land, kept, land_corner, sems,
        )
        self.a = land.shape[1]
        self.half = self.a // 2
        self.cross = Cross(peers, kept.at[1], kept.at[2], land_x, land_y, c_sems)

    def block(self, t):
        return self.total.at[pl.ds(t * self.a, self.a), :]

    def to_core(self, k):
        return send(
            self.peers, "core", self.block(2 * k + 1), self.land.at[k], self.sems.at[4 + k], self.sems.at[k]
        )

    def to_side(self, h):
        src = self.kept.at[3, pl.ds(h * self.half, self.half), :]
        return send(self.peers, "xy"[1 - h], src, self.land_corner.at[h], self.sems.at[10 + h], self.sems.at[8 + h])

    def start(self):
        for k in (3, 1, 2, 0):
            self.to_core(k).start()

    def corner(self):
        for k in (3, 1, 2, 0):
            self.to_core(k).wait_recv()
            sum_rows(self.kept.at[k], self.block(2 * k), self.land.at[k])
            if k == 3:
                self.to_side(0).start()
                self.to_side(1).start()

    def sides(self):
        for h in range(2):
            self.to_side(h).wait_recv()
            rows = pl.ds(h * self.half, self.half)
            mine = self.kept.at[1 + h, rows, :]
            sum_rows(mine, mine, self.land_corner.at[h])
        self.cross.start()

    def finish(self, out):
        self.cross.finish(self.kept.at[0], out)
        for k in range(4):
            self.to_core(k).wait_send()
        for h in range(2):
            self.to_side(h).wait_send()


class Deal:
    def __init__(self, peers, total, by_rows, land, sems):
        self.peers, self.total, self.by_rows, self.land, self.sems = peers, total, by_rows, land, sems

    def part(self, s):
        n = self.total.shape[0 if self.by_rows else 1] // 4
        return self.total.at[pl.ds(s * n, n), :] if self.by_rows else self.total.at[:, pl.ds(s * n, n)]

    def copy(self, s):
        return send(self.peers, 4 - s, self.part(s), self.land.at[s - 1], self.sems.at[2 + s], self.sems.at[s - 1])

    def start(self):
        for s in (2, 1, 3):
            self.copy(s).start()

    def finish(self, out):
        for s in (1, 2, 3):
            self.copy(s).wait()
        sum_rows(out, self.part(0), self.land.at[0], self.land.at[1], self.land.at[2])


class LineDeal:
    def __init__(self, peers, total, by_rows, land, tmp, sems):
        self.peers, self.land, self.tmp, self.sems = peers, land, tmp, sems
        self.part = Deal(peers, total, by_rows, None, None).part

    def copy(self, up, b, row, src):
        go = (b - row if up else row - b) - 1
        at = (0 if up else 3) + go
        return send(
            self.peers, 1 if up else 3, src, self.land.at[0 if up else 1, go], self.sems.at[at], self.sems.at[6 + at]
        )

    def slot(self, b, row):
        return (row - b) % 4

    def first(self, up, b, row):
        return self.copy(up, b, row, self.part(self.slot(b, row)))

    def pass_on(self, up, b, row):
        go = (b - row if up else row - b) - 1
        tmp = self.tmp.at[0 if up else 1, go]
        return self.copy(up, b, row, tmp), tmp

    def got(self, up, b, row):
        go = b - row if up else row - b
        at = (0 if up else 3) + go
        land = self.land.at[0 if up else 1, go]
        send(self.peers, 1 if up else 3, land, land, self.sems.at[at], self.sems.at[6 + at]).wait_recv()
        return land

    STEPS = (((1, True, 3), (1, True, 2), (2, False, 0), (2, False, 1)), ((2, True, 3), (1, False, 0)))
    STARTS = ((0, True, 3), (0, True, 2), (0, True, 1), (3, False, 0), (3, False, 1), (3, False, 2))

    def when(self, row, run):
        pl.when(self.peers.r == row)(run)

    def start(self):
        for row, up, b in self.STARTS:
            self.when(row, lambda up=up, b=b, row=row: self.first(up, b, row).start())

    def step(self, k):
        for row, up, b in self.STEPS[k]:
            def run(row=row, up=up, b=b):
                land = self.got(up, b, row)
                copy, tmp = self.pass_on(up, b, row)
                sum_rows(tmp, land, self.part(self.slot(b, row)))
                copy.start()

            self.when(row, run)

    def finish(self, out):
        for row in range(4):
            def run(row=row):
                lands = []
                if row > 0:
                    lands.append(self.got(True, row, row))
                if row < 3:
                    lands.append(self.got(False, row, row))
                sum_rows(out, self.part(0), *lands)

            self.when(row, run)
        for row, up, b in self.STARTS:
            self.when(row, lambda up=up, b=b, row=row: self.first(up, b, row).wait_send())
        for moves in self.STEPS:
            for row, up, b in moves:
                self.when(row, lambda up=up, b=b, row=row: self.pass_on(up, b, row)[0].wait_send())


class Spread:
    def __init__(self, peers, own, place, sems):
        d = lax.axis_index("dp")
        self.peers, self.own, self.sems, self.here = peers, own, sems, place(d)
        self.from_x = place(lax.rem(d + 2, 4))

    def local(self):
        return pltpu.make_async_copy(self.own, self.here, self.sems.at[6])

    def copies(self):
        s = self.sems
        return (
            send(self.peers, "x", self.own, self.here, s.at[0], s.at[1]),
            send(self.peers, "core", self.own, self.here, s.at[2], s.at[3]),
            send(self.peers, "core", self.from_x, self.from_x, s.at[4], s.at[5]),
        )

    def start(self):
        to_x, to_core, _ = self.copies()
        to_x.start()
        to_core.start()
        self.local().start()

    def relay(self):
        to_x, _, on = self.copies()
        to_x.wait_recv()
        on.start()

    def finish(self):
        to_x, to_core, on = self.copies()
        to_x.wait_send()
        to_core.wait()
        on.wait()
        self.local().wait()


class Outward:
    def __init__(self, peers, rows, block, buf, sems, parts=(2, 1, 3, 0)):
        self.peers, self.rows, self.block, self.buf, self.sems = peers, rows, block, buf, sems
        self.away = [s for s in parts if s]
        self.stays = 0 in parts
        self.n = SEQ // CHUNKS

    def ends(self, s, first, count):
        f = self.block.shape[1]
        mine = pl.ds(pl.multiple_of(self.peers.r * SEQ + first * self.n, self.n), count * self.n)
        return self.rows.at[pl.ds(first * self.n, count * self.n), pl.ds(s * f, f)], self.block.at[mine, :]

    def copy(self, s, k):
        return send(self.peers, 4 - s, *self.ends(s, k, 1), self.sems.at[0, s, k], self.sems.at[1, s, k])

    def load(self):
        return pltpu.make_async_copy(self.ends(0, 0, CHUNKS)[0], self.buf, self.sems.at[0, 0, 0])

    def store(self):
        src, dst = self.ends(0, 0, CHUNKS)
        return pltpu.make_async_copy(src if self.buf is None else self.buf, dst, self.sems.at[1, 0, 0])

    def start(self, *chunks):
        for k in chunks:
            for s in self.away:
                self.copy(s, k).start()

    def settle(self):
        self.load().wait()
        self.store().start()

    def finish(self):
        if self.stays:
            self.store().wait()
        for k in range(CHUNKS):
            for s in self.away:
                self.copy(s, k).wait()


def ff_down_bwd_kernel(
    r2_ref, wd_ref, act_ref, slope_ref, out, out_block, gp_ref, bu_ref, kept_ref,
    gfed, out_own, stage, land, corner, land_corner, f_sems, o_sems,
):
    j = pl.program_id(0)
    peers = Peers()
    outward = Outward(peers, out, out_block, out_own, o_sems, (2, 0))
    fold = Fold(peers, ORDER, stage, land, corner, land_corner, f_sems)

    @pl.when(j == 0)
    def _():
        peers.hello(ALL_PEERS)
        outward.load().start()

        def body(rows):
            gfed[rows, :] = r2_ref[rows, :].astype(BF)

        row_blocks(body)
        peers.meet(ALL_PEERS)
        outward.start(*range(CHUNKS))

    bsum = jnp.zeros((1, bu_ref.shape[2]), F32)
    for i in range(SEQ // 256):
        rows = slice(i * 256, (i + 1) * 256)
        g = (mm_t(gfed[rows, :], wd_ref[...]) * slope_ref[rows, :].astype(F32)).astype(BF)
        gp_ref[rows, :] = g
        bsum += jnp.sum(g.astype(F32), axis=0, keepdims=True)
    bu_ref[0] = bsum
    fold.before(j)
    stage[lax.rem(j, 2)] = tmm(act_ref[...], gfed[...]).astype(BF)
    fold.after(j, {t: kept_ref.at[0] for t in (0, 2, 4)})

    @pl.when(j == 1)
    def _():
        outward.settle()

    @pl.when(j == 7)
    def _():
        fold.finish()
        outward.finish()


def kept_spec(a, b):
    return pl.BlockSpec((1, a, b), lambda j: (jnp.maximum(j - 5, 0), 0, 0))


def ff_down_bwd(r2, wd, act, slope, out):
    units, width = wd.shape
    n = units // 8
    return pl.pallas_call(
        ff_down_bwd_kernel,
        grid=(8,),
        in_specs=[
            const(SEQ, width),
            pl.BlockSpec((n, width), lambda j: (slot_at(j), 0)),
            pl.BlockSpec((SEQ, n), lambda j: (0, slot_at(j))),
            pl.BlockSpec((SEQ, n), lambda j: (0, slot_at(j))),
            ANY,
        ],
        out_specs=[
            ANY,
            pl.BlockSpec((SEQ, n), lambda j: (0, slot_at(j))),
            pl.BlockSpec((1, 1, n), lambda j: (slot_at(j), 0, 0)),
            kept_spec(n, width),
        ],
        out_shape=[
            jax.ShapeDtypeStruct((4 * SEQ, width // 4), BF),
            jax.ShapeDtypeStruct((SEQ, units), BF),
            jax.ShapeDtypeStruct((8, 1, n), F32),
            jax.ShapeDtypeStruct((3, n, width), BF),
        ],
        scratch_shapes=[
            pltpu.VMEM((SEQ, width), BF),
            pltpu.VMEM((SEQ, width // 4), BF),
            *Fold.scratch(n, width),
            sems_of_exchange(),
        ],
        compiler_params=pltpu.CompilerParams(vmem_limit_bytes=VMEM_LIMIT, collective_id=3, has_side_effects=True),
        name="ff_down_bwd",
    )(r2, wd, act, slope, out)


def ff_up_bwd_kernel(
    r2_ref, hlow_ref, gp_ref, wu_ref, normed1_ref, inv1_ref, vec_ref, out, out_block_in, kept_d,
    out_block, r1_ref, gattn_ref, vg_ref, kept_ref, own_ref,
    hlow_t, stage, land, corner, land_corner, f_sems, own_d, land_x, land_y, c_sems, o_sems,
):
    j = pl.program_id(0)
    peers = Peers()
    outward = Outward(peers, out, out_block, None, o_sems, (1, 3))
    fold = Fold(peers, ORDER, stage, land, corner, land_corner, f_sems)
    cross = Cross(peers, kept_d.at[1], kept_d.at[2], land_x, land_y, c_sems, 2)
    load = pltpu.make_async_copy(kept_d.at[0], own_d, c_sems.at[8])

    @pl.when(j == 0)
    def _():
        peers.hello(ALL_PEERS)
        load.start()
        r1_ref[...] = r2_ref[...]
        for i in range(SEQ // 256):
            rows = slice(i * 256, (i + 1) * 256)
            hlow_t[:, rows] = jnp.transpose(hlow_ref[rows, :])
        peers.meet(ALL_PEERS)
        cross.start()
        outward.start(*range(CHUNKS))

    fold.before(j)
    stage[lax.rem(j, 2)] = mm(hlow_t[...], gp_ref[...]).astype(BF)
    fold.after(j, {t: kept_ref.at[0] for t in (0, 2, 4)})

    @pl.when(j == 1)
    def _():
        cross.start(h=1)

    r1_ref[...] += mm_t(gp_ref[...], wu_ref[...])

    @pl.when(j == 7)
    def _():
        vg_ref[...] = jnp.zeros_like(vg_ref)

        def body(rows):
            gh = r1_ref[rows, :]
            normed = normed1_ref[rows, :]
            r1 = norm_rows_back(gh * vec_ref[1:2, :], normed, inv1_ref[rows, 0:1])
            r1_ref[rows, :] = r1
            low = r1.astype(BF)
            gattn_ref[rows, :] = low
            vg_ref[0:1, :] += jnp.sum(gh * normed, axis=0, keepdims=True)
            vg_ref[1:2, :] += jnp.sum(gh, axis=0, keepdims=True)
            vg_ref[2:3, :] += jnp.sum(low.astype(F32), axis=0, keepdims=True)

        row_blocks(body)
        load.wait()
        cross.finish(own_d, own_ref)
        fold.finish()
        outward.finish()


def ff_up_bwd(r2, hlow, gp, wu, normed1, inv1, vec, out, out_block, kept_d):
    width, units = wu.shape
    n = units // 8
    return pl.pallas_call(
        ff_up_bwd_kernel,
        grid=(8,),
        in_specs=[
            const(SEQ, width),
            const(SEQ, width),
            pl.BlockSpec((SEQ, n), lambda j: (0, slot_at(j))),
            pl.BlockSpec((width, n), lambda j: (0, slot_at(j))),
            const(SEQ, width),
            const(SEQ, 128),
            const(8, width),
            ANY,
            ANY,
            ANY,
        ],
        out_specs=[
            ANY,
            const(SEQ, width),
            const(SEQ, width),
            const(8, width),
            kept_spec(width, n),
            const(n, width),
        ],
        out_shape=[
            jax.ShapeDtypeStruct(out_block.shape, BF),
            jax.ShapeDtypeStruct((SEQ, width), F32),
            jax.ShapeDtypeStruct((SEQ, width), BF),
            jax.ShapeDtypeStruct((8, width), F32),
            jax.ShapeDtypeStruct((3, width, n), BF),
            jax.ShapeDtypeStruct((n, width), BF),
        ],
        input_output_aliases={8: 0},
        scratch_shapes=[
            pltpu.VMEM((width, SEQ), BF),
            *Fold.scratch(width, n),
            pltpu.VMEM((n, width), BF),
            pltpu.VMEM((n, width), BF),
            pltpu.VMEM((n, width), BF),
            DMA((9,)),
            sems_of_exchange(),
        ],
        compiler_params=pltpu.CompilerParams(vmem_limit_bytes=VMEM_LIMIT, collective_id=4, has_side_effects=True),
        name="ff_up_bwd",
    )(r2, hlow, gp, wu, normed1, inv1, vec, out, out_block, kept_d)


def attend_bwd_kernel(
    gattn_ref, wo_ref, att_ref, qkv_ref, linv_ref, p_ref, x_t, att_all, tot_d, kept_u,
    g_ref, gsum_ref, tot_q, tot_o, down_ref, up_ref,
    ds_ref,
    q_stage, q_land, q_corner, q_land_corner, q_sems,
    q_kept, q_x, q_y, q_c, o_total, o_land, o_kept, o_land_corner, o_x, o_y, o_sems, o_c,
    zd_land, zd_sems, own_u, land_x, land_y, c_sems, tot_u, zu_land, zu_sems,
):
    j = pl.program_id(0)
    peers = Peers()
    fold_q = Fold(peers, PAIRS, q_stage, q_land, q_corner, q_land_corner, q_sems)
    whole_o = Whole(peers, o_total, o_land, o_kept, o_land_corner, o_x, o_y, o_sems, o_c)
    cross_q = Cross(peers, q_kept.at[1], q_kept.at[2], q_x, q_y, q_c)
    deal_d = Deal(peers, tot_d, False, zd_land, zd_sems)
    cross_u = Cross(peers, kept_u.at[1], kept_u.at[2], land_x, land_y, c_sems)
    deal_u = Deal(peers, tot_u, True, zu_land, zu_sems)
    load_u = pltpu.make_async_copy(kept_u.at[0], own_u, c_sems.at[4])

    @pl.when(j == 0)
    def _():
        load_u.start()
        peers.hello(ALL_PEERS)
        load_u.wait()
        peers.meet(ALL_PEERS)
        cross_u.start()
        deal_d.start()
        o_total[...] = tmm(att_all[...], gattn_ref[...]).astype(BF)
        whole_o.start()

    @pl.when(j == 1)
    def _():
        whole_o.corner()

    @pl.when(j == 3)
    def _():
        whole_o.sides()

    @pl.when(j == 6)
    def _():
        whole_o.finish(tot_o)

    @pl.when(j == 4)
    def _():
        cross_u.finish(own_u, tot_u)
        deal_u.start()
        deal_d.finish(down_ref)

    lane = lax.broadcasted_iota(jnp.int32, (SEQ, 128), 1)
    scale = HD ** (-0.5)
    fold_q.before(j)
    q = qkv_ref[:, 0:128]
    k = qkv_ref[:, 128:256]
    v = qkv_ref[:, 256:384]
    do = mm_t(gattn_ref[...], wo_ref[...]).astype(BF).astype(F32) * linv_ref[...]
    prod = do * att_ref[...].astype(F32)
    dob = do.astype(BF)
    q_t = jnp.transpose(q)
    k_t = jnp.transpose(k)
    do_t = jnp.transpose(dob)
    dq_t, dk_t, dv_t = [], [], []
    for h in range(2):
        mine = (lane < HD) if h == 0 else (lane >= HD)
        delta = jnp.sum(jnp.where(mine, prod, 0.0), axis=1, keepdims=True)
        dom = jnp.where(mine, dob, jnp.zeros_like(dob))
        for i in range(SEQ // QB):
            rows = slice(i * QB, (i + 1) * QB)
            dp = mm_t(dom[rows], v)
            ds_ref[h, rows, :] = (p_ref[h, rows, :].astype(F32) * (dp - delta[rows])).astype(BF)
        feats = slice(h * HD, (h + 1) * HD)
        dq_t.append(mm_t(k_t[feats], ds_ref[h]))
        dk_t.append(mm(q_t[feats], ds_ref[h]))
        dv_t.append(mm(do_t[feats], p_ref[h]))
    g_ref[:, 0:128] = (jnp.transpose(jnp.concatenate(dq_t, 0)) * scale).astype(BF)
    g_ref[:, 128:256] = (jnp.transpose(jnp.concatenate(dk_t, 0)) * scale).astype(BF)
    g_ref[:, 256:384] = jnp.transpose(jnp.concatenate(dv_t, 0)).astype(BF)
    gsum_ref[0] = jnp.sum(g_ref[...].astype(F32), axis=0, keepdims=True)
    q_stage[lax.rem(j, 2)] = mm(x_t[...], g_ref[...]).astype(BF)
    fold_q.after(j, {t: q_kept.at[t // 2] for t in (0, 2, 4)})

    @pl.when(j == PAIRS.index(2))
    def _():
        cross_q.start("x")

    @pl.when(j == PAIRS.index(4))
    def _():
        cross_q.start("y")

    @pl.when(j == 7)
    def _():
        deal_u.finish(up_ref)
        fold_q.finish()
        cross_q.finish(q_kept.at[0], tot_q)


def attend_bwd(gattn, wo, att, qkv, linv, p, x_t, tot_d, kept_u):
    width = wo.shape[1]
    heads = 128
    n = tot_d.shape[0]
    return pl.pallas_call(
        attend_bwd_kernel,
        grid=(8,),
        in_specs=[
            const(SEQ, width),
            pl.BlockSpec((heads, width), lambda j: (pair_at(j), 0)),
            pl.BlockSpec((SEQ, heads), lambda j: (0, pair_at(j))),
            pl.BlockSpec((SEQ, 3 * heads), lambda j: (0, pair_at(j))),
            pl.BlockSpec((SEQ, heads), lambda j: (0, pair_at(j))),
            pl.BlockSpec((2, SEQ, SEQ), lambda j: (pair_at(j), 0, 0)),
            const(*x_t.shape),
            const(SEQ, width),
            const(n, width),
            ANY,
        ],
        out_specs=[
            pl.BlockSpec((SEQ, 3 * heads), lambda j: (0, pair_at(j))),
            pl.BlockSpec((1, 1, 3 * heads), lambda j: (pair_at(j), 0, 0)),
            const(width, 3 * heads),
            const(heads, width),
            const(n, width // 4),
            const(width // 4, n),
        ],
        out_shape=[
            jax.ShapeDtypeStruct((SEQ, 24 * heads), BF),
            jax.ShapeDtypeStruct((8, 1, 3 * heads), F32),
            jax.ShapeDtypeStruct((width, 3 * heads), BF),
            jax.ShapeDtypeStruct((heads, width), BF),
            jax.ShapeDtypeStruct((n, width // 4), BF),
            jax.ShapeDtypeStruct((width // 4, n), BF),
        ],
        scratch_shapes=[
            pltpu.VMEM((2, SEQ, SEQ), BF),
            *Fold.scratch(width, 3 * heads),
            pltpu.VMEM((3, width, 3 * heads), BF),
            pltpu.VMEM((width, 3 * heads), BF),
            pltpu.VMEM((width, 3 * heads), BF),
            DMA((4,)),
            *Whole.scratch(heads, width),
            pltpu.VMEM((3, n, width // 4), BF),
            DMA((6,)),
            pltpu.VMEM((width, n), BF),
            pltpu.VMEM((width, n), BF),
            pltpu.VMEM((width, n), BF),
            DMA((5,)),
            pltpu.VMEM((width, n), BF),
            pltpu.VMEM((3, width // 4, n), BF),
            DMA((6,)),
        ],
        compiler_params=pltpu.CompilerParams(vmem_limit_bytes=VMEM_LIMIT, collective_id=5, has_side_effects=True),
        name="attend_bwd",
    )(gattn, wo, att, qkv, linv, p, x_t, att, tot_d, kept_u)


def last_kernel(
    tot_q, tot_o, own_d, own_u, g_part, u_part, vec1, vec2, g, w, r1,
    x_block, gq, go, gd, gu, slot_out, feat_ref,
    g_buf, w_buf, acc, xg, ld_sems,
    q_land, q_tmp, q_z, q_sum, o_land, o_tmp, o_z, o_sum,
    vec_ref, v1, v2, v3, l1, l2, l3, l4, v_own, v_sems, out_sems, s_sems,
):
    peers = Peers()
    outward = Outward(peers, xg, x_block, None, out_sems)
    deal_q = LineDeal(peers, tot_q, True, q_land, q_tmp, q_z)
    deal_o = LineDeal(peers, tot_o, False, o_land, o_tmp, o_z)
    loads = (
        pltpu.make_async_copy(w, w_buf, ld_sems.at[0]),
        pltpu.make_async_copy(g, g_buf, ld_sems.at[1]),
        pltpu.make_async_copy(r1, acc, ld_sems.at[2]),
    )
    peers.hello(ALL_PEERS)
    for c in loads:
        c.start()

    def products(k):
        rows = slice(k * (SEQ // CHUNKS), (k + 1) * (SEQ // CHUNKS))
        xg[rows, :] = (mm_t(g_buf[rows, :], w_buf[...]) + acc[rows, :]).astype(BF)
        outward.start(k)

    vec_ref[...] = jnp.zeros_like(vec_ref)
    heads3, units = g_part.shape[2], u_part.shape[2]
    for k, t in enumerate((0, 4, 2, 6, 1, 5, 3, 7)):
        k = k if k < 4 else k + 8
        for i in range(heads3 // 128):
            vec_ref[k, i : i + 1, :] = g_part[t, :, i * 128 : (i + 1) * 128]
        for i in range(units // 128):
            at = heads3 // 128 + i
            vec_ref[k, at : at + 1, :] = u_part[t, :, i * 128 : (i + 1) * 128]
    f = vec1.shape[1] // 4
    rows = [(vec1, 2), (vec1, 0), (vec1, 1), (vec2, 2), (vec2, 0), (vec2, 1)]
    for k in range(4):
        for v, (ref, row) in enumerate(rows):
            for i in range(f // 128):
                at = v * (f // 128) + i
                first = k * f + i * 128
                vec_ref[4 + 2 * k + at // 8, at % 8 : at % 8 + 1, :] = ref[row : row + 1, first : first + 128]

    def rows_at(ref):
        n = ref.shape[0] // 4
        return lambda q: ref.at[pl.ds(pl.multiple_of(q * n, n), n), :]

    def cols_at(ref, first, n):
        return lambda q: ref.at[:, pl.ds(pl.multiple_of(first + q * n, n), n)]

    heads = q_sum.shape[1] // 3
    units = own_u.shape[1]
    spread_d = Spread(peers, own_d, rows_at(gd), s_sems.at[0])
    spread_u = Spread(peers, own_u, cols_at(gu, 0, units), s_sems.at[1])
    spread_o = Spread(peers, o_sum, rows_at(go), s_sems.at[2])
    spread_q = [
        Spread(peers, q_sum.at[:, pl.ds(i * heads, heads)], cols_at(gq, 4 * i * heads, heads), s_sems.at[3 + i])
        for i in range(3)
    ]
    spread_v = Spread(peers, v_own, lambda q: slot_out.at[q], s_sems.at[6])

    to_core = send(peers, "core", vec_ref.at[pl.ds(4, 12)], l1, v_sems.at[0], v_sems.at[1])
    to_x = send(peers, "x", v1.at[pl.ds(2, 10)], l2, v_sems.at[2], v_sems.at[3])
    to_y = send(peers, "y", v2.at[pl.ds(1, 11)], l3, v_sems.at[4], v_sems.at[5])
    to_rows = []
    for i in (1, 2, 3):
        to_rows.append(send(peers, i, v3.at[0], l4.at[i - 1, 0], v_sems.at[6 + 4 * i], v_sems.at[7 + 4 * i]))
        src = v3.at[pl.ds(4 + 2 * (4 - i), 2)]
        to_rows.append(send(peers, i, src, l4.at[i - 1, pl.ds(1, 2)], v_sems.at[8 + 4 * i], v_sems.at[9 + 4 * i]))

    peers.meet(ALL_PEERS)
    deal_o.start()
    deal_q.start()
    to_core.start()
    spread_d.start()
    spread_u.start()
    for c in loads:
        c.wait()
    products(0)
    deal_o.step(0)
    deal_q.step(0)
    products(1)
    to_core.wait()
    v1[0:4] = vec_ref[0:4] + l1[8:12]
    v1[4:12] = vec_ref[4:12] + l1[0:8]
    to_x.start()
    deal_o.step(1)
    deal_q.step(1)
    products(2)
    products(3)
    outward.store().start()
    to_x.wait()
    v2[0:2] = v1[0:2] + l2[0:2]
    v2[4:12] = v1[4:12] + l2[2:10]
    v2[2:4] = v1[2:4]
    to_y.start()
    spread_d.relay()
    spread_u.relay()
    deal_o.finish(o_sum)
    spread_o.start()
    deal_q.finish(q_sum)
    for sp in spread_q:
        sp.start()
    to_y.wait()
    v3[0:1] = v2[0:1] + l3[0:1]
    v3[4:12] = v2[4:12] + l3[3:11]
    for c in to_rows:
        c.start()
    spread_o.relay()
    for sp in spread_q:
        sp.relay()
    for c in to_rows:
        c.wait()
    v_own[...] = v3[0] + l4[0, 0] + l4[1, 0] + l4[2, 0]
    feat_ref[...] = v3[4:6] + l4[0, 1:3] + l4[1, 1:3] + l4[2, 1:3]
    spread_v.start()
    spread_v.relay()
    for sp in (spread_d, spread_u, spread_o, spread_v, *spread_q):
        sp.finish()
    outward.finish()


def last(tot_q, tot_o, own_d, own_u, g_part, u_part, vec1, vec2, g, w, r1):
    width = r1.shape[1]
    part = width // 4
    n = own_d.shape[0]
    heads = tot_o.shape[0]
    vmem = pl.BlockSpec(memory_space=pltpu.VMEM)

    def bufs(a, b, by_rows):
        piece = (a // 4, b) if by_rows else (a, b // 4)
        return [pltpu.VMEM((2, 3, *piece), BF), pltpu.VMEM((2, 2, *piece), BF), DMA((12,)), pltpu.VMEM(piece, BF)]

    return pl.pallas_call(
        last_kernel,
        in_specs=[vmem] * 8 + [ANY] * 3,
        out_specs=[ANY, ANY, ANY, ANY, ANY, ANY, vmem],
        out_shape=[
            jax.ShapeDtypeStruct((4 * SEQ, part), BF),
            jax.ShapeDtypeStruct((part, 12 * heads), BF),
            jax.ShapeDtypeStruct((4 * heads, part), BF),
            jax.ShapeDtypeStruct((4 * n, part), BF),
            jax.ShapeDtypeStruct((part, 4 * n), BF),
            jax.ShapeDtypeStruct((4, 8, 128), F32),
            jax.ShapeDtypeStruct((2, 8, 128), F32),
        ],
        scratch_shapes=[
            pltpu.VMEM((SEQ, 24 * heads), BF),
            pltpu.VMEM((width, 24 * heads), BF),
            pltpu.VMEM((SEQ, width), F32),
            pltpu.VMEM((SEQ, width), BF),
            DMA((3,)),
            *bufs(width, 3 * heads, True),
            *bufs(heads, width, False),
            pltpu.VMEM((16, 8, 128), F32),
            pltpu.VMEM((12, 8, 128), F32),
            pltpu.VMEM((12, 8, 128), F32),
            pltpu.VMEM((12, 8, 128), F32),
            pltpu.VMEM((12, 8, 128), F32),
            pltpu.VMEM((10, 8, 128), F32),
            pltpu.VMEM((11, 8, 128), F32),
            pltpu.VMEM((3, 3, 8, 128), F32),
            pltpu.VMEM((8, 128), F32),
            DMA((24,)),
            sems_of_exchange(),
            DMA((7, 7)),
        ],
        compiler_params=pltpu.CompilerParams(vmem_limit_bytes=VMEM_LIMIT, collective_id=6, has_side_effects=True),
        name="last",
    )(tot_q, tot_o, own_d, own_u, g_part, u_part, vec1, vec2, g, w, r1)


def whole_sequences(
    tokens, segments, w_query, b_query, w_key, w_value, b_value, w_out, b_out, norm1_gain, norm1_shift,
    w_up, b_up, w_down, b_down, norm2_gain, norm2_shift, cotangent,
):
    R = lax.axis_size("row")
    feat = tokens.shape[1]
    hq = b_query.shape[0] // 4
    unit = b_up.shape[0] // 4
    vectors = (b_out, norm1_gain, norm1_shift, b_down, norm2_gain, norm2_shift, b_query, b_value, b_up)
    size = sum(v.shape[0] for v in vectors)
    first_at, packed = 0, 0.0
    for v in vectors:
        packed += jnp.pad(v.astype(F32), (first_at, size - first_at - v.shape[0]))
        first_at += v.shape[0]
    vectors = packed.reshape(1, -1)
    x, w_qkv, wo, wu, wd, feat_all, b_slot, seg = first(
        tokens,
        segments.reshape(2, 8, 128),
        (w_query, w_key, w_value, w_out, w_up, w_down),
        vectors,
    )

    qkv, att, prob, linv, x_t, wo, wu, wd, cot_first = attend_fwd(x, w_qkv, b_slot, seg, cotangent, wo, wu, wd)
    wu, wd, act, slope, hidden_low, normed1, inv1, output, grad_r2, vg2 = ff_fwd(
        x, att, wo, feat_all, b_slot, cotangent, cot_first, wu, wd
    )

    out_block, grad_pre, bu_part, kept_d = ff_down_bwd(grad_r2, wd, act, slope, output)
    out_block, grad_r1, grad_attn, vg1, kept_u, tot_d = ff_up_bwd(
        grad_r2, hidden_low, grad_pre, wu, normed1, inv1, feat_all, output, out_block, kept_d
    )
    g_qkv, g_part, tot_q, tot_o, own_d, own_u = attend_bwd(
        grad_attn, wo, att, qkv, linv, prob, x_t, tot_d, kept_u
    )

    x_grad_block, gq, go, gd, gu, slot_sum, own = last(
        tot_q, tot_o, own_d, own_u, g_part, bu_part, vg1, vg2, g_qkv, w_qkv, grad_r1
    )
    wq_grad, wk_grad, wv_grad = [gq[:, i * 4 * hq : (i + 1) * 4 * hq].astype(F32) for i in range(3)]
    w_out_grad, w_up_grad, w_down_grad = go.astype(F32), gu.astype(F32), gd.astype(F32)
    slot_sum = slot_sum.reshape(4, 1024)
    bq_grad = slot_sum[:, :hq].reshape(-1)
    bv_grad = slot_sum[:, 2 * hq : 3 * hq].reshape(-1)
    bu_grad = slot_sum[:, 3 * hq : 3 * hq + unit].reshape(-1)
    own = own.reshape(-1)[: 6 * feat].reshape(6, feat)
    return (
        out_block, x_grad_block, wq_grad, bq_grad, wk_grad, wv_grad, bv_grad, w_out_grad, own[0], own[1], own[2],
        w_up_grad, bu_grad, w_down_grad, own[3], own[4], own[5],
    )


def tokens_cols(source):
    return lax.all_gather(source, "col", axis=0, tiled=True)


def tokens_rows(source):
    return lax.all_gather(source, "row", axis=0, tiled=True)


def product(row_piece, weight, flipped):
    if flipped:
        return lax.dot_general(
            row_piece, weight, (((1,), (1,)), ((), ())), preferred_element_type=jnp.float32
        )
    return jnp.dot(row_piece, weight, preferred_element_type=jnp.float32)


def outer_sum(left, right):
    return lax.dot_general(
        left, right, (((0,), (0,)), ((), ())), preferred_element_type=jnp.float32
    )


def settle_rows(gathered, weight, flipped, own_rows):

    def product_term(first_row, row_count):
        return product(gathered, weight, flipped)

    return lax.psum_scatter(
        product_term(jnp.int32(0), own_rows * lax.axis_size("row")),
        "row",
        scatter_dimension=0,
        tiled=True,
    )


def settle_cols(gathered, weight, flipped, own_rows):

    def product_term(first_row, row_count):
        return product(gathered, weight, flipped)

    return lax.psum_scatter(
        product_term(jnp.int32(0), own_rows * lax.axis_size("col")),
        "col",
        scatter_dimension=0,
        tiled=True,
    )


def row_sums(first_part, second_part):
    return lax.psum((jnp.sum(first_part, axis=1), jnp.sum(second_part, axis=1)), "row")


def norm_forward(residual, norm_gain, norm_shift):
    total_sum, square_sum = row_sums(residual, residual * residual)
    row_mean = (total_sum / WIDTH)[:, None]
    variance = (square_sum / WIDTH)[:, None] - row_mean * row_mean
    inv_std = lax.rsqrt(variance + NORM_EPS)
    normed = (residual - row_mean) * inv_std
    return (normed * norm_gain + norm_shift, normed, inv_std)


def norm_backward(grad_in, normed, inv_std, norm_gain):
    grad_norm = grad_in * norm_gain
    total_sum, cross_sum = row_sums(grad_norm, grad_norm * normed)
    grad_resid = inv_std * (grad_norm - total_sum[:, None] / WIDTH - normed * cross_sum[:, None] / WIDTH)
    return (grad_resid, jnp.sum(grad_in * normed, axis=0), jnp.sum(grad_in, axis=0))


def split_heads(array, seq_count):
    return array.reshape(seq_count, SEQ, array.shape[1] // HD, HD)


def pair_scores(queries, key_heads, segment_ids):
    position = jnp.arange(SEQ)
    same_doc = (segment_ids[:, None] == segment_ids[None, :]) & (segment_ids[None, :] != 0)
    allowed = same_doc | (position[:, None] == position[None, :])
    raw_scores = jnp.einsum(
        "qhd,khd->hqk", queries, key_heads, preferred_element_type=jnp.float32
    ) * HD ** (-0.5)
    return jnp.where(allowed[None], raw_scores, -1000000000.0)


def attend_forward(source):
    queries, key_heads, values, segment_ids = source
    scores = pair_scores(queries, key_heads, segment_ids)
    top_score = jnp.max(scores, axis=2, keepdims=True)
    exp_scores = jnp.exp(scores - top_score)
    total_sum = jnp.sum(exp_scores, axis=2, keepdims=True)
    soft_low = (exp_scores / total_sum).astype(jnp.bfloat16)
    attended = jnp.einsum("hqk,khd->qhd", soft_low, values, preferred_element_type=jnp.float32)
    return (attended.astype(jnp.bfloat16), (top_score + jnp.log(total_sum))[:, :, 0])


def attend_backward(source):
    queries, key_heads, values, segment_ids, grad_out, log_total = source
    scores = pair_scores(queries, key_heads, segment_ids)
    soft_weights = jnp.exp(scores - log_total[:, :, None])
    soft_low = soft_weights.astype(jnp.bfloat16)
    grad_values = jnp.einsum("hqk,qhd->khd", soft_low, grad_out, preferred_element_type=jnp.float32)
    grad_soft = jnp.einsum("qhd,khd->hqk", grad_out, values, preferred_element_type=jnp.float32)
    grad_scores = soft_weights * (
        grad_soft - jnp.sum(soft_weights * grad_soft, axis=2, keepdims=True)
    )
    grad_scores = grad_scores.astype(jnp.bfloat16)
    scale_factor = HD ** (-0.5)
    grad_queries = (
        jnp.einsum("hqk,khd->qhd", grad_scores, key_heads, preferred_element_type=jnp.float32)
        * scale_factor
    )
    grad_keys = (
        jnp.einsum("hqk,qhd->khd", grad_scores, queries, preferred_element_type=jnp.float32)
        * scale_factor
    )
    return (
        grad_queries.astype(jnp.bfloat16),
        grad_keys.astype(jnp.bfloat16),
        grad_values.astype(jnp.bfloat16),
    )


def split_heads_plan(
    tokens,
    segments,
    w_query,
    b_query,
    w_key,
    w_value,
    b_value,
    w_out,
    b_out,
    norm1_gain,
    norm1_shift,
    w_up,
    b_up,
    w_down,
    b_down,
    norm2_gain,
    norm2_shift,
    cotangent,
):
    rows_b = tokens.shape[0]
    rows_a = segments.shape[0]
    head_cols = w_query.shape[1]
    seq_count = rows_a // SEQ
    segment_seqs = segments.reshape(seq_count, SEQ)
    gathered_x = tokens_cols(tokens)
    stacked = jnp.concatenate([w_query, w_key, w_value], axis=1)
    projected = settle_rows(gathered_x, stacked, False, rows_a)
    queries = (projected[:, :head_cols] + b_query).astype(jnp.bfloat16)
    key_heads = projected[:, head_cols : 2 * head_cols].astype(jnp.bfloat16)
    values = (projected[:, 2 * head_cols :] + b_value).astype(jnp.bfloat16)
    query_seqs = split_heads(queries, seq_count)
    key_seqs = split_heads(key_heads, seq_count)
    value_seqs = split_heads(values, seq_count)
    attended, log_total = lax.map(attend_forward, (query_seqs, key_seqs, value_seqs, segment_seqs))
    attended = attended.reshape(rows_a, head_cols)
    gathered_o = tokens_rows(attended)
    attn_out = settle_cols(gathered_o, w_out, False, rows_b) + b_out
    hidden, normed1, inv_std1 = norm_forward(
        tokens.astype(jnp.float32) + attn_out, norm1_gain, norm1_shift
    )
    hidden_low = hidden.astype(jnp.bfloat16)
    gathered_h = tokens_cols(hidden_low)
    pre_act = settle_rows(gathered_h, w_up, False, rows_a) + b_up
    active = gelu_exact(pre_act).astype(jnp.bfloat16)
    gathered_a = tokens_rows(active)
    fed = settle_cols(gathered_a, w_down, False, rows_b) + b_down
    output, normed2, inv_std2 = norm_forward(hidden + fed, norm2_gain, norm2_shift)
    grad_r2, grad_gain2, grad_shift2 = norm_backward(
        cotangent.astype(jnp.float32), normed2, inv_std2, norm2_gain
    )
    grad_fed = grad_r2.astype(jnp.bfloat16)
    gathered_f = tokens_cols(grad_fed)
    grad_w_down = outer_sum(gathered_a, gathered_f)
    grad_active = settle_rows(gathered_f, w_down, True, rows_a)
    unused_out, slope_pull = jax.vjp(gelu_exact, pre_act)
    grad_pre = slope_pull(grad_active)[0].astype(jnp.bfloat16)
    gathered_p = tokens_rows(grad_pre)
    grad_w_up = outer_sum(gathered_h, gathered_p)
    grad_from_ff = settle_cols(gathered_p, w_up, True, rows_b)
    bias_up_part = jnp.sum(grad_pre.astype(jnp.float32), axis=0)
    bias_down_part = jnp.sum(grad_fed.astype(jnp.float32), axis=0)
    grad_r1, grad_gain1, grad_shift1 = norm_backward(
        grad_from_ff + grad_r2, normed1, inv_std1, norm1_gain
    )
    grad_attn = grad_r1.astype(jnp.bfloat16)
    gathered_d = tokens_cols(grad_attn)
    grad_w_out = outer_sum(gathered_o, gathered_d)
    grad_attended = settle_rows(gathered_d, w_out, True, rows_a).astype(jnp.bfloat16)
    grad_q, grad_k, grad_v = lax.map(
        attend_backward,
        (
            query_seqs,
            key_seqs,
            value_seqs,
            segment_seqs,
            split_heads(grad_attended, seq_count),
            log_total,
        ),
    )
    grad_q = grad_q.reshape(rows_a, head_cols)
    grad_k = grad_k.reshape(rows_a, head_cols)
    grad_v = grad_v.reshape(rows_a, head_cols)
    grad_proj = jnp.concatenate([grad_q, grad_k, grad_v], axis=1)
    gathered_g = tokens_rows(grad_proj)
    grad_stacked = outer_sum(gathered_x, gathered_g)
    tokens_grad = settle_cols(gathered_g, stacked, True, rows_b) + grad_r1
    bias_q, bias_v, bias_up = lax.psum(
        (
            jnp.sum(grad_q.astype(jnp.float32), axis=0),
            jnp.sum(grad_v.astype(jnp.float32), axis=0),
            bias_up_part,
        ),
        ("dp", "row"),
    )
    bias_out, bias_down, gain_one, shift_one, gain_two, shift_two = lax.psum(
        (
            jnp.sum(grad_attn.astype(jnp.float32), axis=0),
            bias_down_part,
            grad_gain1,
            grad_shift1,
            grad_gain2,
            grad_shift2,
        ),
        ("dp", "col"),
    )
    sum_stacked, sum_out, sum_up, sum_down = (
        lax.psum(grad_stacked.astype(jnp.bfloat16), "dp").astype(jnp.float32),
        lax.psum(grad_w_out.astype(jnp.bfloat16), "dp").astype(jnp.float32),
        lax.psum(grad_w_up.astype(jnp.bfloat16), "dp").astype(jnp.float32),
        lax.psum(grad_w_down.astype(jnp.bfloat16), "dp").astype(jnp.float32),
    )
    return (
        output.astype(jnp.bfloat16),
        tokens_grad.astype(jnp.bfloat16),
        sum_stacked[:, :head_cols],
        bias_q,
        sum_stacked[:, head_cols : 2 * head_cols],
        sum_stacked[:, 2 * head_cols :],
        bias_v,
        sum_out,
        bias_out,
        gain_one,
        shift_one,
        sum_up,
        bias_up,
        sum_down,
        bias_down,
        gain_two,
        shift_two,
    )


def solution(mesh):
    dp, rows, cols = (mesh.shape[name] for name in ("dp", "row", "col"))
    whole = TOKENS // SEQ == dp * rows * cols and dp == 4 and cols == 2
    plan = whole_sequences if whole else split_heads_plan
    placed = (
        P(("dp", "col"), "row"),
        P(("dp", "row")),
        P("row", "col"),
        P("col"),
        P("row", "col"),
        P("row", "col"),
        P("col"),
        P("col", "row"),
        P("row"),
        P("row"),
        P("row"),
        P("row", "col"),
        P("col"),
        P("col", "row"),
        P("row"),
        P("row"),
        P("row"),
        P(("dp", "col"), "row"),
    )
    return jax.shard_map(
        plan,
        mesh=mesh,
        in_specs=placed,
        out_specs=(
            P(("dp", "col"), "row"),
            P(("dp", "col"), "row"),
            P("row", "col"),
            P("col"),
            P("row", "col"),
            P("row", "col"),
            P("col"),
            P("col", "row"),
            P("row"),
            P("row"),
            P("row"),
            P("row", "col"),
            P("col"),
            P("col", "row"),
            P("row"),
            P("row"),
            P("row"),
        ),
        check_vma=False,
    )
```

```python
import math

import jax
import jax.numpy as jnp
from jax import lax
from jax.experimental import pallas as pl
from jax.experimental.pallas import tpu as pltpu
from jax.sharding import PartitionSpec as P

HD = 64
SEQ = 1024
WIDTH = 1024
TOKENS = 32768
NORM_EPS = 1e-05
BF = jnp.bfloat16
F32 = jnp.float32
NEG = -1e30
QB = 256
VMEM_LIMIT = 56 * 1024 * 1024
MESH = pl.DeviceIdType.MESH
ANY = pl.BlockSpec(memory_space=pl.ANY)
DMA = pltpu.SemaphoreType.DMA
ONCE = pl.Buffered(1)


def const(*shape):
    return pl.BlockSpec(shape, lambda j: (0,) * len(shape), pipeline_mode=ONCE)


def mm(a, b):
    return jnp.dot(a, b, preferred_element_type=F32)


def mm_t(a, b):
    return lax.dot_general(a, b, (((1,), (1,)), ((), ())), preferred_element_type=F32)


def tmm(a, b):
    return lax.dot_general(a, b, (((0,), (0,)), ((), ())), preferred_element_type=F32)


def gelu_exact(v):
    return jax.nn.gelu(v, approximate=False)


def attend_rows(qkv_ref, seg_col_ref, seg_row, o_ref, p_ref, linv_ref):
    lane = lax.broadcasted_iota(jnp.int32, (QB, 128), 1)
    scale = HD ** (-0.5) * math.log2(math.e)
    k = qkv_ref[:, 128:256]
    v = qkv_ref[:, 256:384]
    units = [(i, h) for i in range(SEQ // QB) for h in range(2)]

    def scores(i, h):
        q = qkv_ref[i * QB : (i + 1) * QB, 0:128]
        mine = (lane < HD) if h == 0 else (lane >= HD)
        return mm_t(jnp.where(mine, q, jnp.zeros_like(q)), k)

    ahead = scores(*units[0])
    outs = []
    for at, (i, h) in enumerate(units):
        rows = slice(i * QB, (i + 1) * QB)
        s = ahead
        if at + 1 < len(units):
            ahead = scores(*units[at + 1])
        s = jnp.where(seg_col_ref[rows, 0:1] == seg_row, s * scale, NEG)
        top = jnp.max(s, axis=1, keepdims=True)
        p = jnp.exp2(s - top)
        total = jnp.sum(p, axis=1, keepdims=True)
        pb = p.astype(BF)
        p_ref[h, rows, :] = pb
        inv = 1.0 / total
        outs.append((mm(pb, v) * inv, jnp.broadcast_to(inv, (QB, 128))))
        if h == 1:
            o_ref[rows, :] = jnp.where(lane < HD, outs[0][0], outs[1][0]).astype(BF)
            linv_ref[rows, :] = jnp.where(lane < HD, outs[0][1], outs[1][1])
            outs = []


def attend_fwd_kernel(
    x_ref, w_ref, b_ref, seg_ref, cot, wo_in, wu_in, wd_in,
    qkv_ref, o_ref, p_ref, linv_ref, wo, wu, wd, cot_first,
    x_buf, seg_col_ref, seg_row_ref, cot_own, i_sems, o_recv, o_sent, u_recv, u_sent, d_recv, d_sent,
):
    j = pl.program_id(0)
    peers = Peers()
    go = Gather(peers, None, wo, False, o_recv, o_sent, RING + LATER_NEAR + FAR)
    gu = Gather(peers, None, wu, True, u_recv, u_sent, RING + LATER_NEAR + far_edges(0))
    gd = Gather(peers, None, wd, False, d_recv, d_sent, RING + DOWN_NEAR + far_edges(0, 1))
    every = (go, gu, gd)
    inward = Inward(peers, cot, cot_first, cot_own, i_sems, (0,))

    plan = {
        2: ((go, (1, 0)), (gu, (1, 0)), (gu, (0, 6)), (gd, (0, 6))),
        3: ((gd, (1, 0)), (go, (1, 2), (1, 4), (2, 0))),
        4: ((gu, (1, 2), (1, 4), (2, 0)), (go, (0, 6), (1, 6))),
        5: ((gd, (1, 2), (1, 4), (2, 0)), (go, (2, 2), (2, 4), (3, 0))),
        6: ((gu, (2, 2), (2, 4)), (gu, (3, 0))),
        7: ((gd, (2, 2), (2, 4)), (go, (2, 6), (3, 2), (3, 4))),
        8: ((gd, (3, 0)), (gu, (3, 2), (3, 4)), (go, (3, 6))),
    }

    def relay(step):
        for g, *blocks in plan[step]:
            g.relay(*blocks)

    @pl.when(j == 0)
    def _():
        peers.hello(ALL_PEERS)
        inward.load()
        f = x_ref.shape[2]
        for s in range(4):
            x_buf[:, s * f : (s + 1) * f] = x_ref[s]
        tile = seg_ref[4 * peers.c + peers.r]
        for i in range(8):
            row = tile[i : i + 1, :]
            at = lax.broadcasted_iota(jnp.int32, (1, 128), 1) + i * 128
            row = jnp.where(row == 0, -1 - at, row)
            seg_row_ref[:, i * 128 : (i + 1) * 128] = row
            seg_col_ref[i * 128 : (i + 1) * 128, :] = jnp.transpose(jnp.broadcast_to(row, (128, 128)))

    qkv_ref[...] = (mm(x_buf[...], w_ref[...]) + b_ref[0, :, 0:384]).astype(BF)
    @pl.when(j == 0)
    def _():
        peers.meet(ALL_PEERS)
        for g in every:
            g.emit(0, 0)
        go.emit(0, 2)
        gu.emit(0, 2)
        gd.emit(0, 4)

    for at in range(2, 8):
        @pl.when(j == at)
        def _(at=at):
            relay(at)
            if at == 5:
                inward.settle()
                inward.start(0)

    seg_row = seg_row_ref[...]
    attend_rows(qkv_ref, seg_col_ref, seg_row, o_ref, p_ref, linv_ref)

    @pl.when(j == 7)
    def _():
        relay(8)
        for g in every:
            g.finish()
        inward.finish()


def attend_fwd(x, w_qkv, b_slot, seg, cot, wo, wu, wd):
    slots = w_qkv.shape[1] // 384
    return pl.pallas_call(
        attend_fwd_kernel,
        grid=(slots,),
        in_specs=[
            const(*x.shape),
            pl.BlockSpec((w_qkv.shape[0], 384), lambda j: (0, j)),
            pl.BlockSpec((1, 1, b_slot.shape[2]), lambda j: (j, 0, 0)),
            const(8, 8, 128),
            ANY,
            ANY,
            ANY,
            ANY,
        ],
        out_specs=[
            pl.BlockSpec((SEQ, 384), lambda j: (0, j)),
            pl.BlockSpec((SEQ, 128), lambda j: (0, j)),
            pl.BlockSpec((2, SEQ, SEQ), lambda j: (j, 0, 0)),
            pl.BlockSpec((SEQ, 128), lambda j: (0, j)),
            ANY,
            ANY,
            ANY,
            ANY,
        ],
        out_shape=[
            jax.ShapeDtypeStruct((SEQ, slots * 384), BF),
            jax.ShapeDtypeStruct((SEQ, slots * 128), BF),
            jax.ShapeDtypeStruct((slots * 2, SEQ, SEQ), BF),
            jax.ShapeDtypeStruct((SEQ, slots * 128), F32),
            jax.ShapeDtypeStruct(wo.shape, BF),
            jax.ShapeDtypeStruct(wu.shape, BF),
            jax.ShapeDtypeStruct(wd.shape, BF),
            jax.ShapeDtypeStruct((SEQ // CHUNKS, w_qkv.shape[0]), BF),
        ],
        input_output_aliases={5: 4, 6: 5, 7: 6},
        scratch_shapes=[
            pltpu.VMEM((SEQ, w_qkv.shape[0]), BF),
            pltpu.VMEM((SEQ, 128), jnp.int32),
            pltpu.VMEM((1, SEQ), jnp.int32),
            pltpu.VMEM((SEQ // CHUNKS, cot.shape[1]), BF),
            sems_of_exchange(),
            *[DMA((32,))] * 6,
        ],
        compiler_params=pltpu.CompilerParams(vmem_limit_bytes=VMEM_LIMIT, collective_id=1, has_side_effects=True),
        name="attend_fwd",
    )(x, w_qkv, b_slot, seg, cot, wo, wu, wd)


class Peers:
    def __init__(self):
        self.r = lax.axis_index("row")
        self.c = lax.axis_index("col")
        self.d = d = lax.axis_index("dp")
        self.ids = {
            "core": {"dp": d + 1 - 2 * lax.rem(d, 2)},
            "x": {"dp": lax.rem(d + 2, 4)},
            "y": {"col": 1 - self.c},
            1: {"row": lax.rem(self.r + 1, 4)},
            2: {"row": lax.rem(self.r + 2, 4)},
            3: {"row": lax.rem(self.r + 3, 4)},
        }

    def hello(self, names):
        barrier = pltpu.get_barrier_semaphore()
        for name in names:
            pl.semaphore_signal(barrier, inc=1, device_id=self.ids[name], device_id_type=MESH)

    def meet(self, names):
        pl.semaphore_wait(pltpu.get_barrier_semaphore(), len(names))


def send(peers, name, src, dst, send_sem, recv_sem):
    return pltpu.make_async_remote_copy(
        src_ref=src, dst_ref=dst, send_sem=send_sem, recv_sem=recv_sem, device_id=peers.ids[name], device_id_type=MESH
    )


def near_edges(s):
    return [("x", s, 0, s, 2), ("y", s, 0, s, 4), ("core", s, 0, s, 1)]


def second_edges(s):
    return [("core", s, 2, s, 3), ("core", s, 4, s, 5)]


def far_edges(s, flip=0):
    return [("y", s, 2, s, 6) if (s + flip) % 2 == 0 else ("x", s, 4, s, 6), ("core", s, 6, s, 7)]


def emit_far(gather, s, flip=0):
    gather.emit(s, 2 if (s + flip) % 2 == 0 else 4)


RING = [(1, s, 0, s + 1, 0) for s in range(3)]
NEAR = [e for s in range(4) for e in near_edges(s) + second_edges(s)]
FAR = [e for s in range(4) for e in far_edges(s)]
OWN_BLOCK = near_edges(0) + second_edges(0)
LATER_NEAR = [e for e in NEAR if e[1] > 0]
UP_FAR = [e for s in (1, 2, 3) for e in far_edges(s)]
DOWN_FAR = [e for s in (1, 2, 3) for e in far_edges(s, 1)]
DOWN_NEAR = [e for e in LATER_NEAR if e[1] < 3] + [("core", 3, 0, 3, 1)]
DOWN_REST = [e for e in near_edges(3) if e[0] != "core"] + second_edges(3) + DOWN_FAR


class Gather:
    def __init__(self, peers, piece, full, by_rows, recv, sent, edges):
        self.peers, self.piece, self.full, self.recv, self.sent = peers, piece, full, recv, sent
        self.by_rows = by_rows
        self.n = full.shape[1 if by_rows else 0] // 8
        self.m = full.shape[0 if by_rows else 1] // 4
        self.edges = edges
        self.waited = set()
        self.emitted = set()

    def blk(self, s, t):
        a = pl.ds(s * self.m, self.m)
        b = pl.ds(t * self.n, self.n)
        return self.full.at[a, b] if self.by_rows else self.full.at[b, a]

    def copy(self, at):
        name, s, t, s2, t2 = self.edges[at]
        src = self.piece if (s, t) == (0, 0) and self.piece is not None else self.blk(s, t)
        return send(self.peers, name, src, self.blk(s2, t2), self.sent.at[at], self.recv.at[at])

    def emit(self, s, t):
        for at, e in enumerate(self.edges):
            if e[1:3] == (s, t):
                assert at not in self.emitted
                self.emitted.add(at)
                self.copy(at).start()

    def emit_own_slot(self, s):
        for at, e in enumerate(self.edges):
            if e[1:3] == (s, 0):
                self.emitted.add(at)
                self.copy(at).start()

    def arrived(self, s, t):
        for at, e in enumerate(self.edges):
            if e[3:5] == (s, t) and at not in self.waited:
                self.waited.add(at)
                self.copy(at).wait_recv()

    def relay(self, *blocks):
        for s, t in blocks:
            self.arrived(s, t)
            self.emit(s, t)

    def own(self):
        return pltpu.make_async_copy(self.piece, self.blk(0, 0), self.sent.at[len(self.edges)])

    def start(self):
        self.emit(0, 0)
        self.own().start()

    def finish(self):
        if self.piece is not None:
            self.own().wait()
        for at, e in enumerate(self.edges):
            if at not in self.waited:
                self.waited.add(at)
                self.copy(at).wait_recv()
        assert len(self.emitted) == len(self.edges)
        for at in range(len(self.edges)):
            self.copy(at).wait_send()


class Line:
    WAVES = ((3, 2, 1), (1, 3, 2), (1, 3, 2), (1, 2, 3))

    def __init__(self, peers, gather, sems):
        self.peers, self.gather, self.sems = peers, gather, sems

    def copy(self, up, s):
        s2 = s + 1 if up else (s - 1 if s else 3)
        g = self.gather
        src = g.piece if s == 0 else g.blk(s, 0)
        return send(
            self.peers, 1 if up else 3, src, g.blk(s2, 0), self.sems.at[(0 if up else 4) + s], self.sems.at[7 + s2]
        )

    def each(self, what):
        r = self.peers.r
        for s in range(3):
            @pl.when((r >= s) & (r < 3))
            def _(s=s):
                what(self.copy(True, s))
        for s in (0, 3, 2):
            @pl.when((r > 0) & (r <= (3 if s == 0 else s - 1)))
            def _(s=s):
                what(self.copy(False, s))

    def start(self):
        r = self.peers.r

        @pl.when(r < 3)
        def _():
            self.copy(True, 0).start()

        @pl.when(r > 0)
        def _():
            self.copy(False, 0).start()

    def wave(self, k):
        for row, order in enumerate(self.WAVES):
            s = order[k]

            @pl.when(self.peers.r == row)
            def _(row=row, s=s):
                self.copy(True, s - 1).wait_recv()
                below = row >= s
                if below and row < 3:
                    self.copy(True, s).start()
                if not below and row > 0:
                    self.copy(False, s).start()
                self.gather.emit_own_slot(s)

    def finish(self):
        self.each(lambda c: c.wait_send())


CHUNKS = 4
FINE = 8


def sems_of_exchange(cuts=CHUNKS):
    return DMA((2, 4, cuts))


class Inward:
    def __init__(self, peers, block, rows, buf, sems, chunks=range(CHUNKS), cuts=CHUNKS):
        self.peers, self.block, self.rows, self.buf, self.sems, self.chunks = peers, block, rows, buf, sems, chunks
        self.n = SEQ // cuts

    def ends(self, s, first, count):
        r = lax.rem(self.peers.r + s, 4)
        f = self.block.shape[1]
        src = self.block.at[pl.ds(pl.multiple_of(r * SEQ + first * self.n, self.n), count * self.n), :]
        at = first if self.rows.shape[-2] == SEQ else first - self.chunks[0]
        rows = pl.ds(at * self.n, count * self.n)
        return src, self.rows.at[s, rows, :] if len(self.rows.shape) == 3 else self.rows.at[rows, pl.ds(s * f, f)]

    def copy(self, s, k):
        return send(self.peers, s, *self.ends(s, k, 1), self.sems.at[0, s, k], self.sems.at[1, s, k])

    def own(self):
        src, dst = self.ends(0, self.chunks[0], len(self.chunks))
        return (
            pltpu.make_async_copy(src, self.buf, self.sems.at[0, 0, 0]),
            pltpu.make_async_copy(self.buf, dst, self.sems.at[1, 0, 0]),
        )

    def start(self, *chunks):
        for k in chunks:
            for s in (2, 1, 3):
                self.copy(s, k).start()

    def load(self):
        self.own()[0].start()

    def settle(self):
        self.own()[0].wait()
        self.own()[1].start()

    def finish(self):
        self.own()[1].wait()
        for k in self.chunks:
            for s in (1, 2, 3):
                self.copy(s, k).wait()


ALL_PEERS = ("core", "x", "y", 1, 2, 3)


def first_kernel(
    tokens, segments, w_query, w_key, w_value, w_out, w_up, w_down,
    vectors,
    x, w, wo, wu, wd, feat_out, slot_out, seg_out,
    pq, po, pu, pd, rows_buf, feat, slot, l_sems, q_recv, q_sent, o_recv, o_sent, u_recv, u_sent, d_recv, d_sent,
    i_sems, v_sems, z_sems,
):
    peers = Peers()
    r, d = peers.r, peers.d

    def own_cols(ref):
        n = ref.shape[1] // 4
        return ref.at[:, pl.ds(pl.multiple_of(d * n, n), n)]

    def own_rows(ref):
        n = ref.shape[0] // 4
        return ref.at[pl.ds(pl.multiple_of(d * n, n), n), :]

    peers.hello(ALL_PEERS)
    heads = w_query.shape[1] // 4
    loads = [
        pltpu.make_async_copy(own_cols(ref), pq.at[:, pl.ds(i * heads, heads)], l_sems.at[i])
        for i, ref in enumerate((w_query, w_key, w_value))
    ]
    loads += [
        pltpu.make_async_copy(own_rows(w_out), po, l_sems.at[3]),
        pltpu.make_async_copy(own_cols(w_up), pu, l_sems.at[4]),
        pltpu.make_async_copy(own_rows(w_down), pd, l_sems.at[5]),
    ]
    for c in loads:
        c.start()
    feat[...] = jnp.zeros_like(feat)
    f = feat.shape[1]
    for i in range(6):
        feat[i : i + 1, :] = vectors[:, i * f : (i + 1) * f]
    units = slot.shape[2] - 3 * heads
    at_q, at_v, at_u = 6 * f, 6 * f + 4 * heads, 6 * f + 8 * heads

    def quarter(first, n, q):
        return vectors[:, pl.ds(pl.multiple_of(first + q * n, 128), n)]

    for t in range(4):
        q = d
        if t % 2:
            q = q + 1 - 2 * lax.rem(q, 2)
        if t // 2:
            q = lax.rem(q + 2, 4)
        slot[t, :, 0:heads] = quarter(at_q, heads, q)
        slot[t, :, heads : 2 * heads] = jnp.zeros((1, heads), F32)
        slot[t, :, 2 * heads : 3 * heads] = quarter(at_v, heads, q)
        slot[t, :, 3 * heads :] = quarter(at_u, units, q)
    for c in loads:
        c.wait()

    gq = Gather(peers, pq, w, True, q_recv, q_sent, NEAR + FAR)
    line = Line(peers, gq, z_sems)
    go = Gather(peers, po, wo, False, o_recv, o_sent, OWN_BLOCK)
    gu = Gather(peers, pu, wu, True, u_recv, u_sent, OWN_BLOCK)
    gd = Gather(peers, pd, wd, False, d_recv, d_sent, OWN_BLOCK)
    later = (go, gu, gd)
    inward = Inward(peers, tokens, x, rows_buf, i_sems, range(FINE), FINE)
    inward.load()
    here = seg_out.at[pl.ds(2 * r, 2)]
    small = [
        pltpu.make_async_copy(feat, feat_out.at[:, pl.ds(0, f)], v_sems.at[0]),
        pltpu.make_async_copy(slot, slot_out.at[pl.ds(0, 4)], v_sems.at[1]),
        pltpu.make_async_copy(segments, here, v_sems.at[2]),
        send(peers, "y", slot, slot_out.at[pl.ds(4, 4)], v_sems.at[3], v_sems.at[4]),
    ]
    for i in (1, 2, 3):
        small.append(send(peers, i, feat, feat_out.at[:, pl.ds(i * f, f)], v_sems.at[3 + 2 * i], v_sems.at[4 + 2 * i]))
        small.append(send(peers, i, segments, here, v_sems.at[9 + 2 * i], v_sems.at[10 + 2 * i]))

    peers.meet(ALL_PEERS)
    line.start()
    gq.start()
    for c in small:
        c.start()
    for g in later:
        g.start()
    inward.start(0)
    line.wave(0)
    inward.start(1)
    inward.settle()
    gq.relay((0, 2), (0, 4))
    line.wave(1)
    inward.start(2)
    for g in later:
        g.relay((0, 2), (0, 4))
    line.wave(2)
    inward.start(*range(3, FINE))
    for s in (1, 2, 3):
        gq.relay((s, 2), (s, 4))
    for s in range(4):
        gq.relay((s, 6))
    for c in small:
        c.wait()
    for g in (gq, *later):
        g.finish()
    line.finish()
    inward.finish()


def first(tokens, segments, weights, vectors):
    w_query, _, _, w_out, w_up, w_down = weights
    width = 4 * tokens.shape[1]
    heads = w_query.shape[1] // 4
    units = w_up.shape[1] // 4
    vmem = pl.BlockSpec(memory_space=pltpu.VMEM)
    return pl.pallas_call(
        first_kernel,
        in_specs=[ANY, vmem] + [ANY] * 6 + [vmem],
        out_specs=[ANY] * 8,
        out_shape=[
            jax.ShapeDtypeStruct((4, SEQ, width // 4), BF),
            jax.ShapeDtypeStruct((width, 24 * heads), BF),
            jax.ShapeDtypeStruct((8 * heads, width), BF),
            jax.ShapeDtypeStruct((width, 8 * units), BF),
            jax.ShapeDtypeStruct((8 * units, width), BF),
            jax.ShapeDtypeStruct((8, width), F32),
            jax.ShapeDtypeStruct((8, 1, 3 * heads + units), F32),
            jax.ShapeDtypeStruct((8, 8, 128), jnp.int32),
        ],
        scratch_shapes=[
            pltpu.VMEM((width // 4, 3 * heads), BF),
            pltpu.VMEM((heads, width // 4), BF),
            pltpu.VMEM((width // 4, units), BF),
            pltpu.VMEM((units, width // 4), BF),
            pltpu.VMEM((SEQ, width // 4), BF),
            pltpu.VMEM((8, width // 4), F32),
            pltpu.VMEM((4, 1, 3 * heads + units), F32),
            DMA((6,)),
            *[DMA((32,))] * 8,
            sems_of_exchange(FINE),
            DMA((20,)),
            DMA((11,)),
        ],
        compiler_params=pltpu.CompilerParams(vmem_limit_bytes=VMEM_LIMIT, collective_id=0, has_side_effects=True),
        name="first",
    )(tokens, segments, *weights, vectors)


RB = 256


def norm_rows(v):
    mean = jnp.mean(v, axis=1, keepdims=True)
    variance = jnp.mean(v * v, axis=1, keepdims=True) - mean * mean
    inv = lax.rsqrt(variance + NORM_EPS)
    return (v - mean) * inv, inv


def norm_rows_back(g, normed, inv):
    mean_g = jnp.mean(g, axis=1, keepdims=True)
    mean_gn = jnp.mean(g * normed, axis=1, keepdims=True)
    return inv * (g - mean_g - normed * mean_gn)


def gelu_and_slope(v):
    t = 1.0 / (1.0 + (0.3275911 * 0.5 ** 0.5) * jnp.abs(v))
    half = (0.127414796, -0.142248368, 0.7107068705, -0.7265760135, 0.5307027145)
    poly = t * (half[0] + t * (half[1] + t * (half[2] + t * (half[3] + t * half[4]))))
    bell = jnp.exp2(v * v * (-0.5 * math.log2(math.e)))
    tail = poly * bell
    cdf = jnp.where(v >= 0, 1.0 - tail, tail)
    return v * cdf, cdf + v * bell * (1.0 / math.sqrt(2.0 * math.pi))


def row_blocks(body, n=RB):
    def run(i, carry):
        body(pl.ds(pl.multiple_of(i * n, n), n))
        return carry

    lax.fori_loop(0, SEQ // n, run, 0)


def ff_fwd_kernel(
    x_ref, att_ref, wo_ref, vec_ref, b_ref, cot, cot_first, wu_in, wd_in,
    wu, wd, act_ref, slope_ref, hlow_ref, normed1_ref, inv1_ref, out_ref, r2_ref, vg_ref,
    acc, wu_buf, wd_buf, cot_buf, cot_own, buf_sem, u_recv, u_sent, d_recv, d_sent, i_sems, c_sem,
):
    j = pl.program_id(0)
    peers = Peers()
    gu = Gather(peers, None, wu, True, u_recv, u_sent, UP_FAR)
    gd = Gather(peers, None, wd, False, d_recv, d_sent, DOWN_REST)
    inward = Inward(peers, cot, cot_buf, cot_own, i_sems, range(1, CHUNKS))
    early = pltpu.make_async_copy(cot_first, cot_buf.at[pl.ds(0, SEQ // CHUNKS), :], c_sem)
    n = wu_buf.shape[2]

    def fetch(t, slot):
        cols = pl.ds(pl.multiple_of(t * n, n), n)
        return (
            pltpu.make_async_copy(wu.at[:, cols], wu_buf.at[slot], buf_sem.at[0, slot]),
            pltpu.make_async_copy(wd.at[cols, :], wd_buf.at[slot], buf_sem.at[1, slot]),
        )

    @pl.when(j == 0)
    def _():
        peers.hello(ALL_PEERS)
        for t in range(2):
            for c in fetch(t, t):
                c.start()
        early.start()
        inward.load()
        acc[...] = jnp.zeros_like(acc)
        peers.meet(ALL_PEERS)
        gd.emit(3, 0)
        for s in (1, 2):
            emit_far(gu, s)
            emit_far(gd, s, 1)
        emit_far(gu, 3)
        inward.start(*inward.chunks)

        def body(rows):
            x = jnp.concatenate([x_ref[s, rows, :] for s in range(4)], 1)
            v = x.astype(F32) + mm(att_ref[rows, :], wo_ref[...]) + vec_ref[0:1, :]
            normed, inv = norm_rows(v)
            normed1_ref[rows, :] = normed
            inv1_ref[rows, :] = jnp.broadcast_to(inv, (RB, 128))
            hlow_ref[rows, :] = (normed * vec_ref[1:2, :] + vec_ref[2:3, :]).astype(BF)

        row_blocks(body)
        gd.relay((3, 2), (3, 4))

    @pl.when(j == 1)
    def _():
        gd.arrived(3, 3)
        inward.settle()

    @pl.when(j == 2)
    def _():
        gd.arrived(3, 5)

    @pl.when(j == 4)
    def _():
        for g in (gu, gd):
            g.relay((1, 6), (2, 6), (3, 6))

    @pl.when(j == 5)
    def _():
        for s in (1, 2, 3):
            gu.arrived(s, 7)
            gd.arrived(s, 7)

    slot = lax.rem(j, 2)
    for c in fetch(j, slot):
        c.wait()
    w_up = wu_buf.at[slot]
    w_down = wd_buf.at[slot]
    bias = b_ref[0, :, 384:]
    for i in range(SEQ // 512):
        rows = slice(i * 512, (i + 1) * 512)
        act, slope = gelu_and_slope(mm(hlow_ref[rows, :], w_up[...]) + bias)
        act = act.astype(BF)
        act_ref[rows, :] = act
        slope_ref[rows, :] = slope.astype(BF)
        acc[rows, :] += mm(act, w_down[...])

    @pl.when(j < 6)
    def _():
        for c in fetch(j + 2, slot):
            c.start()

    @pl.when(j == 7)
    def _():
        inward.finish()
        early.wait()
        vg_ref[...] = jnp.zeros_like(vg_ref)

        def body(rows):
            hidden = normed1_ref[rows, :] * vec_ref[1:2, :] + vec_ref[2:3, :]
            normed, inv = norm_rows(hidden + (acc[rows, :] + vec_ref[3:4, :]))
            out_ref[rows, :] = (normed * vec_ref[4:5, :] + vec_ref[5:6, :]).astype(BF)
            c = cot_buf[rows, :].astype(F32)
            r2 = norm_rows_back(c * vec_ref[4:5, :], normed, inv)
            r2_ref[rows, :] = r2
            vg_ref[0:1, :] += jnp.sum(c * normed, axis=0, keepdims=True)
            vg_ref[1:2, :] += jnp.sum(c, axis=0, keepdims=True)
            vg_ref[2:3, :] += jnp.sum(r2.astype(BF).astype(F32), axis=0, keepdims=True)

        row_blocks(body)
        gu.finish()
        gd.finish()


def ff_fwd(x, att, wo, vec, bu, cot, cot_first, wu, wd):
    width, units = wu.shape
    n = units // 8
    return pl.pallas_call(
        ff_fwd_kernel,
        grid=(8,),
        in_specs=[
            const(*x.shape),
            const(SEQ, width),
            const(width, width),
            const(8, width),
            pl.BlockSpec((1, 1, bu.shape[2]), lambda j: (j, 0, 0)),
            ANY,
            ANY,
            ANY,
            ANY,
        ],
        out_specs=[
            ANY,
            ANY,
            pl.BlockSpec((SEQ, n), lambda j: (0, j)),
            pl.BlockSpec((SEQ, n), lambda j: (0, j)),
            const(SEQ, width),
            const(SEQ, width),
            const(SEQ, 128),
            const(SEQ, width),
            const(SEQ, width),
            const(8, width),
        ],
        out_shape=[
            jax.ShapeDtypeStruct(wu.shape, BF),
            jax.ShapeDtypeStruct(wd.shape, BF),
            jax.ShapeDtypeStruct((SEQ, units), BF),
            jax.ShapeDtypeStruct((SEQ, units), BF),
            jax.ShapeDtypeStruct((SEQ, width), BF),
            jax.ShapeDtypeStruct((SEQ, width), F32),
            jax.ShapeDtypeStruct((SEQ, 128), F32),
            jax.ShapeDtypeStruct((SEQ, width), BF),
            jax.ShapeDtypeStruct((SEQ, width), F32),
            jax.ShapeDtypeStruct((8, width), F32),
        ],
        input_output_aliases={7: 0, 8: 1},
        scratch_shapes=[
            pltpu.VMEM((SEQ, width), F32),
            pltpu.VMEM((2, width, n), BF),
            pltpu.VMEM((2, n, width), BF),
            pltpu.VMEM((SEQ, width), BF),
            pltpu.VMEM((SEQ - SEQ // CHUNKS, width // 4), BF),
            DMA((2, 2)),
            DMA((32,)),
            DMA((32,)),
            DMA((32,)),
            DMA((32,)),
            sems_of_exchange(),
            DMA,
        ],
        compiler_params=pltpu.CompilerParams(vmem_limit_bytes=VMEM_LIMIT, collective_id=2, has_side_effects=True),
        name="ff_fwd",
    )(x, att, wo, vec, bu, cot, cot_first, wu, wd)


ORDER = (7, 6, 1, 3, 5, 0, 2, 4)
PAIRS = (7, 6, 3, 2, 5, 4, 1, 0)


def slot_at(j):
    return jnp.where(j < 2, 7 - j, jnp.where(j < 5, 2 * j - 3, 2 * j - 10))


def pair_at(j):
    return jnp.where(j < 2, 7 - j, jnp.where(j < 4, 5 - j, jnp.where(j < 6, 9 - j, 7 - j)))


def sum_rows(dst, *srcs):
    n = dst.shape[0]
    step = min(n, 64)

    def run(i, carry):
        rows = pl.ds(pl.multiple_of(i * step, step), step)
        total = srcs[0][rows, :].astype(F32)
        for src in srcs[1:]:
            total += src[rows, :].astype(F32)
        dst[rows, :] = total.astype(BF)
        return carry

    lax.fori_loop(0, n // step, run, 0)


class Fold:
    @staticmethod
    def scratch(a, b):
        return [
            pltpu.VMEM((2, a, b), BF),
            pltpu.VMEM((4, a, b), BF),
            pltpu.VMEM((a, b), BF),
            pltpu.VMEM((2, a // 2, b), BF),
            DMA((12,)),
        ]

    def __init__(self, peers, order, stage, land, corner, land_corner, sems):
        self.peers, self.order, self.stage, self.land, self.corner, self.land_corner, self.sems = (
            peers, order, stage, land, corner, land_corner, sems,
        )
        self.half = corner.shape[0] // 2

    def to_core(self, p):
        k = (self.order[p] - 1) // 2
        return send(self.peers, "core", self.stage.at[p % 2], self.land.at[k], self.sems.at[4 + k], self.sems.at[k])

    def to_side(self, h):
        src = self.corner.at[pl.ds(h * self.half, self.half), :]
        return send(self.peers, "xy"[1 - h], src, self.land_corner.at[h], self.sems.at[10 + h], self.sems.at[8 + h])

    def before(self, j):
        for p in range(2, 8):
            if self.order[p - 2] % 2 == 0:
                continue

            @pl.when(j == p)
            def _(p=p):
                self.to_core(p - 2).wait_send()

    def from_core(self, t):
        k = t // 2
        self.to_core(self.order.index(t + 1)).wait_recv()
        return self.land.at[k]

    def after(self, j, outs):
        for p, t in enumerate(self.order):
            @pl.when(j == p)
            def _(p=p, t=t):
                mine = self.stage.at[p % 2]
                if t % 2 == 1:
                    self.to_core(p).start()
                    return
                theirs = self.from_core(t)
                if t == 6:
                    sum_rows(self.corner, mine, theirs)
                    self.to_side(0).start()
                    self.to_side(1).start()
                    return
                out = outs[t]
                if t == 0:
                    sum_rows(out, mine, theirs)
                    return
                h = t // 2 - 1
                self.to_side(h).wait_recv()
                for q in range(2):
                    rows = pl.ds(q * self.half, self.half)
                    more = (self.land_corner.at[h],) if q == h else ()
                    sum_rows(out.at[rows, :], mine.at[rows, :], theirs.at[rows, :], *more)

    def finish(self):
        for p in (6, 7):
            if self.order[p] % 2:
                self.to_core(p).wait_send()
        self.to_side(0).wait_send()
        self.to_side(1).wait_send()


class Cross:
    def __init__(self, peers, for_x, for_y, land_x, land_y, sems, cuts=1):
        self.peers, self.sems, self.cuts = peers, sems, cuts
        self.ends = {"x": (for_x, land_x), "y": (for_y, land_y)}
        self.n = land_x.shape[0] // cuts

    def copy(self, way, h=0):
        src, dst = self.ends[way]
        rows = pl.ds(h * self.n, self.n)
        at = 4 * h + 2 * "xy".index(way)
        return send(self.peers, way, src.at[rows, :], dst.at[rows, :], self.sems.at[at], self.sems.at[at + 1])

    def start(self, ways="xy", h=0):
        for way in ways:
            self.copy(way, h).start()

    def finish(self, own, out):
        for h in range(self.cuts):
            for way in "xy":
                self.copy(way, h).wait()
        sum_rows(out, own, self.ends["x"][1], self.ends["y"][1])


class Whole:
    @staticmethod
    def scratch(a, b):
        return [
            pltpu.VMEM((8 * a, b), BF),
            pltpu.VMEM((4, a, b), BF),
            pltpu.VMEM((4, a, b), BF),
            pltpu.VMEM((2, a // 2, b), BF),
            pltpu.VMEM((a, b), BF),
            pltpu.VMEM((a, b), BF),
            DMA((12,)),
            DMA((4,)),
        ]

    def __init__(self, peers, total, land, kept, land_corner, land_x, land_y, sems, c_sems):
        self.peers, self.total, self.land, self.kept, self.land_corner, self.sems = (
            peers, total, land, kept, land_corner, sems,
        )
        self.a = land.shape[1]
        self.half = self.a // 2
        self.cross = Cross(peers, kept.at[1], kept.at[2], land_x, land_y, c_sems)

    def block(self, t):
        return self.total.at[pl.ds(t * self.a, self.a), :]

    def to_core(self, k):
        return send(
            self.peers, "core", self.block(2 * k + 1), self.land.at[k], self.sems.at[4 + k], self.sems.at[k]
        )

    def to_side(self, h):
        src = self.kept.at[3, pl.ds(h * self.half, self.half), :]
        return send(self.peers, "xy"[1 - h], src, self.land_corner.at[h], self.sems.at[10 + h], self.sems.at[8 + h])

    def start(self):
        for k in (3, 1, 2, 0):
            self.to_core(k).start()

    def corner(self):
        for k in (3, 1, 2, 0):
            self.to_core(k).wait_recv()
            sum_rows(self.kept.at[k], self.block(2 * k), self.land.at[k])
            if k == 3:
                self.to_side(0).start()
                self.to_side(1).start()

    def sides(self):
        for h in range(2):
            self.to_side(h).wait_recv()
            rows = pl.ds(h * self.half, self.half)
            mine = self.kept.at[1 + h, rows, :]
            sum_rows(mine, mine, self.land_corner.at[h])
        self.cross.start()

    def finish(self, out):
        self.cross.finish(self.kept.at[0], out)
        for k in range(4):
            self.to_core(k).wait_send()
        for h in range(2):
            self.to_side(h).wait_send()


class Deal:
    def __init__(self, peers, total, by_rows, land, sems):
        self.peers, self.total, self.by_rows, self.land, self.sems = peers, total, by_rows, land, sems

    def part(self, s):
        n = self.total.shape[0 if self.by_rows else 1] // 4
        return self.total.at[pl.ds(s * n, n), :] if self.by_rows else self.total.at[:, pl.ds(s * n, n)]

    def copy(self, s):
        return send(self.peers, 4 - s, self.part(s), self.land.at[s - 1], self.sems.at[2 + s], self.sems.at[s - 1])

    def start(self):
        for s in (2, 1, 3):
            self.copy(s).start()

    def finish(self, out):
        for s in (1, 2, 3):
            self.copy(s).wait()
        sum_rows(out, self.part(0), self.land.at[0], self.land.at[1], self.land.at[2])


class LineDeal:
    def __init__(self, peers, total, by_rows, land, tmp, sems):
        self.peers, self.land, self.tmp, self.sems = peers, land, tmp, sems
        self.part = Deal(peers, total, by_rows, None, None).part

    def copy(self, up, b, row, src):
        go = (b - row if up else row - b) - 1
        at = (0 if up else 3) + go
        return send(
            self.peers, 1 if up else 3, src, self.land.at[0 if up else 1, go], self.sems.at[at], self.sems.at[6 + at]
        )

    def slot(self, b, row):
        return (row - b) % 4

    def first(self, up, b, row):
        return self.copy(up, b, row, self.part(self.slot(b, row)))

    def pass_on(self, up, b, row):
        go = (b - row if up else row - b) - 1
        tmp = self.tmp.at[0 if up else 1, go]
        return self.copy(up, b, row, tmp), tmp

    def got(self, up, b, row):
        go = b - row if up else row - b
        at = (0 if up else 3) + go
        land = self.land.at[0 if up else 1, go]
        send(self.peers, 1 if up else 3, land, land, self.sems.at[at], self.sems.at[6 + at]).wait_recv()
        return land

    STEPS = (((1, True, 3), (1, True, 2), (2, False, 0), (2, False, 1)), ((2, True, 3), (1, False, 0)))
    STARTS = ((0, True, 3), (0, True, 2), (0, True, 1), (3, False, 0), (3, False, 1), (3, False, 2))

    def when(self, row, run):
        pl.when(self.peers.r == row)(run)

    def start(self):
        for row, up, b in self.STARTS:
            self.when(row, lambda up=up, b=b, row=row: self.first(up, b, row).start())

    def step(self, k):
        for row, up, b in self.STEPS[k]:
            def run(row=row, up=up, b=b):
                land = self.got(up, b, row)
                copy, tmp = self.pass_on(up, b, row)
                sum_rows(tmp, land, self.part(self.slot(b, row)))
                copy.start()

            self.when(row, run)

    def finish(self, out):
        for row in range(4):
            def run(row=row):
                lands = []
                if row > 0:
                    lands.append(self.got(True, row, row))
                if row < 3:
                    lands.append(self.got(False, row, row))
                sum_rows(out, self.part(0), *lands)

            self.when(row, run)
        for row, up, b in self.STARTS:
            self.when(row, lambda up=up, b=b, row=row: self.first(up, b, row).wait_send())
        for moves in self.STEPS:
            for row, up, b in moves:
                self.when(row, lambda up=up, b=b, row=row: self.pass_on(up, b, row)[0].wait_send())


class Spread:
    def __init__(self, peers, own, place, sems):
        d = lax.axis_index("dp")
        self.peers, self.own, self.sems, self.here = peers, own, sems, place(d)
        self.from_x = place(lax.rem(d + 2, 4))

    def local(self):
        return pltpu.make_async_copy(self.own, self.here, self.sems.at[6])

    def copies(self):
        s = self.sems
        return (
            send(self.peers, "x", self.own, self.here, s.at[0], s.at[1]),
            send(self.peers, "core", self.own, self.here, s.at[2], s.at[3]),
            send(self.peers, "core", self.from_x, self.from_x, s.at[4], s.at[5]),
        )

    def start(self):
        to_x, to_core, _ = self.copies()
        to_x.start()
        to_core.start()
        self.local().start()

    def relay(self):
        to_x, _, on = self.copies()
        to_x.wait_recv()
        on.start()

    def finish(self):
        to_x, to_core, on = self.copies()
        to_x.wait_send()
        to_core.wait()
        on.wait()
        self.local().wait()


class Outward:
    def __init__(self, peers, rows, block, buf, sems, parts=(2, 1, 3, 0)):
        self.peers, self.rows, self.block, self.buf, self.sems = peers, rows, block, buf, sems
        self.away = [s for s in parts if s]
        self.stays = 0 in parts
        self.n = SEQ // CHUNKS

    def ends(self, s, first, count):
        f = self.block.shape[1]
        mine = pl.ds(pl.multiple_of(self.peers.r * SEQ + first * self.n, self.n), count * self.n)
        return self.rows.at[pl.ds(first * self.n, count * self.n), pl.ds(s * f, f)], self.block.at[mine, :]

    def copy(self, s, k):
        return send(self.peers, 4 - s, *self.ends(s, k, 1), self.sems.at[0, s, k], self.sems.at[1, s, k])

    def load(self):
        return pltpu.make_async_copy(self.ends(0, 0, CHUNKS)[0], self.buf, self.sems.at[0, 0, 0])

    def store(self):
        src, dst = self.ends(0, 0, CHUNKS)
        return pltpu.make_async_copy(src if self.buf is None else self.buf, dst, self.sems.at[1, 0, 0])

    def start(self, *chunks):
        for k in chunks:
            for s in self.away:
                self.copy(s, k).start()

    def settle(self):
        self.load().wait()
        self.store().start()

    def finish(self):
        if self.stays:
            self.store().wait()
        for k in range(CHUNKS):
            for s in self.away:
                self.copy(s, k).wait()


def ff_down_bwd_kernel(
    r2_ref, wd_ref, act_ref, slope_ref, out, out_block, gp_ref, bu_ref, kept_ref,
    gfed, out_own, stage, land, corner, land_corner, f_sems, o_sems,
):
    j = pl.program_id(0)
    peers = Peers()
    outward = Outward(peers, out, out_block, out_own, o_sems, (2, 0))
    fold = Fold(peers, ORDER, stage, land, corner, land_corner, f_sems)

    @pl.when(j == 0)
    def _():
        peers.hello(ALL_PEERS)
        outward.load().start()

        def body(rows):
            gfed[rows, :] = r2_ref[rows, :].astype(BF)

        row_blocks(body)
        peers.meet(ALL_PEERS)
        outward.start(*range(CHUNKS))

    bsum = jnp.zeros((1, bu_ref.shape[2]), F32)
    for i in range(SEQ // 256):
        rows = slice(i * 256, (i + 1) * 256)
        g = (mm_t(gfed[rows, :], wd_ref[...]) * slope_ref[rows, :].astype(F32)).astype(BF)
        gp_ref[rows, :] = g
        bsum += jnp.sum(g.astype(F32), axis=0, keepdims=True)
    bu_ref[0] = bsum
    fold.before(j)
    stage[lax.rem(j, 2)] = tmm(act_ref[...], gfed[...]).astype(BF)
    fold.after(j, {t: kept_ref.at[0] for t in (0, 2, 4)})

    @pl.when(j == 1)
    def _():
        outward.settle()

    @pl.when(j == 7)
    def _():
        fold.finish()
        outward.finish()


def kept_spec(a, b):
    return pl.BlockSpec((1, a, b), lambda j: (jnp.maximum(j - 5, 0), 0, 0))


def ff_down_bwd(r2, wd, act, slope, out):
    units, width = wd.shape
    n = units // 8
    return pl.pallas_call(
        ff_down_bwd_kernel,
        grid=(8,),
        in_specs=[
            const(SEQ, width),
            pl.BlockSpec((n, width), lambda j: (slot_at(j), 0)),
            pl.BlockSpec((SEQ, n), lambda j: (0, slot_at(j))),
            pl.BlockSpec((SEQ, n), lambda j: (0, slot_at(j))),
            ANY,
        ],
        out_specs=[
            ANY,
            pl.BlockSpec((SEQ, n), lambda j: (0, slot_at(j))),
            pl.BlockSpec((1, 1, n), lambda j: (slot_at(j), 0, 0)),
            kept_spec(n, width),
        ],
        out_shape=[
            jax.ShapeDtypeStruct((4 * SEQ, width // 4), BF),
            jax.ShapeDtypeStruct((SEQ, units), BF),
            jax.ShapeDtypeStruct((8, 1, n), F32),
            jax.ShapeDtypeStruct((3, n, width), BF),
        ],
        scratch_shapes=[
            pltpu.VMEM((SEQ, width), BF),
            pltpu.VMEM((SEQ, width // 4), BF),
            *Fold.scratch(n, width),
            sems_of_exchange(),
        ],
        compiler_params=pltpu.CompilerParams(vmem_limit_bytes=VMEM_LIMIT, collective_id=3, has_side_effects=True),
        name="ff_down_bwd",
    )(r2, wd, act, slope, out)


def ff_up_bwd_kernel(
    r2_ref, hlow_ref, gp_ref, wu_ref, normed1_ref, inv1_ref, vec_ref, out, out_block_in, kept_d,
    out_block, r1_ref, gattn_ref, vg_ref, kept_ref, own_ref,
    hlow_t, stage, land, corner, land_corner, f_sems, own_d, land_x, land_y, c_sems, o_sems,
):
    j = pl.program_id(0)
    peers = Peers()
    outward = Outward(peers, out, out_block, None, o_sems, (1, 3))
    fold = Fold(peers, ORDER, stage, land, corner, land_corner, f_sems)
    cross = Cross(peers, kept_d.at[1], kept_d.at[2], land_x, land_y, c_sems, 2)
    load = pltpu.make_async_copy(kept_d.at[0], own_d, c_sems.at[8])

    @pl.when(j == 0)
    def _():
        peers.hello(ALL_PEERS)
        load.start()
        r1_ref[...] = r2_ref[...]
        for i in range(SEQ // 256):
            rows = slice(i * 256, (i + 1) * 256)
            hlow_t[:, rows] = jnp.transpose(hlow_ref[rows, :])
        peers.meet(ALL_PEERS)
        cross.start()
        outward.start(*range(CHUNKS))

    fold.before(j)
    stage[lax.rem(j, 2)] = mm(hlow_t[...], gp_ref[...]).astype(BF)
    fold.after(j, {t: kept_ref.at[0] for t in (0, 2, 4)})

    @pl.when(j == 1)
    def _():
        cross.start(h=1)

    r1_ref[...] += mm_t(gp_ref[...], wu_ref[...])

    @pl.when(j == 7)
    def _():
        vg_ref[...] = jnp.zeros_like(vg_ref)

        def body(rows):
            gh = r1_ref[rows, :]
            normed = normed1_ref[rows, :]
            r1 = norm_rows_back(gh * vec_ref[1:2, :], normed, inv1_ref[rows, 0:1])
            r1_ref[rows, :] = r1
            low = r1.astype(BF)
            gattn_ref[rows, :] = low
            vg_ref[0:1, :] += jnp.sum(gh * normed, axis=0, keepdims=True)
            vg_ref[1:2, :] += jnp.sum(gh, axis=0, keepdims=True)
            vg_ref[2:3, :] += jnp.sum(low.astype(F32), axis=0, keepdims=True)

        row_blocks(body)
        load.wait()
        cross.finish(own_d, own_ref)
        fold.finish()
        outward.finish()


def ff_up_bwd(r2, hlow, gp, wu, normed1, inv1, vec, out, out_block, kept_d):
    width, units = wu.shape
    n = units // 8
    return pl.pallas_call(
        ff_up_bwd_kernel,
        grid=(8,),
        in_specs=[
            const(SEQ, width),
            const(SEQ, width),
            pl.BlockSpec((SEQ, n), lambda j: (0, slot_at(j))),
            pl.BlockSpec((width, n), lambda j: (0, slot_at(j))),
            const(SEQ, width),
            const(SEQ, 128),
            const(8, width),
            ANY,
            ANY,
            ANY,
        ],
        out_specs=[
            ANY,
            const(SEQ, width),
            const(SEQ, width),
            const(8, width),
            kept_spec(width, n),
            const(n, width),
        ],
        out_shape=[
            jax.ShapeDtypeStruct(out_block.shape, BF),
            jax.ShapeDtypeStruct((SEQ, width), F32),
            jax.ShapeDtypeStruct((SEQ, width), BF),
            jax.ShapeDtypeStruct((8, width), F32),
            jax.ShapeDtypeStruct((3, width, n), BF),
            jax.ShapeDtypeStruct((n, width), BF),
        ],
        input_output_aliases={8: 0},
        scratch_shapes=[
            pltpu.VMEM((width, SEQ), BF),
            *Fold.scratch(width, n),
            pltpu.VMEM((n, width), BF),
            pltpu.VMEM((n, width), BF),
            pltpu.VMEM((n, width), BF),
            DMA((9,)),
            sems_of_exchange(),
        ],
        compiler_params=pltpu.CompilerParams(vmem_limit_bytes=VMEM_LIMIT, collective_id=4, has_side_effects=True),
        name="ff_up_bwd",
    )(r2, hlow, gp, wu, normed1, inv1, vec, out, out_block, kept_d)


def attend_bwd_kernel(
    gattn_ref, wo_ref, att_ref, qkv_ref, linv_ref, p_ref, x_ref, att_all, tot_d, kept_u,
    g_ref, gsum_ref, tot_q, tot_o, down_ref, up_ref,
    x_t, ds_ref,
    q_stage, q_land, q_corner, q_land_corner, q_sems,
    q_kept, q_x, q_y, q_c, o_total, o_land, o_kept, o_land_corner, o_x, o_y, o_sems, o_c,
    zd_land, zd_sems, own_u, land_x, land_y, c_sems, tot_u, zu_land, zu_sems,
):
    j = pl.program_id(0)
    peers = Peers()
    fold_q = Fold(peers, PAIRS, q_stage, q_land, q_corner, q_land_corner, q_sems)
    whole_o = Whole(peers, o_total, o_land, o_kept, o_land_corner, o_x, o_y, o_sems, o_c)
    cross_q = Cross(peers, q_kept.at[1], q_kept.at[2], q_x, q_y, q_c)
    deal_d = Deal(peers, tot_d, False, zd_land, zd_sems)
    cross_u = Cross(peers, kept_u.at[1], kept_u.at[2], land_x, land_y, c_sems)
    deal_u = Deal(peers, tot_u, True, zu_land, zu_sems)
    load_u = pltpu.make_async_copy(kept_u.at[0], own_u, c_sems.at[4])

    @pl.when(j == 0)
    def _():
        load_u.start()
        peers.hello(ALL_PEERS)
        f = x_ref.shape[2]
        for s in range(4):
            x_t[s * f : (s + 1) * f, :] = jnp.transpose(x_ref[s])
        load_u.wait()
        peers.meet(ALL_PEERS)
        cross_u.start()
        deal_d.start()
        o_total[...] = tmm(att_all[...], gattn_ref[...]).astype(BF)
        whole_o.start()

    @pl.when(j == 1)
    def _():
        whole_o.corner()

    @pl.when(j == 3)
    def _():
        whole_o.sides()

    @pl.when(j == 6)
    def _():
        whole_o.finish(tot_o)

    @pl.when(j == 4)
    def _():
        cross_u.finish(own_u, tot_u)
        deal_u.start()
        deal_d.finish(down_ref)

    lane = lax.broadcasted_iota(jnp.int32, (SEQ, 128), 1)
    scale = HD ** (-0.5)
    fold_q.before(j)
    q = qkv_ref[:, 0:128]
    k = qkv_ref[:, 128:256]
    v = qkv_ref[:, 256:384]
    do = mm_t(gattn_ref[...], wo_ref[...]).astype(BF).astype(F32) * linv_ref[...]
    prod = do * att_ref[...].astype(F32)
    dob = do.astype(BF)
    q_t = jnp.transpose(q)
    k_t = jnp.transpose(k)
    do_t = jnp.transpose(dob)
    dq_t, dk_t, dv_t = [], [], []
    for h in range(2):
        mine = (lane < HD) if h == 0 else (lane >= HD)
        delta = jnp.sum(jnp.where(mine, prod, 0.0), axis=1, keepdims=True)
        dom = jnp.where(mine, dob, jnp.zeros_like(dob))
        for i in range(SEQ // QB):
            rows = slice(i * QB, (i + 1) * QB)
            dp = mm_t(dom[rows], v)
            ds_ref[h, rows, :] = (p_ref[h, rows, :].astype(F32) * (dp - delta[rows])).astype(BF)
        feats = slice(h * HD, (h + 1) * HD)
        dq_t.append(mm_t(k_t[feats], ds_ref[h]))
        dk_t.append(mm(q_t[feats], ds_ref[h]))
        dv_t.append(mm(do_t[feats], p_ref[h]))
    g_ref[:, 0:128] = (jnp.transpose(jnp.concatenate(dq_t, 0)) * scale).astype(BF)
    g_ref[:, 128:256] = (jnp.transpose(jnp.concatenate(dk_t, 0)) * scale).astype(BF)
    g_ref[:, 256:384] = jnp.transpose(jnp.concatenate(dv_t, 0)).astype(BF)
    gsum_ref[0] = jnp.sum(g_ref[...].astype(F32), axis=0, keepdims=True)
    q_stage[lax.rem(j, 2)] = mm(x_t[...], g_ref[...]).astype(BF)
    fold_q.after(j, {t: q_kept.at[t // 2] for t in (0, 2, 4)})

    @pl.when(j == PAIRS.index(2))
    def _():
        cross_q.start("x")

    @pl.when(j == PAIRS.index(4))
    def _():
        cross_q.start("y")

    @pl.when(j == 7)
    def _():
        deal_u.finish(up_ref)
        fold_q.finish()
        cross_q.finish(q_kept.at[0], tot_q)


def attend_bwd(gattn, wo, att, qkv, linv, p, x, tot_d, kept_u):
    width = wo.shape[1]
    heads = 128
    n = tot_d.shape[0]
    return pl.pallas_call(
        attend_bwd_kernel,
        grid=(8,),
        in_specs=[
            const(SEQ, width),
            pl.BlockSpec((heads, width), lambda j: (pair_at(j), 0)),
            pl.BlockSpec((SEQ, heads), lambda j: (0, pair_at(j))),
            pl.BlockSpec((SEQ, 3 * heads), lambda j: (0, pair_at(j))),
            pl.BlockSpec((SEQ, heads), lambda j: (0, pair_at(j))),
            pl.BlockSpec((2, SEQ, SEQ), lambda j: (pair_at(j), 0, 0)),
            const(*x.shape),
            const(SEQ, width),
            const(n, width),
            ANY,
        ],
        out_specs=[
            pl.BlockSpec((SEQ, 3 * heads), lambda j: (0, pair_at(j))),
            pl.BlockSpec((1, 1, 3 * heads), lambda j: (pair_at(j), 0, 0)),
            const(width, 3 * heads),
            const(heads, width),
            const(n, width // 4),
            const(width // 4, n),
        ],
        out_shape=[
            jax.ShapeDtypeStruct((SEQ, 24 * heads), BF),
            jax.ShapeDtypeStruct((8, 1, 3 * heads), F32),
            jax.ShapeDtypeStruct((width, 3 * heads), BF),
            jax.ShapeDtypeStruct((heads, width), BF),
            jax.ShapeDtypeStruct((n, width // 4), BF),
            jax.ShapeDtypeStruct((width // 4, n), BF),
        ],
        scratch_shapes=[
            pltpu.VMEM((width, SEQ), BF),
            pltpu.VMEM((2, SEQ, SEQ), BF),
            *Fold.scratch(width, 3 * heads),
            pltpu.VMEM((3, width, 3 * heads), BF),
            pltpu.VMEM((width, 3 * heads), BF),
            pltpu.VMEM((width, 3 * heads), BF),
            DMA((4,)),
            *Whole.scratch(heads, width),
            pltpu.VMEM((3, n, width // 4), BF),
            DMA((6,)),
            pltpu.VMEM((width, n), BF),
            pltpu.VMEM((width, n), BF),
            pltpu.VMEM((width, n), BF),
            DMA((5,)),
            pltpu.VMEM((width, n), BF),
            pltpu.VMEM((3, width // 4, n), BF),
            DMA((6,)),
        ],
        compiler_params=pltpu.CompilerParams(vmem_limit_bytes=VMEM_LIMIT, collective_id=5, has_side_effects=True),
        name="attend_bwd",
    )(gattn, wo, att, qkv, linv, p, x, att, tot_d, kept_u)


def last_kernel(
    tot_q, tot_o, own_d, own_u, g_part, u_part, vec1, vec2, g, w, r1,
    x_block, gq, go, gd, gu, slot_out, feat_ref,
    g_buf, w_buf, acc, xg, ld_sems,
    q_land, q_tmp, q_z, q_sum, o_land, o_tmp, o_z, o_sum,
    vec_ref, v1, v2, v3, l1, l2, l3, l4, v_own, v_sems, out_sems, s_sems,
):
    peers = Peers()
    outward = Outward(peers, xg, x_block, None, out_sems)
    deal_q = LineDeal(peers, tot_q, True, q_land, q_tmp, q_z)
    deal_o = LineDeal(peers, tot_o, False, o_land, o_tmp, o_z)
    loads = (
        pltpu.make_async_copy(w, w_buf, ld_sems.at[0]),
        pltpu.make_async_copy(g, g_buf, ld_sems.at[1]),
        pltpu.make_async_copy(r1, acc, ld_sems.at[2]),
    )
    peers.hello(ALL_PEERS)
    for c in loads:
        c.start()

    def products(k):
        rows = slice(k * (SEQ // CHUNKS), (k + 1) * (SEQ // CHUNKS))
        xg[rows, :] = (mm_t(g_buf[rows, :], w_buf[...]) + acc[rows, :]).astype(BF)
        outward.start(k)

    vec_ref[...] = jnp.zeros_like(vec_ref)
    heads3, units = g_part.shape[2], u_part.shape[2]
    for k, t in enumerate((0, 4, 2, 6, 1, 5, 3, 7)):
        k = k if k < 4 else k + 8
        for i in range(heads3 // 128):
            vec_ref[k, i : i + 1, :] = g_part[t, :, i * 128 : (i + 1) * 128]
        for i in range(units // 128):
            at = heads3 // 128 + i
            vec_ref[k, at : at + 1, :] = u_part[t, :, i * 128 : (i + 1) * 128]
    f = vec1.shape[1] // 4
    rows = [(vec1, 2), (vec1, 0), (vec1, 1), (vec2, 2), (vec2, 0), (vec2, 1)]
    for k in range(4):
        for v, (ref, row) in enumerate(rows):
            for i in range(f // 128):
                at = v * (f // 128) + i
                first = k * f + i * 128
                vec_ref[4 + 2 * k + at // 8, at % 8 : at % 8 + 1, :] = ref[row : row + 1, first : first + 128]

    def rows_at(ref):
        n = ref.shape[0] // 4
        return lambda q: ref.at[pl.ds(pl.multiple_of(q * n, n), n), :]

    def cols_at(ref, first, n):
        return lambda q: ref.at[:, pl.ds(pl.multiple_of(first + q * n, n), n)]

    heads = q_sum.shape[1] // 3
    units = own_u.shape[1]
    spread_d = Spread(peers, own_d, rows_at(gd), s_sems.at[0])
    spread_u = Spread(peers, own_u, cols_at(gu, 0, units), s_sems.at[1])
    spread_o = Spread(peers, o_sum, rows_at(go), s_sems.at[2])
    spread_q = [
        Spread(peers, q_sum.at[:, pl.ds(i * heads, heads)], cols_at(gq, 4 * i * heads, heads), s_sems.at[3 + i])
        for i in range(3)
    ]
    spread_v = Spread(peers, v_own, lambda q: slot_out.at[q], s_sems.at[6])

    to_core = send(peers, "core", vec_ref.at[pl.ds(4, 12)], l1, v_sems.at[0], v_sems.at[1])
    to_x = send(peers, "x", v1.at[pl.ds(2, 10)], l2, v_sems.at[2], v_sems.at[3])
    to_y = send(peers, "y", v2.at[pl.ds(1, 11)], l3, v_sems.at[4], v_sems.at[5])
    to_rows = []
    for i in (1, 2, 3):
        to_rows.append(send(peers, i, v3.at[0], l4.at[i - 1, 0], v_sems.at[6 + 4 * i], v_sems.at[7 + 4 * i]))
        src = v3.at[pl.ds(4 + 2 * (4 - i), 2)]
        to_rows.append(send(peers, i, src, l4.at[i - 1, pl.ds(1, 2)], v_sems.at[8 + 4 * i], v_sems.at[9 + 4 * i]))

    peers.meet(ALL_PEERS)
    deal_o.start()
    deal_q.start()
    to_core.start()
    spread_d.start()
    spread_u.start()
    for c in loads:
        c.wait()
    products(0)
    deal_o.step(0)
    deal_q.step(0)
    products(1)
    to_core.wait()
    v1[0:4] = vec_ref[0:4] + l1[8:12]
    v1[4:12] = vec_ref[4:12] + l1[0:8]
    to_x.start()
    deal_o.step(1)
    deal_q.step(1)
    products(2)
    products(3)
    outward.store().start()
    to_x.wait()
    v2[0:2] = v1[0:2] + l2[0:2]
    v2[4:12] = v1[4:12] + l2[2:10]
    v2[2:4] = v1[2:4]
    to_y.start()
    spread_d.relay()
    spread_u.relay()
    deal_o.finish(o_sum)
    spread_o.start()
    deal_q.finish(q_sum)
    for sp in spread_q:
        sp.start()
    to_y.wait()
    v3[0:1] = v2[0:1] + l3[0:1]
    v3[4:12] = v2[4:12] + l3[3:11]
    for c in to_rows:
        c.start()
    spread_o.relay()
    for sp in spread_q:
        sp.relay()
    for c in to_rows:
        c.wait()
    v_own[...] = v3[0] + l4[0, 0] + l4[1, 0] + l4[2, 0]
    feat_ref[...] = v3[4:6] + l4[0, 1:3] + l4[1, 1:3] + l4[2, 1:3]
    spread_v.start()
    spread_v.relay()
    for sp in (spread_d, spread_u, spread_o, spread_v, *spread_q):
        sp.finish()
    outward.finish()


def last(tot_q, tot_o, own_d, own_u, g_part, u_part, vec1, vec2, g, w, r1):
    width = r1.shape[1]
    part = width // 4
    n = own_d.shape[0]
    heads = tot_o.shape[0]
    vmem = pl.BlockSpec(memory_space=pltpu.VMEM)

    def bufs(a, b, by_rows):
        piece = (a // 4, b) if by_rows else (a, b // 4)
        return [pltpu.VMEM((2, 3, *piece), BF), pltpu.VMEM((2, 2, *piece), BF), DMA((12,)), pltpu.VMEM(piece, BF)]

    return pl.pallas_call(
        last_kernel,
        in_specs=[vmem] * 8 + [ANY] * 3,
        out_specs=[ANY, ANY, ANY, ANY, ANY, ANY, vmem],
        out_shape=[
            jax.ShapeDtypeStruct((4 * SEQ, part), BF),
            jax.ShapeDtypeStruct((part, 12 * heads), BF),
            jax.ShapeDtypeStruct((4 * heads, part), BF),
            jax.ShapeDtypeStruct((4 * n, part), BF),
            jax.ShapeDtypeStruct((part, 4 * n), BF),
            jax.ShapeDtypeStruct((4, 8, 128), F32),
            jax.ShapeDtypeStruct((2, 8, 128), F32),
        ],
        scratch_shapes=[
            pltpu.VMEM((SEQ, 24 * heads), BF),
            pltpu.VMEM((width, 24 * heads), BF),
            pltpu.VMEM((SEQ, width), F32),
            pltpu.VMEM((SEQ, width), BF),
            DMA((3,)),
            *bufs(width, 3 * heads, True),
            *bufs(heads, width, False),
            pltpu.VMEM((16, 8, 128), F32),
            pltpu.VMEM((12, 8, 128), F32),
            pltpu.VMEM((12, 8, 128), F32),
            pltpu.VMEM((12, 8, 128), F32),
            pltpu.VMEM((12, 8, 128), F32),
            pltpu.VMEM((10, 8, 128), F32),
            pltpu.VMEM((11, 8, 128), F32),
            pltpu.VMEM((3, 3, 8, 128), F32),
            pltpu.VMEM((8, 128), F32),
            DMA((24,)),
            sems_of_exchange(),
            DMA((7, 7)),
        ],
        compiler_params=pltpu.CompilerParams(vmem_limit_bytes=VMEM_LIMIT, collective_id=6, has_side_effects=True),
        name="last",
    )(tot_q, tot_o, own_d, own_u, g_part, u_part, vec1, vec2, g, w, r1)


def whole_sequences(
    tokens, segments, w_query, b_query, w_key, w_value, b_value, w_out, b_out, norm1_gain, norm1_shift,
    w_up, b_up, w_down, b_down, norm2_gain, norm2_shift, cotangent,
):
    R = lax.axis_size("row")
    feat = tokens.shape[1]
    hq = b_query.shape[0] // 4
    unit = b_up.shape[0] // 4
    vectors = (b_out, norm1_gain, norm1_shift, b_down, norm2_gain, norm2_shift, b_query, b_value, b_up)
    size = sum(v.shape[0] for v in vectors)
    first_at, packed = 0, 0.0
    for v in vectors:
        packed += jnp.pad(v.astype(F32), (first_at, size - first_at - v.shape[0]))
        first_at += v.shape[0]
    vectors = packed.reshape(1, -1)
    x, w_qkv, wo, wu, wd, feat_all, b_slot, seg = first(
        tokens,
        segments.reshape(2, 8, 128),
        (w_query, w_key, w_value, w_out, w_up, w_down),
        vectors,
    )

    qkv, att, prob, linv, wo, wu, wd, cot_first = attend_fwd(x, w_qkv, b_slot, seg, cotangent, wo, wu, wd)
    wu, wd, act, slope, hidden_low, normed1, inv1, output, grad_r2, vg2 = ff_fwd(
        x, att, wo, feat_all, b_slot, cotangent, cot_first, wu, wd
    )

    out_block, grad_pre, bu_part, kept_d = ff_down_bwd(grad_r2, wd, act, slope, output)
    out_block, grad_r1, grad_attn, vg1, kept_u, tot_d = ff_up_bwd(
        grad_r2, hidden_low, grad_pre, wu, normed1, inv1, feat_all, output, out_block, kept_d
    )
    g_qkv, g_part, tot_q, tot_o, own_d, own_u = attend_bwd(
        grad_attn, wo, att, qkv, linv, prob, x, tot_d, kept_u
    )

    x_grad_block, gq, go, gd, gu, slot_sum, own = last(
        tot_q, tot_o, own_d, own_u, g_part, bu_part, vg1, vg2, g_qkv, w_qkv, grad_r1
    )
    wq_grad, wk_grad, wv_grad = [gq[:, i * 4 * hq : (i + 1) * 4 * hq].astype(F32) for i in range(3)]
    w_out_grad, w_up_grad, w_down_grad = go.astype(F32), gu.astype(F32), gd.astype(F32)
    slot_sum = slot_sum.reshape(4, 1024)
    bq_grad = slot_sum[:, :hq].reshape(-1)
    bv_grad = slot_sum[:, 2 * hq : 3 * hq].reshape(-1)
    bu_grad = slot_sum[:, 3 * hq : 3 * hq + unit].reshape(-1)
    own = own.reshape(-1)[: 6 * feat].reshape(6, feat)
    return (
        out_block, x_grad_block, wq_grad, bq_grad, wk_grad, wv_grad, bv_grad, w_out_grad, own[0], own[1], own[2],
        w_up_grad, bu_grad, w_down_grad, own[3], own[4], own[5],
    )


def tokens_cols(source):
    return lax.all_gather(source, "col", axis=0, tiled=True)


def tokens_rows(source):
    return lax.all_gather(source, "row", axis=0, tiled=True)


def product(row_piece, weight, flipped):
    if flipped:
        return lax.dot_general(
            row_piece, weight, (((1,), (1,)), ((), ())), preferred_element_type=jnp.float32
        )
    return jnp.dot(row_piece, weight, preferred_element_type=jnp.float32)


def outer_sum(left, right):
    return lax.dot_general(
        left, right, (((0,), (0,)), ((), ())), preferred_element_type=jnp.float32
    )


def settle_rows(gathered, weight, flipped, own_rows):

    def product_term(first_row, row_count):
        return product(gathered, weight, flipped)

    return lax.psum_scatter(
        product_term(jnp.int32(0), own_rows * lax.axis_size("row")),
        "row",
        scatter_dimension=0,
        tiled=True,
    )


def settle_cols(gathered, weight, flipped, own_rows):

    def product_term(first_row, row_count):
        return product(gathered, weight, flipped)

    return lax.psum_scatter(
        product_term(jnp.int32(0), own_rows * lax.axis_size("col")),
        "col",
        scatter_dimension=0,
        tiled=True,
    )


def row_sums(first_part, second_part):
    return lax.psum((jnp.sum(first_part, axis=1), jnp.sum(second_part, axis=1)), "row")


def norm_forward(residual, norm_gain, norm_shift):
    total_sum, square_sum = row_sums(residual, residual * residual)
    row_mean = (total_sum / WIDTH)[:, None]
    variance = (square_sum / WIDTH)[:, None] - row_mean * row_mean
    inv_std = lax.rsqrt(variance + NORM_EPS)
    normed = (residual - row_mean) * inv_std
    return (normed * norm_gain + norm_shift, normed, inv_std)


def norm_backward(grad_in, normed, inv_std, norm_gain):
    grad_norm = grad_in * norm_gain
    total_sum, cross_sum = row_sums(grad_norm, grad_norm * normed)
    grad_resid = inv_std * (grad_norm - total_sum[:, None] / WIDTH - normed * cross_sum[:, None] / WIDTH)
    return (grad_resid, jnp.sum(grad_in * normed, axis=0), jnp.sum(grad_in, axis=0))


def split_heads(array, seq_count):
    return array.reshape(seq_count, SEQ, array.shape[1] // HD, HD)


def pair_scores(queries, key_heads, segment_ids):
    position = jnp.arange(SEQ)
    same_doc = (segment_ids[:, None] == segment_ids[None, :]) & (segment_ids[None, :] != 0)
    allowed = same_doc | (position[:, None] == position[None, :])
    raw_scores = jnp.einsum(
        "qhd,khd->hqk", queries, key_heads, preferred_element_type=jnp.float32
    ) * HD ** (-0.5)
    return jnp.where(allowed[None], raw_scores, -1000000000.0)


def attend_forward(source):
    queries, key_heads, values, segment_ids = source
    scores = pair_scores(queries, key_heads, segment_ids)
    top_score = jnp.max(scores, axis=2, keepdims=True)
    exp_scores = jnp.exp(scores - top_score)
    total_sum = jnp.sum(exp_scores, axis=2, keepdims=True)
    soft_low = (exp_scores / total_sum).astype(jnp.bfloat16)
    attended = jnp.einsum("hqk,khd->qhd", soft_low, values, preferred_element_type=jnp.float32)
    return (attended.astype(jnp.bfloat16), (top_score + jnp.log(total_sum))[:, :, 0])


def attend_backward(source):
    queries, key_heads, values, segment_ids, grad_out, log_total = source
    scores = pair_scores(queries, key_heads, segment_ids)
    soft_weights = jnp.exp(scores - log_total[:, :, None])
    soft_low = soft_weights.astype(jnp.bfloat16)
    grad_values = jnp.einsum("hqk,qhd->khd", soft_low, grad_out, preferred_element_type=jnp.float32)
    grad_soft = jnp.einsum("qhd,khd->hqk", grad_out, values, preferred_element_type=jnp.float32)
    grad_scores = soft_weights * (
        grad_soft - jnp.sum(soft_weights * grad_soft, axis=2, keepdims=True)
    )
    grad_scores = grad_scores.astype(jnp.bfloat16)
    scale_factor = HD ** (-0.5)
    grad_queries = (
        jnp.einsum("hqk,khd->qhd", grad_scores, key_heads, preferred_element_type=jnp.float32)
        * scale_factor
    )
    grad_keys = (
        jnp.einsum("hqk,qhd->khd", grad_scores, queries, preferred_element_type=jnp.float32)
        * scale_factor
    )
    return (
        grad_queries.astype(jnp.bfloat16),
        grad_keys.astype(jnp.bfloat16),
        grad_values.astype(jnp.bfloat16),
    )


def split_heads_plan(
    tokens,
    segments,
    w_query,
    b_query,
    w_key,
    w_value,
    b_value,
    w_out,
    b_out,
    norm1_gain,
    norm1_shift,
    w_up,
    b_up,
    w_down,
    b_down,
    norm2_gain,
    norm2_shift,
    cotangent,
):
    rows_b = tokens.shape[0]
    rows_a = segments.shape[0]
    head_cols = w_query.shape[1]
    seq_count = rows_a // SEQ
    segment_seqs = segments.reshape(seq_count, SEQ)
    gathered_x = tokens_cols(tokens)
    stacked = jnp.concatenate([w_query, w_key, w_value], axis=1)
    projected = settle_rows(gathered_x, stacked, False, rows_a)
    queries = (projected[:, :head_cols] + b_query).astype(jnp.bfloat16)
    key_heads = projected[:, head_cols : 2 * head_cols].astype(jnp.bfloat16)
    values = (projected[:, 2 * head_cols :] + b_value).astype(jnp.bfloat16)
    query_seqs = split_heads(queries, seq_count)
    key_seqs = split_heads(key_heads, seq_count)
    value_seqs = split_heads(values, seq_count)
    attended, log_total = lax.map(attend_forward, (query_seqs, key_seqs, value_seqs, segment_seqs))
    attended = attended.reshape(rows_a, head_cols)
    gathered_o = tokens_rows(attended)
    attn_out = settle_cols(gathered_o, w_out, False, rows_b) + b_out
    hidden, normed1, inv_std1 = norm_forward(
        tokens.astype(jnp.float32) + attn_out, norm1_gain, norm1_shift
    )
    hidden_low = hidden.astype(jnp.bfloat16)
    gathered_h = tokens_cols(hidden_low)
    pre_act = settle_rows(gathered_h, w_up, False, rows_a) + b_up
    active = gelu_exact(pre_act).astype(jnp.bfloat16)
    gathered_a = tokens_rows(active)
    fed = settle_cols(gathered_a, w_down, False, rows_b) + b_down
    output, normed2, inv_std2 = norm_forward(hidden + fed, norm2_gain, norm2_shift)
    grad_r2, grad_gain2, grad_shift2 = norm_backward(
        cotangent.astype(jnp.float32), normed2, inv_std2, norm2_gain
    )
    grad_fed = grad_r2.astype(jnp.bfloat16)
    gathered_f = tokens_cols(grad_fed)
    grad_w_down = outer_sum(gathered_a, gathered_f)
    grad_active = settle_rows(gathered_f, w_down, True, rows_a)
    unused_out, slope_pull = jax.vjp(gelu_exact, pre_act)
    grad_pre = slope_pull(grad_active)[0].astype(jnp.bfloat16)
    gathered_p = tokens_rows(grad_pre)
    grad_w_up = outer_sum(gathered_h, gathered_p)
    grad_from_ff = settle_cols(gathered_p, w_up, True, rows_b)
    bias_up_part = jnp.sum(grad_pre.astype(jnp.float32), axis=0)
    bias_down_part = jnp.sum(grad_fed.astype(jnp.float32), axis=0)
    grad_r1, grad_gain1, grad_shift1 = norm_backward(
        grad_from_ff + grad_r2, normed1, inv_std1, norm1_gain
    )
    grad_attn = grad_r1.astype(jnp.bfloat16)
    gathered_d = tokens_cols(grad_attn)
    grad_w_out = outer_sum(gathered_o, gathered_d)
    grad_attended = settle_rows(gathered_d, w_out, True, rows_a).astype(jnp.bfloat16)
    grad_q, grad_k, grad_v = lax.map(
        attend_backward,
        (
            query_seqs,
            key_seqs,
            value_seqs,
            segment_seqs,
            split_heads(grad_attended, seq_count),
            log_total,
        ),
    )
    grad_q = grad_q.reshape(rows_a, head_cols)
    grad_k = grad_k.reshape(rows_a, head_cols)
    grad_v = grad_v.reshape(rows_a, head_cols)
    grad_proj = jnp.concatenate([grad_q, grad_k, grad_v], axis=1)
    gathered_g = tokens_rows(grad_proj)
    grad_stacked = outer_sum(gathered_x, gathered_g)
    tokens_grad = settle_cols(gathered_g, stacked, True, rows_b) + grad_r1
    bias_q, bias_v, bias_up = lax.psum(
        (
            jnp.sum(grad_q.astype(jnp.float32), axis=0),
            jnp.sum(grad_v.astype(jnp.float32), axis=0),
            bias_up_part,
        ),
        ("dp", "row"),
    )
    bias_out, bias_down, gain_one, shift_one, gain_two, shift_two = lax.psum(
        (
            jnp.sum(grad_attn.astype(jnp.float32), axis=0),
            bias_down_part,
            grad_gain1,
            grad_shift1,
            grad_gain2,
            grad_shift2,
        ),
        ("dp", "col"),
    )
    sum_stacked, sum_out, sum_up, sum_down = (
        lax.psum(grad_stacked.astype(jnp.bfloat16), "dp").astype(jnp.float32),
        lax.psum(grad_w_out.astype(jnp.bfloat16), "dp").astype(jnp.float32),
        lax.psum(grad_w_up.astype(jnp.bfloat16), "dp").astype(jnp.float32),
        lax.psum(grad_w_down.astype(jnp.bfloat16), "dp").astype(jnp.float32),
    )
    return (
        output.astype(jnp.bfloat16),
        tokens_grad.astype(jnp.bfloat16),
        sum_stacked[:, :head_cols],
        bias_q,
        sum_stacked[:, head_cols : 2 * head_cols],
        sum_stacked[:, 2 * head_cols :],
        bias_v,
        sum_out,
        bias_out,
        gain_one,
        shift_one,
        sum_up,
        bias_up,
        sum_down,
        bias_down,
        gain_two,
        shift_two,
    )


def solution(mesh):
    dp, rows, cols = (mesh.shape[name] for name in ("dp", "row", "col"))
    whole = TOKENS // SEQ == dp * rows * cols and dp == 4 and cols == 2
    plan = whole_sequences if whole else split_heads_plan
    placed = (
        P(("dp", "col"), "row"),
        P(("dp", "row")),
        P("row", "col"),
        P("col"),
        P("row", "col"),
        P("row", "col"),
        P("col"),
        P("col", "row"),
        P("row"),
        P("row"),
        P("row"),
        P("row", "col"),
        P("col"),
        P("col", "row"),
        P("row"),
        P("row"),
        P("row"),
        P(("dp", "col"), "row"),
    )
    return jax.shard_map(
        plan,
        mesh=mesh,
        in_specs=placed,
        out_specs=(
            P(("dp", "col"), "row"),
            P(("dp", "col"), "row"),
            P("row", "col"),
            P("col"),
            P("row", "col"),
            P("row", "col"),
            P("col"),
            P("col", "row"),
            P("row"),
            P("row"),
            P("row"),
            P("row", "col"),
            P("col"),
            P("col", "row"),
            P("row"),
            P("row"),
            P("row"),
        ),
        check_vma=False,
    )
```

```python
import math

import jax
import jax.numpy as jnp
from jax import lax
from jax.experimental import pallas as pl
from jax.experimental.pallas import tpu as pltpu
from jax.sharding import PartitionSpec as P

HD = 64
SEQ = 1024
WIDTH = 1024
TOKENS = 32768
NORM_EPS = 1e-05
BF = jnp.bfloat16
F32 = jnp.float32
NEG = -1e30
QB = 256
VMEM_LIMIT = 56 * 1024 * 1024
MESH = pl.DeviceIdType.MESH
ANY = pl.BlockSpec(memory_space=pl.ANY)
DMA = pltpu.SemaphoreType.DMA
ONCE = pl.Buffered(1)


def const(*shape):
    return pl.BlockSpec(shape, lambda j: (0,) * len(shape), pipeline_mode=ONCE)


def mm(a, b):
    return jnp.dot(a, b, preferred_element_type=F32)


def mm_t(a, b):
    return lax.dot_general(a, b, (((1,), (1,)), ((), ())), preferred_element_type=F32)


def tmm(a, b):
    return lax.dot_general(a, b, (((0,), (0,)), ((), ())), preferred_element_type=F32)


def gelu_exact(v):
    return jax.nn.gelu(v, approximate=False)


def attend_rows(qkv_ref, seg_col_ref, seg_row, o_ref, p_ref, linv_ref):
    lane = lax.broadcasted_iota(jnp.int32, (QB, 128), 1)
    scale = HD ** (-0.5) * math.log2(math.e)
    k = qkv_ref[:, 128:256]
    v = qkv_ref[:, 256:384]
    units = [(i, h) for i in range(SEQ // QB) for h in range(2)]

    def scores(i, h):
        q = qkv_ref[i * QB : (i + 1) * QB, 0:128]
        mine = (lane < HD) if h == 0 else (lane >= HD)
        return mm_t(jnp.where(mine, q, jnp.zeros_like(q)), k)

    ahead = scores(*units[0])
    outs = []
    for at, (i, h) in enumerate(units):
        rows = slice(i * QB, (i + 1) * QB)
        s = ahead
        if at + 1 < len(units):
            ahead = scores(*units[at + 1])
        s = jnp.where(seg_col_ref[rows, 0:1] == seg_row, s * scale, NEG)
        top = jnp.max(s, axis=1, keepdims=True)
        p = jnp.exp2(s - top)
        total = jnp.sum(p, axis=1, keepdims=True)
        pb = p.astype(BF)
        p_ref[h, rows, :] = pb
        inv = 1.0 / total
        outs.append((mm(pb, v) * inv, jnp.broadcast_to(inv, (QB, 128))))
        if h == 1:
            o_ref[rows, :] = jnp.where(lane < HD, outs[0][0], outs[1][0]).astype(BF)
            linv_ref[rows, :] = jnp.where(lane < HD, outs[0][1], outs[1][1])
            outs = []


def attend_fwd_kernel(
    x_ref, w_ref, b_ref, seg_ref, cot, wo_in, wu_in, wd_in,
    qkv_ref, o_ref, p_ref, linv_ref, wo, wu, wd, cot_first,
    x_buf, seg_col_ref, seg_row_ref, cot_own, i_sems, o_recv, o_sent, u_recv, u_sent, d_recv, d_sent,
):
    j = pl.program_id(0)
    peers = Peers()
    go = Gather(peers, None, wo, False, o_recv, o_sent, RING + LATER_NEAR + FAR)
    gu = Gather(peers, None, wu, True, u_recv, u_sent, RING + LATER_NEAR + far_edges(0))
    gd = Gather(peers, None, wd, False, d_recv, d_sent, RING + DOWN_NEAR + far_edges(0, 1))
    every = (go, gu, gd)
    inward = Inward(peers, cot, cot_first, cot_own, i_sems, (0,))

    plan = {
        2: ((go, (1, 0)), (gu, (1, 0)), (gu, (0, 6)), (gd, (0, 6))),
        3: ((gd, (1, 0)), (go, (1, 2), (1, 4), (2, 0))),
        4: ((gu, (1, 2), (1, 4), (2, 0)), (go, (0, 6), (1, 6))),
        5: ((gd, (1, 2), (1, 4), (2, 0)), (go, (2, 2), (2, 4), (3, 0))),
        6: ((gu, (2, 2), (2, 4)), (gu, (3, 0))),
        7: ((gd, (2, 2), (2, 4)), (go, (2, 6), (3, 2), (3, 4))),
        8: ((gd, (3, 0)), (gu, (3, 2), (3, 4)), (go, (3, 6))),
    }

    def relay(step):
        for g, *blocks in plan[step]:
            g.relay(*blocks)

    @pl.when(j == 0)
    def _():
        peers.hello(ALL_PEERS)
        inward.load()
        f = x_ref.shape[2]
        for s in range(4):
            x_buf[:, s * f : (s + 1) * f] = x_ref[s]
        tile = seg_ref[4 * peers.c + peers.r]
        for i in range(8):
            row = tile[i : i + 1, :]
            at = lax.broadcasted_iota(jnp.int32, (1, 128), 1) + i * 128
            row = jnp.where(row == 0, -1 - at, row)
            seg_row_ref[:, i * 128 : (i + 1) * 128] = row
            seg_col_ref[i * 128 : (i + 1) * 128, :] = jnp.transpose(jnp.broadcast_to(row, (128, 128)))

    qkv_ref[...] = (mm(x_buf[...], w_ref[...]) + b_ref[0, :, 0:384]).astype(BF)
    @pl.when(j == 0)
    def _():
        peers.meet(ALL_PEERS)
        for g in every:
            g.emit(0, 0)
        go.emit(0, 2)
        gu.emit(0, 2)
        gd.emit(0, 4)

    for at in range(2, 8):
        @pl.when(j == at)
        def _(at=at):
            relay(at)
            if at == 5:
                inward.settle()
                inward.start(0)

    seg_row = seg_row_ref[...]
    attend_rows(qkv_ref, seg_col_ref, seg_row, o_ref, p_ref, linv_ref)

    @pl.when(j == 7)
    def _():
        relay(8)
        for g in every:
            g.finish()
        inward.finish()


def attend_fwd(x, w_qkv, b_slot, seg, cot, wo, wu, wd):
    slots = w_qkv.shape[1] // 384
    return pl.pallas_call(
        attend_fwd_kernel,
        grid=(slots,),
        in_specs=[
            const(*x.shape),
            pl.BlockSpec((w_qkv.shape[0], 384), lambda j: (0, j)),
            pl.BlockSpec((1, 1, b_slot.shape[2]), lambda j: (j, 0, 0)),
            const(8, 8, 128),
            ANY,
            ANY,
            ANY,
            ANY,
        ],
        out_specs=[
            pl.BlockSpec((SEQ, 384), lambda j: (0, j)),
            pl.BlockSpec((SEQ, 128), lambda j: (0, j)),
            pl.BlockSpec((2, SEQ, SEQ), lambda j: (j, 0, 0)),
            pl.BlockSpec((SEQ, 128), lambda j: (0, j)),
            ANY,
            ANY,
            ANY,
            ANY,
        ],
        out_shape=[
            jax.ShapeDtypeStruct((SEQ, slots * 384), BF),
            jax.ShapeDtypeStruct((SEQ, slots * 128), BF),
            jax.ShapeDtypeStruct((slots * 2, SEQ, SEQ), BF),
            jax.ShapeDtypeStruct((SEQ, slots * 128), F32),
            jax.ShapeDtypeStruct(wo.shape, BF),
            jax.ShapeDtypeStruct(wu.shape, BF),
            jax.ShapeDtypeStruct(wd.shape, BF),
            jax.ShapeDtypeStruct((SEQ // CHUNKS, w_qkv.shape[0]), BF),
        ],
        input_output_aliases={5: 4, 6: 5, 7: 6},
        scratch_shapes=[
            pltpu.VMEM((SEQ, w_qkv.shape[0]), BF),
            pltpu.VMEM((SEQ, 128), jnp.int32),
            pltpu.VMEM((1, SEQ), jnp.int32),
            pltpu.VMEM((SEQ // CHUNKS, cot.shape[1]), BF),
            sems_of_exchange(),
            *[DMA((32,))] * 6,
        ],
        compiler_params=pltpu.CompilerParams(vmem_limit_bytes=VMEM_LIMIT, collective_id=1, has_side_effects=True),
        name="attend_fwd",
    )(x, w_qkv, b_slot, seg, cot, wo, wu, wd)


class Peers:
    def __init__(self):
        self.r = lax.axis_index("row")
        self.c = lax.axis_index("col")
        self.d = d = lax.axis_index("dp")
        self.ids = {
            "core": {"dp": d + 1 - 2 * lax.rem(d, 2)},
            "x": {"dp": lax.rem(d + 2, 4)},
            "y": {"col": 1 - self.c},
            1: {"row": lax.rem(self.r + 1, 4)},
            2: {"row": lax.rem(self.r + 2, 4)},
            3: {"row": lax.rem(self.r + 3, 4)},
        }

    def hello(self, names):
        barrier = pltpu.get_barrier_semaphore()
        for name in names:
            pl.semaphore_signal(barrier, inc=1, device_id=self.ids[name], device_id_type=MESH)

    def meet(self, names):
        pl.semaphore_wait(pltpu.get_barrier_semaphore(), len(names))


def send(peers, name, src, dst, send_sem, recv_sem):
    return pltpu.make_async_remote_copy(
        src_ref=src, dst_ref=dst, send_sem=send_sem, recv_sem=recv_sem, device_id=peers.ids[name], device_id_type=MESH
    )


def near_edges(s):
    return [("x", s, 0, s, 2), ("y", s, 0, s, 4), ("core", s, 0, s, 1)]


def second_edges(s):
    return [("core", s, 2, s, 3), ("core", s, 4, s, 5)]


def far_edges(s, flip=0):
    return [("y", s, 2, s, 6) if (s + flip) % 2 == 0 else ("x", s, 4, s, 6), ("core", s, 6, s, 7)]


def emit_far(gather, s, flip=0):
    gather.emit(s, 2 if (s + flip) % 2 == 0 else 4)


RING = [(1, s, 0, s + 1, 0) for s in range(3)]
NEAR = [e for s in range(4) for e in near_edges(s) + second_edges(s)]
FAR = [e for s in range(4) for e in far_edges(s)]
OWN_BLOCK = near_edges(0) + second_edges(0)
LATER_NEAR = [e for e in NEAR if e[1] > 0]
UP_FAR = [e for s in (1, 2, 3) for e in far_edges(s)]
DOWN_FAR = [e for s in (1, 2, 3) for e in far_edges(s, 1)]
DOWN_NEAR = [e for e in LATER_NEAR if e[1] < 3] + [("core", 3, 0, 3, 1)]
DOWN_REST = [e for e in near_edges(3) if e[0] != "core"] + second_edges(3) + DOWN_FAR


class Gather:
    def __init__(self, peers, piece, full, by_rows, recv, sent, edges):
        self.peers, self.piece, self.full, self.recv, self.sent = peers, piece, full, recv, sent
        self.by_rows = by_rows
        self.n = full.shape[1 if by_rows else 0] // 8
        self.m = full.shape[0 if by_rows else 1] // 4
        self.edges = edges
        self.waited = set()
        self.emitted = set()

    def blk(self, s, t):
        a = pl.ds(s * self.m, self.m)
        b = pl.ds(t * self.n, self.n)
        return self.full.at[a, b] if self.by_rows else self.full.at[b, a]

    def copy(self, at):
        name, s, t, s2, t2 = self.edges[at]
        src = self.piece if (s, t) == (0, 0) and self.piece is not None else self.blk(s, t)
        return send(self.peers, name, src, self.blk(s2, t2), self.sent.at[at], self.recv.at[at])

    def emit(self, s, t):
        for at, e in enumerate(self.edges):
            if e[1:3] == (s, t):
                assert at not in self.emitted
                self.emitted.add(at)
                self.copy(at).start()

    def emit_own_slot(self, s):
        for at, e in enumerate(self.edges):
            if e[1:3] == (s, 0):
                self.emitted.add(at)
                self.copy(at).start()

    def arrived(self, s, t):
        for at, e in enumerate(self.edges):
            if e[3:5] == (s, t) and at not in self.waited:
                self.waited.add(at)
                self.copy(at).wait_recv()

    def relay(self, *blocks):
        for s, t in blocks:
            self.arrived(s, t)
            self.emit(s, t)

    def own(self):
        return pltpu.make_async_copy(self.piece, self.blk(0, 0), self.sent.at[len(self.edges)])

    def start(self):
        self.emit(0, 0)
        self.own().start()

    def finish(self):
        if self.piece is not None:
            self.own().wait()
        for at, e in enumerate(self.edges):
            if at not in self.waited:
                self.waited.add(at)
                self.copy(at).wait_recv()
        assert len(self.emitted) == len(self.edges)
        for at in range(len(self.edges)):
            self.copy(at).wait_send()


class Line:
    WAVES = ((3, 2, 1), (1, 3, 2), (1, 3, 2), (1, 2, 3))

    def __init__(self, peers, gather, sems):
        self.peers, self.gather, self.sems = peers, gather, sems

    def copy(self, up, s):
        s2 = s + 1 if up else (s - 1 if s else 3)
        g = self.gather
        src = g.piece if s == 0 else g.blk(s, 0)
        return send(
            self.peers, 1 if up else 3, src, g.blk(s2, 0), self.sems.at[(0 if up else 4) + s], self.sems.at[7 + s2]
        )

    def each(self, what):
        r = self.peers.r
        for s in range(3):
            @pl.when((r >= s) & (r < 3))
            def _(s=s):
                what(self.copy(True, s))
        for s in (0, 3, 2):
            @pl.when((r > 0) & (r <= (3 if s == 0 else s - 1)))
            def _(s=s):
                what(self.copy(False, s))

    def start(self):
        r = self.peers.r

        @pl.when(r < 3)
        def _():
            self.copy(True, 0).start()

        @pl.when(r > 0)
        def _():
            self.copy(False, 0).start()

    def wave(self, k):
        for row, order in enumerate(self.WAVES):
            s = order[k]

            @pl.when(self.peers.r == row)
            def _(row=row, s=s):
                self.copy(True, s - 1).wait_recv()
                below = row >= s
                if below and row < 3:
                    self.copy(True, s).start()
                if not below and row > 0:
                    self.copy(False, s).start()
                self.gather.emit_own_slot(s)

    def finish(self):
        self.each(lambda c: c.wait_send())


CHUNKS = 4
FINE = 8


def sems_of_exchange(cuts=CHUNKS):
    return DMA((2, 4, cuts))


class Inward:
    def __init__(self, peers, block, rows, buf, sems, chunks=range(CHUNKS), cuts=CHUNKS):
        self.peers, self.block, self.rows, self.buf, self.sems, self.chunks = peers, block, rows, buf, sems, chunks
        self.n = SEQ // cuts

    def ends(self, s, first, count):
        r = lax.rem(self.peers.r + s, 4)
        f = self.block.shape[1]
        src = self.block.at[pl.ds(pl.multiple_of(r * SEQ + first * self.n, self.n), count * self.n), :]
        at = first if self.rows.shape[-2] == SEQ else first - self.chunks[0]
        rows = pl.ds(at * self.n, count * self.n)
        return src, self.rows.at[s, rows, :] if len(self.rows.shape) == 3 else self.rows.at[rows, pl.ds(s * f, f)]

    def copy(self, s, k):
        return send(self.peers, s, *self.ends(s, k, 1), self.sems.at[0, s, k], self.sems.at[1, s, k])

    def own(self):
        src, dst = self.ends(0, self.chunks[0], len(self.chunks))
        return (
            pltpu.make_async_copy(src, self.buf, self.sems.at[0, 0, 0]),
            pltpu.make_async_copy(self.buf, dst, self.sems.at[1, 0, 0]),
        )

    def start(self, *chunks):
        for k in chunks:
            for s in (2, 1, 3):
                self.copy(s, k).start()

    def load(self):
        self.own()[0].start()

    def settle(self):
        self.own()[0].wait()
        self.own()[1].start()

    def finish(self):
        self.own()[1].wait()
        for k in self.chunks:
            for s in (1, 2, 3):
                self.copy(s, k).wait()


ALL_PEERS = ("core", "x", "y", 1, 2, 3)


def first_kernel(
    tokens, segments, w_query, w_key, w_value, w_out, w_up, w_down,
    vectors,
    x, w, wo, wu, wd, feat_out, slot_out, seg_out,
    pq, po, pu, pd, rows_buf, feat, slot, l_sems, q_recv, q_sent, o_recv, o_sent, u_recv, u_sent, d_recv, d_sent,
    i_sems, v_sems, z_sems,
):
    peers = Peers()
    r, d = peers.r, peers.d

    def own_cols(ref):
        n = ref.shape[1] // 4
        return ref.at[:, pl.ds(pl.multiple_of(d * n, n), n)]

    def own_rows(ref):
        n = ref.shape[0] // 4
        return ref.at[pl.ds(pl.multiple_of(d * n, n), n), :]

    peers.hello(ALL_PEERS)
    heads = w_query.shape[1] // 4
    loads = [
        pltpu.make_async_copy(own_cols(ref), pq.at[:, pl.ds(i * heads, heads)], l_sems.at[i])
        for i, ref in enumerate((w_query, w_key, w_value))
    ]
    loads += [
        pltpu.make_async_copy(own_rows(w_out), po, l_sems.at[3]),
        pltpu.make_async_copy(own_cols(w_up), pu, l_sems.at[4]),
        pltpu.make_async_copy(own_rows(w_down), pd, l_sems.at[5]),
    ]
    for c in loads:
        c.start()
    feat[...] = jnp.zeros_like(feat)
    f = feat.shape[1]
    for i in range(6):
        feat[i : i + 1, :] = vectors[:, i * f : (i + 1) * f]
    units = slot.shape[2] - 3 * heads
    at_q, at_v, at_u = 6 * f, 6 * f + 4 * heads, 6 * f + 8 * heads

    def quarter(first, n, q):
        return vectors[:, pl.ds(pl.multiple_of(first + q * n, 128), n)]

    for t in range(4):
        q = d
        if t % 2:
            q = q + 1 - 2 * lax.rem(q, 2)
        if t // 2:
            q = lax.rem(q + 2, 4)
        slot[t, :, 0:heads] = quarter(at_q, heads, q)
        slot[t, :, heads : 2 * heads] = jnp.zeros((1, heads), F32)
        slot[t, :, 2 * heads : 3 * heads] = quarter(at_v, heads, q)
        slot[t, :, 3 * heads :] = quarter(at_u, units, q)
    for c in loads:
        c.wait()

    gq = Gather(peers, pq, w, True, q_recv, q_sent, NEAR + FAR)
    line = Line(peers, gq, z_sems)
    go = Gather(peers, po, wo, False, o_recv, o_sent, OWN_BLOCK)
    gu = Gather(peers, pu, wu, True, u_recv, u_sent, OWN_BLOCK)
    gd = Gather(peers, pd, wd, False, d_recv, d_sent, OWN_BLOCK)
    later = (go, gu, gd)
    inward = Inward(peers, tokens, x, rows_buf, i_sems, range(FINE), FINE)
    inward.load()
    here = seg_out.at[pl.ds(2 * r, 2)]
    small = [
        pltpu.make_async_copy(feat, feat_out.at[:, pl.ds(0, f)], v_sems.at[0]),
        pltpu.make_async_copy(slot, slot_out.at[pl.ds(0, 4)], v_sems.at[1]),
        pltpu.make_async_copy(segments, here, v_sems.at[2]),
        send(peers, "y", slot, slot_out.at[pl.ds(4, 4)], v_sems.at[3], v_sems.at[4]),
    ]
    for i in (1, 2, 3):
        small.append(send(peers, i, feat, feat_out.at[:, pl.ds(i * f, f)], v_sems.at[3 + 2 * i], v_sems.at[4 + 2 * i]))
        small.append(send(peers, i, segments, here, v_sems.at[9 + 2 * i], v_sems.at[10 + 2 * i]))

    peers.meet(ALL_PEERS)
    line.start()
    gq.start()
    for c in small:
        c.start()
    for g in later:
        g.start()
    inward.start(0)
    line.wave(0)
    inward.start(1)
    inward.settle()
    gq.relay((0, 2), (0, 4))
    line.wave(1)
    inward.start(2)
    for g in later:
        g.relay((0, 2), (0, 4))
    line.wave(2)
    inward.start(*range(3, FINE))
    for s in (1, 2, 3):
        gq.relay((s, 2), (s, 4))
    for s in range(4):
        gq.relay((s, 6))
    for c in small:
        c.wait()
    for g in (gq, *later):
        g.finish()
    line.finish()
    inward.finish()


def first(tokens, segments, weights, vectors):
    w_query, _, _, w_out, w_up, w_down = weights
    width = 4 * tokens.shape[1]
    heads = w_query.shape[1] // 4
    units = w_up.shape[1] // 4
    vmem = pl.BlockSpec(memory_space=pltpu.VMEM)
    return pl.pallas_call(
        first_kernel,
        in_specs=[ANY, vmem] + [ANY] * 6 + [vmem],
        out_specs=[ANY] * 8,
        out_shape=[
            jax.ShapeDtypeStruct((4, SEQ, width // 4), BF),
            jax.ShapeDtypeStruct((width, 24 * heads), BF),
            jax.ShapeDtypeStruct((8 * heads, width), BF),
            jax.ShapeDtypeStruct((width, 8 * units), BF),
            jax.ShapeDtypeStruct((8 * units, width), BF),
            jax.ShapeDtypeStruct((8, width), F32),
            jax.ShapeDtypeStruct((8, 1, 3 * heads + units), F32),
            jax.ShapeDtypeStruct((8, 8, 128), jnp.int32),
        ],
        scratch_shapes=[
            pltpu.VMEM((width // 4, 3 * heads), BF),
            pltpu.VMEM((heads, width // 4), BF),
            pltpu.VMEM((width // 4, units), BF),
            pltpu.VMEM((units, width // 4), BF),
            pltpu.VMEM((SEQ, width // 4), BF),
            pltpu.VMEM((8, width // 4), F32),
            pltpu.VMEM((4, 1, 3 * heads + units), F32),
            DMA((6,)),
            *[DMA((32,))] * 8,
            sems_of_exchange(FINE),
            DMA((20,)),
            DMA((11,)),
        ],
        compiler_params=pltpu.CompilerParams(vmem_limit_bytes=VMEM_LIMIT, collective_id=0, has_side_effects=True),
        name="first",
    )(tokens, segments, *weights, vectors)


RB = 256


def norm_rows(v):
    mean = jnp.mean(v, axis=1, keepdims=True)
    variance = jnp.mean(v * v, axis=1, keepdims=True) - mean * mean
    inv = lax.rsqrt(variance + NORM_EPS)
    return (v - mean) * inv, inv


def norm_rows_back(g, normed, inv):
    mean_g = jnp.mean(g, axis=1, keepdims=True)
    mean_gn = jnp.mean(g * normed, axis=1, keepdims=True)
    return inv * (g - mean_g - normed * mean_gn)


def gelu_and_slope(v):
    t = 1.0 / (1.0 + (0.3275911 * 0.5 ** 0.5) * jnp.abs(v))
    half = (0.127414796, -0.142248368, 0.7107068705, -0.7265760135, 0.5307027145)
    poly = t * (half[0] + t * (half[1] + t * (half[2] + t * (half[3] + t * half[4]))))
    bell = jnp.exp2(v * v * (-0.5 * math.log2(math.e)))
    tail = poly * bell
    cdf = jnp.where(v >= 0, 1.0 - tail, tail)
    return v * cdf, cdf + v * bell * (1.0 / math.sqrt(2.0 * math.pi))


def row_blocks(body, n=RB):
    def run(i, carry):
        body(pl.ds(pl.multiple_of(i * n, n), n))
        return carry

    lax.fori_loop(0, SEQ // n, run, 0)


def ff_fwd_kernel(
    x_ref, att_ref, wo_ref, vec_ref, b_ref, cot, cot_first, wu_in, wd_in,
    wu, wd, act_ref, slope_ref, hlow_ref, normed1_ref, inv1_ref, out_ref, r2_ref, vg_ref,
    acc, wu_buf, wd_buf, cot_buf, cot_own, buf_sem, u_recv, u_sent, d_recv, d_sent, i_sems, c_sem,
):
    j = pl.program_id(0)
    peers = Peers()
    gu = Gather(peers, None, wu, True, u_recv, u_sent, UP_FAR)
    gd = Gather(peers, None, wd, False, d_recv, d_sent, DOWN_REST)
    inward = Inward(peers, cot, cot_buf, cot_own, i_sems, range(1, CHUNKS))
    early = pltpu.make_async_copy(cot_first, cot_buf.at[pl.ds(0, SEQ // CHUNKS), :], c_sem)
    n = wu_buf.shape[2]

    def fetch(t, slot):
        cols = pl.ds(pl.multiple_of(t * n, n), n)
        return (
            pltpu.make_async_copy(wu.at[:, cols], wu_buf.at[slot], buf_sem.at[0, slot]),
            pltpu.make_async_copy(wd.at[cols, :], wd_buf.at[slot], buf_sem.at[1, slot]),
        )

    @pl.when(j == 0)
    def _():
        peers.hello(ALL_PEERS)
        for t in range(2):
            for c in fetch(t, t):
                c.start()
        early.start()
        inward.load()
        acc[...] = jnp.zeros_like(acc)
        peers.meet(ALL_PEERS)
        gd.emit(3, 0)
        for s in (1, 2):
            emit_far(gu, s)
            emit_far(gd, s, 1)
        emit_far(gu, 3)
        inward.start(*inward.chunks)

        def body(rows):
            x = jnp.concatenate([x_ref[s, rows, :] for s in range(4)], 1)
            v = x.astype(F32) + mm(att_ref[rows, :], wo_ref[...]) + vec_ref[0:1, :]
            normed, inv = norm_rows(v)
            normed1_ref[rows, :] = normed
            inv1_ref[rows, :] = jnp.broadcast_to(inv, (RB, 128))
            hlow_ref[rows, :] = (normed * vec_ref[1:2, :] + vec_ref[2:3, :]).astype(BF)

        row_blocks(body)
        gd.relay((3, 2), (3, 4))

    @pl.when(j == 1)
    def _():
        gd.arrived(3, 3)
        inward.settle()

    @pl.when(j == 2)
    def _():
        gd.arrived(3, 5)

    @pl.when(j == 4)
    def _():
        for g in (gu, gd):
            g.relay((1, 6), (2, 6), (3, 6))

    @pl.when(j == 5)
    def _():
        for s in (1, 2, 3):
            gu.arrived(s, 7)
            gd.arrived(s, 7)

    slot = lax.rem(j, 2)
    for c in fetch(j, slot):
        c.wait()
    w_up = wu_buf.at[slot]
    w_down = wd_buf.at[slot]
    bias = b_ref[0, :, 384:]
    for i in range(SEQ // 512):
        rows = slice(i * 512, (i + 1) * 512)
        act, slope = gelu_and_slope(mm(hlow_ref[rows, :], w_up[...]) + bias)
        act = act.astype(BF)
        act_ref[rows, :] = act
        slope_ref[rows, :] = slope.astype(BF)
        acc[rows, :] += mm(act, w_down[...])

    @pl.when(j < 6)
    def _():
        for c in fetch(j + 2, slot):
            c.start()

    @pl.when(j == 7)
    def _():
        inward.finish()
        early.wait()
        vg_ref[...] = jnp.zeros_like(vg_ref)

        def body(rows):
            hidden = normed1_ref[rows, :] * vec_ref[1:2, :] + vec_ref[2:3, :]
            normed, inv = norm_rows(hidden + (acc[rows, :] + vec_ref[3:4, :]))
            out_ref[rows, :] = (normed * vec_ref[4:5, :] + vec_ref[5:6, :]).astype(BF)
            c = cot_buf[rows, :].astype(F32)
            r2 = norm_rows_back(c * vec_ref[4:5, :], normed, inv)
            r2_ref[rows, :] = r2
            vg_ref[0:1, :] += jnp.sum(c * normed, axis=0, keepdims=True)
            vg_ref[1:2, :] += jnp.sum(c, axis=0, keepdims=True)
            vg_ref[2:3, :] += jnp.sum(r2.astype(BF).astype(F32), axis=0, keepdims=True)

        row_blocks(body)
        gu.finish()
        gd.finish()


def ff_fwd(x, att, wo, vec, bu, cot, cot_first, wu, wd):
    width, units = wu.shape
    n = units // 8
    return pl.pallas_call(
        ff_fwd_kernel,
        grid=(8,),
        in_specs=[
            const(*x.shape),
            const(SEQ, width),
            const(width, width),
            const(8, width),
            pl.BlockSpec((1, 1, bu.shape[2]), lambda j: (j, 0, 0)),
            ANY,
            ANY,
            ANY,
            ANY,
        ],
        out_specs=[
            ANY,
            ANY,
            pl.BlockSpec((SEQ, n), lambda j: (0, j)),
            pl.BlockSpec((SEQ, n), lambda j: (0, j)),
            const(SEQ, width),
            const(SEQ, width),
            const(SEQ, 128),
            const(SEQ, width),
            const(SEQ, width),
            const(8, width),
        ],
        out_shape=[
            jax.ShapeDtypeStruct(wu.shape, BF),
            jax.ShapeDtypeStruct(wd.shape, BF),
            jax.ShapeDtypeStruct((SEQ, units), BF),
            jax.ShapeDtypeStruct((SEQ, units), BF),
            jax.ShapeDtypeStruct((SEQ, width), BF),
            jax.ShapeDtypeStruct((SEQ, width), F32),
            jax.ShapeDtypeStruct((SEQ, 128), F32),
            jax.ShapeDtypeStruct((SEQ, width), BF),
            jax.ShapeDtypeStruct((SEQ, width), F32),
            jax.ShapeDtypeStruct((8, width), F32),
        ],
        input_output_aliases={7: 0, 8: 1},
        scratch_shapes=[
            pltpu.VMEM((SEQ, width), F32),
            pltpu.VMEM((2, width, n), BF),
            pltpu.VMEM((2, n, width), BF),
            pltpu.VMEM((SEQ, width), BF),
            pltpu.VMEM((SEQ - SEQ // CHUNKS, width // 4), BF),
            DMA((2, 2)),
            DMA((32,)),
            DMA((32,)),
            DMA((32,)),
            DMA((32,)),
            sems_of_exchange(),
            DMA,
        ],
        compiler_params=pltpu.CompilerParams(vmem_limit_bytes=VMEM_LIMIT, collective_id=2, has_side_effects=True),
        name="ff_fwd",
    )(x, att, wo, vec, bu, cot, cot_first, wu, wd)


ORDER = (7, 6, 1, 3, 5, 0, 2, 4)
PAIRS = (7, 6, 3, 2, 5, 4, 1, 0)


def slot_at(j):
    return jnp.where(j < 2, 7 - j, jnp.where(j < 5, 2 * j - 3, 2 * j - 10))


def pair_at(j):
    return jnp.where(j < 2, 7 - j, jnp.where(j < 4, 5 - j, jnp.where(j < 6, 9 - j, 7 - j)))


def sum_rows(dst, *srcs):
    n = dst.shape[0]
    step = min(n, 256)

    def run(i, carry):
        rows = pl.ds(pl.multiple_of(i * step, step), step)
        total = srcs[0][rows, :].astype(F32)
        for src in srcs[1:]:
            total += src[rows, :].astype(F32)
        dst[rows, :] = total.astype(BF)
        return carry

    lax.fori_loop(0, n // step, run, 0)


class Fold:
    @staticmethod
    def scratch(a, b):
        return [
            pltpu.VMEM((2, a, b), BF),
            pltpu.VMEM((4, a, b), BF),
            pltpu.VMEM((a, b), BF),
            pltpu.VMEM((2, a // 2, b), BF),
            DMA((12,)),
        ]

    def __init__(self, peers, order, stage, land, corner, land_corner, sems):
        self.peers, self.order, self.stage, self.land, self.corner, self.land_corner, self.sems = (
            peers, order, stage, land, corner, land_corner, sems,
        )
        self.half = corner.shape[0] // 2

    def to_core(self, p):
        k = (self.order[p] - 1) // 2
        return send(self.peers, "core", self.stage.at[p % 2], self.land.at[k], self.sems.at[4 + k], self.sems.at[k])

    def to_side(self, h):
        src = self.corner.at[pl.ds(h * self.half, self.half), :]
        return send(self.peers, "xy"[1 - h], src, self.land_corner.at[h], self.sems.at[10 + h], self.sems.at[8 + h])

    def before(self, j):
        for p in range(2, 8):
            if self.order[p - 2] % 2 == 0:
                continue

            @pl.when(j == p)
            def _(p=p):
                self.to_core(p - 2).wait_send()

    def from_core(self, t):
        k = t // 2
        self.to_core(self.order.index(t + 1)).wait_recv()
        return self.land.at[k]

    def after(self, j, outs):
        for p, t in enumerate(self.order):
            @pl.when(j == p)
            def _(p=p, t=t):
                mine = self.stage.at[p % 2]
                if t % 2 == 1:
                    self.to_core(p).start()
                    return
                theirs = self.from_core(t)
                if t == 6:
                    sum_rows(self.corner, mine, theirs)
                    self.to_side(0).start()
                    self.to_side(1).start()
                    return
                out = outs[t]
                if t == 0:
                    sum_rows(out, mine, theirs)
                    return
                h = t // 2 - 1
                self.to_side(h).wait_recv()
                for q in range(2):
                    rows = pl.ds(q * self.half, self.half)
                    more = (self.land_corner.at[h],) if q == h else ()
                    sum_rows(out.at[rows, :], mine.at[rows, :], theirs.at[rows, :], *more)

    def finish(self):
        for p in (6, 7):
            if self.order[p] % 2:
                self.to_core(p).wait_send()
        self.to_side(0).wait_send()
        self.to_side(1).wait_send()


class Cross:
    def __init__(self, peers, for_x, for_y, land_x, land_y, sems, cuts=1):
        self.peers, self.sems, self.cuts = peers, sems, cuts
        self.ends = {"x": (for_x, land_x), "y": (for_y, land_y)}
        self.n = land_x.shape[0] // cuts

    def copy(self, way, h=0):
        src, dst = self.ends[way]
        rows = pl.ds(h * self.n, self.n)
        at = 4 * h + 2 * "xy".index(way)
        return send(self.peers, way, src.at[rows, :], dst.at[rows, :], self.sems.at[at], self.sems.at[at + 1])

    def start(self, ways="xy", h=0):
        for way in ways:
            self.copy(way, h).start()

    def finish(self, own, out):
        for h in range(self.cuts):
            for way in "xy":
                self.copy(way, h).wait()
        sum_rows(out, own, self.ends["x"][1], self.ends["y"][1])


class Whole:
    @staticmethod
    def scratch(a, b):
        return [
            pltpu.VMEM((8 * a, b), BF),
            pltpu.VMEM((4, a, b), BF),
            pltpu.VMEM((4, a, b), BF),
            pltpu.VMEM((2, a // 2, b), BF),
            pltpu.VMEM((a, b), BF),
            pltpu.VMEM((a, b), BF),
            DMA((12,)),
            DMA((4,)),
        ]

    def __init__(self, peers, total, land, kept, land_corner, land_x, land_y, sems, c_sems):
        self.peers, self.total, self.land, self.kept, self.land_corner, self.sems = (
            peers, total, land, kept, land_corner, sems,
        )
        self.a = land.shape[1]
        self.half = self.a // 2
        self.cross = Cross(peers, kept.at[1], kept.at[2], land_x, land_y, c_sems)

    def block(self, t):
        return self.total.at[pl.ds(t * self.a, self.a), :]

    def to_core(self, k):
        return send(
            self.peers, "core", self.block(2 * k + 1), self.land.at[k], self.sems.at[4 + k], self.sems.at[k]
        )

    def to_side(self, h):
        src = self.kept.at[3, pl.ds(h * self.half, self.half), :]
        return send(self.peers, "xy"[1 - h], src, self.land_corner.at[h], self.sems.at[10 + h], self.sems.at[8 + h])

    def start(self):
        for k in (3, 1, 2, 0):
            self.to_core(k).start()

    def corner(self):
        for k in (3, 1, 2, 0):
            self.to_core(k).wait_recv()
            sum_rows(self.kept.at[k], self.block(2 * k), self.land.at[k])
            if k == 3:
                self.to_side(0).start()
                self.to_side(1).start()

    def sides(self):
        for h in range(2):
            self.to_side(h).wait_recv()
            rows = pl.ds(h * self.half, self.half)
            mine = self.kept.at[1 + h, rows, :]
            sum_rows(mine, mine, self.land_corner.at[h])
        self.cross.start()

    def finish(self, out):
        self.cross.finish(self.kept.at[0], out)
        for k in range(4):
            self.to_core(k).wait_send()
        for h in range(2):
            self.to_side(h).wait_send()


class Deal:
    def __init__(self, peers, total, by_rows, land, sems):
        self.peers, self.total, self.by_rows, self.land, self.sems = peers, total, by_rows, land, sems

    def part(self, s):
        n = self.total.shape[0 if self.by_rows else 1] // 4
        return self.total.at[pl.ds(s * n, n), :] if self.by_rows else self.total.at[:, pl.ds(s * n, n)]

    def copy(self, s):
        return send(self.peers, 4 - s, self.part(s), self.land.at[s - 1], self.sems.at[2 + s], self.sems.at[s - 1])

    def start(self):
        for s in (2, 1, 3):
            self.copy(s).start()

    def finish(self, out):
        for s in (1, 2, 3):
            self.copy(s).wait()
        sum_rows(out, self.part(0), self.land.at[0], self.land.at[1], self.land.at[2])


class LineDeal:
    def __init__(self, peers, total, by_rows, land, tmp, sems):
        self.peers, self.land, self.tmp, self.sems = peers, land, tmp, sems
        self.part = Deal(peers, total, by_rows, None, None).part

    def copy(self, up, b, row, src):
        go = (b - row if up else row - b) - 1
        at = (0 if up else 3) + go
        return send(
            self.peers, 1 if up else 3, src, self.land.at[0 if up else 1, go], self.sems.at[at], self.sems.at[6 + at]
        )

    def slot(self, b, row):
        return (row - b) % 4

    def first(self, up, b, row):
        return self.copy(up, b, row, self.part(self.slot(b, row)))

    def pass_on(self, up, b, row):
        go = (b - row if up else row - b) - 1
        tmp = self.tmp.at[0 if up else 1, go]
        return self.copy(up, b, row, tmp), tmp

    def got(self, up, b, row):
        go = b - row if up else row - b
        at = (0 if up else 3) + go
        land = self.land.at[0 if up else 1, go]
        send(self.peers, 1 if up else 3, land, land, self.sems.at[at], self.sems.at[6 + at]).wait_recv()
        return land

    STEPS = (((1, True, 3), (1, True, 2), (2, False, 0), (2, False, 1)), ((2, True, 3), (1, False, 0)))
    STARTS = ((0, True, 3), (0, True, 2), (0, True, 1), (3, False, 0), (3, False, 1), (3, False, 2))

    def when(self, row, run):
        pl.when(self.peers.r == row)(run)

    def start(self):
        for row, up, b in self.STARTS:
            self.when(row, lambda up=up, b=b, row=row: self.first(up, b, row).start())

    def step(self, k):
        for row, up, b in self.STEPS[k]:
            def run(row=row, up=up, b=b):
                land = self.got(up, b, row)
                copy, tmp = self.pass_on(up, b, row)
                sum_rows(tmp, land, self.part(self.slot(b, row)))
                copy.start()

            self.when(row, run)

    def finish(self, out):
        for row in range(4):
            def run(row=row):
                lands = []
                if row > 0:
                    lands.append(self.got(True, row, row))
                if row < 3:
                    lands.append(self.got(False, row, row))
                sum_rows(out, self.part(0), *lands)

            self.when(row, run)
        for row, up, b in self.STARTS:
            self.when(row, lambda up=up, b=b, row=row: self.first(up, b, row).wait_send())
        for moves in self.STEPS:
            for row, up, b in moves:
                self.when(row, lambda up=up, b=b, row=row: self.pass_on(up, b, row)[0].wait_send())


class Spread:
    def __init__(self, peers, own, place, sems):
        d = lax.axis_index("dp")
        self.peers, self.own, self.sems, self.here = peers, own, sems, place(d)
        self.from_x = place(lax.rem(d + 2, 4))

    def local(self):
        return pltpu.make_async_copy(self.own, self.here, self.sems.at[6])

    def copies(self):
        s = self.sems
        return (
            send(self.peers, "x", self.own, self.here, s.at[0], s.at[1]),
            send(self.peers, "core", self.own, self.here, s.at[2], s.at[3]),
            send(self.peers, "core", self.from_x, self.from_x, s.at[4], s.at[5]),
        )

    def start(self):
        to_x, to_core, _ = self.copies()
        to_x.start()
        to_core.start()
        self.local().start()

    def relay(self):
        to_x, _, on = self.copies()
        to_x.wait_recv()
        on.start()

    def finish(self):
        to_x, to_core, on = self.copies()
        to_x.wait_send()
        to_core.wait()
        on.wait()
        self.local().wait()


class Outward:
    def __init__(self, peers, rows, block, buf, sems, parts=(2, 1, 3, 0)):
        self.peers, self.rows, self.block, self.buf, self.sems = peers, rows, block, buf, sems
        self.away = [s for s in parts if s]
        self.stays = 0 in parts
        self.n = SEQ // CHUNKS

    def ends(self, s, first, count):
        f = self.block.shape[1]
        mine = pl.ds(pl.multiple_of(self.peers.r * SEQ + first * self.n, self.n), count * self.n)
        return self.rows.at[pl.ds(first * self.n, count * self.n), pl.ds(s * f, f)], self.block.at[mine, :]

    def copy(self, s, k):
        return send(self.peers, 4 - s, *self.ends(s, k, 1), self.sems.at[0, s, k], self.sems.at[1, s, k])

    def load(self):
        return pltpu.make_async_copy(self.ends(0, 0, CHUNKS)[0], self.buf, self.sems.at[0, 0, 0])

    def store(self):
        src, dst = self.ends(0, 0, CHUNKS)
        return pltpu.make_async_copy(src if self.buf is None else self.buf, dst, self.sems.at[1, 0, 0])

    def start(self, *chunks):
        for k in chunks:
            for s in self.away:
                self.copy(s, k).start()

    def settle(self):
        self.load().wait()
        self.store().start()

    def finish(self):
        if self.stays:
            self.store().wait()
        for k in range(CHUNKS):
            for s in self.away:
                self.copy(s, k).wait()


def ff_down_bwd_kernel(
    r2_ref, wd_ref, act_ref, slope_ref, out, out_block, gp_ref, bu_ref, kept_ref,
    gfed, out_own, stage, land, corner, land_corner, f_sems, o_sems,
):
    j = pl.program_id(0)
    peers = Peers()
    outward = Outward(peers, out, out_block, out_own, o_sems, (2, 0))
    fold = Fold(peers, ORDER, stage, land, corner, land_corner, f_sems)

    @pl.when(j == 0)
    def _():
        peers.hello(ALL_PEERS)
        outward.load().start()

        def body(rows):
            gfed[rows, :] = r2_ref[rows, :].astype(BF)

        row_blocks(body)
        peers.meet(ALL_PEERS)
        outward.start(*range(CHUNKS))

    bsum = jnp.zeros((1, bu_ref.shape[2]), F32)
    for i in range(SEQ // 256):
        rows = slice(i * 256, (i + 1) * 256)
        g = (mm_t(gfed[rows, :], wd_ref[...]) * slope_ref[rows, :].astype(F32)).astype(BF)
        gp_ref[rows, :] = g
        bsum += jnp.sum(g.astype(F32), axis=0, keepdims=True)
    bu_ref[0] = bsum
    fold.before(j)
    stage[lax.rem(j, 2)] = tmm(act_ref[...], gfed[...]).astype(BF)
    fold.after(j, {t: kept_ref.at[0] for t in (0, 2, 4)})

    @pl.when(j == 1)
    def _():
        outward.settle()

    @pl.when(j == 7)
    def _():
        fold.finish()
        outward.finish()


def kept_spec(a, b):
    return pl.BlockSpec((1, a, b), lambda j: (jnp.maximum(j - 5, 0), 0, 0))


def ff_down_bwd(r2, wd, act, slope, out):
    units, width = wd.shape
    n = units // 8
    return pl.pallas_call(
        ff_down_bwd_kernel,
        grid=(8,),
        in_specs=[
            const(SEQ, width),
            pl.BlockSpec((n, width), lambda j: (slot_at(j), 0)),
            pl.BlockSpec((SEQ, n), lambda j: (0, slot_at(j))),
            pl.BlockSpec((SEQ, n), lambda j: (0, slot_at(j))),
            ANY,
        ],
        out_specs=[
            ANY,
            pl.BlockSpec((SEQ, n), lambda j: (0, slot_at(j))),
            pl.BlockSpec((1, 1, n), lambda j: (slot_at(j), 0, 0)),
            kept_spec(n, width),
        ],
        out_shape=[
            jax.ShapeDtypeStruct((4 * SEQ, width // 4), BF),
            jax.ShapeDtypeStruct((SEQ, units), BF),
            jax.ShapeDtypeStruct((8, 1, n), F32),
            jax.ShapeDtypeStruct((3, n, width), BF),
        ],
        scratch_shapes=[
            pltpu.VMEM((SEQ, width), BF),
            pltpu.VMEM((SEQ, width // 4), BF),
            *Fold.scratch(n, width),
            sems_of_exchange(),
        ],
        compiler_params=pltpu.CompilerParams(vmem_limit_bytes=VMEM_LIMIT, collective_id=3, has_side_effects=True),
        name="ff_down_bwd",
    )(r2, wd, act, slope, out)


def ff_up_bwd_kernel(
    r2_ref, hlow_ref, gp_ref, wu_ref, normed1_ref, inv1_ref, vec_ref, out, out_block_in, kept_d,
    out_block, r1_ref, gattn_ref, vg_ref, kept_ref, own_ref,
    hlow_t, stage, land, corner, land_corner, f_sems, own_d, land_x, land_y, c_sems, o_sems,
):
    j = pl.program_id(0)
    peers = Peers()
    outward = Outward(peers, out, out_block, None, o_sems, (1, 3))
    fold = Fold(peers, ORDER, stage, land, corner, land_corner, f_sems)
    cross = Cross(peers, kept_d.at[1], kept_d.at[2], land_x, land_y, c_sems, 2)
    load = pltpu.make_async_copy(kept_d.at[0], own_d, c_sems.at[8])

    @pl.when(j == 0)
    def _():
        peers.hello(ALL_PEERS)
        load.start()
        r1_ref[...] = r2_ref[...]
        for i in range(SEQ // 256):
            rows = slice(i * 256, (i + 1) * 256)
            hlow_t[:, rows] = jnp.transpose(hlow_ref[rows, :])
        peers.meet(ALL_PEERS)
        cross.start()
        outward.start(*range(CHUNKS))

    fold.before(j)
    stage[lax.rem(j, 2)] = mm(hlow_t[...], gp_ref[...]).astype(BF)
    fold.after(j, {t: kept_ref.at[0] for t in (0, 2, 4)})

    @pl.when(j == 1)
    def _():
        cross.start(h=1)

    r1_ref[...] += mm_t(gp_ref[...], wu_ref[...])

    @pl.when(j == 7)
    def _():
        vg_ref[...] = jnp.zeros_like(vg_ref)

        def body(rows):
            gh = r1_ref[rows, :]
            normed = normed1_ref[rows, :]
            r1 = norm_rows_back(gh * vec_ref[1:2, :], normed, inv1_ref[rows, 0:1])
            r1_ref[rows, :] = r1
            low = r1.astype(BF)
            gattn_ref[rows, :] = low
            vg_ref[0:1, :] += jnp.sum(gh * normed, axis=0, keepdims=True)
            vg_ref[1:2, :] += jnp.sum(gh, axis=0, keepdims=True)
            vg_ref[2:3, :] += jnp.sum(low.astype(F32), axis=0, keepdims=True)

        row_blocks(body)
        load.wait()
        cross.finish(own_d, own_ref)
        fold.finish()
        outward.finish()


def ff_up_bwd(r2, hlow, gp, wu, normed1, inv1, vec, out, out_block, kept_d):
    width, units = wu.shape
    n = units // 8
    return pl.pallas_call(
        ff_up_bwd_kernel,
        grid=(8,),
        in_specs=[
            const(SEQ, width),
            const(SEQ, width),
            pl.BlockSpec((SEQ, n), lambda j: (0, slot_at(j))),
            pl.BlockSpec((width, n), lambda j: (0, slot_at(j))),
            const(SEQ, width),
            const(SEQ, 128),
            const(8, width),
            ANY,
            ANY,
            ANY,
        ],
        out_specs=[
            ANY,
            const(SEQ, width),
            const(SEQ, width),
            const(8, width),
            kept_spec(width, n),
            const(n, width),
        ],
        out_shape=[
            jax.ShapeDtypeStruct(out_block.shape, BF),
            jax.ShapeDtypeStruct((SEQ, width), F32),
            jax.ShapeDtypeStruct((SEQ, width), BF),
            jax.ShapeDtypeStruct((8, width), F32),
            jax.ShapeDtypeStruct((3, width, n), BF),
            jax.ShapeDtypeStruct((n, width), BF),
        ],
        input_output_aliases={8: 0},
        scratch_shapes=[
            pltpu.VMEM((width, SEQ), BF),
            *Fold.scratch(width, n),
            pltpu.VMEM((n, width), BF),
            pltpu.VMEM((n, width), BF),
            pltpu.VMEM((n, width), BF),
            DMA((9,)),
            sems_of_exchange(),
        ],
        compiler_params=pltpu.CompilerParams(vmem_limit_bytes=VMEM_LIMIT, collective_id=4, has_side_effects=True),
        name="ff_up_bwd",
    )(r2, hlow, gp, wu, normed1, inv1, vec, out, out_block, kept_d)


def attend_bwd_kernel(
    gattn_ref, wo_ref, att_ref, qkv_ref, linv_ref, p_ref, x_ref, att_all, tot_d, kept_u,
    g_ref, gsum_ref, tot_q, tot_o, down_ref, up_ref,
    x_t, ds_ref,
    q_stage, q_land, q_corner, q_land_corner, q_sems,
    q_kept, q_x, q_y, q_c, o_total, o_land, o_kept, o_land_corner, o_x, o_y, o_sems, o_c,
    zd_land, zd_sems, own_u, land_x, land_y, c_sems, tot_u, zu_land, zu_sems,
):
    j = pl.program_id(0)
    peers = Peers()
    fold_q = Fold(peers, PAIRS, q_stage, q_land, q_corner, q_land_corner, q_sems)
    whole_o = Whole(peers, o_total, o_land, o_kept, o_land_corner, o_x, o_y, o_sems, o_c)
    cross_q = Cross(peers, q_kept.at[1], q_kept.at[2], q_x, q_y, q_c)
    deal_d = Deal(peers, tot_d, False, zd_land, zd_sems)
    cross_u = Cross(peers, kept_u.at[1], kept_u.at[2], land_x, land_y, c_sems)
    deal_u = Deal(peers, tot_u, True, zu_land, zu_sems)
    load_u = pltpu.make_async_copy(kept_u.at[0], own_u, c_sems.at[4])

    @pl.when(j == 0)
    def _():
        load_u.start()
        peers.hello(ALL_PEERS)
        f = x_ref.shape[2]
        for s in range(4):
            x_t[s * f : (s + 1) * f, :] = jnp.transpose(x_ref[s])
        load_u.wait()
        peers.meet(ALL_PEERS)
        cross_u.start()
        deal_d.start()
        o_total[...] = tmm(att_all[...], gattn_ref[...]).astype(BF)
        whole_o.start()

    @pl.when(j == 1)
    def _():
        whole_o.corner()

    @pl.when(j == 3)
    def _():
        whole_o.sides()

    @pl.when(j == 6)
    def _():
        whole_o.finish(tot_o)

    @pl.when(j == 4)
    def _():
        cross_u.finish(own_u, tot_u)
        deal_u.start()
        deal_d.finish(down_ref)

    lane = lax.broadcasted_iota(jnp.int32, (SEQ, 128), 1)
    scale = HD ** (-0.5)
    fold_q.before(j)
    q = qkv_ref[:, 0:128]
    k = qkv_ref[:, 128:256]
    v = qkv_ref[:, 256:384]
    do = mm_t(gattn_ref[...], wo_ref[...]).astype(BF).astype(F32) * linv_ref[...]
    prod = do * att_ref[...].astype(F32)
    dob = do.astype(BF)
    q_t = jnp.transpose(q)
    k_t = jnp.transpose(k)
    do_t = jnp.transpose(dob)
    dq_t, dk_t, dv_t = [], [], []
    for h in range(2):
        mine = (lane < HD) if h == 0 else (lane >= HD)
        delta = jnp.sum(jnp.where(mine, prod, 0.0), axis=1, keepdims=True)
        dom = jnp.where(mine, dob, jnp.zeros_like(dob))
        for i in range(SEQ // QB):
            rows = slice(i * QB, (i + 1) * QB)
            dp = mm_t(dom[rows], v)
            ds_ref[h, rows, :] = (p_ref[h, rows, :].astype(F32) * (dp - delta[rows])).astype(BF)
        feats = slice(h * HD, (h + 1) * HD)
        dq_t.append(mm_t(k_t[feats], ds_ref[h]))
        dk_t.append(mm(q_t[feats], ds_ref[h]))
        dv_t.append(mm(do_t[feats], p_ref[h]))
    g_ref[:, 0:128] = (jnp.transpose(jnp.concatenate(dq_t, 0)) * scale).astype(BF)
    g_ref[:, 128:256] = (jnp.transpose(jnp.concatenate(dk_t, 0)) * scale).astype(BF)
    g_ref[:, 256:384] = jnp.transpose(jnp.concatenate(dv_t, 0)).astype(BF)
    gsum_ref[0] = jnp.sum(g_ref[...].astype(F32), axis=0, keepdims=True)
    q_stage[lax.rem(j, 2)] = mm(x_t[...], g_ref[...]).astype(BF)
    fold_q.after(j, {t: q_kept.at[t // 2] for t in (0, 2, 4)})

    @pl.when(j == PAIRS.index(2))
    def _():
        cross_q.start("x")

    @pl.when(j == PAIRS.index(4))
    def _():
        cross_q.start("y")

    @pl.when(j == 7)
    def _():
        deal_u.finish(up_ref)
        fold_q.finish()
        cross_q.finish(q_kept.at[0], tot_q)


def attend_bwd(gattn, wo, att, qkv, linv, p, x, tot_d, kept_u):
    width = wo.shape[1]
    heads = 128
    n = tot_d.shape[0]
    return pl.pallas_call(
        attend_bwd_kernel,
        grid=(8,),
        in_specs=[
            const(SEQ, width),
            pl.BlockSpec((heads, width), lambda j: (pair_at(j), 0)),
            pl.BlockSpec((SEQ, heads), lambda j: (0, pair_at(j))),
            pl.BlockSpec((SEQ, 3 * heads), lambda j: (0, pair_at(j))),
            pl.BlockSpec((SEQ, heads), lambda j: (0, pair_at(j))),
            pl.BlockSpec((2, SEQ, SEQ), lambda j: (pair_at(j), 0, 0)),
            const(*x.shape),
            const(SEQ, width),
            const(n, width),
            ANY,
        ],
        out_specs=[
            pl.BlockSpec((SEQ, 3 * heads), lambda j: (0, pair_at(j))),
            pl.BlockSpec((1, 1, 3 * heads), lambda j: (pair_at(j), 0, 0)),
            const(width, 3 * heads),
            const(heads, width),
            const(n, width // 4),
            const(width // 4, n),
        ],
        out_shape=[
            jax.ShapeDtypeStruct((SEQ, 24 * heads), BF),
            jax.ShapeDtypeStruct((8, 1, 3 * heads), F32),
            jax.ShapeDtypeStruct((width, 3 * heads), BF),
            jax.ShapeDtypeStruct((heads, width), BF),
            jax.ShapeDtypeStruct((n, width // 4), BF),
            jax.ShapeDtypeStruct((width // 4, n), BF),
        ],
        scratch_shapes=[
            pltpu.VMEM((width, SEQ), BF),
            pltpu.VMEM((2, SEQ, SEQ), BF),
            *Fold.scratch(width, 3 * heads),
            pltpu.VMEM((3, width, 3 * heads), BF),
            pltpu.VMEM((width, 3 * heads), BF),
            pltpu.VMEM((width, 3 * heads), BF),
            DMA((4,)),
            *Whole.scratch(heads, width),
            pltpu.VMEM((3, n, width // 4), BF),
            DMA((6,)),
            pltpu.VMEM((width, n), BF),
            pltpu.VMEM((width, n), BF),
            pltpu.VMEM((width, n), BF),
            DMA((5,)),
            pltpu.VMEM((width, n), BF),
            pltpu.VMEM((3, width // 4, n), BF),
            DMA((6,)),
        ],
        compiler_params=pltpu.CompilerParams(vmem_limit_bytes=VMEM_LIMIT, collective_id=5, has_side_effects=True),
        name="attend_bwd",
    )(gattn, wo, att, qkv, linv, p, x, att, tot_d, kept_u)


def last_kernel(
    tot_q, tot_o, own_d, own_u, g_part, u_part, vec1, vec2, g, w, r1,
    x_block, gq, go, gd, gu, slot_out, feat_ref,
    g_buf, w_buf, acc, xg, ld_sems,
    q_land, q_tmp, q_z, q_sum, o_land, o_tmp, o_z, o_sum,
    vec_ref, v1, v2, v3, l1, l2, l3, l4, v_own, v_sems, out_sems, s_sems,
):
    peers = Peers()
    outward = Outward(peers, xg, x_block, None, out_sems)
    deal_q = LineDeal(peers, tot_q, True, q_land, q_tmp, q_z)
    deal_o = LineDeal(peers, tot_o, False, o_land, o_tmp, o_z)
    loads = (
        pltpu.make_async_copy(w, w_buf, ld_sems.at[0]),
        pltpu.make_async_copy(g, g_buf, ld_sems.at[1]),
        pltpu.make_async_copy(r1, acc, ld_sems.at[2]),
    )
    peers.hello(ALL_PEERS)
    for c in loads:
        c.start()

    def products(k):
        rows = slice(k * (SEQ // CHUNKS), (k + 1) * (SEQ // CHUNKS))
        xg[rows, :] = (mm_t(g_buf[rows, :], w_buf[...]) + acc[rows, :]).astype(BF)
        outward.start(k)

    vec_ref[...] = jnp.zeros_like(vec_ref)
    heads3, units = g_part.shape[2], u_part.shape[2]
    for k, t in enumerate((0, 4, 2, 6, 1, 5, 3, 7)):
        k = k if k < 4 else k + 8
        for i in range(heads3 // 128):
            vec_ref[k, i : i + 1, :] = g_part[t, :, i * 128 : (i + 1) * 128]
        for i in range(units // 128):
            at = heads3 // 128 + i
            vec_ref[k, at : at + 1, :] = u_part[t, :, i * 128 : (i + 1) * 128]
    f = vec1.shape[1] // 4
    rows = [(vec1, 2), (vec1, 0), (vec1, 1), (vec2, 2), (vec2, 0), (vec2, 1)]
    for k in range(4):
        for v, (ref, row) in enumerate(rows):
            for i in range(f // 128):
                at = v * (f // 128) + i
                first = k * f + i * 128
                vec_ref[4 + 2 * k + at // 8, at % 8 : at % 8 + 1, :] = ref[row : row + 1, first : first + 128]

    def rows_at(ref):
        n = ref.shape[0] // 4
        return lambda q: ref.at[pl.ds(pl.multiple_of(q * n, n), n), :]

    def cols_at(ref, first, n):
        return lambda q: ref.at[:, pl.ds(pl.multiple_of(first + q * n, n), n)]

    heads = q_sum.shape[1] // 3
    units = own_u.shape[1]
    spread_d = Spread(peers, own_d, rows_at(gd), s_sems.at[0])
    spread_u = Spread(peers, own_u, cols_at(gu, 0, units), s_sems.at[1])
    spread_o = Spread(peers, o_sum, rows_at(go), s_sems.at[2])
    spread_q = [
        Spread(peers, q_sum.at[:, pl.ds(i * heads, heads)], cols_at(gq, 4 * i * heads, heads), s_sems.at[3 + i])
        for i in range(3)
    ]
    spread_v = Spread(peers, v_own, lambda q: slot_out.at[q], s_sems.at[6])

    to_core = send(peers, "core", vec_ref.at[pl.ds(4, 12)], l1, v_sems.at[0], v_sems.at[1])
    to_x = send(peers, "x", v1.at[pl.ds(2, 10)], l2, v_sems.at[2], v_sems.at[3])
    to_y = send(peers, "y", v2.at[pl.ds(1, 11)], l3, v_sems.at[4], v_sems.at[5])
    to_rows = []
    for i in (1, 2, 3):
        to_rows.append(send(peers, i, v3.at[0], l4.at[i - 1, 0], v_sems.at[6 + 4 * i], v_sems.at[7 + 4 * i]))
        src = v3.at[pl.ds(4 + 2 * (4 - i), 2)]
        to_rows.append(send(peers, i, src, l4.at[i - 1, pl.ds(1, 2)], v_sems.at[8 + 4 * i], v_sems.at[9 + 4 * i]))

    peers.meet(ALL_PEERS)
    deal_o.start()
    deal_q.start()
    to_core.start()
    spread_d.start()
    spread_u.start()
    for c in loads:
        c.wait()
    products(0)
    deal_o.step(0)
    deal_q.step(0)
    products(1)
    to_core.wait()
    v1[0:4] = vec_ref[0:4] + l1[8:12]
    v1[4:12] = vec_ref[4:12] + l1[0:8]
    to_x.start()
    deal_o.step(1)
    deal_q.step(1)
    products(2)
    products(3)
    outward.store().start()
    to_x.wait()
    v2[0:2] = v1[0:2] + l2[0:2]
    v2[4:12] = v1[4:12] + l2[2:10]
    v2[2:4] = v1[2:4]
    to_y.start()
    spread_d.relay()
    spread_u.relay()
    deal_o.finish(o_sum)
    spread_o.start()
    deal_q.finish(q_sum)
    for sp in spread_q:
        sp.start()
    to_y.wait()
    v3[0:1] = v2[0:1] + l3[0:1]
    v3[4:12] = v2[4:12] + l3[3:11]
    for c in to_rows:
        c.start()
    spread_o.relay()
    for sp in spread_q:
        sp.relay()
    for c in to_rows:
        c.wait()
    v_own[...] = v3[0] + l4[0, 0] + l4[1, 0] + l4[2, 0]
    feat_ref[...] = v3[4:6] + l4[0, 1:3] + l4[1, 1:3] + l4[2, 1:3]
    spread_v.start()
    spread_v.relay()
    for sp in (spread_d, spread_u, spread_o, spread_v, *spread_q):
        sp.finish()
    outward.finish()


def last(tot_q, tot_o, own_d, own_u, g_part, u_part, vec1, vec2, g, w, r1):
    width = r1.shape[1]
    part = width // 4
    n = own_d.shape[0]
    heads = tot_o.shape[0]
    vmem = pl.BlockSpec(memory_space=pltpu.VMEM)

    def bufs(a, b, by_rows):
        piece = (a // 4, b) if by_rows else (a, b // 4)
        return [pltpu.VMEM((2, 3, *piece), BF), pltpu.VMEM((2, 2, *piece), BF), DMA((12,)), pltpu.VMEM(piece, BF)]

    return pl.pallas_call(
        last_kernel,
        in_specs=[vmem] * 8 + [ANY] * 3,
        out_specs=[ANY, ANY, ANY, ANY, ANY, ANY, vmem],
        out_shape=[
            jax.ShapeDtypeStruct((4 * SEQ, part), BF),
            jax.ShapeDtypeStruct((part, 12 * heads), BF),
            jax.ShapeDtypeStruct((4 * heads, part), BF),
            jax.ShapeDtypeStruct((4 * n, part), BF),
            jax.ShapeDtypeStruct((part, 4 * n), BF),
            jax.ShapeDtypeStruct((4, 8, 128), F32),
            jax.ShapeDtypeStruct((2, 8, 128), F32),
        ],
        scratch_shapes=[
            pltpu.VMEM((SEQ, 24 * heads), BF),
            pltpu.VMEM((width, 24 * heads), BF),
            pltpu.VMEM((SEQ, width), F32),
            pltpu.VMEM((SEQ, width), BF),
            DMA((3,)),
            *bufs(width, 3 * heads, True),
            *bufs(heads, width, False),
            pltpu.VMEM((16, 8, 128), F32),
            pltpu.VMEM((12, 8, 128), F32),
            pltpu.VMEM((12, 8, 128), F32),
            pltpu.VMEM((12, 8, 128), F32),
            pltpu.VMEM((12, 8, 128), F32),
            pltpu.VMEM((10, 8, 128), F32),
            pltpu.VMEM((11, 8, 128), F32),
            pltpu.VMEM((3, 3, 8, 128), F32),
            pltpu.VMEM((8, 128), F32),
            DMA((24,)),
            sems_of_exchange(),
            DMA((7, 7)),
        ],
        compiler_params=pltpu.CompilerParams(vmem_limit_bytes=VMEM_LIMIT, collective_id=6, has_side_effects=True),
        name="last",
    )(tot_q, tot_o, own_d, own_u, g_part, u_part, vec1, vec2, g, w, r1)


def whole_sequences(
    tokens, segments, w_query, b_query, w_key, w_value, b_value, w_out, b_out, norm1_gain, norm1_shift,
    w_up, b_up, w_down, b_down, norm2_gain, norm2_shift, cotangent,
):
    R = lax.axis_size("row")
    feat = tokens.shape[1]
    hq = b_query.shape[0] // 4
    unit = b_up.shape[0] // 4
    vectors = (b_out, norm1_gain, norm1_shift, b_down, norm2_gain, norm2_shift, b_query, b_value, b_up)
    size = sum(v.shape[0] for v in vectors)
    first_at, packed = 0, 0.0
    for v in vectors:
        packed += jnp.pad(v.astype(F32), (first_at, size - first_at - v.shape[0]))
        first_at += v.shape[0]
    vectors = packed.reshape(1, -1)
    x, w_qkv, wo, wu, wd, feat_all, b_slot, seg = first(
        tokens,
        segments.reshape(2, 8, 128),
        (w_query, w_key, w_value, w_out, w_up, w_down),
        vectors,
    )

    qkv, att, prob, linv, wo, wu, wd, cot_first = attend_fwd(x, w_qkv, b_slot, seg, cotangent, wo, wu, wd)
    wu, wd, act, slope, hidden_low, normed1, inv1, output, grad_r2, vg2 = ff_fwd(
        x, att, wo, feat_all, b_slot, cotangent, cot_first, wu, wd
    )

    out_block, grad_pre, bu_part, kept_d = ff_down_bwd(grad_r2, wd, act, slope, output)
    out_block, grad_r1, grad_attn, vg1, kept_u, tot_d = ff_up_bwd(
        grad_r2, hidden_low, grad_pre, wu, normed1, inv1, feat_all, output, out_block, kept_d
    )
    g_qkv, g_part, tot_q, tot_o, own_d, own_u = attend_bwd(
        grad_attn, wo, att, qkv, linv, prob, x, tot_d, kept_u
    )

    x_grad_block, gq, go, gd, gu, slot_sum, own = last(
        tot_q, tot_o, own_d, own_u, g_part, bu_part, vg1, vg2, g_qkv, w_qkv, grad_r1
    )
    wq_grad, wk_grad, wv_grad = [gq[:, i * 4 * hq : (i + 1) * 4 * hq].astype(F32) for i in range(3)]
    w_out_grad, w_up_grad, w_down_grad = go.astype(F32), gu.astype(F32), gd.astype(F32)
    slot_sum = slot_sum.reshape(4, 1024)
    bq_grad = slot_sum[:, :hq].reshape(-1)
    bv_grad = slot_sum[:, 2 * hq : 3 * hq].reshape(-1)
    bu_grad = slot_sum[:, 3 * hq : 3 * hq + unit].reshape(-1)
    own = own.reshape(-1)[: 6 * feat].reshape(6, feat)
    return (
        out_block, x_grad_block, wq_grad, bq_grad, wk_grad, wv_grad, bv_grad, w_out_grad, own[0], own[1], own[2],
        w_up_grad, bu_grad, w_down_grad, own[3], own[4], own[5],
    )


def tokens_cols(source):
    return lax.all_gather(source, "col", axis=0, tiled=True)


def tokens_rows(source):
    return lax.all_gather(source, "row", axis=0, tiled=True)


def product(row_piece, weight, flipped):
    if flipped:
        return lax.dot_general(
            row_piece, weight, (((1,), (1,)), ((), ())), preferred_element_type=jnp.float32
        )
    return jnp.dot(row_piece, weight, preferred_element_type=jnp.float32)


def outer_sum(left, right):
    return lax.dot_general(
        left, right, (((0,), (0,)), ((), ())), preferred_element_type=jnp.float32
    )


def settle_rows(gathered, weight, flipped, own_rows):

    def product_term(first_row, row_count):
        return product(gathered, weight, flipped)

    return lax.psum_scatter(
        product_term(jnp.int32(0), own_rows * lax.axis_size("row")),
        "row",
        scatter_dimension=0,
        tiled=True,
    )


def settle_cols(gathered, weight, flipped, own_rows):

    def product_term(first_row, row_count):
        return product(gathered, weight, flipped)

    return lax.psum_scatter(
        product_term(jnp.int32(0), own_rows * lax.axis_size("col")),
        "col",
        scatter_dimension=0,
        tiled=True,
    )


def row_sums(first_part, second_part):
    return lax.psum((jnp.sum(first_part, axis=1), jnp.sum(second_part, axis=1)), "row")


def norm_forward(residual, norm_gain, norm_shift):
    total_sum, square_sum = row_sums(residual, residual * residual)
    row_mean = (total_sum / WIDTH)[:, None]
    variance = (square_sum / WIDTH)[:, None] - row_mean * row_mean
    inv_std = lax.rsqrt(variance + NORM_EPS)
    normed = (residual - row_mean) * inv_std
    return (normed * norm_gain + norm_shift, normed, inv_std)


def norm_backward(grad_in, normed, inv_std, norm_gain):
    grad_norm = grad_in * norm_gain
    total_sum, cross_sum = row_sums(grad_norm, grad_norm * normed)
    grad_resid = inv_std * (grad_norm - total_sum[:, None] / WIDTH - normed * cross_sum[:, None] / WIDTH)
    return (grad_resid, jnp.sum(grad_in * normed, axis=0), jnp.sum(grad_in, axis=0))


def split_heads(array, seq_count):
    return array.reshape(seq_count, SEQ, array.shape[1] // HD, HD)


def pair_scores(queries, key_heads, segment_ids):
    position = jnp.arange(SEQ)
    same_doc = (segment_ids[:, None] == segment_ids[None, :]) & (segment_ids[None, :] != 0)
    allowed = same_doc | (position[:, None] == position[None, :])
    raw_scores = jnp.einsum(
        "qhd,khd->hqk", queries, key_heads, preferred_element_type=jnp.float32
    ) * HD ** (-0.5)
    return jnp.where(allowed[None], raw_scores, -1000000000.0)


def attend_forward(source):
    queries, key_heads, values, segment_ids = source
    scores = pair_scores(queries, key_heads, segment_ids)
    top_score = jnp.max(scores, axis=2, keepdims=True)
    exp_scores = jnp.exp(scores - top_score)
    total_sum = jnp.sum(exp_scores, axis=2, keepdims=True)
    soft_low = (exp_scores / total_sum).astype(jnp.bfloat16)
    attended = jnp.einsum("hqk,khd->qhd", soft_low, values, preferred_element_type=jnp.float32)
    return (attended.astype(jnp.bfloat16), (top_score + jnp.log(total_sum))[:, :, 0])


def attend_backward(source):
    queries, key_heads, values, segment_ids, grad_out, log_total = source
    scores = pair_scores(queries, key_heads, segment_ids)
    soft_weights = jnp.exp(scores - log_total[:, :, None])
    soft_low = soft_weights.astype(jnp.bfloat16)
    grad_values = jnp.einsum("hqk,qhd->khd", soft_low, grad_out, preferred_element_type=jnp.float32)
    grad_soft = jnp.einsum("qhd,khd->hqk", grad_out, values, preferred_element_type=jnp.float32)
    grad_scores = soft_weights * (
        grad_soft - jnp.sum(soft_weights * grad_soft, axis=2, keepdims=True)
    )
    grad_scores = grad_scores.astype(jnp.bfloat16)
    scale_factor = HD ** (-0.5)
    grad_queries = (
        jnp.einsum("hqk,khd->qhd", grad_scores, key_heads, preferred_element_type=jnp.float32)
        * scale_factor
    )
    grad_keys = (
        jnp.einsum("hqk,qhd->khd", grad_scores, queries, preferred_element_type=jnp.float32)
        * scale_factor
    )
    return (
        grad_queries.astype(jnp.bfloat16),
        grad_keys.astype(jnp.bfloat16),
        grad_values.astype(jnp.bfloat16),
    )


def split_heads_plan(
    tokens,
    segments,
    w_query,
    b_query,
    w_key,
    w_value,
    b_value,
    w_out,
    b_out,
    norm1_gain,
    norm1_shift,
    w_up,
    b_up,
    w_down,
    b_down,
    norm2_gain,
    norm2_shift,
    cotangent,
):
    rows_b = tokens.shape[0]
    rows_a = segments.shape[0]
    head_cols = w_query.shape[1]
    seq_count = rows_a // SEQ
    segment_seqs = segments.reshape(seq_count, SEQ)
    gathered_x = tokens_cols(tokens)
    stacked = jnp.concatenate([w_query, w_key, w_value], axis=1)
    projected = settle_rows(gathered_x, stacked, False, rows_a)
    queries = (projected[:, :head_cols] + b_query).astype(jnp.bfloat16)
    key_heads = projected[:, head_cols : 2 * head_cols].astype(jnp.bfloat16)
    values = (projected[:, 2 * head_cols :] + b_value).astype(jnp.bfloat16)
    query_seqs = split_heads(queries, seq_count)
    key_seqs = split_heads(key_heads, seq_count)
    value_seqs = split_heads(values, seq_count)
    attended, log_total = lax.map(attend_forward, (query_seqs, key_seqs, value_seqs, segment_seqs))
    attended = attended.reshape(rows_a, head_cols)
    gathered_o = tokens_rows(attended)
    attn_out = settle_cols(gathered_o, w_out, False, rows_b) + b_out
    hidden, normed1, inv_std1 = norm_forward(
        tokens.astype(jnp.float32) + attn_out, norm1_gain, norm1_shift
    )
    hidden_low = hidden.astype(jnp.bfloat16)
    gathered_h = tokens_cols(hidden_low)
    pre_act = settle_rows(gathered_h, w_up, False, rows_a) + b_up
    active = gelu_exact(pre_act).astype(jnp.bfloat16)
    gathered_a = tokens_rows(active)
    fed = settle_cols(gathered_a, w_down, False, rows_b) + b_down
    output, normed2, inv_std2 = norm_forward(hidden + fed, norm2_gain, norm2_shift)
    grad_r2, grad_gain2, grad_shift2 = norm_backward(
        cotangent.astype(jnp.float32), normed2, inv_std2, norm2_gain
    )
    grad_fed = grad_r2.astype(jnp.bfloat16)
    gathered_f = tokens_cols(grad_fed)
    grad_w_down = outer_sum(gathered_a, gathered_f)
    grad_active = settle_rows(gathered_f, w_down, True, rows_a)
    unused_out, slope_pull = jax.vjp(gelu_exact, pre_act)
    grad_pre = slope_pull(grad_active)[0].astype(jnp.bfloat16)
    gathered_p = tokens_rows(grad_pre)
    grad_w_up = outer_sum(gathered_h, gathered_p)
    grad_from_ff = settle_cols(gathered_p, w_up, True, rows_b)
    bias_up_part = jnp.sum(grad_pre.astype(jnp.float32), axis=0)
    bias_down_part = jnp.sum(grad_fed.astype(jnp.float32), axis=0)
    grad_r1, grad_gain1, grad_shift1 = norm_backward(
        grad_from_ff + grad_r2, normed1, inv_std1, norm1_gain
    )
    grad_attn = grad_r1.astype(jnp.bfloat16)
    gathered_d = tokens_cols(grad_attn)
    grad_w_out = outer_sum(gathered_o, gathered_d)
    grad_attended = settle_rows(gathered_d, w_out, True, rows_a).astype(jnp.bfloat16)
    grad_q, grad_k, grad_v = lax.map(
        attend_backward,
        (
            query_seqs,
            key_seqs,
            value_seqs,
            segment_seqs,
            split_heads(grad_attended, seq_count),
            log_total,
        ),
    )
    grad_q = grad_q.reshape(rows_a, head_cols)
    grad_k = grad_k.reshape(rows_a, head_cols)
    grad_v = grad_v.reshape(rows_a, head_cols)
    grad_proj = jnp.concatenate([grad_q, grad_k, grad_v], axis=1)
    gathered_g = tokens_rows(grad_proj)
    grad_stacked = outer_sum(gathered_x, gathered_g)
    tokens_grad = settle_cols(gathered_g, stacked, True, rows_b) + grad_r1
    bias_q, bias_v, bias_up = lax.psum(
        (
            jnp.sum(grad_q.astype(jnp.float32), axis=0),
            jnp.sum(grad_v.astype(jnp.float32), axis=0),
            bias_up_part,
        ),
        ("dp", "row"),
    )
    bias_out, bias_down, gain_one, shift_one, gain_two, shift_two = lax.psum(
        (
            jnp.sum(grad_attn.astype(jnp.float32), axis=0),
            bias_down_part,
            grad_gain1,
            grad_shift1,
            grad_gain2,
            grad_shift2,
        ),
        ("dp", "col"),
    )
    sum_stacked, sum_out, sum_up, sum_down = (
        lax.psum(grad_stacked.astype(jnp.bfloat16), "dp").astype(jnp.float32),
        lax.psum(grad_w_out.astype(jnp.bfloat16), "dp").astype(jnp.float32),
        lax.psum(grad_w_up.astype(jnp.bfloat16), "dp").astype(jnp.float32),
        lax.psum(grad_w_down.astype(jnp.bfloat16), "dp").astype(jnp.float32),
    )
    return (
        output.astype(jnp.bfloat16),
        tokens_grad.astype(jnp.bfloat16),
        sum_stacked[:, :head_cols],
        bias_q,
        sum_stacked[:, head_cols : 2 * head_cols],
        sum_stacked[:, 2 * head_cols :],
        bias_v,
        sum_out,
        bias_out,
        gain_one,
        shift_one,
        sum_up,
        bias_up,
        sum_down,
        bias_down,
        gain_two,
        shift_two,
    )


def solution(mesh):
    dp, rows, cols = (mesh.shape[name] for name in ("dp", "row", "col"))
    whole = TOKENS // SEQ == dp * rows * cols and dp == 4 and cols == 2
    plan = whole_sequences if whole else split_heads_plan
    placed = (
        P(("dp", "col"), "row"),
        P(("dp", "row")),
        P("row", "col"),
        P("col"),
        P("row", "col"),
        P("row", "col"),
        P("col"),
        P("col", "row"),
        P("row"),
        P("row"),
        P("row"),
        P("row", "col"),
        P("col"),
        P("col", "row"),
        P("row"),
        P("row"),
        P("row"),
        P(("dp", "col"), "row"),
    )
    return jax.shard_map(
        plan,
        mesh=mesh,
        in_specs=placed,
        out_specs=(
            P(("dp", "col"), "row"),
            P(("dp", "col"), "row"),
            P("row", "col"),
            P("col"),
            P("row", "col"),
            P("row", "col"),
            P("col"),
            P("col", "row"),
            P("row"),
            P("row"),
            P("row"),
            P("row", "col"),
            P("col"),
            P("col", "row"),
            P("row"),
            P("row"),
            P("row"),
        ),
        check_vma=False,
    )
```
